32 devices in a mesh: occi: 4 (over z), occj: 8 (over y, x, core).
Axes of the slice: x: 2, y: 2, z: 4, core: 2. Of those that a mesh axis runs over, the one named last changes fastest.
Arguments:
- amplitudes: float32 [8, 8, 512, 512], P('occi', 'occj'), may hold values from -6 to 6
- vectors: bfloat16 [3, 512, 512], P(None, 'occj'), may hold values from -0.25 to 0.25
- occupied_fock_block: bfloat16 [8, 8], replicated, may hold values from -2 to 2
- occ_energy: float32 [8], replicated, may hold values from -3 to -0.3
- vir_energy: float32 [512], replicated, may hold values from 0.2 to 4
Outputs:
- updated: float32 [8, 8, 512, 512], P('occi', 'occj')
The draws below stay inside these ranges and needn't reach their ends.
All inputs are finite; a program needn't handle non-finite values.
Results may differ from the reference program's by a relative error of at most 0.0028.
Values may be sent and summed in bfloat16 or wider, within the bound.
No kernel may reach another device: no remote copies, remote signals or barrier semaphores. Data moves between devices by JAX's collectives and lax.ppermute only.
A program may use at most 64 MiB of HBM per device.

```python
import jax
import jax.numpy as jnp
from jax import lax

V = 512
NCHOL = 3
ITERS = 2
NO = 8


def levels(own_key, extent, cuts, low, largest):
    gain = 1.0
    for dim, parts in cuts:
        steps = jax.random.uniform(jax.random.fold_in(jax.random.fold_in(own_key, 6), dim), (parts,), jnp.float32, low / len(cuts), largest / len(cuts))
        gain = gain * jnp.repeat(jnp.exp(steps), extent[dim] // parts).reshape((-1,) + (1,) * (len(extent) - 1 - dim))
    return gain


def gaussian(rng, shape, deviation, most, split=(), kind=jnp.bfloat16):
    loudness = levels(rng, shape, split, -0.22, 0.18) if split else 1.0
    values = jax.random.normal(rng, shape, jnp.float32) * deviation * loudness
    return jnp.minimum(jnp.maximum(values, -most), most).astype(kind)


def setup_inputs(seed: int = 0) -> dict:
    streams_of = jax.random.split(jax.random.key(seed), 6)
    amplitudes = gaussian(streams_of[0], (NO, NO, V, V), 1.0, 6.0, ((0, 4), (1, 8)), jnp.float32)
    vectors = gaussian(streams_of[1], (NCHOL, V, V), V ** -0.5, 0.25, ((1, 8),))
    occupied_fock_block = gaussian(streams_of[2], (NO, NO), NO ** -0.5, 2.0)
    occ_energy = jnp.clip(jax.random.uniform(streams_of[3], (NO,), jnp.float32, -3.0, -0.3), -3.0, -0.3)
    vir_energy = jnp.clip(jax.random.uniform(streams_of[4], (V,), jnp.float32, 0.2, 4.0), 0.2, 4.0)
    return {"amplitudes": amplitudes, "vectors": vectors, "occupied_fock_block": occupied_fock_block, "occ_energy": occ_energy, "vir_energy": vir_energy}


def round_trip(values):
    return lax.optimization_barrier(values.astype(jnp.bfloat16)).astype(jnp.float32)


def half_residual(reduced_precision_copy, occupied_fock_block, vectors):
    vec_full = vectors.astype(jnp.float32)
    rounded_wide = reduced_precision_copy.astype(jnp.float32)
    flattened_row_list = rounded_wide.reshape(reduced_precision_copy.shape[0], -1)
    fock_wide = occupied_fock_block.astype(jnp.float32)

    def one_row(position):
        pair_rows = rounded_wide[position]
        running = jnp.zeros(pair_rows.shape, jnp.float32)
        for vector_id in range(NCHOL):
            single = vec_full[vector_id]
            inner = jnp.einsum("jcd,bd->jcb", pair_rows, single, precision=lax.Precision.HIGHEST)
            inner = round_trip(inner)
            running = running + jnp.einsum("ac,jcb->jab", single, inner, precision=lax.Precision.HIGHEST)
        ladder = round_trip(running)
        column = lax.dynamic_slice_in_dim(fock_wide, position, 1, 1)
        mixed = -jnp.dot(column[:, 0][None, :], flattened_row_list, precision=lax.Precision.HIGHEST).reshape(pair_rows.shape)
        return (ladder + mixed).astype(jnp.bfloat16)

    return lax.map(one_row, jnp.arange(NO, dtype=jnp.int32))


def reference(amplitudes, vectors, occupied_fock_block, occ_energy, vir_energy):
    denominator = ((occ_energy[:, None, None, None] + occ_energy[None, :, None, None])
                   - vir_energy[None, None, :, None]) - vir_energy[None, None, None, :]
    current = amplitudes
    for iteration in range(ITERS):
        reduced_precision_copy = current.astype(jnp.bfloat16)
        half = half_residual(reduced_precision_copy, occupied_fock_block, vectors).astype(jnp.float32)
        residual = half + jnp.transpose(half, (1, 0, 3, 2))
        current = current + residual / denominator
    return current
```

```python
import functools
import math

import jax
import jax.numpy as jnp
from jax import lax
from jax.experimental import pallas as pl
from jax.experimental.pallas import tpu as pltpu
from jax.sharding import PartitionSpec as P

VMEM = pl.BlockSpec(memory_space=pltpu.VMEM)
SMEM = pl.BlockSpec(memory_space=pltpu.SMEM)
PARAMS = pltpu.CompilerParams(vmem_limit_bytes=50 * 2**20)
WIDE = jnp.float32
NARROW = jnp.bfloat16


class Tiles:
    def __init__(self, devices, virtual):
        n = math.isqrt(2 * devices)
        assert n * n == 2 * devices and n % 2 == 0 and virtual % n == 0
        self.n = n
        self.edge = virtual // n
        self.rows = self.edge // 2
        self.above = [(a, b) for a in range(n) for b in range(a + 1, n)]
        self.diagonal = [(len(self.above) + k // 2, k % 2, k) for k in range(n)]

    def span(self, k):
        return slice(k * self.edge, (k + 1) * self.edge)

    def mirror_within(self, x):
        e, g = self.edge, self.rows
        parts = []
        for c in range(2):
            tile = jnp.concatenate([x[c * g:(c + 1) * g, :e], x[c * g:(c + 1) * g, e:]], axis=0).T
            parts.append(jnp.concatenate([tile[:g], tile[g:]], axis=1))
        return jnp.concatenate(parts, axis=0)

    def mirror_across(self, x):
        return jnp.concatenate([x[:, self.edge:], x[:, :self.edge]], axis=1)


def call(body, outs, scratch, flops, moved, *operands, specs, aliases=None):
    return pl.pallas_call(
        body,
        out_shape=outs,
        in_specs=specs,
        out_specs=jax.tree.map(lambda _: VMEM, outs),
        scratch_shapes=scratch,
        compiler_params=PARAMS,
        input_output_aliases=aliases or {},
        cost_estimate=pl.CostEstimate(flops=flops, bytes_accessed=moved, transcendentals=0),
    )(*operands)


def pack_pair(tiles, source, out, pair, mirrored=False):
    e, g = tiles.edge, tiles.rows
    straight, turned = (slice(e, None), slice(0, e)) if mirrored else (slice(0, e), slice(e, None))
    for d, (a, b) in enumerate(tiles.above):
        out[d, pair, :, straight] = source[tiles.span(a), tiles.span(b)].astype(NARROW)
        out[d, pair, :, turned] = source[tiles.span(b), tiles.span(a)].astype(WIDE).T.astype(NARROW)
    for d, c, k in tiles.diagonal:
        tile = source[tiles.span(k), tiles.span(k)]
        tile = tile.astype(WIDE).T.astype(NARROW) if mirrored else tile.astype(NARROW)
        out[d, pair, c * g:(c + 1) * g, :e] = tile[:g]
        out[d, pair, c * g:(c + 1) * g, e:] = tile[g:]


def unpack_pair(tiles, blocks, pair, put):
    e, g = tiles.edge, tiles.rows
    for d, (a, b) in enumerate(tiles.above):
        put(a, b, blocks[d, pair, :, :e].astype(WIDE))
        put(b, a, blocks[d, pair, :, e:].astype(WIDE).T)
    for d, c, k in tiles.diagonal:
        upper = blocks[d, pair, c * g:(c + 1) * g, :e]
        lower = blocks[d, pair, c * g:(c + 1) * g, e:]
        put(k, k, jnp.concatenate([upper, lower], axis=0).astype(WIDE))


def pack_kernel(tiles, source, out):
    for pair in range(source.shape[0]):
        pack_pair(tiles, source.at[pair], out, pair, mirrored=True)


def pack(tiles, devices, amplitudes):
    count = amplitudes.shape[0]
    out = jax.ShapeDtypeStruct((devices, count, tiles.edge, 2 * tiles.edge), NARROW)
    return call(functools.partial(pack_kernel, tiles), out, [], amplitudes.size, amplitudes.size * 6,
                amplitudes, specs=[VMEM])


def assemble(place, order, pieces, whole):
    k = 0
    for piece in pieces:
        rows = piece.shape[2]
        for block in range(piece.shape[0]):
            start = pl.multiple_of((place[1] ^ order[k]) * rows, rows)
            for single in range(piece.shape[1]):
                whole[single, pl.ds(start, rows), :] = piece[block, single]
            k += 1


def ladder_pair(matrix, whole, total):
    def one(single, carry):
        vector = whole[single]
        inner = lax.dot_general(matrix, vector, (((1,), (1,)), ((), ())), preferred_element_type=WIDE)
        term = jnp.dot(vector, inner.astype(NARROW), preferred_element_type=WIDE)
        total[...] += term
        return carry

    total[...] = jnp.zeros_like(total)
    lax.fori_loop(0, whole.shape[0], one, 0)


def first_ladder_kernel(tiles, order, place, source, low, high, out, whole, total):
    assemble(place, order, (low, high), whole)
    for pair in range(source.shape[0]):
        ladder_pair(source[pair].astype(NARROW), whole, total)
        pack_pair(tiles, total, out, pair)


def second_ladder_kernel(tiles, order, count, place, occ, source, blocks, row, column, low, high, out,
                         whole, total, matrix):
    assemble(place, order, (low, high), whole)
    for pair in range(count):
        def put(a, b, tile):
            matrix[tiles.span(a), tiles.span(b)] = tile.astype(NARROW)

        unpack_pair(tiles, blocks, pair, put)
        ladder_pair(matrix[...], whole, total)
        base = occ[place[0] * count + pair] + occ[place[1]]

        def finish(step, carry):
            at = pl.ds(pl.multiple_of(step * 16, 16), 16)
            own = base - row[at, :1] - column[...]
            out[pair, at, :] = (
                source[pair, at, :] + 2.0 * matrix[at, :].astype(WIDE) + (2.0 * total[at, :]) / own
            )
            return carry

        lax.fori_loop(0, total.shape[0] // 16, finish, 0)


def add_kernel(tiles, source, blocks, out):
    for pair in range(source.shape[0]):
        def put(a, b, tile):
            here = (pair, tiles.span(a), tiles.span(b))
            out[here] = source[here] + tile

        unpack_pair(tiles, blocks, pair, put)


def mix(place, fock, first, load, store, rows, width):
    total = fock.shape[0]
    strips = rows // 16

    def strip(step, carry):
        u = step // strips
        at = pl.ds(pl.multiple_of(lax.rem(step, strips) * 16, 16), 16)
        taken = [load(k // first, u, k % first, at) for k in range(total)]
        for k in range(total):
            column = (place[0] ^ (k // first)) * first + k % first
            result = None
            for m in range(total):
                line = (place[0] ^ (m // first)) * first + m % first
                term = (-fock[line, column]) * taken[m]
                result = term if result is None else result + term
            store(k // first, u, k % first, column, at, result)
        return carry

    lax.fori_loop(0, first * strips, strip, 0)


def half_kernel(tiles, groups, first, place, fock, ladder, *refs):
    held, out = refs[:groups], refs[groups:]

    def load(s, u, r, at):
        return held[s][u, r, at, :].astype(WIDE)

    def store(s, u, w, column, at, result):
        out[s][u, w, at, :] = (ladder[column, u, at, :].astype(WIDE) + result).astype(NARROW)

    mix(place, fock, first, load, store, tiles.edge, 2 * tiles.edge)


def with_mirror(tiles, place, x, finish):
    across = place[1] < len(tiles.above)

    @pl.when(across)
    def _():
        finish(tiles.mirror_across(x))

    @pl.when(jnp.logical_not(across))
    def _():
        finish(tiles.mirror_within(x))


def update_kernel(tiles, groups, first, place, fock, occ, sums, *refs):
    own, other = refs[:groups], refs[groups:2 * groups]
    sent, rest = refs[2 * groups:2 * groups + 2]
    out = refs[2 * groups + 2:3 * groups + 2]
    update = refs[3 * groups + 2]

    def one(step, carry):
        u, w = step // first, lax.rem(step, first)
        for s in range(groups):
            column = (place[0] ^ s) * first + w
            base = occ[place[0] * first + u] + occ[column]

            def finish(mirrored):
                value = (own[s][u, w].astype(WIDE) + mirrored) / (base - sums[...])
                narrow = value.astype(NARROW)
                update[u, s * first + w] = value
                sent[column, u] = narrow
                rest[u, s * first + w] = (2.0 * (value - narrow.astype(WIDE))).astype(NARROW)

            with_mirror(tiles, place, other[s][w, u].astype(WIDE), finish)
        return carry

    lax.fori_loop(0, first * first, one, 0)

    def load(s, u, r, at):
        return update[u, s * first + r, at, :]

    def store(s, u, w, column, at, result):
        out[s][u, w, at, :] = result.astype(NARROW)

    mix(place, fock, first, load, store, tiles.edge, 2 * tiles.edge)


def rest_kernel(tiles, groups, first, place, occ, sums, rest, *refs):
    own, other, out = refs[:groups], refs[groups:2 * groups], refs[2 * groups]

    def one(step, carry):
        u, w = step // first, lax.rem(step, first)
        for s in range(groups):
            column = (place[0] ^ s) * first + w
            base = occ[place[0] * first + u] + occ[column]

            def finish(mirrored):
                value = (own[s][u, w].astype(WIDE) + mirrored) / (base - sums[...])
                out[column, u] = (rest[u, s * first + w].astype(WIDE) + value).astype(NARROW)

            with_mirror(tiles, place, other[s][w, u].astype(WIDE), finish)
        return carry

    lax.fori_loop(0, first * first, one, 0)


def exchange(blocks):
    return lax.all_to_all(blocks, "occj", split_axis=0, concat_axis=0, tiled=True)


def across_first(parts, groups):
    return [parts[0]] + [
        lax.ppermute(parts[s], "occi", [(k, k ^ s) for k in range(groups)]) for s in range(1, groups)
    ]


def gather_vectors(vectors, devices):
    held, order = vectors[None], [0]
    step = devices // 2
    while True:
        other = lax.ppermute(held, "occj", [(k, k ^ step) for k in range(devices)])
        order = order + [k ^ step for k in order]
        if step == 1:
            return held, other, order
        held = jnp.concatenate([held, other], axis=0)
        step //= 2


def virtual_sums(tiles, vir_energy, q):
    e, g = tiles.edge, tiles.rows
    n_above = len(tiles.above)
    first = jnp.array([a for a, _ in tiles.above] + list(range(0, tiles.n, 2)), jnp.int32)[q]
    second = jnp.array([b for _, b in tiles.above] + list(range(1, tiles.n, 2)), jnp.int32)[q]
    a = lax.dynamic_slice_in_dim(vir_energy, first * e, e)
    b = lax.dynamic_slice_in_dim(vir_energy, second * e, e)
    pair = a[:, None] + b[None, :]
    across = jnp.concatenate([pair, pair], axis=1)
    halves = [
        jnp.concatenate([t[:g, None] + t[None, :], t[g:, None] + t[None, :]], axis=1) for t in (a, b)
    ]
    return jnp.where(q < n_above, across, jnp.concatenate(halves, axis=0))


def local(groups, devices, amplitudes, vectors, occupied_fock_block, occ_energy, vir_energy):
    first, second, virtual = amplitudes.shape[:3]
    assert second == 1 and groups * first == devices
    assert groups & (groups - 1) == 0 and devices & (devices - 1) == 0
    tiles = Tiles(devices, virtual)
    edge = tiles.edge
    current = amplitudes.reshape(first, virtual, virtual)
    count = current.size
    fock = occupied_fock_block.astype(WIDE)
    p, q = lax.axis_index("occi"), lax.axis_index("occj")
    place = jnp.stack([p, q]).astype(jnp.int32)
    part = jax.ShapeDtypeStruct((first, first, edge, 2 * edge), NARROW)
    packed = jax.ShapeDtypeStruct((devices, first, edge, 2 * edge), NARROW)
    vector_rows = virtual // devices

    low, high, order = gather_vectors(vectors, devices)
    held = exchange(pack(tiles, devices, current)).reshape(groups, first, first, edge, 2 * edge)
    mirror = across_first([held[p ^ s] for s in range(groups)], groups)
    sums = virtual_sums(tiles, vir_energy, q)

    ladder_flops = first * vectors.shape[0] * 4 * virtual**3
    ladder = exchange(call(
        functools.partial(first_ladder_kernel, tiles, order), packed,
        [pltpu.VMEM((vectors.shape[0], virtual, virtual), NARROW), pltpu.VMEM((virtual, virtual), WIDE)],
        ladder_flops, 8 * count, place, current, low, high, specs=[SMEM, VMEM, VMEM, VMEM],
    ))
    half = call(
        functools.partial(half_kernel, tiles, groups, first), [part] * groups, [],
        2 * devices * count, 6 * count, place, fock, ladder, *mirror, specs=[SMEM] * 2 + [VMEM] * (groups + 1),
    )
    other = across_first(half, groups)
    sent, rest, *mixed = call(
        functools.partial(update_kernel, tiles, groups, first),
        [packed, jax.ShapeDtypeStruct((first, devices, edge, 2 * edge), NARROW)] + [part] * groups,
        [pltpu.VMEM((first, devices, edge, 2 * edge), WIDE)],
        2 * devices * count, 10 * count, place, fock, occ_energy, sums, *half, *other,
        specs=[SMEM] * 3 + [VMEM] * (2 * groups + 1),
    )
    other = across_first(mixed, groups)
    back = exchange(sent)
    base = call(
        functools.partial(second_ladder_kernel, tiles, order, first),
        jax.ShapeDtypeStruct(current.shape, WIDE),
        [pltpu.VMEM((vectors.shape[0], virtual, virtual), NARROW), pltpu.VMEM((virtual, virtual), WIDE),
         pltpu.VMEM((virtual, virtual), NARROW)],
        ladder_flops, 12 * count, place, occ_energy, current, back,
        jnp.broadcast_to(vir_energy[:, None], (virtual, 128)), vir_energy[None, :], low, high,
        specs=[SMEM] * 2 + [VMEM] * 6,
    )
    rest = exchange(call(
        functools.partial(rest_kernel, tiles, groups, first), packed, [],
        4 * count, 8 * count, place, occ_energy, sums, rest, *mixed, *other,
        specs=[SMEM] * 2 + [VMEM] * (2 * groups + 2),
    ))
    done = call(
        functools.partial(add_kernel, tiles), jax.ShapeDtypeStruct(current.shape, WIDE), [],
        count, 10 * count, base, rest, specs=[VMEM, VMEM], aliases={0: 0},
    )
    return done.reshape(amplitudes.shape)


def solution(mesh):
    sizes = (mesh.shape["occi"], mesh.shape["occj"])
    return jax.shard_map(
        functools.partial(local, *sizes),
        mesh=mesh,
        in_specs=(P("occi", "occj", None, None), P(None, "occj", None), P(), P(), P()),
        out_specs=P("occi", "occj", None, None),
        check_vma=False,
    )
```

```python
import functools
import math

import jax
import jax.numpy as jnp
from jax import lax
from jax.experimental import pallas as pl
from jax.experimental.pallas import tpu as pltpu
from jax.sharding import PartitionSpec as P

VMEM = pl.BlockSpec(memory_space=pltpu.VMEM)
SMEM = pl.BlockSpec(memory_space=pltpu.SMEM)
PARAMS = pltpu.CompilerParams(vmem_limit_bytes=50 * 2**20)
WIDE = jnp.float32
NARROW = jnp.bfloat16


class Tiles:
    def __init__(self, devices, virtual):
        n = math.isqrt(2 * devices)
        assert n * n == 2 * devices and n % 2 == 0 and virtual % n == 0
        self.n = n
        self.edge = virtual // n
        self.rows = self.edge // 2
        self.above = [(a, b) for a in range(n) for b in range(a + 1, n)]
        self.diagonal = [(len(self.above) + k // 2, k % 2, k) for k in range(n)]

    def span(self, k):
        return slice(k * self.edge, (k + 1) * self.edge)

    def mirror_within(self, x):
        e, g = self.edge, self.rows
        tile = jnp.concatenate([x[:, :e], x[:, e:]], axis=0).T
        return jnp.concatenate([tile[:g], tile[g:]], axis=1)

    def mirror_across(self, x):
        return jnp.concatenate([x[:, self.edge:], x[:, :self.edge]], axis=1)


def call(body, outs, scratch, flops, moved, *operands, specs, aliases=None):
    return pl.pallas_call(
        body,
        out_shape=outs,
        in_specs=specs,
        out_specs=jax.tree.map(lambda _: VMEM, outs),
        scratch_shapes=scratch,
        compiler_params=PARAMS,
        input_output_aliases=aliases or {},
        cost_estimate=pl.CostEstimate(flops=flops, bytes_accessed=moved, transcendentals=0),
    )(*operands)


def pack_pair(tiles, source, outs, pair, mirrored=False):
    e, g = tiles.edge, tiles.rows
    straight, turned = (slice(e, None), slice(0, e)) if mirrored else (slice(0, e), slice(e, None))
    for d, (a, b) in enumerate(tiles.above):
        tile = source[tiles.span(a), tiles.span(b)].astype(NARROW)
        other = source[tiles.span(b), tiles.span(a)].astype(WIDE).T.astype(NARROW)
        for c, out in enumerate(outs):
            out[d, pair, :, straight] = tile[c * g:(c + 1) * g]
            out[d, pair, :, turned] = other[c * g:(c + 1) * g]
    for d, c, k in tiles.diagonal:
        tile = source[tiles.span(k), tiles.span(k)]
        tile = tile.astype(WIDE).T.astype(NARROW) if mirrored else tile.astype(NARROW)
        outs[c][d, pair, :, :e] = tile[:g]
        outs[c][d, pair, :, e:] = tile[g:]


def unpack_pair(tiles, blocks, c, pair, put):
    e, g = tiles.edge, tiles.rows
    for d, (a, b) in enumerate(tiles.above):
        strip = slice(a * e + c * g, a * e + (c + 1) * g)
        put(strip, tiles.span(b), blocks[d, pair, :, :e].astype(WIDE))
        put(tiles.span(b), strip, blocks[d, pair, :, e:].astype(WIDE).T)
    for d, chunk, k in tiles.diagonal:
        if chunk == c:
            put(slice(k * e, k * e + g), tiles.span(k), blocks[d, pair, :, :e].astype(WIDE))
            put(slice(k * e + g, (k + 1) * e), tiles.span(k), blocks[d, pair, :, e:].astype(WIDE))


def pack_kernel(tiles, source, *outs):
    for pair in range(source.shape[0]):
        pack_pair(tiles, source.at[pair], outs, pair, mirrored=True)


def assemble(place, order, pieces, whole):
    k = 0
    for piece in pieces:
        rows = piece.shape[2]
        for block in range(piece.shape[0]):
            start = pl.multiple_of((place[1] ^ order[k]) * rows, rows)
            for single in range(piece.shape[1]):
                whole[single, pl.ds(start, rows), :] = piece[block, single]
            k += 1


def ladder_pair(matrix, whole, total):
    def one(single, carry):
        vector = whole[single]
        inner = lax.dot_general(matrix, vector, (((1,), (1,)), ((), ())), preferred_element_type=WIDE)
        term = jnp.dot(vector, inner.astype(NARROW), preferred_element_type=WIDE)
        total[...] += term
        return carry

    total[...] = jnp.zeros_like(total)
    lax.fori_loop(0, whole.shape[0], one, 0)


def first_ladder_kernel(tiles, order, place, source, low, high, *refs):
    outs, (whole, total) = refs[:2], refs[2:]
    assemble(place, order, (low, high), whole)
    for pair in range(source.shape[0]):
        ladder_pair(source[pair].astype(NARROW), whole, total)
        pack_pair(tiles, total, outs, pair)


def second_ladder_kernel(tiles, order, place, occ, source, upper, lower, row, column, low, high, out,
                         whole, total, matrix):
    assemble(place, order, (low, high), whole)
    count = source.shape[0]
    for pair in range(count):
        def put(rows, columns, values):
            matrix[rows, columns] = values.astype(NARROW)

        unpack_pair(tiles, upper, 0, pair, put)
        unpack_pair(tiles, lower, 1, pair, put)
        ladder_pair(matrix[...], whole, total)
        base = occ[place[0] * count + pair] + occ[place[1]]

        def finish(step, carry):
            at = pl.ds(pl.multiple_of(step * 16, 16), 16)
            own = base - row[at, :1] - column[...]
            out[pair, at, :] = (
                source[pair, at, :] + 2.0 * matrix[at, :].astype(WIDE) + (2.0 * total[at, :]) / own
            )
            return carry

        lax.fori_loop(0, total.shape[0] // 16, finish, 0)


def add_kernel(tiles, source, upper, lower, out):
    for pair in range(source.shape[0]):
        def put(rows, columns, values):
            out[pair, rows, columns] = source[pair, rows, columns] + values

        unpack_pair(tiles, upper, 0, pair, put)
        unpack_pair(tiles, lower, 1, pair, put)


def mix(place, fock, first, load, store, rows):
    total = fock.shape[0]
    strips = rows // 16

    def strip(step, carry):
        u = step // strips
        at = pl.ds(pl.multiple_of(lax.rem(step, strips) * 16, 16), 16)
        taken = [load(k // first, u, k % first, at) for k in range(total)]
        for k in range(total):
            column = (place[0] ^ (k // first)) * first + k % first
            result = None
            for m in range(total):
                line = (place[0] ^ (m // first)) * first + m % first
                term = (-fock[line, column]) * taken[m]
                result = term if result is None else result + term
            store(k // first, u, k % first, column, at, result)
        return carry

    lax.fori_loop(0, first * strips, strip, 0)


def half_kernel(tiles, groups, first, place, fock, ladder, *refs):
    held, out = refs[:groups], refs[groups:]

    def load(s, u, r, at):
        return held[s][u, r, at, :].astype(WIDE)

    def store(s, u, w, column, at, result):
        out[s][u, w, at, :] = (ladder[column, u, at, :].astype(WIDE) + result).astype(NARROW)

    mix(place, fock, first, load, store, tiles.rows)


def with_mirror(tiles, place, x, finish):
    across = place[1] < len(tiles.above)

    @pl.when(across)
    def _():
        finish(tiles.mirror_across(x))

    @pl.when(jnp.logical_not(across))
    def _():
        finish(tiles.mirror_within(x))


def update_kernel(tiles, groups, first, place, fock, occ, sums, *refs):
    own, other = refs[:groups], refs[groups:2 * groups]
    sent, rest = refs[2 * groups:2 * groups + 2]
    out = refs[2 * groups + 2:3 * groups + 2]
    update = refs[3 * groups + 2]

    def one(step, carry):
        u, w = step // first, lax.rem(step, first)
        for s in range(groups):
            column = (place[0] ^ s) * first + w
            base = occ[place[0] * first + u] + occ[column]

            def finish(mirrored):
                value = (own[s][u, w].astype(WIDE) + mirrored) / (base - sums[...])
                narrow = value.astype(NARROW)
                update[u, s * first + w] = value
                sent[column, u] = narrow
                rest[u, s * first + w] = (2.0 * (value - narrow.astype(WIDE))).astype(NARROW)

            with_mirror(tiles, place, other[s][w, u].astype(WIDE), finish)
        return carry

    lax.fori_loop(0, first * first, one, 0)

    def load(s, u, r, at):
        return update[u, s * first + r, at, :]

    def store(s, u, w, column, at, result):
        out[s][u, w, at, :] = result.astype(NARROW)

    mix(place, fock, first, load, store, tiles.rows)


def rest_kernel(tiles, groups, first, place, occ, sums, rest, *refs):
    own, other, out = refs[:groups], refs[groups:2 * groups], refs[2 * groups]

    def one(step, carry):
        u, w = step // first, lax.rem(step, first)
        for s in range(groups):
            column = (place[0] ^ s) * first + w
            base = occ[place[0] * first + u] + occ[column]

            def finish(mirrored):
                value = (own[s][u, w].astype(WIDE) + mirrored) / (base - sums[...])
                out[column, u] = (rest[u, s * first + w].astype(WIDE) + value).astype(NARROW)

            with_mirror(tiles, place, other[s][w, u].astype(WIDE), finish)
        return carry

    lax.fori_loop(0, first * first, one, 0)


def exchange(blocks):
    return lax.all_to_all(blocks, "occj", split_axis=0, concat_axis=0, tiled=True)


def across_first(parts, groups):
    return [parts[0]] + [
        lax.ppermute(parts[s], "occi", [(k, k ^ s) for k in range(groups)]) for s in range(1, groups)
    ]


def tie(x, *others):
    return lax.optimization_barrier((x, *others))[0]


def gather_vectors(vectors, devices, late):
    held, order = vectors[None], [0]
    step = devices // 2
    while True:
        if step == 1:
            held = tie(held, late)
        other = lax.ppermute(held, "occj", [(k, k ^ step) for k in range(devices)])
        order = order + [k ^ step for k in order]
        if step == 1:
            return held, other, order
        held = jnp.concatenate([held, other], axis=0)
        step //= 2


def virtual_sums(tiles, vir_energy, q):
    e, g = tiles.edge, tiles.rows
    n_above = len(tiles.above)
    first = jnp.array([a for a, _ in tiles.above] + list(range(0, tiles.n, 2)), jnp.int32)[q]
    second = jnp.array([b for _, b in tiles.above] + list(range(1, tiles.n, 2)), jnp.int32)[q]
    a = lax.dynamic_slice_in_dim(vir_energy, first * e, e)
    b = lax.dynamic_slice_in_dim(vir_energy, second * e, e)
    sums = []
    for c, own in enumerate((a, b)):
        pair = a[c * g:(c + 1) * g, None] + b[None, :]
        across = jnp.concatenate([pair, pair], axis=1)
        within = jnp.concatenate([own[:g, None] + own[None, :], own[g:, None] + own[None, :]], axis=1)
        sums.append(jnp.where(q < n_above, across, within))
    return sums


def local(groups, devices, amplitudes, vectors, occupied_fock_block, occ_energy, vir_energy):
    first, second, virtual = amplitudes.shape[:3]
    assert second == 1 and groups * first == devices
    assert groups & (groups - 1) == 0 and devices & (devices - 1) == 0
    tiles = Tiles(devices, virtual)
    block = (tiles.rows, 2 * tiles.edge)
    current = amplitudes.reshape(first, virtual, virtual)
    count = current.size
    fock = occupied_fock_block.astype(WIDE)
    p, q = lax.axis_index("occi"), lax.axis_index("occj")
    place = jnp.stack([p, q]).astype(jnp.int32)
    part = jax.ShapeDtypeStruct((first, first, *block), NARROW)
    packed = jax.ShapeDtypeStruct((devices, first, *block), NARROW)
    whole = pltpu.VMEM((vectors.shape[0], virtual, virtual), NARROW)
    square = pltpu.VMEM((virtual, virtual), WIDE)
    chunks = range(2)

    started = call(functools.partial(pack_kernel, tiles), [packed] * 2, [], count, 6 * count,
                   current, specs=[VMEM])
    held = [exchange(x).reshape(groups, first, first, *block) for x in started]
    mirror = [across_first([x[p ^ s] for s in range(groups)], groups) for x in held]

    low, high, order = gather_vectors(tie(vectors, *started), devices, held[0])
    ladder_flops = first * vectors.shape[0] * 4 * virtual**3
    ladder = [exchange(x) for x in call(
        functools.partial(first_ladder_kernel, tiles, order), [packed] * 2, [whole, square],
        ladder_flops, 8 * count, place, current, low, high, specs=[SMEM] + [VMEM] * 3,
    )]
    sums = virtual_sums(tiles, vir_energy, q)

    sent, rest, mixed = [], [], []
    for c in chunks:
        half = call(
            functools.partial(half_kernel, tiles, groups, first), [part] * groups, [],
            devices * count, 3 * count, place, fock, ladder[c], *mirror[c],
            specs=[SMEM] * 2 + [VMEM] * (groups + 1),
        )
        other = across_first(half, groups)
        sent_one, rest_one, *mixed_one = call(
            functools.partial(update_kernel, tiles, groups, first),
            [packed, jax.ShapeDtypeStruct((first, devices, *block), NARROW)] + [part] * groups,
            [pltpu.VMEM((first, devices, *block), WIDE)],
            devices * count, 5 * count, place, fock, occ_energy, sums[c], *half, *other,
            specs=[SMEM] * 3 + [VMEM] * (2 * groups + 1),
        )
        sent.append(exchange(sent_one))
        rest.append(rest_one)
        mixed.append(mixed_one)

    base = call(
        functools.partial(second_ladder_kernel, tiles, order), jax.ShapeDtypeStruct(current.shape, WIDE),
        [whole, square, pltpu.VMEM((virtual, virtual), NARROW)],
        ladder_flops, 12 * count, place, occ_energy, current, *sent,
        jnp.broadcast_to(vir_energy[:, None], (virtual, 128)), vir_energy[None, :], low, high,
        specs=[SMEM] * 2 + [VMEM] * 7,
    )
    last = [
        exchange(call(
            functools.partial(rest_kernel, tiles, groups, first), packed, [],
            2 * count, 4 * count, place, occ_energy, sums[c], rest[c], *mixed[c],
            *across_first(mixed[c], groups), specs=[SMEM] * 2 + [VMEM] * (2 * groups + 2),
        )) for c in chunks
    ]
    done = call(
        functools.partial(add_kernel, tiles), jax.ShapeDtypeStruct(current.shape, WIDE), [],
        count, 10 * count, base, *last, specs=[VMEM] * 3, aliases={0: 0},
    )
    return done.reshape(amplitudes.shape)


def solution(mesh):
    sizes = (mesh.shape["occi"], mesh.shape["occj"])
    return jax.shard_map(
        functools.partial(local, *sizes),
        mesh=mesh,
        in_specs=(P("occi", "occj", None, None), P(None, "occj", None), P(), P(), P()),
        out_specs=P("occi", "occj", None, None),
        check_vma=False,
    )
```

```python
import functools
import math

import jax
import jax.numpy as jnp
from jax import lax
from jax.experimental import pallas as pl
from jax.experimental.pallas import tpu as pltpu
from jax.sharding import PartitionSpec as P

VMEM = pl.BlockSpec(memory_space=pltpu.VMEM)
SMEM = pl.BlockSpec(memory_space=pltpu.SMEM)
PARAMS = pltpu.CompilerParams(vmem_limit_bytes=50 * 2**20)
WIDE = jnp.float32
NARROW = jnp.bfloat16


class Tiles:
    def __init__(self, devices, virtual):
        n = math.isqrt(2 * devices)
        assert n * n == 2 * devices and n % 2 == 0 and virtual % n == 0
        self.n = n
        self.edge = virtual // n
        self.rows = self.edge // 2
        self.above = [(a, b) for a in range(n) for b in range(a + 1, n)]
        self.diagonal = [(len(self.above) + k // 2, k % 2, k) for k in range(n)]

    def span(self, k):
        return slice(k * self.edge, (k + 1) * self.edge)

    def mirror_within(self, x):
        e, g = self.edge, self.rows
        parts = []
        for c in range(2):
            tile = jnp.concatenate([x[c * g:(c + 1) * g, :e], x[c * g:(c + 1) * g, e:]], axis=0).T
            parts.append(jnp.concatenate([tile[:g], tile[g:]], axis=1))
        return jnp.concatenate(parts, axis=0)

    def mirror_across(self, x):
        return jnp.concatenate([x[:, self.edge:], x[:, :self.edge]], axis=1)


def call(body, outs, scratch, flops, moved, *operands, specs, aliases=None):
    return pl.pallas_call(
        body,
        out_shape=outs,
        in_specs=specs,
        out_specs=jax.tree.map(lambda _: VMEM, outs),
        scratch_shapes=scratch,
        compiler_params=PARAMS,
        input_output_aliases=aliases or {},
        cost_estimate=pl.CostEstimate(flops=flops, bytes_accessed=moved, transcendentals=0),
    )(*operands)


def pack_pair(tiles, source, out, pair, mirrored=False):
    e, g = tiles.edge, tiles.rows
    straight, turned = (slice(e, None), slice(0, e)) if mirrored else (slice(0, e), slice(e, None))
    for d, (a, b) in enumerate(tiles.above):
        out[d, pair, :, straight] = source[tiles.span(a), tiles.span(b)].astype(NARROW)
        out[d, pair, :, turned] = source[tiles.span(b), tiles.span(a)].astype(WIDE).T.astype(NARROW)
    for d, c, k in tiles.diagonal:
        tile = source[tiles.span(k), tiles.span(k)]
        tile = tile.astype(WIDE).T.astype(NARROW) if mirrored else tile.astype(NARROW)
        out[d, pair, c * g:(c + 1) * g, :e] = tile[:g]
        out[d, pair, c * g:(c + 1) * g, e:] = tile[g:]


def unpack_pair(tiles, blocks, pair, put):
    e, g = tiles.edge, tiles.rows
    for d, (a, b) in enumerate(tiles.above):
        put(a, b, blocks[d, pair, :, :e].astype(WIDE))
        put(b, a, blocks[d, pair, :, e:].astype(WIDE).T)
    for d, c, k in tiles.diagonal:
        upper = blocks[d, pair, c * g:(c + 1) * g, :e]
        lower = blocks[d, pair, c * g:(c + 1) * g, e:]
        put(k, k, jnp.concatenate([upper, lower], axis=0).astype(WIDE))


def pack_kernel(tiles, source, out):
    for pair in range(source.shape[0]):
        pack_pair(tiles, source.at[pair], out, pair, mirrored=True)


def pack(tiles, devices, amplitudes):
    count = amplitudes.shape[0]
    out = jax.ShapeDtypeStruct((devices, count, tiles.edge, 2 * tiles.edge), NARROW)
    return call(functools.partial(pack_kernel, tiles), out, [], amplitudes.size, amplitudes.size * 6,
                amplitudes, specs=[VMEM])


def assemble(place, order, pieces, whole):
    k = 0
    for piece in pieces:
        count, rows, virtual = piece.shape[-3:]
        for block in range(piece.shape[0] if len(piece.shape) == 4 else 1):
            start = pl.multiple_of((place[1] ^ order[k]) * rows, rows)
            for single in range(count):
                values = piece[block, single] if len(piece.shape) == 4 else piece[single]
                whole[pl.ds(start, rows), single * virtual:(single + 1) * virtual] = values
            k += 1


def ladder_pair(matrix, whole, inner, total):
    virtual = matrix.shape[0]
    for single in range(whole.shape[1] // virtual):
        at = slice(single * virtual, (single + 1) * virtual)
        inner[at, :] = lax.dot_general(
            matrix, whole[:, at], (((1,), (1,)), ((), ())), preferred_element_type=WIDE
        ).astype(NARROW)
    total[...] = jnp.dot(whole[...], inner[...], preferred_element_type=WIDE)


def inverse(x):
    guess = pl.reciprocal(x, approx=True)
    return guess * (2.0 - x * guess)


def first_ladder_kernel(tiles, order, place, source, *refs):
    pieces, (out, whole, inner, total) = refs[:-4], refs[-4:]
    assemble(place, order, pieces, whole)
    for pair in range(source.shape[0]):
        ladder_pair(source[pair].astype(NARROW), whole, inner, total)
        pack_pair(tiles, total, out, pair)


def second_ladder_kernel(tiles, order, place, occ, source, blocks, row, column, *refs):
    pieces, (out, whole, inner, total, matrix) = refs[:-5], refs[-5:]
    assemble(place, order, pieces, whole)
    count = source.shape[0]
    for pair in range(count):
        def put(a, b, tile):
            matrix[tiles.span(a), tiles.span(b)] = tile.astype(NARROW)

        unpack_pair(tiles, blocks, pair, put)
        ladder_pair(matrix[...], whole, inner, total)
        base = occ[place[0] * count + pair] + occ[place[1]]

        def finish(step, carry):
            at = pl.ds(pl.multiple_of(step * 16, 16), 16)
            own = base - row[at, :1] - column[...]
            out[pair, at, :] = (
                source[pair, at, :] + 2.0 * (matrix[at, :].astype(WIDE) + total[at, :] * inverse(own))
            )
            return carry

        lax.fori_loop(0, total.shape[0] // 16, finish, 0)


def add_kernel(tiles, source, blocks, out):
    for pair in range(source.shape[0]):
        def put(a, b, tile):
            here = (pair, tiles.span(a), tiles.span(b))
            out[here] = source[here] + tile

        unpack_pair(tiles, blocks, pair, put)


def mix(place, fock, first, load, store, rows, width):
    total = fock.shape[0]
    strips = rows // 16

    def strip(step, carry):
        u = step // strips
        at = pl.ds(pl.multiple_of(lax.rem(step, strips) * 16, 16), 16)
        taken = [load(k // first, u, k % first, at) for k in range(total)]
        for k in range(total):
            column = (place[0] ^ (k // first)) * first + k % first
            result = None
            for m in range(total):
                line = (place[0] ^ (m // first)) * first + m % first
                term = (-fock[line, column]) * taken[m]
                result = term if result is None else result + term
            store(k // first, u, k % first, column, at, result)
        return carry

    lax.fori_loop(0, first * strips, strip, 0)


def half_kernel(tiles, groups, first, place, fock, ladder, *refs):
    held, out = refs[:groups], refs[groups:]

    def load(s, u, r, at):
        return held[s][u, r, at, :].astype(WIDE)

    def store(s, u, w, column, at, result):
        out[s][u, w, at, :] = (ladder[column, u, at, :].astype(WIDE) + result).astype(NARROW)

    mix(place, fock, first, load, store, tiles.edge, 2 * tiles.edge)


def with_mirror(tiles, place, x, finish):
    across = place[1] < len(tiles.above)

    @pl.when(across)
    def _():
        finish(tiles.mirror_across(x))

    @pl.when(jnp.logical_not(across))
    def _():
        finish(tiles.mirror_within(x))


def update_kernel(tiles, groups, first, place, fock, occ, sums, *refs):
    own, other = refs[:groups], refs[groups:2 * groups]
    sent, rest = refs[2 * groups:2 * groups + 2]
    out = refs[2 * groups + 2:3 * groups + 2]
    update = refs[3 * groups + 2]

    def one(step, carry):
        u, w = step // first, lax.rem(step, first)
        for s in range(groups):
            column = (place[0] ^ s) * first + w
            base = occ[place[0] * first + u] + occ[column]

            def finish(mirrored):
                value = (own[s][u, w].astype(WIDE) + mirrored) * inverse(base - sums[...])
                narrow = value.astype(NARROW)
                update[u, s * first + w] = value
                sent[column, u] = narrow
                rest[u, s * first + w] = (2.0 * (value - narrow.astype(WIDE))).astype(NARROW)

            with_mirror(tiles, place, other[s][w, u].astype(WIDE), finish)
        return carry

    lax.fori_loop(0, first * first, one, 0)

    def load(s, u, r, at):
        return update[u, s * first + r, at, :]

    def store(s, u, w, column, at, result):
        out[s][u, w, at, :] = result.astype(NARROW)

    mix(place, fock, first, load, store, tiles.edge, 2 * tiles.edge)


def rest_kernel(tiles, groups, first, place, occ, sums, rest, *refs):
    own, other, out = refs[:groups], refs[groups:2 * groups], refs[2 * groups]

    def one(step, carry):
        u, w = step // first, lax.rem(step, first)
        for s in range(groups):
            column = (place[0] ^ s) * first + w
            base = occ[place[0] * first + u] + occ[column]

            def finish(mirrored):
                value = (own[s][u, w].astype(WIDE) + mirrored) * inverse(base - sums[...])
                out[column, u] = (rest[u, s * first + w].astype(WIDE) + value).astype(NARROW)

            with_mirror(tiles, place, other[s][w, u].astype(WIDE), finish)
        return carry

    lax.fori_loop(0, first * first, one, 0)


def exchange(blocks):
    return lax.all_to_all(blocks, "occj", split_axis=0, concat_axis=0, tiled=True)


def across_first(parts, groups):
    return [parts[0]] + [
        lax.ppermute(parts[s], "occi", [(k, k ^ s) for k in range(groups)])
        for s in range(groups - 1, 0, -1)
    ][::-1]


def tie(x, *others):
    return lax.optimization_barrier((x, *others))[0]


def gather_vectors(vectors, devices):
    def turn(x, k):
        return lax.ppermute(x, "occj", [(d, d ^ k) for d in range(devices)])

    even = list(range(0, devices, 2))
    held = [vectors] + [turn(vectors, k) for k in even[1:]]
    other = turn(jnp.stack(held), 1)
    return [*held, other], even + [k ^ 1 for k in even]


def virtual_sums(tiles, vir_energy, q):
    e, g = tiles.edge, tiles.rows
    n_above = len(tiles.above)
    first = jnp.array([a for a, _ in tiles.above] + list(range(0, tiles.n, 2)), jnp.int32)[q]
    second = jnp.array([b for _, b in tiles.above] + list(range(1, tiles.n, 2)), jnp.int32)[q]
    a = lax.dynamic_slice_in_dim(vir_energy, first * e, e)
    b = lax.dynamic_slice_in_dim(vir_energy, second * e, e)
    pair = a[:, None] + b[None, :]
    across = jnp.concatenate([pair, pair], axis=1)
    halves = [
        jnp.concatenate([t[:g, None] + t[None, :], t[g:, None] + t[None, :]], axis=1) for t in (a, b)
    ]
    return jnp.where(q < n_above, across, jnp.concatenate(halves, axis=0))


def local(groups, devices, amplitudes, vectors, occupied_fock_block, occ_energy, vir_energy):
    first, second, virtual = amplitudes.shape[:3]
    assert second == 1 and groups * first == devices
    assert groups & (groups - 1) == 0 and devices & (devices - 1) == 0
    tiles = Tiles(devices, virtual)
    edge = tiles.edge
    current = amplitudes.reshape(first, virtual, virtual)
    count = current.size
    fock = occupied_fock_block.astype(WIDE)
    p, q = lax.axis_index("occi"), lax.axis_index("occj")
    place = jnp.stack([p, q]).astype(jnp.int32)
    part = jax.ShapeDtypeStruct((first, first, edge, 2 * edge), NARROW)
    packed = jax.ShapeDtypeStruct((devices, first, edge, 2 * edge), NARROW)
    singles = vectors.shape[0]
    whole = pltpu.VMEM((virtual, singles * virtual), NARROW)
    inner = pltpu.VMEM((singles * virtual, virtual), NARROW)
    square = pltpu.VMEM((virtual, virtual), WIDE)

    started = pack(tiles, devices, current)
    held = exchange(started)
    pieces, order = gather_vectors(tie(vectors, started), devices)
    parts = held.reshape(groups, first, first, edge, 2 * edge)
    mirror = across_first([parts[p ^ s] for s in range(groups)], groups)
    sums = virtual_sums(tiles, vir_energy, q)

    ladder_flops = first * singles * 4 * virtual**3
    ladder = exchange(call(
        functools.partial(first_ladder_kernel, tiles, order), packed, [whole, inner, square],
        ladder_flops, 8 * count, tie(place, held), current, *pieces,
        specs=[SMEM] + [VMEM] * (1 + len(pieces)),
    ))
    half = call(
        functools.partial(half_kernel, tiles, groups, first), [part] * groups, [],
        2 * devices * count, 6 * count, place, fock, ladder, *mirror, specs=[SMEM] * 2 + [VMEM] * (groups + 1),
    )
    other = across_first(half, groups)
    sent, rest, *mixed = call(
        functools.partial(update_kernel, tiles, groups, first),
        [packed, jax.ShapeDtypeStruct((first, devices, edge, 2 * edge), NARROW)] + [part] * groups,
        [pltpu.VMEM((first, devices, edge, 2 * edge), WIDE)],
        2 * devices * count, 10 * count, place, fock, occ_energy, sums, *half, *other,
        specs=[SMEM] * 3 + [VMEM] * (2 * groups + 1),
    )
    other = across_first(mixed, groups)
    back = exchange(tie(sent, other[1]))
    base = call(
        functools.partial(second_ladder_kernel, tiles, order), jax.ShapeDtypeStruct(current.shape, WIDE),
        [whole, inner, square, pltpu.VMEM((virtual, virtual), NARROW)],
        ladder_flops, 12 * count, place, occ_energy, current, back,
        jnp.broadcast_to(vir_energy[:, None], (virtual, 128)), vir_energy[None, :], *pieces,
        specs=[SMEM] * 2 + [VMEM] * (4 + len(pieces)),
    )
    rest = exchange(call(
        functools.partial(rest_kernel, tiles, groups, first), packed, [],
        4 * count, 8 * count, place, occ_energy, sums, rest, *mixed, *other,
        specs=[SMEM] * 2 + [VMEM] * (2 * groups + 2),
    ))
    done = call(
        functools.partial(add_kernel, tiles), jax.ShapeDtypeStruct(current.shape, WIDE), [],
        count, 10 * count, base, rest, specs=[VMEM, VMEM], aliases={0: 0},
    )
    return done.reshape(amplitudes.shape)


def solution(mesh):
    sizes = (mesh.shape["occi"], mesh.shape["occj"])
    return jax.shard_map(
        functools.partial(local, *sizes),
        mesh=mesh,
        in_specs=(P("occi", "occj", None, None), P(None, "occj", None), P(), P(), P()),
        out_specs=P("occi", "occj", None, None),
        check_vma=False,
    )
```

```python
import functools
import math

import jax
import jax.numpy as jnp
from jax import lax
from jax.experimental import pallas as pl
from jax.experimental.pallas import tpu as pltpu
from jax.sharding import PartitionSpec as P

VMEM = pl.BlockSpec(memory_space=pltpu.VMEM)
SMEM = pl.BlockSpec(memory_space=pltpu.SMEM)
PARAMS = pltpu.CompilerParams(vmem_limit_bytes=50 * 2**20)
WIDE = jnp.float32
LONG = 3 * 10**10
NARROW = jnp.bfloat16


class Tiles:
    def __init__(self, devices, virtual):
        n = math.isqrt(2 * devices)
        assert n * n == 2 * devices and n % 2 == 0 and virtual % n == 0
        self.n = n
        self.edge = virtual // n
        self.rows = self.edge // 2
        self.above = [(a, b) for a in range(n) for b in range(a + 1, n)]
        self.diagonal = [(len(self.above) + k // 2, k % 2, k) for k in range(n)]

    def span(self, k):
        return slice(k * self.edge, (k + 1) * self.edge)

    def mirror_within(self, x):
        e, g = self.edge, self.rows
        parts = []
        for c in range(2):
            tile = jnp.concatenate([x[c * g:(c + 1) * g, :e], x[c * g:(c + 1) * g, e:]], axis=0).T
            parts.append(jnp.concatenate([tile[:g], tile[g:]], axis=1))
        return jnp.concatenate(parts, axis=0)

    def mirror_across(self, x):
        return jnp.concatenate([x[:, self.edge:], x[:, :self.edge]], axis=1)


def call(body, outs, scratch, flops, moved, *operands, specs, aliases=None):
    return pl.pallas_call(
        body,
        out_shape=outs,
        in_specs=specs,
        out_specs=jax.tree.map(lambda _: VMEM, outs),
        scratch_shapes=scratch,
        compiler_params=PARAMS,
        input_output_aliases=aliases or {},
        cost_estimate=pl.CostEstimate(flops=flops, bytes_accessed=moved, transcendentals=0),
    )(*operands)


def pack_pair(tiles, source, out, pair, mirrored=False):
    e, g = tiles.edge, tiles.rows
    straight, turned = (slice(e, None), slice(0, e)) if mirrored else (slice(0, e), slice(e, None))
    for d, (a, b) in enumerate(tiles.above):
        out[d, pair, :, straight] = source[tiles.span(a), tiles.span(b)].astype(NARROW)
        out[d, pair, :, turned] = source[tiles.span(b), tiles.span(a)].astype(WIDE).T.astype(NARROW)
    for d, c, k in tiles.diagonal:
        tile = source[tiles.span(k), tiles.span(k)]
        tile = tile.astype(WIDE).T.astype(NARROW) if mirrored else tile.astype(NARROW)
        out[d, pair, c * g:(c + 1) * g, :e] = tile[:g]
        out[d, pair, c * g:(c + 1) * g, e:] = tile[g:]


def unpack_pair(tiles, blocks, pair, put):
    e, g = tiles.edge, tiles.rows
    for d, (a, b) in enumerate(tiles.above):
        put(a, b, blocks[d, pair, :, :e].astype(WIDE))
        put(b, a, blocks[d, pair, :, e:].astype(WIDE).T)
    for d, c, k in tiles.diagonal:
        upper = blocks[d, pair, c * g:(c + 1) * g, :e]
        lower = blocks[d, pair, c * g:(c + 1) * g, e:]
        put(k, k, jnp.concatenate([upper, lower], axis=0).astype(WIDE))


def pack_kernel(tiles, source, out):
    for pair in range(source.shape[0]):
        pack_pair(tiles, source.at[pair], out, pair, mirrored=True)


def pack(tiles, devices, amplitudes):
    count = amplitudes.shape[0]
    out = jax.ShapeDtypeStruct((devices, count, tiles.edge, 2 * tiles.edge), NARROW)
    return call(functools.partial(pack_kernel, tiles), out, [], amplitudes.size, amplitudes.size * 6,
                amplitudes, specs=[VMEM])


def assemble(place, order, pieces, whole):
    k = 0
    for piece in pieces:
        count, rows, virtual = piece.shape[-3:]
        for block in range(piece.shape[0] if len(piece.shape) == 4 else 1):
            start = pl.multiple_of((place[1] ^ order[k]) * rows, rows)
            for single in range(count):
                values = piece[block, single] if len(piece.shape) == 4 else piece[single]
                whole[pl.ds(start, rows), single * virtual:(single + 1) * virtual] = values
            k += 1


def ladder_pair(matrix, whole, inner, total):
    virtual = matrix.shape[0]
    for single in range(whole.shape[1] // virtual):
        at = slice(single * virtual, (single + 1) * virtual)
        inner[at, :] = lax.dot_general(
            matrix, whole[:, at], (((1,), (1,)), ((), ())), preferred_element_type=WIDE
        ).astype(NARROW)
    total[...] = jnp.dot(whole[...], inner[...], preferred_element_type=WIDE)


def inverse(x):
    guess = pl.reciprocal(x, approx=True)
    return guess * (2.0 - x * guess)


def first_ladder_kernel(tiles, order, place, source, *refs):
    pieces, (out, whole, inner, total) = refs[:-4], refs[-4:]
    assemble(place, order, pieces, whole)
    for pair in range(source.shape[0]):
        ladder_pair(source[pair].astype(NARROW), whole, inner, total)
        pack_pair(tiles, total, out, pair)


def second_ladder_kernel(tiles, order, place, occ, source, blocks, row, column, *refs):
    pieces, (out, whole, inner, total, matrix) = refs[:-5], refs[-5:]
    assemble(place, order, pieces, whole)
    count = source.shape[0]
    for pair in range(count):
        def put(a, b, tile):
            matrix[tiles.span(a), tiles.span(b)] = tile.astype(NARROW)

        unpack_pair(tiles, blocks, pair, put)
        ladder_pair(matrix[...], whole, inner, total)
        base = occ[place[0] * count + pair] + occ[place[1]]

        def finish(step, carry):
            at = pl.ds(pl.multiple_of(step * 16, 16), 16)
            own = base - row[at, :1] - column[...]
            out[pair, at, :] = (
                source[pair, at, :] + 2.0 * (matrix[at, :].astype(WIDE) + total[at, :] * inverse(own))
            )
            return carry

        lax.fori_loop(0, total.shape[0] // 16, finish, 0)


def add_kernel(tiles, source, blocks, out):
    for pair in range(source.shape[0]):
        def put(a, b, tile):
            here = (pair, tiles.span(a), tiles.span(b))
            out[here] = source[here] + tile

        unpack_pair(tiles, blocks, pair, put)


def mix(place, fock, first, load, store, rows, width):
    total = fock.shape[0]
    strips = rows // 16

    def strip(step, carry):
        u = step // strips
        at = pl.ds(pl.multiple_of(lax.rem(step, strips) * 16, 16), 16)
        taken = [load(k // first, u, k % first, at) for k in range(total)]
        for k in range(total):
            column = (place[0] ^ (k // first)) * first + k % first
            result = None
            for m in range(total):
                line = (place[0] ^ (m // first)) * first + m % first
                term = (-fock[line, column]) * taken[m]
                result = term if result is None else result + term
            store(k // first, u, k % first, column, at, result)
        return carry

    lax.fori_loop(0, first * strips, strip, 0)


def half_kernel(tiles, groups, first, place, fock, ladder, *refs):
    held, out = refs[:groups], refs[groups:]

    def load(s, u, r, at):
        return held[s][u, r, at, :].astype(WIDE)

    def store(s, u, w, column, at, result):
        out[s][u, w, at, :] = (ladder[column, u, at, :].astype(WIDE) + result).astype(NARROW)

    mix(place, fock, first, load, store, tiles.edge, 2 * tiles.edge)


def with_mirror(tiles, place, x, finish):
    across = place[1] < len(tiles.above)

    @pl.when(across)
    def _():
        finish(tiles.mirror_across(x))

    @pl.when(jnp.logical_not(across))
    def _():
        finish(tiles.mirror_within(x))


def update_kernel(tiles, groups, first, place, fock, occ, sums, *refs):
    own, other = refs[:groups], refs[groups:2 * groups]
    sent, rest = refs[2 * groups:2 * groups + 2]
    out = refs[2 * groups + 2:3 * groups + 2]
    update = refs[3 * groups + 2]

    def one(step, carry):
        u, w = step // first, lax.rem(step, first)
        for s in range(groups):
            column = (place[0] ^ s) * first + w
            base = occ[place[0] * first + u] + occ[column]

            def finish(mirrored):
                value = (own[s][u, w].astype(WIDE) + mirrored) * inverse(base - sums[...])
                narrow = value.astype(NARROW)
                update[u, s * first + w] = value
                sent[column, u] = narrow
                rest[u, s * first + w] = (2.0 * (value - narrow.astype(WIDE))).astype(NARROW)

            with_mirror(tiles, place, other[s][w, u].astype(WIDE), finish)
        return carry

    lax.fori_loop(0, first * first, one, 0)

    def load(s, u, r, at):
        return update[u, s * first + r, at, :]

    def store(s, u, w, column, at, result):
        out[s][u, w, at, :] = result.astype(NARROW)

    mix(place, fock, first, load, store, tiles.edge, 2 * tiles.edge)


def rest_kernel(tiles, groups, first, place, occ, sums, rest, *refs):
    own, other, out = refs[:groups], refs[groups:2 * groups], refs[2 * groups]

    def one(step, carry):
        u, w = step // first, lax.rem(step, first)
        for s in range(groups):
            column = (place[0] ^ s) * first + w
            base = occ[place[0] * first + u] + occ[column]

            def finish(mirrored):
                value = (own[s][u, w].astype(WIDE) + mirrored) * inverse(base - sums[...])
                out[column, u] = (rest[u, s * first + w].astype(WIDE) + value).astype(NARROW)

            with_mirror(tiles, place, other[s][w, u].astype(WIDE), finish)
        return carry

    lax.fori_loop(0, first * first, one, 0)


def exchange(blocks):
    return lax.all_to_all(blocks, "occj", split_axis=0, concat_axis=0, tiled=True)


def across_first(parts, groups):
    return [parts[0]] + [
        lax.ppermute(parts[s], "occi", [(k, k ^ s) for k in range(groups)])
        for s in range(groups - 1, 0, -1)
    ][::-1]


def tie(x, *others):
    return lax.optimization_barrier((x, *others))[0]


def copy_kernel(source, out):
    for k in range(source.shape[0]):
        out[k] = source[k]


def after(x, *others):
    return pl.pallas_call(
        copy_kernel,
        out_shape=jax.ShapeDtypeStruct(x.shape, x.dtype),
        in_specs=[SMEM],
        out_specs=SMEM,
        cost_estimate=pl.CostEstimate(flops=LONG, bytes_accessed=8, transcendentals=0),
    )(tie(x, *others))


def gather_vectors(vectors, devices):
    def turn(x, k):
        return lax.ppermute(x, "occj", [(d, d ^ k) for d in range(devices)])

    even = list(range(0, devices, 2))
    held = [vectors] + [turn(vectors, k) for k in even[1:]]
    other = turn(jnp.stack(held), 1)
    return [*held, other], even + [k ^ 1 for k in even]


def virtual_sums(tiles, vir_energy, q):
    e, g = tiles.edge, tiles.rows
    n_above = len(tiles.above)
    first = jnp.array([a for a, _ in tiles.above] + list(range(0, tiles.n, 2)), jnp.int32)[q]
    second = jnp.array([b for _, b in tiles.above] + list(range(1, tiles.n, 2)), jnp.int32)[q]
    a = lax.dynamic_slice_in_dim(vir_energy, first * e, e)
    b = lax.dynamic_slice_in_dim(vir_energy, second * e, e)
    pair = a[:, None] + b[None, :]
    across = jnp.concatenate([pair, pair], axis=1)
    halves = [
        jnp.concatenate([t[:g, None] + t[None, :], t[g:, None] + t[None, :]], axis=1) for t in (a, b)
    ]
    return jnp.where(q < n_above, across, jnp.concatenate(halves, axis=0))


def local(groups, devices, amplitudes, vectors, occupied_fock_block, occ_energy, vir_energy):
    first, second, virtual = amplitudes.shape[:3]
    assert second == 1 and groups * first == devices
    assert groups & (groups - 1) == 0 and devices & (devices - 1) == 0
    tiles = Tiles(devices, virtual)
    edge = tiles.edge
    current = amplitudes.reshape(first, virtual, virtual)
    count = current.size
    fock = occupied_fock_block.astype(WIDE)
    p, q = lax.axis_index("occi"), lax.axis_index("occj")
    place = jnp.stack([p, q]).astype(jnp.int32)
    part = jax.ShapeDtypeStruct((first, first, edge, 2 * edge), NARROW)
    packed = jax.ShapeDtypeStruct((devices, first, edge, 2 * edge), NARROW)
    singles = vectors.shape[0]
    whole = pltpu.VMEM((virtual, singles * virtual), NARROW)
    inner = pltpu.VMEM((singles * virtual, virtual), NARROW)
    square = pltpu.VMEM((virtual, virtual), WIDE)

    started = pack(tiles, devices, current)
    held = exchange(started)
    pieces, order = gather_vectors(tie(vectors, started), devices)
    parts = held.reshape(groups, first, first, edge, 2 * edge)
    mirror = across_first([parts[p ^ s] for s in range(groups)], groups)
    sums = virtual_sums(tiles, vir_energy, q)

    ladder_flops = first * singles * 4 * virtual**3
    ladder = exchange(call(
        functools.partial(first_ladder_kernel, tiles, order), packed, [whole, inner, square],
        ladder_flops, 8 * count, tie(place, held), current, *pieces,
        specs=[SMEM] + [VMEM] * (1 + len(pieces)),
    ))
    half = call(
        functools.partial(half_kernel, tiles, groups, first), [part] * groups, [],
        2 * devices * count, 6 * count, after(place, *mirror), fock, ladder, *mirror,
        specs=[SMEM] * 2 + [VMEM] * (groups + 1),
    )
    other = across_first(half, groups)
    sent, rest, *mixed = call(
        functools.partial(update_kernel, tiles, groups, first),
        [packed, jax.ShapeDtypeStruct((first, devices, edge, 2 * edge), NARROW)] + [part] * groups,
        [pltpu.VMEM((first, devices, edge, 2 * edge), WIDE)],
        2 * devices * count, 10 * count, place, fock, occ_energy, sums, *half, *other,
        specs=[SMEM] * 3 + [VMEM] * (2 * groups + 1),
    )
    other = across_first(mixed, groups)
    back = exchange(sent)
    base = call(
        functools.partial(second_ladder_kernel, tiles, order), jax.ShapeDtypeStruct(current.shape, WIDE),
        [whole, inner, square, pltpu.VMEM((virtual, virtual), NARROW)],
        ladder_flops, 12 * count, place, occ_energy, current, back,
        jnp.broadcast_to(vir_energy[:, None], (virtual, 128)), vir_energy[None, :], *pieces,
        specs=[SMEM] * 2 + [VMEM] * (4 + len(pieces)),
    )
    rest = exchange(call(
        functools.partial(rest_kernel, tiles, groups, first), packed, [],
        LONG, 8 * count, place, occ_energy, sums, rest, *mixed, *other,
        specs=[SMEM] * 2 + [VMEM] * (2 * groups + 2),
    ))
    done = call(
        functools.partial(add_kernel, tiles), jax.ShapeDtypeStruct(current.shape, WIDE), [],
        count, 10 * count, base, rest, specs=[VMEM, VMEM], aliases={0: 0},
    )
    return done.reshape(amplitudes.shape)


def solution(mesh):
    sizes = (mesh.shape["occi"], mesh.shape["occj"])
    return jax.shard_map(
        functools.partial(local, *sizes),
        mesh=mesh,
        in_specs=(P("occi", "occj", None, None), P(None, "occj", None), P(), P(), P()),
        out_specs=P("occi", "occj", None, None),
        check_vma=False,
    )
```

```python
import functools
import math

import jax
import jax.numpy as jnp
from jax import lax
from jax.experimental import pallas as pl
from jax.experimental.pallas import tpu as pltpu
from jax.sharding import PartitionSpec as P

VMEM = pl.BlockSpec(memory_space=pltpu.VMEM)
SMEM = pl.BlockSpec(memory_space=pltpu.SMEM)
PARAMS = pltpu.CompilerParams(vmem_limit_bytes=50 * 2**20)
WIDE = jnp.float32
LONG = 3 * 10**10
NARROW = jnp.bfloat16


class Tiles:
    def __init__(self, devices, virtual):
        n = math.isqrt(2 * devices)
        assert n * n == 2 * devices and n % 2 == 0 and virtual % n == 0
        self.n = n
        self.edge = virtual // n
        self.rows = self.edge // 2
        self.above = [(a, b) for a in range(n) for b in range(a + 1, n)]
        self.diagonal = [(len(self.above) + k // 2, k % 2, k) for k in range(n)]

    def span(self, k):
        return slice(k * self.edge, (k + 1) * self.edge)

    def mirror_within(self, x):
        e, g = self.edge, self.rows
        parts = []
        for c in range(2):
            tile = jnp.concatenate([x[c * g:(c + 1) * g, :e], x[c * g:(c + 1) * g, e:]], axis=0).T
            parts.append(jnp.concatenate([tile[:g], tile[g:]], axis=1))
        return jnp.concatenate(parts, axis=0)

    def mirror_across(self, x):
        return jnp.concatenate([x[:, self.edge:], x[:, :self.edge]], axis=1)


def call(body, outs, scratch, flops, moved, *operands, specs, aliases=None):
    return pl.pallas_call(
        body,
        out_shape=outs,
        in_specs=specs,
        out_specs=jax.tree.map(lambda _: VMEM, outs),
        scratch_shapes=scratch,
        compiler_params=PARAMS,
        input_output_aliases=aliases or {},
        cost_estimate=pl.CostEstimate(flops=flops, bytes_accessed=moved, transcendentals=0),
    )(*operands)


def pack_pair(tiles, source, out, pair, mirrored=False):
    e, g = tiles.edge, tiles.rows
    straight, turned = (slice(e, None), slice(0, e)) if mirrored else (slice(0, e), slice(e, None))
    for d, (a, b) in enumerate(tiles.above):
        out[d, pair, :, straight] = source[tiles.span(a), tiles.span(b)].astype(NARROW)
        out[d, pair, :, turned] = source[tiles.span(b), tiles.span(a)].astype(WIDE).T.astype(NARROW)
    for d, c, k in tiles.diagonal:
        tile = source[tiles.span(k), tiles.span(k)]
        tile = tile.astype(WIDE).T.astype(NARROW) if mirrored else tile.astype(NARROW)
        out[d, pair, c * g:(c + 1) * g, :e] = tile[:g]
        out[d, pair, c * g:(c + 1) * g, e:] = tile[g:]


def unpack_pair(tiles, blocks, pair, put):
    e, g = tiles.edge, tiles.rows
    for d, (a, b) in enumerate(tiles.above):
        put(a, b, blocks[d, pair, :, :e].astype(WIDE))
        put(b, a, blocks[d, pair, :, e:].astype(WIDE).T)
    for d, c, k in tiles.diagonal:
        upper = blocks[d, pair, c * g:(c + 1) * g, :e]
        lower = blocks[d, pair, c * g:(c + 1) * g, e:]
        put(k, k, jnp.concatenate([upper, lower], axis=0).astype(WIDE))


def pack_kernel(tiles, source, out):
    for pair in range(source.shape[0]):
        pack_pair(tiles, source.at[pair], out, pair, mirrored=True)


def pack(tiles, devices, amplitudes):
    count = amplitudes.shape[0]
    out = jax.ShapeDtypeStruct((devices, count, tiles.edge, 2 * tiles.edge), NARROW)
    return call(functools.partial(pack_kernel, tiles), out, [], amplitudes.size, amplitudes.size * 6,
                amplitudes, specs=[VMEM])


def assemble(place, order, pieces, whole):
    k = 0
    for piece in pieces:
        count, rows, virtual = piece.shape[-3:]
        for block in range(piece.shape[0] if len(piece.shape) == 4 else 1):
            start = pl.multiple_of((place[1] ^ order[k]) * rows, rows)
            for single in range(count):
                values = piece[block, single] if len(piece.shape) == 4 else piece[single]
                whole[pl.ds(start, rows), single * virtual:(single + 1) * virtual] = values
            k += 1


def ladder_pair(matrix, whole, inner, total):
    virtual = matrix.shape[0]
    for single in range(whole.shape[1] // virtual):
        at = slice(single * virtual, (single + 1) * virtual)
        inner[at, :] = lax.dot_general(
            matrix, whole[:, at], (((1,), (1,)), ((), ())), preferred_element_type=WIDE
        ).astype(NARROW)
    total[...] = jnp.dot(whole[...], inner[...], preferred_element_type=WIDE)


def inverse(x):
    guess = pl.reciprocal(x, approx=True)
    return guess * (2.0 - x * guess)


def first_ladder_kernel(tiles, order, place, source, *refs):
    pieces, (out, whole, inner, total) = refs[:-4], refs[-4:]
    assemble(place, order, pieces, whole)
    for pair in range(source.shape[0]):
        ladder_pair(source[pair].astype(NARROW), whole, inner, total)
        pack_pair(tiles, total, out, pair)


def second_ladder_kernel(tiles, order, place, occ, source, blocks, row, column, *refs):
    pieces, (out, whole, inner, total, matrix) = refs[:-5], refs[-5:]
    assemble(place, order, pieces, whole)
    count = source.shape[0]
    for pair in range(count):
        def put(a, b, tile):
            matrix[tiles.span(a), tiles.span(b)] = tile.astype(NARROW)

        unpack_pair(tiles, blocks, pair, put)
        ladder_pair(matrix[...], whole, inner, total)
        base = occ[place[0] * count + pair] + occ[place[1]]

        def finish(step, carry):
            at = pl.ds(pl.multiple_of(step * 16, 16), 16)
            own = base - row[at, :1] - column[...]
            out[pair, at, :] = (
                source[pair, at, :] + 2.0 * (matrix[at, :].astype(WIDE) + total[at, :] * inverse(own))
            )
            return carry

        lax.fori_loop(0, total.shape[0] // 16, finish, 0)


def add_kernel(tiles, source, blocks, out):
    for pair in range(source.shape[0]):
        def put(a, b, tile):
            here = (pair, tiles.span(a), tiles.span(b))
            out[here] = source[here] + tile

        unpack_pair(tiles, blocks, pair, put)


def mix(place, fock, first, load, store, rows, width):
    total = fock.shape[0]
    strips = rows // 16

    def strip(step, carry):
        u = step // strips
        at = pl.ds(pl.multiple_of(lax.rem(step, strips) * 16, 16), 16)
        taken = [load(k // first, u, k % first, at) for k in range(total)]
        for k in range(total):
            column = (place[0] ^ (k // first)) * first + k % first
            result = None
            for m in range(total):
                line = (place[0] ^ (m // first)) * first + m % first
                term = (-fock[line, column]) * taken[m]
                result = term if result is None else result + term
            store(k // first, u, k % first, column, at, result)
        return carry

    lax.fori_loop(0, first * strips, strip, 0)


def half_kernel(tiles, groups, first, place, fock, ladder, *refs):
    held, out = refs[:groups], refs[groups:]

    def load(s, u, r, at):
        return held[s][u, r, at, :].astype(WIDE)

    def store(s, u, w, column, at, result):
        out[s][u, w, at, :] = (ladder[column, u, at, :].astype(WIDE) + result).astype(NARROW)

    mix(place, fock, first, load, store, tiles.edge, 2 * tiles.edge)


def with_mirror(tiles, place, x, finish):
    across = place[1] < len(tiles.above)

    @pl.when(across)
    def _():
        finish(tiles.mirror_across(x))

    @pl.when(jnp.logical_not(across))
    def _():
        finish(tiles.mirror_within(x))


def update_kernel(tiles, groups, first, place, fock, occ, sums, *refs):
    own, other = refs[:groups], refs[groups:2 * groups]
    sent, rest = refs[2 * groups:2 * groups + 2]
    out = refs[2 * groups + 2:3 * groups + 2]
    update = refs[3 * groups + 2]

    def one(step, carry):
        u, w = step // first, lax.rem(step, first)
        for s in range(groups):
            column = (place[0] ^ s) * first + w
            base = occ[place[0] * first + u] + occ[column]

            def finish(mirrored):
                value = (own[s][u, w].astype(WIDE) + mirrored) * inverse(base - sums[...])
                narrow = value.astype(NARROW)
                update[u, s * first + w] = value
                sent[column, u] = narrow
                rest[u, s * first + w] = (2.0 * (value - narrow.astype(WIDE))).astype(NARROW)

            with_mirror(tiles, place, other[s][w, u].astype(WIDE), finish)
        return carry

    lax.fori_loop(0, first * first, one, 0)

    def load(s, u, r, at):
        return update[u, s * first + r, at, :]

    def store(s, u, w, column, at, result):
        out[s][u, w, at, :] = result.astype(NARROW)

    mix(place, fock, first, load, store, tiles.edge, 2 * tiles.edge)


def rest_kernel(tiles, groups, first, place, occ, sums, rest, *refs):
    own, other, out = refs[:groups], refs[groups:2 * groups], refs[2 * groups]

    def one(step, carry):
        u, w = step // first, lax.rem(step, first)
        for s in range(groups):
            column = (place[0] ^ s) * first + w
            base = occ[place[0] * first + u] + occ[column]

            def finish(mirrored):
                value = (own[s][u, w].astype(WIDE) + mirrored) * inverse(base - sums[...])
                out[column, u] = (rest[u, s * first + w].astype(WIDE) + value).astype(NARROW)

            with_mirror(tiles, place, other[s][w, u].astype(WIDE), finish)
        return carry

    lax.fori_loop(0, first * first, one, 0)


def exchange(blocks):
    return lax.all_to_all(blocks, "occj", split_axis=0, concat_axis=0, tiled=True)


def across_first(parts, groups):
    return [parts[0]] + [
        lax.ppermute(parts[s], "occi", [(k, k ^ s) for k in range(groups)])
        for s in range(groups - 1, 0, -1)
    ][::-1]


def tie(x, *others):
    return lax.optimization_barrier((x, *others))[0]


def copy_kernel(source, out):
    for k in range(source.shape[0]):
        out[k] = source[k]


def after(x, *others):
    return pl.pallas_call(
        copy_kernel,
        out_shape=jax.ShapeDtypeStruct(x.shape, x.dtype),
        in_specs=[SMEM],
        out_specs=SMEM,
        cost_estimate=pl.CostEstimate(flops=LONG, bytes_accessed=8, transcendentals=0),
    )(tie(x, *others))


def gather_vectors(vectors, devices):
    def turn(x, k):
        return lax.ppermute(x, "occj", [(d, d ^ k) for d in range(devices)])

    even = list(range(0, devices, 2))
    held = [vectors] + [turn(vectors, k) for k in even[1:]]
    other = turn(jnp.stack(held), 1)
    return [*held, other], even + [k ^ 1 for k in even]


def virtual_sums(tiles, vir_energy, q):
    e, g = tiles.edge, tiles.rows
    n_above = len(tiles.above)
    first = jnp.array([a for a, _ in tiles.above] + list(range(0, tiles.n, 2)), jnp.int32)[q]
    second = jnp.array([b for _, b in tiles.above] + list(range(1, tiles.n, 2)), jnp.int32)[q]
    a = lax.dynamic_slice_in_dim(vir_energy, first * e, e)
    b = lax.dynamic_slice_in_dim(vir_energy, second * e, e)
    pair = a[:, None] + b[None, :]
    across = jnp.concatenate([pair, pair], axis=1)
    halves = [
        jnp.concatenate([t[:g, None] + t[None, :], t[g:, None] + t[None, :]], axis=1) for t in (a, b)
    ]
    return jnp.where(q < n_above, across, jnp.concatenate(halves, axis=0))


def local(groups, devices, amplitudes, vectors, occupied_fock_block, occ_energy, vir_energy):
    first, second, virtual = amplitudes.shape[:3]
    assert second == 1 and groups * first == devices
    assert groups & (groups - 1) == 0 and devices & (devices - 1) == 0
    tiles = Tiles(devices, virtual)
    edge = tiles.edge
    current = amplitudes.reshape(first, virtual, virtual)
    count = current.size
    fock = occupied_fock_block.astype(WIDE)
    p, q = lax.axis_index("occi"), lax.axis_index("occj")
    place = jnp.stack([p, q]).astype(jnp.int32)
    part = jax.ShapeDtypeStruct((first, first, edge, 2 * edge), NARROW)
    packed = jax.ShapeDtypeStruct((devices, first, edge, 2 * edge), NARROW)
    singles = vectors.shape[0]
    whole = pltpu.VMEM((virtual, singles * virtual), NARROW)
    inner = pltpu.VMEM((singles * virtual, virtual), NARROW)
    square = pltpu.VMEM((virtual, virtual), WIDE)

    started = pack(tiles, devices, current)
    pieces, order = gather_vectors(vectors, devices)
    held = exchange(tie(started, *pieces[:-1]))
    sums = virtual_sums(tiles, vir_energy, q)

    ladder_flops = first * singles * 4 * virtual**3
    ladder = call(
        functools.partial(first_ladder_kernel, tiles, order), packed, [whole, inner, square],
        ladder_flops, 8 * count, place, current, *pieces, specs=[SMEM] + [VMEM] * (1 + len(pieces)),
    )
    parts = tie(held, ladder).reshape(groups, first, first, edge, 2 * edge)
    mirror = across_first([parts[p ^ s] for s in range(groups)], groups)
    ladder = exchange(ladder)
    half = call(
        functools.partial(half_kernel, tiles, groups, first), [part] * groups, [],
        2 * devices * count, 6 * count, after(place, *mirror), fock, ladder, *mirror,
        specs=[SMEM] * 2 + [VMEM] * (groups + 1),
    )
    other = across_first(half, groups)
    sent, rest, *mixed = call(
        functools.partial(update_kernel, tiles, groups, first),
        [packed, jax.ShapeDtypeStruct((first, devices, edge, 2 * edge), NARROW)] + [part] * groups,
        [pltpu.VMEM((first, devices, edge, 2 * edge), WIDE)],
        2 * devices * count, 10 * count, place, fock, occ_energy, sums, *half, *other,
        specs=[SMEM] * 3 + [VMEM] * (2 * groups + 1),
    )
    other = across_first(mixed, groups)
    back = exchange(sent)
    base = call(
        functools.partial(second_ladder_kernel, tiles, order), jax.ShapeDtypeStruct(current.shape, WIDE),
        [whole, inner, square, pltpu.VMEM((virtual, virtual), NARROW)],
        ladder_flops, 12 * count, place, occ_energy, current, back,
        jnp.broadcast_to(vir_energy[:, None], (virtual, 128)), vir_energy[None, :], *pieces,
        specs=[SMEM] * 2 + [VMEM] * (4 + len(pieces)),
    )
    rest = exchange(call(
        functools.partial(rest_kernel, tiles, groups, first), packed, [],
        LONG, 8 * count, place, occ_energy, sums, rest, *mixed, *other,
        specs=[SMEM] * 2 + [VMEM] * (2 * groups + 2),
    ))
    done = call(
        functools.partial(add_kernel, tiles), jax.ShapeDtypeStruct(current.shape, WIDE), [],
        count, 10 * count, base, rest, specs=[VMEM, VMEM], aliases={0: 0},
    )
    return done.reshape(amplitudes.shape)


def solution(mesh):
    sizes = (mesh.shape["occi"], mesh.shape["occj"])
    return jax.shard_map(
        functools.partial(local, *sizes),
        mesh=mesh,
        in_specs=(P("occi", "occj", None, None), P(None, "occj", None), P(), P(), P()),
        out_specs=P("occi", "occj", None, None),
        check_vma=False,
    )
```

```python
import functools
import math

import jax
import jax.numpy as jnp
from jax import lax
from jax.experimental import pallas as pl
from jax.experimental.pallas import tpu as pltpu
from jax.sharding import PartitionSpec as P

VMEM = pl.BlockSpec(memory_space=pltpu.VMEM)
SMEM = pl.BlockSpec(memory_space=pltpu.SMEM)
PARAMS = pltpu.CompilerParams(vmem_limit_bytes=50 * 2**20)
WIDE = jnp.float32
LONG = 3 * 10**10
NARROW = jnp.bfloat16


class Tiles:
    def __init__(self, devices, virtual):
        n = math.isqrt(2 * devices)
        assert n * n == 2 * devices and n % 2 == 0 and virtual % n == 0
        self.n = n
        self.edge = virtual // n
        self.rows = self.edge // 2
        self.above = [(a, b) for a in range(n) for b in range(a + 1, n)]
        self.diagonal = [(len(self.above) + k // 2, k % 2, k) for k in range(n)]

    def span(self, k):
        return slice(k * self.edge, (k + 1) * self.edge)

    def mirror_within(self, x):
        e, g = self.edge, self.rows
        tile = jnp.concatenate([x[:, :e], x[:, e:]], axis=0).T
        return jnp.concatenate([tile[:g], tile[g:]], axis=1)

    def mirror_across(self, x):
        return jnp.concatenate([x[:, self.edge:], x[:, :self.edge]], axis=1)


def call(body, outs, scratch, flops, moved, *operands, specs, aliases=None):
    return pl.pallas_call(
        body,
        out_shape=outs,
        in_specs=specs,
        out_specs=jax.tree.map(lambda _: VMEM, outs),
        scratch_shapes=scratch,
        compiler_params=PARAMS,
        input_output_aliases=aliases or {},
        cost_estimate=pl.CostEstimate(flops=flops, bytes_accessed=moved, transcendentals=0),
    )(*operands)


def pack_pair(tiles, source, outs, pair, mirrored=False):
    e, g = tiles.edge, tiles.rows
    straight, turned = (slice(e, None), slice(0, e)) if mirrored else (slice(0, e), slice(e, None))
    for d, (a, b) in enumerate(tiles.above):
        tile = source[tiles.span(a), tiles.span(b)].astype(NARROW)
        other = source[tiles.span(b), tiles.span(a)].astype(WIDE).T.astype(NARROW)
        for c, out in enumerate(outs):
            out[d, pair, :, straight] = tile[c * g:(c + 1) * g]
            out[d, pair, :, turned] = other[c * g:(c + 1) * g]
    for d, c, k in tiles.diagonal:
        tile = source[tiles.span(k), tiles.span(k)]
        tile = tile.astype(WIDE).T.astype(NARROW) if mirrored else tile.astype(NARROW)
        outs[c][d, pair, :, :e] = tile[:g]
        outs[c][d, pair, :, e:] = tile[g:]


def unpack_pair(tiles, chunks, pair, put):
    e = tiles.edge
    for d, (a, b) in enumerate(tiles.above):
        block = jnp.concatenate([chunk[d, pair] for chunk in chunks], axis=0).astype(WIDE)
        put(a, b, block[:, :e])
        put(b, a, block[:, e:].T)
    for d, c, k in tiles.diagonal:
        block = chunks[c][d, pair].astype(WIDE)
        put(k, k, jnp.concatenate([block[:, :e], block[:, e:]], axis=0))


def pack_kernel(tiles, source, *outs):
    for pair in range(source.shape[0]):
        pack_pair(tiles, source.at[pair], outs, pair, mirrored=True)


def assemble(place, order, pieces, whole):
    k = 0
    for piece in pieces:
        count, rows, virtual = piece.shape[-3:]
        for block in range(piece.shape[0] if len(piece.shape) == 4 else 1):
            start = pl.multiple_of((place[1] ^ order[k]) * rows, rows)
            for single in range(count):
                values = piece[block, single] if len(piece.shape) == 4 else piece[single]
                whole[pl.ds(start, rows), single * virtual:(single + 1) * virtual] = values
            k += 1


def ladder_pair(matrix, whole, inner, total):
    virtual = matrix.shape[0]
    for single in range(whole.shape[1] // virtual):
        at = slice(single * virtual, (single + 1) * virtual)
        inner[at, :] = lax.dot_general(
            matrix, whole[:, at], (((1,), (1,)), ((), ())), preferred_element_type=WIDE
        ).astype(NARROW)
    total[...] = jnp.dot(whole[...], inner[...], preferred_element_type=WIDE)


def inverse(x):
    guess = pl.reciprocal(x, approx=True)
    return guess * (2.0 - x * guess)


def first_ladder_kernel(tiles, order, place, source, *refs):
    pieces, outs, (whole, inner, total) = refs[:-5], refs[-5:-3], refs[-3:]
    assemble(place, order, pieces, whole)
    for pair in range(source.shape[0]):
        ladder_pair(source[pair].astype(NARROW), whole, inner, total)
        pack_pair(tiles, total, outs, pair)


def second_ladder_kernel(tiles, order, place, occ, source, upper, lower, row, column, *refs):
    pieces, (out, whole, inner, total, matrix) = refs[:-5], refs[-5:]
    assemble(place, order, pieces, whole)
    count = source.shape[0]
    for pair in range(count):
        def put(a, b, tile):
            matrix[tiles.span(a), tiles.span(b)] = tile.astype(NARROW)

        unpack_pair(tiles, (upper, lower), pair, put)
        ladder_pair(matrix[...], whole, inner, total)
        base = occ[place[0] * count + pair] + occ[place[1]]

        def finish(step, carry):
            at = pl.ds(pl.multiple_of(step * 16, 16), 16)
            own = base - row[at, :1] - column[...]
            out[pair, at, :] = (
                source[pair, at, :] + 2.0 * (matrix[at, :].astype(WIDE) + total[at, :] * inverse(own))
            )
            return carry

        lax.fori_loop(0, total.shape[0] // 16, finish, 0)


def add_kernel(tiles, source, blocks, out):
    chunks = [blocks.at[:, :, :tiles.rows], blocks.at[:, :, tiles.rows:]]
    for pair in range(source.shape[0]):
        def put(a, b, tile):
            here = (pair, tiles.span(a), tiles.span(b))
            out[here] = source[here] + tile

        unpack_pair(tiles, chunks, pair, put)


def mix(place, fock, first, load, store, rows):
    total = fock.shape[0]
    strips = rows // 16

    def strip(step, carry):
        u = step // strips
        at = pl.ds(pl.multiple_of(lax.rem(step, strips) * 16, 16), 16)
        taken = [load(k // first, u, k % first, at) for k in range(total)]
        for k in range(total):
            column = (place[0] ^ (k // first)) * first + k % first
            result = None
            for m in range(total):
                line = (place[0] ^ (m // first)) * first + m % first
                term = (-fock[line, column]) * taken[m]
                result = term if result is None else result + term
            store(k // first, u, k % first, column, at, result)
        return carry

    lax.fori_loop(0, first * strips, strip, 0)


def half_kernel(tiles, groups, first, place, fock, ladder, *refs):
    held, out = refs[:groups], refs[groups:]

    def load(s, u, r, at):
        return held[s][u, r, at, :].astype(WIDE)

    def store(s, u, w, column, at, result):
        out[s][u, w, at, :] = (ladder[column, u, at, :].astype(WIDE) + result).astype(NARROW)

    mix(place, fock, first, load, store, tiles.rows)


def with_mirror(tiles, place, x, finish):
    across = place[1] < len(tiles.above)

    @pl.when(across)
    def _():
        finish(tiles.mirror_across(x))

    @pl.when(jnp.logical_not(across))
    def _():
        finish(tiles.mirror_within(x))


def update_kernel(tiles, groups, first, chunk, place, fock, occ, sums, *refs):
    own, other = refs[:groups], refs[groups:2 * groups]
    sent, rest = refs[2 * groups:2 * groups + 2]
    out = refs[2 * groups + 2:3 * groups + 2]
    update = refs[3 * groups + 2]
    here = slice(chunk * tiles.rows, (chunk + 1) * tiles.rows)

    def one(step, carry):
        u, w = step // first, lax.rem(step, first)
        for s in range(groups):
            column = (place[0] ^ s) * first + w
            base = occ[place[0] * first + u] + occ[column]

            def finish(mirrored):
                value = (own[s][u, w].astype(WIDE) + mirrored) * inverse(base - sums[here])
                narrow = value.astype(NARROW)
                update[u, s * first + w] = value
                sent[column, u] = narrow
                rest[u, s * first + w] = (2.0 * (value - narrow.astype(WIDE))).astype(NARROW)

            with_mirror(tiles, place, other[s][w, u].astype(WIDE), finish)
        return carry

    lax.fori_loop(0, first * first, one, 0)

    def load(s, u, r, at):
        return update[u, s * first + r, at, :]

    def store(s, u, w, column, at, result):
        out[s][u, w, at, :] = result.astype(NARROW)

    mix(place, fock, first, load, store, tiles.rows)


def rest_kernel(tiles, groups, first, chunk, place, occ, sums, rest, *refs):
    before, refs = refs[:chunk], refs[chunk:]
    own, other, out = refs[:groups], refs[groups:2 * groups], refs[2 * groups]
    here = slice(chunk * tiles.rows, (chunk + 1) * tiles.rows)
    for ref in before:
        out[:, :, :tiles.rows, :] = ref[...]

    def one(step, carry):
        u, w = step // first, lax.rem(step, first)
        for s in range(groups):
            column = (place[0] ^ s) * first + w
            base = occ[place[0] * first + u] + occ[column]

            def finish(mirrored):
                value = (own[s][u, w].astype(WIDE) + mirrored) * inverse(base - sums[here])
                out[column, u, here] = (rest[u, s * first + w].astype(WIDE) + value).astype(NARROW)

            with_mirror(tiles, place, other[s][w, u].astype(WIDE), finish)
        return carry

    lax.fori_loop(0, first * first, one, 0)


def exchange(blocks):
    return lax.all_to_all(blocks, "occj", split_axis=0, concat_axis=0, tiled=True)


def across_first(parts, groups):
    return [parts[0]] + [
        lax.ppermute(parts[s], "occi", [(k, k ^ s) for k in range(groups)])
        for s in range(groups - 1, 0, -1)
    ][::-1]


def tie(x, *others):
    return lax.optimization_barrier((x, *others))[0]


def copy_kernel(source, out):
    for k in range(source.shape[0]):
        out[k] = source[k]


def after(x, *others):
    return pl.pallas_call(
        copy_kernel,
        out_shape=jax.ShapeDtypeStruct(x.shape, x.dtype),
        in_specs=[SMEM],
        out_specs=SMEM,
        cost_estimate=pl.CostEstimate(flops=LONG, bytes_accessed=8, transcendentals=0),
    )(tie(x, *others))


def gather_vectors(vectors, devices, packed):
    def turn(x, k):
        return lax.ppermute(x, "occj", [(d, d ^ k) for d in range(devices)])

    even = list(range(0, devices, 2))
    held = [vectors] + [turn(vectors, k) for k in even[1:]]
    other = turn(tie(jnp.stack(held), packed), 1)
    return [*held, other], even + [k ^ 1 for k in even]


def virtual_sums(tiles, vir_energy, q):
    e, g = tiles.edge, tiles.rows
    n_above = len(tiles.above)
    first = jnp.array([a for a, _ in tiles.above] + list(range(0, tiles.n, 2)), jnp.int32)[q]
    second = jnp.array([b for _, b in tiles.above] + list(range(1, tiles.n, 2)), jnp.int32)[q]
    a = lax.dynamic_slice_in_dim(vir_energy, first * e, e)
    b = lax.dynamic_slice_in_dim(vir_energy, second * e, e)
    pair = a[:, None] + b[None, :]
    across = jnp.concatenate([pair, pair], axis=1)
    halves = [
        jnp.concatenate([t[:g, None] + t[None, :], t[g:, None] + t[None, :]], axis=1) for t in (a, b)
    ]
    return jnp.where(q < n_above, across, jnp.concatenate(halves, axis=0))


def local(groups, devices, amplitudes, vectors, occupied_fock_block, occ_energy, vir_energy):
    first, second, virtual = amplitudes.shape[:3]
    assert second == 1 and groups * first == devices
    assert groups & (groups - 1) == 0 and devices & (devices - 1) == 0
    tiles = Tiles(devices, virtual)
    edge = tiles.edge
    current = amplitudes.reshape(first, virtual, virtual)
    count = current.size
    fock = occupied_fock_block.astype(WIDE)
    p, q = lax.axis_index("occi"), lax.axis_index("occj")
    place = jnp.stack([p, q]).astype(jnp.int32)
    packed = jax.ShapeDtypeStruct((devices, first, edge, 2 * edge), NARROW)
    upper = jax.ShapeDtypeStruct((devices, first, tiles.rows, 2 * edge), NARROW)
    part = jax.ShapeDtypeStruct((first, first, tiles.rows, 2 * edge), NARROW)
    singles = vectors.shape[0]
    whole = pltpu.VMEM((virtual, singles * virtual), NARROW)
    inner = pltpu.VMEM((singles * virtual, virtual), NARROW)
    square = pltpu.VMEM((virtual, virtual), WIDE)
    chunks = range(2)

    started = call(functools.partial(pack_kernel, tiles), [upper] * 2, [], count, 6 * count, current, specs=[VMEM])
    pieces, order = gather_vectors(vectors, devices, started[0])
    held = [exchange(tie(started[0], *pieces[:-1])), exchange(started[1])]
    sums = virtual_sums(tiles, vir_energy, q)

    ladder_flops = first * singles * 4 * virtual**3
    ladder = call(
        functools.partial(first_ladder_kernel, tiles, order), [upper] * 2, [whole, inner, square],
        ladder_flops, 8 * count, place, current, *pieces, specs=[SMEM] + [VMEM] * (1 + len(pieces)),
    )
    mirror = []
    for c in chunks:
        parts = tie(held[c], *ladder).reshape(groups, first, *part.shape[1:])
        mirror.append(across_first([parts[p ^ s] for s in range(groups)], groups))
    ladder = [exchange(x) for x in ladder]

    half, other = [], []
    for c in chunks:
        half.append(call(
            functools.partial(half_kernel, tiles, groups, first), [part] * groups, [],
            LONG, 6 * count, after(place, *mirror[c]) if c == 0 else place, fock, ladder[c], *mirror[c],
            specs=[SMEM] * 2 + [VMEM] * (groups + 1),
        ))
        other.append(across_first(half[c], groups))
    back, rest, mixed = [], [], []
    for c in chunks:
        sent, rest_one, *mixed_one = call(
            functools.partial(update_kernel, tiles, groups, first, c),
            [upper, jax.ShapeDtypeStruct((first, devices, *part.shape[2:]), NARROW)] + [part] * groups,
            [pltpu.VMEM((first, devices, *part.shape[2:]), WIDE)],
            LONG, 10 * count, place, fock, occ_energy, sums, *half[c], *other[c],
            specs=[SMEM] * 3 + [VMEM] * (2 * groups + 1),
        )
        back, rest, mixed = back + [exchange(sent)], rest + [rest_one], mixed + [mixed_one]
    other = [across_first(x, groups) for x in mixed]
    base = call(
        functools.partial(second_ladder_kernel, tiles, order), jax.ShapeDtypeStruct(current.shape, WIDE),
        [whole, inner, square, pltpu.VMEM((virtual, virtual), NARROW)],
        ladder_flops, 12 * count, place, occ_energy, current, *back,
        jnp.broadcast_to(vir_energy[:, None], (virtual, 128)), vir_energy[None, :], *pieces,
        specs=[SMEM] * 2 + [VMEM] * (5 + len(pieces)),
    )
    last = []
    for c in chunks:
        last = [call(
            functools.partial(rest_kernel, tiles, groups, first, c), (upper, packed)[c], [],
            LONG, 8 * count, place, occ_energy, sums, rest[c], *last, *mixed[c], *other[c],
            specs=[SMEM] * 2 + [VMEM] * (2 * groups + 2 + c),
        )]
    rest = exchange(last[0])
    done = call(
        functools.partial(add_kernel, tiles), jax.ShapeDtypeStruct(current.shape, WIDE), [],
        count, 10 * count, base, rest, specs=[VMEM, VMEM], aliases={0: 0},
    )
    return done.reshape(amplitudes.shape)


def solution(mesh):
    sizes = (mesh.shape["occi"], mesh.shape["occj"])
    return jax.shard_map(
        functools.partial(local, *sizes),
        mesh=mesh,
        in_specs=(P("occi", "occj", None, None), P(None, "occj", None), P(), P(), P()),
        out_specs=P("occi", "occj", None, None),
        check_vma=False,
    )
```

```python
import functools
import math

import jax
import jax.numpy as jnp
from jax import lax
from jax.experimental import pallas as pl
from jax.experimental.pallas import tpu as pltpu
from jax.sharding import PartitionSpec as P

VMEM = pl.BlockSpec(memory_space=pltpu.VMEM)
SMEM = pl.BlockSpec(memory_space=pltpu.SMEM)
PARAMS = pltpu.CompilerParams(vmem_limit_bytes=50 * 2**20)
WIDE = jnp.float32
LONG = 3 * 10**10
NARROW = jnp.bfloat16


class Tiles:
    def __init__(self, devices, virtual):
        n = math.isqrt(2 * devices)
        assert n * n == 2 * devices and n % 2 == 0 and virtual % n == 0
        self.n = n
        self.edge = virtual // n
        self.rows = self.edge // 2
        self.above = [(a, b) for a in range(n) for b in range(a + 1, n)]
        self.diagonal = [(len(self.above) + k // 2, k % 2, k) for k in range(n)]

    def span(self, k):
        return slice(k * self.edge, (k + 1) * self.edge)

    def mirror_within(self, x):
        e, g = self.edge, self.rows
        tile = jnp.concatenate([x[:, :e], x[:, e:]], axis=0).T
        return jnp.concatenate([tile[:g], tile[g:]], axis=1)

    def mirror_across(self, x):
        return jnp.concatenate([x[:, self.edge:], x[:, :self.edge]], axis=1)


def call(body, outs, scratch, flops, moved, *operands, specs, aliases=None):
    return pl.pallas_call(
        body,
        out_shape=outs,
        in_specs=specs,
        out_specs=jax.tree.map(lambda _: VMEM, outs),
        scratch_shapes=scratch,
        compiler_params=PARAMS,
        input_output_aliases=aliases or {},
        cost_estimate=pl.CostEstimate(flops=flops, bytes_accessed=moved, transcendentals=0),
    )(*operands)


def pack_pair(tiles, source, out, pair, mirrored=False):
    e, g = tiles.edge, tiles.rows
    straight, turned = (slice(e, None), slice(0, e)) if mirrored else (slice(0, e), slice(e, None))
    for d, (a, b) in enumerate(tiles.above):
        out[d, pair, :, straight] = source[tiles.span(a), tiles.span(b)].astype(NARROW)
        out[d, pair, :, turned] = source[tiles.span(b), tiles.span(a)].astype(WIDE).T.astype(NARROW)
    for d, c, k in tiles.diagonal:
        tile = source[tiles.span(k), tiles.span(k)]
        tile = tile.astype(WIDE).T.astype(NARROW) if mirrored else tile.astype(NARROW)
        out[d, pair, c * g:(c + 1) * g, :e] = tile[:g]
        out[d, pair, c * g:(c + 1) * g, e:] = tile[g:]


def unpack_pair(tiles, blocks, pair, put):
    e, g = tiles.edge, tiles.rows
    for d, (a, b) in enumerate(tiles.above):
        put(a, b, blocks[d, pair, :, :e].astype(WIDE))
        put(b, a, blocks[d, pair, :, e:].astype(WIDE).T)
    for d, c, k in tiles.diagonal:
        upper = blocks[d, pair, c * g:(c + 1) * g, :e]
        lower = blocks[d, pair, c * g:(c + 1) * g, e:]
        put(k, k, jnp.concatenate([upper, lower], axis=0).astype(WIDE))


def to_distances(place, whole, outs):
    for k, out in enumerate(outs):
        out[...] = whole[place[1] ^ k]


def from_distances(place, pieces, whole):
    for k, piece in enumerate(pieces):
        whole[place[1] ^ k] = piece[...]


def pack_kernel(tiles, place, source, *refs):
    outs, whole = refs[:-1], refs[-1]
    for pair in range(source.shape[0]):
        pack_pair(tiles, source.at[pair], whole, pair, mirrored=True)
    to_distances(place, whole, outs)


def sort_kernel(tiles, groups, place, *refs):
    pieces, outs, whole = refs[:-2 * groups - 1], refs[-2 * groups - 1:-1], refs[-1]
    first = whole.shape[1]
    from_distances(place, pieces, whole)
    for s in range(groups):
        for u in range(first):
            block = whole[(place[0] ^ s) * first + u]
            for c in range(2):
                outs[c * groups + s][u] = block[:, c * tiles.rows:(c + 1) * tiles.rows]


def assemble(place, order, pieces, whole):
    k = 0
    for piece in pieces:
        count, rows, virtual = piece.shape[-3:]
        for block in range(piece.shape[0] if len(piece.shape) == 4 else 1):
            start = pl.multiple_of((place[1] ^ order[k]) * rows, rows)
            for single in range(count):
                values = piece[block, single] if len(piece.shape) == 4 else piece[single]
                whole[pl.ds(start, rows), single * virtual:(single + 1) * virtual] = values
            k += 1


def ladder_pair(matrix, whole, inner, total):
    virtual = matrix.shape[0]
    for single in range(whole.shape[1] // virtual):
        at = slice(single * virtual, (single + 1) * virtual)
        inner[at, :] = lax.dot_general(
            matrix, whole[:, at], (((1,), (1,)), ((), ())), preferred_element_type=WIDE
        ).astype(NARROW)
    total[...] = jnp.dot(whole[...], inner[...], preferred_element_type=WIDE)


def inverse(x):
    guess = pl.reciprocal(x, approx=True)
    return guess * (2.0 - x * guess)


def first_ladder_kernel(tiles, order, place, source, *refs):
    pieces, (out, whole, inner, total) = refs[:-4], refs[-4:]
    assemble(place, order, pieces, whole)
    for pair in range(source.shape[0]):
        ladder_pair(source[pair].astype(NARROW), whole, inner, total)
        pack_pair(tiles, total, out, pair)


def second_ladder_kernel(tiles, order, place, occ, source, blocks, row, column, *refs):
    pieces, (out, whole, inner, total, matrix) = refs[:-5], refs[-5:]
    assemble(place, order, pieces, whole)
    count = source.shape[0]
    for pair in range(count):
        def put(a, b, tile):
            matrix[tiles.span(a), tiles.span(b)] = tile.astype(NARROW)

        unpack_pair(tiles, blocks, pair, put)
        ladder_pair(matrix[...], whole, inner, total)
        base = occ[place[0] * count + pair] + occ[place[1]]
        strip = math.gcd(64, total.shape[0])

        def finish(step, carry):
            at = pl.ds(pl.multiple_of(step * strip, strip), strip)
            own = base - row[at, :1] - column[...]
            out[pair, at, :] = (
                source[pair, at, :] + 2.0 * (matrix[at, :].astype(WIDE) + total[at, :] * inverse(own))
            )
            return carry

        lax.fori_loop(0, total.shape[0] // strip, finish, 0)


def add_kernel(tiles, place, source, *refs):
    pieces, (out, whole) = refs[:-2], refs[-2:]
    from_distances(place, pieces, whole)
    for pair in range(source.shape[0]):
        def put(a, b, tile):
            here = (pair, tiles.span(a), tiles.span(b))
            out[here] = source[here] + tile

        unpack_pair(tiles, whole, pair, put)


def mix(place, fock, first, load, store, rows):
    total = fock.shape[0]
    strips = rows // 16

    def strip(step, carry):
        u = step // strips
        at = pl.ds(pl.multiple_of(lax.rem(step, strips) * 16, 16), 16)
        taken = [load(k // first, u, k % first, at) for k in range(total)]
        for k in range(total):
            column = (place[0] ^ (k // first)) * first + k % first
            result = None
            for m in range(total):
                line = (place[0] ^ (m // first)) * first + m % first
                term = (-fock[line, column]) * taken[m]
                result = term if result is None else result + term
            store(k // first, u, k % first, column, at, result)
        return carry

    lax.fori_loop(0, first * strips, strip, 0)


def half_kernel(tiles, groups, first, chunk, place, fock, ladder, *refs):
    held, out = refs[:groups], refs[groups:]

    def load(s, u, r, at):
        return held[s][u, r, at, :].astype(WIDE)

    def store(s, u, w, column, at, result):
        rows = pl.ds(pl.multiple_of(chunk * tiles.rows + at.start, 16), at.size)
        out[s][u, w, at, :] = (ladder[column, u, rows, :].astype(WIDE) + result).astype(NARROW)

    mix(place, fock, first, load, store, tiles.rows)


def with_mirror(tiles, place, x, finish):
    across = place[1] < len(tiles.above)

    @pl.when(across)
    def _():
        finish(tiles.mirror_across(x))

    @pl.when(jnp.logical_not(across))
    def _():
        finish(tiles.mirror_within(x))


def update_kernel(tiles, groups, first, chunk, place, fock, occ, sums, *refs):
    before, refs = refs[:chunk], refs[chunk:]
    own, other = refs[:groups], refs[groups:2 * groups]
    sent, rest = refs[2 * groups:2 * groups + 2]
    out = refs[2 * groups + 2:3 * groups + 2]
    update = refs[3 * groups + 2]
    here = slice(chunk * tiles.rows, (chunk + 1) * tiles.rows)
    for ref in before:
        sent[:, :, :tiles.rows, :] = ref[...]

    def one(step, carry):
        u, w = step // first, lax.rem(step, first)
        for s in range(groups):
            column = (place[0] ^ s) * first + w
            base = occ[place[0] * first + u] + occ[column]

            def finish(mirrored):
                value = (own[s][u, w].astype(WIDE) + mirrored) * inverse(base - sums[here])
                narrow = value.astype(NARROW)
                update[u, s * first + w] = value
                sent[column, u, here] = narrow
                rest[u, s * first + w] = (2.0 * (value - narrow.astype(WIDE))).astype(NARROW)

            with_mirror(tiles, place, other[s][w, u].astype(WIDE), finish)
        return carry

    lax.fori_loop(0, first * first, one, 0)

    def load(s, u, r, at):
        return update[u, s * first + r, at, :]

    def store(s, u, w, column, at, result):
        out[s][u, w, at, :] = result.astype(NARROW)

    mix(place, fock, first, load, store, tiles.rows)


def rest_kernel(tiles, groups, first, chunk, place, occ, sums, rest, *refs):
    own, other, refs = refs[:groups], refs[groups:2 * groups], refs[2 * groups:]
    out = refs[-1]
    here = slice(chunk * tiles.rows, (chunk + 1) * tiles.rows)
    there = here if chunk else slice(None)
    if chunk:
        out[:, :, :tiles.rows, :] = refs[0][...]

    def one(step, carry):
        u, w = step // first, lax.rem(step, first)
        for s in range(groups):
            column = (place[0] ^ s) * first + w
            base = occ[place[0] * first + u] + occ[column]

            def finish(mirrored):
                value = (own[s][u, w].astype(WIDE) + mirrored) * inverse(base - sums[here])
                out[column, u, there] = (rest[u, s * first + w].astype(WIDE) + value).astype(NARROW)

            with_mirror(tiles, place, other[s][w, u].astype(WIDE), finish)
        return carry

    lax.fori_loop(0, first * first, one, 0)
    if chunk:
        to_distances(place, out, refs[1:-1])


def exchange(blocks):
    return lax.all_to_all(blocks, "occj", split_axis=0, concat_axis=0, tiled=True)


def by_distance(parts):
    devices = len(parts)
    return [parts[0]] + [
        lax.ppermute(parts[k], "occj", [(d, d ^ k) for d in range(devices)])
        for k in range(devices - 1, 0, -1)
    ][::-1]


def across_first(parts, groups):
    return [parts[0]] + [
        lax.ppermute(parts[s], "occi", [(k, k ^ s) for k in range(groups)])
        for s in range(groups - 1, 0, -1)
    ][::-1]


def tie(x, *others):
    return lax.optimization_barrier((x, *others))[0]


def copy_kernel(source, out):
    for k in range(source.shape[0]):
        out[k] = source[k]


def after(x, *others):
    return pl.pallas_call(
        copy_kernel,
        out_shape=jax.ShapeDtypeStruct(x.shape, x.dtype),
        in_specs=[SMEM],
        out_specs=SMEM,
        cost_estimate=pl.CostEstimate(flops=LONG, bytes_accessed=8, transcendentals=0),
    )(tie(x, *others))


def gather_vectors(vectors, devices, packed):
    def turn(x, k):
        return lax.ppermute(x, "occj", [(d, d ^ k) for d in range(devices)])

    even = list(range(0, devices, 2))
    held = [vectors] + [turn(vectors, k) for k in even[1:]]
    other = turn(tie(jnp.stack(held), packed), 1)
    return [*held, other], even + [k ^ 1 for k in even]


def virtual_sums(tiles, vir_energy, q):
    e, g = tiles.edge, tiles.rows
    n_above = len(tiles.above)
    first = jnp.array([a for a, _ in tiles.above] + list(range(0, tiles.n, 2)), jnp.int32)[q]
    second = jnp.array([b for _, b in tiles.above] + list(range(1, tiles.n, 2)), jnp.int32)[q]
    a = lax.dynamic_slice_in_dim(vir_energy, first * e, e)
    b = lax.dynamic_slice_in_dim(vir_energy, second * e, e)
    pair = a[:, None] + b[None, :]
    across = jnp.concatenate([pair, pair], axis=1)
    halves = [
        jnp.concatenate([t[:g, None] + t[None, :], t[g:, None] + t[None, :]], axis=1) for t in (a, b)
    ]
    return jnp.where(q < n_above, across, jnp.concatenate(halves, axis=0))


def local(groups, devices, amplitudes, vectors, occupied_fock_block, occ_energy, vir_energy):
    first, second, virtual = amplitudes.shape[:3]
    assert second == 1 and groups * first == devices
    assert groups & (groups - 1) == 0 and devices & (devices - 1) == 0
    tiles = Tiles(devices, virtual)
    edge = tiles.edge
    current = amplitudes.reshape(first, virtual, virtual)
    count = current.size
    fock = occupied_fock_block.astype(WIDE)
    p, q = lax.axis_index("occi"), lax.axis_index("occj")
    place = jnp.stack([p, q]).astype(jnp.int32)
    packed = jax.ShapeDtypeStruct((devices, first, edge, 2 * edge), NARROW)
    upper = jax.ShapeDtypeStruct((devices, first, tiles.rows, 2 * edge), NARROW)
    part = jax.ShapeDtypeStruct((first, first, tiles.rows, 2 * edge), NARROW)
    singles = vectors.shape[0]
    whole = pltpu.VMEM((virtual, singles * virtual), NARROW)
    inner = pltpu.VMEM((singles * virtual, virtual), NARROW)
    square = pltpu.VMEM((virtual, virtual), WIDE)
    chunks = range(2)

    distant = jax.ShapeDtypeStruct((first, edge, 2 * edge), NARROW)
    blocks = pltpu.VMEM(packed.shape, NARROW)
    started = call(functools.partial(pack_kernel, tiles), [distant] * devices, [blocks], count, 6 * count,
                   place, current, specs=[SMEM, VMEM])
    pieces, order = gather_vectors(vectors, devices, started[0])
    held = by_distance(started)
    sums = virtual_sums(tiles, vir_energy, q)

    ladder_flops = first * singles * 4 * virtual**3
    ladder = call(
        functools.partial(first_ladder_kernel, tiles, order), packed, [whole, inner, square],
        ladder_flops, 8 * count, place, current, *pieces, specs=[SMEM] + [VMEM] * (1 + len(pieces)),
    )
    parts = call(
        functools.partial(sort_kernel, tiles, groups), [part] * (2 * groups), [blocks], count, 4 * count,
        tie(place, ladder), *held, specs=[SMEM] + [VMEM] * devices,
    )
    mirror = [across_first(parts[c * groups:(c + 1) * groups], groups) for c in chunks]
    ladder = exchange(ladder)

    half, other = [], []
    for c in chunks:
        half.append(call(
            functools.partial(half_kernel, tiles, groups, first, c), [part] * groups, [],
            LONG, 6 * count, after(place, *mirror[c]) if c == 0 else place, fock, ladder, *mirror[c],
            specs=[SMEM] * 2 + [VMEM] * (groups + 1),
        ))
        other.append(across_first(half[c], groups))
    sent, rest, mixed = [], [], []
    for c in chunks:
        sent_one, rest_one, *mixed_one = call(
            functools.partial(update_kernel, tiles, groups, first, c),
            [(upper, packed)[c], jax.ShapeDtypeStruct((first, devices, *part.shape[2:]), NARROW)] + [part] * groups,
            [pltpu.VMEM((first, devices, *part.shape[2:]), WIDE)],
            LONG, 10 * count, place, fock, occ_energy, sums, *sent, *half[c], *other[c],
            specs=[SMEM] * 3 + [VMEM] * (2 * groups + 1 + c),
        )
        sent, rest, mixed = [sent_one], rest + [rest_one], mixed + [mixed_one]
    other = [across_first(x, groups) for x in mixed]
    back = exchange(sent[0])
    base = call(
        functools.partial(second_ladder_kernel, tiles, order), jax.ShapeDtypeStruct(current.shape, WIDE),
        [whole, inner, square, pltpu.VMEM((virtual, virtual), NARROW)],
        ladder_flops, 12 * count, place, occ_energy, current, back,
        jnp.broadcast_to(vir_energy[:, None], (virtual, 128)), vir_energy[None, :], *pieces,
        specs=[SMEM] * 2 + [VMEM] * (4 + len(pieces)),
    )
    last = []
    for c in chunks:
        last = call(
            functools.partial(rest_kernel, tiles, groups, first, c),
            [distant] * devices if c else [upper], [blocks] if c else [],
            LONG, 8 * count, place, occ_energy, sums, rest[c], *mixed[c], *other[c], *last,
            specs=[SMEM] * 2 + [VMEM] * (2 * groups + 2 + c),
        )
    done = call(
        functools.partial(add_kernel, tiles), jax.ShapeDtypeStruct(current.shape, WIDE), [blocks],
        count, 10 * count, place, base, *by_distance(last), specs=[SMEM] + [VMEM] * (1 + devices),
        aliases={1: 0},
    )
    return done.reshape(amplitudes.shape)


def solution(mesh):
    sizes = (mesh.shape["occi"], mesh.shape["occj"])
    return jax.shard_map(
        functools.partial(local, *sizes),
        mesh=mesh,
        in_specs=(P("occi", "occj", None, None), P(None, "occj", None), P(), P(), P()),
        out_specs=P("occi", "occj", None, None),
        check_vma=False,
    )
```

```python
import functools
import math

import jax
import jax.numpy as jnp
from jax import lax
from jax.experimental import pallas as pl
from jax.experimental.pallas import tpu as pltpu
from jax.sharding import PartitionSpec as P

VMEM = pl.BlockSpec(memory_space=pltpu.VMEM)
SMEM = pl.BlockSpec(memory_space=pltpu.SMEM)
PARAMS = pltpu.CompilerParams(vmem_limit_bytes=50 * 2**20)
WIDE = jnp.float32
LONG = 3 * 10**10
NARROW = jnp.bfloat16


class Tiles:
    def __init__(self, devices, virtual):
        n = math.isqrt(2 * devices)
        assert n * n == 2 * devices and n % 2 == 0 and virtual % n == 0
        self.n = n
        self.edge = virtual // n
        self.rows = self.edge // 2
        self.above = [(a, b) for a in range(n) for b in range(a + 1, n)]
        self.diagonal = [(len(self.above) + k // 2, k % 2, k) for k in range(n)]

    def span(self, k):
        return slice(k * self.edge, (k + 1) * self.edge)

    def mirror_within(self, x):
        e, g = self.edge, self.rows
        tile = jnp.concatenate([x[:, :e], x[:, e:]], axis=0).T
        return jnp.concatenate([tile[:g], tile[g:]], axis=1)

    def mirror_across(self, x):
        return jnp.concatenate([x[:, self.edge:], x[:, :self.edge]], axis=1)


def call(body, outs, scratch, flops, moved, *operands, specs):
    return pl.pallas_call(
        body,
        out_shape=outs,
        in_specs=specs,
        out_specs=jax.tree.map(lambda _: VMEM, outs),
        scratch_shapes=scratch,
        compiler_params=PARAMS,
        cost_estimate=pl.CostEstimate(flops=flops, bytes_accessed=moved, transcendentals=0),
    )(*operands)


def pack_pair(tiles, source, out, pair, mirrored=False):
    e, g = tiles.edge, tiles.rows
    straight, turned = (slice(e, None), slice(0, e)) if mirrored else (slice(0, e), slice(e, None))
    for d, (a, b) in enumerate(tiles.above):
        out[d, pair, :, straight] = source[tiles.span(a), tiles.span(b)].astype(NARROW)
        out[d, pair, :, turned] = source[tiles.span(b), tiles.span(a)].astype(WIDE).T.astype(NARROW)
    for d, c, k in tiles.diagonal:
        tile = source[tiles.span(k), tiles.span(k)]
        tile = tile.astype(WIDE).T.astype(NARROW) if mirrored else tile.astype(NARROW)
        out[d, pair, c * g:(c + 1) * g, :e] = tile[:g]
        out[d, pair, c * g:(c + 1) * g, e:] = tile[g:]


def unpack_pair(tiles, chunks, pair, put):
    e = tiles.edge
    for d, (a, b) in enumerate(tiles.above):
        block = jnp.concatenate([chunk[d, pair] for chunk in chunks], axis=0).astype(WIDE)
        put(a, b, block[:, :e])
        put(b, a, block[:, e:].T)
    for d, c, k in tiles.diagonal:
        block = chunks[c][d, pair].astype(WIDE)
        put(k, k, jnp.concatenate([block[:, :e], block[:, e:]], axis=0))


def to_distances(place, whole, outs):
    for k, out in enumerate(outs):
        out[...] = whole[place[1] ^ k]


def from_distances(place, pieces, whole):
    for k, piece in enumerate(pieces):
        whole[place[1] ^ k] = piece[...]


def pack_kernel(tiles, place, source, *refs):
    outs, whole = refs[:-1], refs[-1]
    for pair in range(source.shape[0]):
        pack_pair(tiles, source.at[pair], whole, pair, mirrored=True)
    to_distances(place, whole, outs)


def sort_kernel(tiles, groups, place, *refs):
    pieces, outs, whole = refs[:-2 * groups - 1], refs[-2 * groups - 1:-1], refs[-1]
    first = whole.shape[1]
    from_distances(place, pieces, whole)
    for s in range(groups):
        for u in range(first):
            block = whole[(place[0] ^ s) * first + u]
            for c in range(2):
                outs[c * groups + s][u] = block[:, c * tiles.rows:(c + 1) * tiles.rows]


def assemble(place, order, pieces, whole):
    k = 0
    for piece in pieces:
        count, rows, virtual = piece.shape[-3:]
        for block in range(piece.shape[0] if len(piece.shape) == 4 else 1):
            start = pl.multiple_of((place[1] ^ order[k]) * rows, rows)
            for single in range(count):
                values = piece[block, single] if len(piece.shape) == 4 else piece[single]
                whole[pl.ds(start, rows), single * virtual:(single + 1) * virtual] = values
            k += 1


def ladder_pair(matrix, whole, inner, total):
    virtual = matrix.shape[0]
    for single in range(whole.shape[1] // virtual):
        at = slice(single * virtual, (single + 1) * virtual)
        inner[at, :] = lax.dot_general(
            matrix, whole[:, at], (((1,), (1,)), ((), ())), preferred_element_type=WIDE
        ).astype(NARROW)
    total[...] = jnp.dot(whole[...], inner[...], preferred_element_type=WIDE)


def inverse(x):
    guess = pl.reciprocal(x, approx=True)
    return guess * (2.0 - x * guess)


def first_ladder_kernel(tiles, order, place, source, *refs):
    pieces, (out, whole, inner, total) = refs[:-4], refs[-4:]
    assemble(place, order, pieces, whole)
    for pair in range(source.shape[0]):
        ladder_pair(source[pair].astype(NARROW), whole, inner, total)
        pack_pair(tiles, total, out, pair)


def second_ladder_kernel(tiles, order, place, occ, source, upper, lower, row, column, *refs):
    pieces, (out, whole, inner, total, matrix) = refs[:-5], refs[-5:]
    assemble(place, order, pieces, whole)
    count = source.shape[0]
    for pair in range(count):
        def put(a, b, tile):
            matrix[tiles.span(a), tiles.span(b)] = tile.astype(NARROW)

        unpack_pair(tiles, (upper, lower), pair, put)
        ladder_pair(matrix[...], whole, inner, total)
        base = occ[place[0] * count + pair] + occ[place[1]]
        strip = math.gcd(64, total.shape[0])

        def finish(step, carry):
            at = pl.ds(pl.multiple_of(step * strip, strip), strip)
            own = base - row[at, :1] - column[...]
            out[pair, at, :] = (
                source[pair, at, :] + 2.0 * (matrix[at, :].astype(WIDE) + total[at, :] * inverse(own))
            )
            return carry

        lax.fori_loop(0, total.shape[0] // strip, finish, 0)


def add_kernel(tiles, place, source, *refs):
    pieces, (out, whole) = refs[:-2], refs[-2:]
    from_distances(place, pieces, whole)

    def put(a, b, tile):
        here = (0, tiles.span(a), tiles.span(b))
        out[here] = source[here] + tile

    unpack_pair(tiles, [whole.at[:, :, :tiles.rows], whole.at[:, :, tiles.rows:]], 0, put)


def mix(place, fock, first, load, store, rows):
    total = fock.shape[0]
    strips = rows // 16

    def strip(step, carry):
        u = step // strips
        at = pl.ds(pl.multiple_of(lax.rem(step, strips) * 16, 16), 16)
        taken = [load(k // first, u, k % first, at) for k in range(total)]
        for k in range(total):
            column = (place[0] ^ (k // first)) * first + k % first
            result = None
            for m in range(total):
                line = (place[0] ^ (m // first)) * first + m % first
                term = (-fock[line, column]) * taken[m]
                result = term if result is None else result + term
            store(k // first, u, k % first, column, at, result)
        return carry

    lax.fori_loop(0, first * strips, strip, 0)


def half_kernel(tiles, groups, first, chunk, place, fock, ladder, *refs):
    held, out = refs[:groups], refs[groups:]

    def load(s, u, r, at):
        return held[s][u, r, at, :].astype(WIDE)

    def store(s, u, w, column, at, result):
        rows = pl.ds(pl.multiple_of(chunk * tiles.rows + at.start, 16), at.size)
        out[s][u, w, at, :] = (ladder[column, u, rows, :].astype(WIDE) + result).astype(NARROW)

    mix(place, fock, first, load, store, tiles.rows)


def with_mirror(tiles, place, x, finish):
    across = place[1] < len(tiles.above)

    @pl.when(across)
    def _():
        finish(tiles.mirror_across(x))

    @pl.when(jnp.logical_not(across))
    def _():
        finish(tiles.mirror_within(x))


def update_kernel(tiles, groups, first, chunk, place, fock, occ, sums, *refs):
    own, other = refs[:groups], refs[groups:2 * groups]
    sent, rest = refs[2 * groups:2 * groups + 2]
    out = refs[2 * groups + 2:3 * groups + 2]
    update = refs[3 * groups + 2]
    here = slice(chunk * tiles.rows, (chunk + 1) * tiles.rows)

    def one(step, carry):
        u, w = step // first, lax.rem(step, first)
        for s in range(groups):
            column = (place[0] ^ s) * first + w
            base = occ[place[0] * first + u] + occ[column]

            def finish(mirrored):
                value = (own[s][u, w].astype(WIDE) + mirrored) * inverse(base - sums[here])
                narrow = value.astype(NARROW)
                update[u, s * first + w] = value
                sent[column, u] = narrow
                rest[u, s * first + w] = (2.0 * (value - narrow.astype(WIDE))).astype(NARROW)

            with_mirror(tiles, place, other[s][w, u].astype(WIDE), finish)
        return carry

    lax.fori_loop(0, first * first, one, 0)

    def load(s, u, r, at):
        return update[u, s * first + r, at, :]

    def store(s, u, w, column, at, result):
        out[s][u, w, at, :] = result.astype(NARROW)

    mix(place, fock, first, load, store, tiles.rows)


def rest_kernel(tiles, groups, first, chunk, place, occ, sums, rest, *refs):
    own, other, refs = refs[:groups], refs[groups:2 * groups], refs[2 * groups:]
    out = refs[-1]
    here = slice(chunk * tiles.rows, (chunk + 1) * tiles.rows)
    there = here if chunk else slice(None)
    if chunk:
        out[:, :, :tiles.rows, :] = refs[0][...]

    def one(step, carry):
        u, w = step // first, lax.rem(step, first)
        for s in range(groups):
            column = (place[0] ^ s) * first + w
            base = occ[place[0] * first + u] + occ[column]

            def finish(mirrored):
                value = (own[s][u, w].astype(WIDE) + mirrored) * inverse(base - sums[here])
                out[column, u, there] = (rest[u, s * first + w].astype(WIDE) + value).astype(NARROW)

            with_mirror(tiles, place, other[s][w, u].astype(WIDE), finish)
        return carry

    lax.fori_loop(0, first * first, one, 0)
    if chunk:
        to_distances(place, out, refs[1:-1])


def exchange(blocks):
    return lax.all_to_all(blocks, "occj", split_axis=0, concat_axis=0, tiled=True)


def by_distance(parts):
    devices = len(parts)
    return [parts[0]] + [
        lax.ppermute(parts[k], "occj", [(d, d ^ k) for d in range(devices)])
        for k in range(devices - 1, 0, -1)
    ][::-1]


def across_first(parts, groups):
    return [parts[0]] + [
        lax.ppermute(parts[s], "occi", [(k, k ^ s) for k in range(groups)])
        for s in range(groups - 1, 0, -1)
    ][::-1]


def tie(x, *others):
    return lax.optimization_barrier((x, *others))[0]


def gather_vectors(vectors, devices, packed):
    def turn(x, k):
        return lax.ppermute(x, "occj", [(d, d ^ k) for d in range(devices)])

    even = list(range(0, devices, 2))
    held = [vectors] + [turn(vectors, k) for k in even[1:]]
    other = turn(tie(jnp.stack(held), packed), 1)
    return [*held, other], even + [k ^ 1 for k in even]


def virtual_sums(tiles, vir_energy, q):
    e, g = tiles.edge, tiles.rows
    n_above = len(tiles.above)
    first = jnp.array([a for a, _ in tiles.above] + list(range(0, tiles.n, 2)), jnp.int32)[q]
    second = jnp.array([b for _, b in tiles.above] + list(range(1, tiles.n, 2)), jnp.int32)[q]
    a = lax.dynamic_slice_in_dim(vir_energy, first * e, e)
    b = lax.dynamic_slice_in_dim(vir_energy, second * e, e)
    pair = a[:, None] + b[None, :]
    across = jnp.concatenate([pair, pair], axis=1)
    halves = [
        jnp.concatenate([t[:g, None] + t[None, :], t[g:, None] + t[None, :]], axis=1) for t in (a, b)
    ]
    return jnp.where(q < n_above, across, jnp.concatenate(halves, axis=0))


def local(groups, devices, amplitudes, vectors, occupied_fock_block, occ_energy, vir_energy):
    first, second, virtual = amplitudes.shape[:3]
    assert second == 1 and groups * first == devices
    assert groups & (groups - 1) == 0 and devices & (devices - 1) == 0
    tiles = Tiles(devices, virtual)
    edge = tiles.edge
    current = amplitudes.reshape(first, virtual, virtual)
    count = current.size
    fock = occupied_fock_block.astype(WIDE)
    p, q = lax.axis_index("occi"), lax.axis_index("occj")
    place = jnp.stack([p, q]).astype(jnp.int32)
    packed = jax.ShapeDtypeStruct((devices, first, edge, 2 * edge), NARROW)
    upper = jax.ShapeDtypeStruct((devices, first, tiles.rows, 2 * edge), NARROW)
    part = jax.ShapeDtypeStruct((first, first, tiles.rows, 2 * edge), NARROW)
    singles = vectors.shape[0]
    whole = pltpu.VMEM((virtual, singles * virtual), NARROW)
    inner = pltpu.VMEM((singles * virtual, virtual), NARROW)
    square = pltpu.VMEM((virtual, virtual), WIDE)
    chunks = range(2)

    distant = jax.ShapeDtypeStruct((first, edge, 2 * edge), NARROW)
    blocks = pltpu.VMEM(packed.shape, NARROW)
    started = call(functools.partial(pack_kernel, tiles), [distant] * devices, [blocks], count, 6 * count,
                   place, current, specs=[SMEM, VMEM])
    pieces, order = gather_vectors(vectors, devices, started[0])
    held = by_distance(started)
    sums = virtual_sums(tiles, vir_energy, q)

    ladder_flops = first * singles * 4 * virtual**3
    ladder = call(
        functools.partial(first_ladder_kernel, tiles, order), packed, [whole, inner, square],
        ladder_flops, 8 * count, place, current, *pieces, specs=[SMEM] + [VMEM] * (1 + len(pieces)),
    )
    parts = call(
        functools.partial(sort_kernel, tiles, groups), [part] * (2 * groups), [blocks], count, 4 * count,
        tie(place, ladder), *held, specs=[SMEM] + [VMEM] * devices,
    )
    mirror = [across_first(parts[c * groups:(c + 1) * groups], groups) for c in chunks]
    ladder = exchange(ladder)

    half, other = [], []
    for c in chunks:
        half.append(call(
            functools.partial(half_kernel, tiles, groups, first, c), [part] * groups, [],
            LONG, 6 * count, place, fock, ladder, *mirror[c],
            specs=[SMEM] * 2 + [VMEM] * (groups + 1),
        ))
        other.append(across_first(half[c], groups))
    back, rest, mixed = [], [], []
    for c in chunks:
        sent, rest_one, *mixed_one = call(
            functools.partial(update_kernel, tiles, groups, first, c),
            [upper, jax.ShapeDtypeStruct((first, devices, *part.shape[2:]), NARROW)] + [part] * groups,
            [pltpu.VMEM((first, devices, *part.shape[2:]), WIDE)],
            LONG, 10 * count, place, fock, occ_energy, sums, *half[c], *other[c],
            specs=[SMEM] * 3 + [VMEM] * (2 * groups + 1),
        )
        back.append(exchange(tie(sent, *back)))
        rest, mixed = rest + [rest_one], mixed + [mixed_one]
    other = [across_first(x, groups) for x in mixed]
    base = call(
        functools.partial(second_ladder_kernel, tiles, order), jax.ShapeDtypeStruct(current.shape, WIDE),
        [whole, inner, square, pltpu.VMEM((virtual, virtual), NARROW)],
        ladder_flops, 12 * count, place, occ_energy, current, *back,
        jnp.broadcast_to(vir_energy[:, None], (virtual, 128)), vir_energy[None, :], *pieces,
        specs=[SMEM] * 2 + [VMEM] * (5 + len(pieces)),
    )
    last = []
    for c in chunks:
        last = call(
            functools.partial(rest_kernel, tiles, groups, first, c),
            [distant] * devices if c else [upper], [blocks] if c else [],
            LONG, 8 * count, place, occ_energy, sums, rest[c], *mixed[c], *other[c], *last,
            specs=[SMEM] * 2 + [VMEM] * (2 * groups + 2 + c),
        )
    def by_pair(*shape):
        return pl.BlockSpec((1, *shape), lambda pair: (pair, 0, 0))

    done = pl.pallas_call(
        functools.partial(add_kernel, tiles),
        grid=(first,),
        out_shape=jax.ShapeDtypeStruct(current.shape, WIDE),
        in_specs=[SMEM, by_pair(virtual, virtual)] + [by_pair(edge, 2 * edge)] * devices,
        out_specs=by_pair(virtual, virtual),
        scratch_shapes=[pltpu.VMEM((devices, 1, edge, 2 * edge), NARROW)],
        compiler_params=PARAMS,
        input_output_aliases={1: 0},
        cost_estimate=pl.CostEstimate(flops=count, bytes_accessed=10 * count, transcendentals=0),
    )(place, base, *by_distance(last))
    return done.reshape(amplitudes.shape)


def solution(mesh):
    sizes = (mesh.shape["occi"], mesh.shape["occj"])
    return jax.shard_map(
        functools.partial(local, *sizes),
        mesh=mesh,
        in_specs=(P("occi", "occj", None, None), P(None, "occj", None), P(), P(), P()),
        out_specs=P("occi", "occj", None, None),
        check_vma=False,
    )
```

```python
import functools
import math

import jax
import jax.numpy as jnp
from jax import lax
from jax.experimental import pallas as pl
from jax.experimental.pallas import tpu as pltpu
from jax.sharding import PartitionSpec as P

VMEM = pl.BlockSpec(memory_space=pltpu.VMEM)
SMEM = pl.BlockSpec(memory_space=pltpu.SMEM)
SMALL = pltpu.CompilerParams(vmem_limit_bytes=16 * 2**20)
LARGE = pltpu.CompilerParams(vmem_limit_bytes=24 * 2**20)
WIDE = jnp.float32
LONG = 3 * 10**10
NARROW = jnp.bfloat16


class Tiles:
    def __init__(self, devices, virtual):
        n = math.isqrt(2 * devices)
        assert n * n == 2 * devices and n % 2 == 0 and virtual % n == 0
        self.n = n
        self.edge = virtual // n
        self.rows = self.edge // 2
        self.above = [(a, b) for a in range(n) for b in range(a + 1, n)]
        self.diagonal = [(len(self.above) + k // 2, k % 2, k) for k in range(n)]

    def span(self, k):
        return slice(k * self.edge, (k + 1) * self.edge)

    def mirror_within(self, x):
        e, g = self.edge, self.rows
        tile = jnp.concatenate([x[:, :e], x[:, e:]], axis=0).T
        return jnp.concatenate([tile[:g], tile[g:]], axis=1)

    def mirror_across(self, x):
        return jnp.concatenate([x[:, self.edge:], x[:, :self.edge]], axis=1)


def call(body, outs, scratch, flops, moved, *operands, specs, params=SMALL):
    return pl.pallas_call(
        body,
        out_shape=outs,
        in_specs=specs,
        out_specs=jax.tree.map(lambda _: VMEM, outs),
        scratch_shapes=scratch,
        compiler_params=params,
        cost_estimate=pl.CostEstimate(flops=flops, bytes_accessed=moved, transcendentals=0),
    )(*operands)


def pack_pair(tiles, source, out, pair, mirrored=False):
    e, g = tiles.edge, tiles.rows
    straight, turned = (slice(e, None), slice(0, e)) if mirrored else (slice(0, e), slice(e, None))
    for d, (a, b) in enumerate(tiles.above):
        out[d, pair, :, straight] = source[tiles.span(a), tiles.span(b)].astype(NARROW)
        out[d, pair, :, turned] = source[tiles.span(b), tiles.span(a)].astype(WIDE).T.astype(NARROW)
    for d, c, k in tiles.diagonal:
        tile = source[tiles.span(k), tiles.span(k)]
        tile = tile.astype(WIDE).T.astype(NARROW) if mirrored else tile.astype(NARROW)
        out[d, pair, c * g:(c + 1) * g, :e] = tile[:g]
        out[d, pair, c * g:(c + 1) * g, e:] = tile[g:]


def unpack_pair(tiles, chunks, pair, put):
    e = tiles.edge
    for d, (a, b) in enumerate(tiles.above):
        block = jnp.concatenate([chunk[d, pair] for chunk in chunks], axis=0).astype(WIDE)
        put(a, b, block[:, :e])
        put(b, a, block[:, e:].T)
    for d, c, k in tiles.diagonal:
        block = chunks[c][d, pair].astype(WIDE)
        put(k, k, jnp.concatenate([block[:, :e], block[:, e:]], axis=0))


def to_distances(place, whole, outs):
    for k, out in enumerate(outs):
        out[...] = whole[place[1] ^ k]


def from_distances(place, pieces, whole):
    for k, piece in enumerate(pieces):
        whole[place[1] ^ k] = piece[...]


def pack_kernel(tiles, place, source, *refs):
    outs, whole = refs[:-1], refs[-1]
    for pair in range(source.shape[0]):
        pack_pair(tiles, source.at[pair], whole, pair, mirrored=True)
    to_distances(place, whole, outs)


def sort_kernel(tiles, groups, place, *refs):
    pieces, outs, whole = refs[:-2 * groups - 1], refs[-2 * groups - 1:-1], refs[-1]
    first = whole.shape[1]
    from_distances(place, pieces, whole)
    for s in range(groups):
        for u in range(first):
            block = whole[(place[0] ^ s) * first + u]
            for c in range(2):
                outs[c * groups + s][u] = block[:, c * tiles.rows:(c + 1) * tiles.rows]


def assemble(place, order, pieces, whole):
    k = 0
    for piece in pieces:
        count, rows, virtual = piece.shape[-3:]
        for block in range(piece.shape[0] if len(piece.shape) == 4 else 1):
            start = pl.multiple_of((place[1] ^ order[k]) * rows, rows)
            for single in range(count):
                values = piece[block, single] if len(piece.shape) == 4 else piece[single]
                whole[pl.ds(start, rows), single * virtual:(single + 1) * virtual] = values
            k += 1


def ladder_pair(matrix, whole, inner, total):
    virtual = matrix.shape[0]
    for single in range(whole.shape[1] // virtual):
        at = slice(single * virtual, (single + 1) * virtual)
        inner[at, :] = lax.dot_general(
            matrix, whole[:, at], (((1,), (1,)), ((), ())), preferred_element_type=WIDE
        ).astype(NARROW)
    total[...] = jnp.dot(whole[...], inner[...], preferred_element_type=WIDE)


def inverse(x):
    guess = pl.reciprocal(x, approx=True)
    return guess * (2.0 - x * guess)


def first_ladder_kernel(tiles, order, place, source, *refs):
    pieces, (out, whole, inner, total) = refs[:-4], refs[-4:]
    assemble(place, order, pieces, whole)
    for pair in range(source.shape[0]):
        ladder_pair(source[pair].astype(NARROW), whole, inner, total)
        pack_pair(tiles, total, out, pair)


def second_ladder_kernel(tiles, order, place, occ, source, upper, lower, row, column, *refs):
    pieces, (out, whole, inner, total, matrix) = refs[:-5], refs[-5:]
    assemble(place, order, pieces, whole)
    count = source.shape[0]
    for pair in range(count):
        def put(a, b, tile):
            matrix[tiles.span(a), tiles.span(b)] = tile.astype(NARROW)

        unpack_pair(tiles, (upper, lower), pair, put)
        ladder_pair(matrix[...], whole, inner, total)
        base = occ[place[0] * count + pair] + occ[place[1]]
        strip = math.gcd(64, total.shape[0])

        def finish(step, carry):
            at = pl.ds(pl.multiple_of(step * strip, strip), strip)
            own = base - row[at, :1] - column[...]
            out[pair, at, :] = (
                source[pair, at, :] + 2.0 * (matrix[at, :].astype(WIDE) + total[at, :] * inverse(own))
            )
            return carry

        lax.fori_loop(0, total.shape[0] // strip, finish, 0)


def add_kernel(tiles, place, source, *refs):
    pieces, (out, whole) = refs[:-2], refs[-2:]
    from_distances(place, pieces, whole)

    def put(a, b, tile):
        here = (0, tiles.span(a), tiles.span(b))
        out[here] = source[here] + tile

    unpack_pair(tiles, [whole.at[:, :, :tiles.rows], whole.at[:, :, tiles.rows:]], 0, put)


def mix(place, fock, first, load, store, rows):
    total = fock.shape[0]
    strips = rows // 16

    def strip(step, carry):
        u = step // strips
        at = pl.ds(pl.multiple_of(lax.rem(step, strips) * 16, 16), 16)
        taken = [load(k // first, u, k % first, at) for k in range(total)]
        for k in range(total):
            column = (place[0] ^ (k // first)) * first + k % first
            result = None
            for m in range(total):
                line = (place[0] ^ (m // first)) * first + m % first
                term = (-fock[line, column]) * taken[m]
                result = term if result is None else result + term
            store(k // first, u, k % first, column, at, result)
        return carry

    lax.fori_loop(0, first * strips, strip, 0)


def half_kernel(tiles, groups, first, chunk, place, fock, ladder, *refs):
    held, out = refs[:groups], refs[groups:]

    def load(s, u, r, at):
        return held[s][u, r, at, :].astype(WIDE)

    def store(s, u, w, column, at, result):
        rows = pl.ds(pl.multiple_of(chunk * tiles.rows + at.start, 16), at.size)
        out[s][u, w, at, :] = (ladder[column, u, rows, :].astype(WIDE) + result).astype(NARROW)

    mix(place, fock, first, load, store, tiles.rows)


def with_mirror(tiles, place, x, finish):
    across = place[1] < len(tiles.above)

    @pl.when(across)
    def _():
        finish(tiles.mirror_across(x))

    @pl.when(jnp.logical_not(across))
    def _():
        finish(tiles.mirror_within(x))


def update_kernel(tiles, groups, first, chunk, place, fock, occ, sums, *refs):
    own, other = refs[:groups], refs[groups:2 * groups]
    sent, rest = refs[2 * groups:2 * groups + 2]
    out = refs[2 * groups + 2:3 * groups + 2]
    update = refs[3 * groups + 2]
    here = slice(chunk * tiles.rows, (chunk + 1) * tiles.rows)

    def one(step, carry):
        u, w = step // first, lax.rem(step, first)
        for s in range(groups):
            column = (place[0] ^ s) * first + w
            base = occ[place[0] * first + u] + occ[column]

            def finish(mirrored):
                value = (own[s][u, w].astype(WIDE) + mirrored) * inverse(base - sums[here])
                narrow = value.astype(NARROW)
                update[u, s * first + w] = value
                sent[column, u] = narrow
                rest[u, s * first + w] = (2.0 * (value - narrow.astype(WIDE))).astype(NARROW)

            with_mirror(tiles, place, other[s][w, u].astype(WIDE), finish)
        return carry

    lax.fori_loop(0, first * first, one, 0)

    def load(s, u, r, at):
        return update[u, s * first + r, at, :]

    def store(s, u, w, column, at, result):
        out[s][u, w, at, :] = result.astype(NARROW)

    mix(place, fock, first, load, store, tiles.rows)


def rest_kernel(tiles, groups, first, chunk, place, occ, sums, rest, *refs):
    own, other, refs = refs[:groups], refs[groups:2 * groups], refs[2 * groups:]
    out = refs[-1]
    here = slice(chunk * tiles.rows, (chunk + 1) * tiles.rows)
    there = here if chunk else slice(None)
    if chunk:
        out[:, :, :tiles.rows, :] = refs[0][...]

    def one(step, carry):
        u, w = step // first, lax.rem(step, first)
        for s in range(groups):
            column = (place[0] ^ s) * first + w
            base = occ[place[0] * first + u] + occ[column]

            def finish(mirrored):
                value = (own[s][u, w].astype(WIDE) + mirrored) * inverse(base - sums[here])
                out[column, u, there] = (rest[u, s * first + w].astype(WIDE) + value).astype(NARROW)

            with_mirror(tiles, place, other[s][w, u].astype(WIDE), finish)
        return carry

    lax.fori_loop(0, first * first, one, 0)
    if chunk:
        to_distances(place, out, refs[1:-1])


def exchange(blocks):
    return lax.all_to_all(blocks, "occj", split_axis=0, concat_axis=0, tiled=True)


def by_distance(parts):
    devices = len(parts)
    return [parts[0]] + [
        lax.ppermute(parts[k], "occj", [(d, d ^ k) for d in range(devices)])
        for k in range(devices - 1, 0, -1)
    ][::-1]


def across_first(parts, groups):
    return [parts[0]] + [
        lax.ppermute(parts[s], "occi", [(k, k ^ s) for k in range(groups)])
        for s in range(groups - 1, 0, -1)
    ][::-1]


def tie(x, *others):
    return lax.optimization_barrier((x, *others))[0]


def copy_kernel(source, out):
    for k in range(source.shape[0]):
        out[k] = source[k]


def after(x, *others):
    return pl.pallas_call(
        copy_kernel,
        out_shape=jax.ShapeDtypeStruct(x.shape, x.dtype),
        in_specs=[SMEM],
        out_specs=SMEM,
        cost_estimate=pl.CostEstimate(flops=LONG, bytes_accessed=8, transcendentals=0),
    )(tie(x, *others))


def gather_vectors(vectors, devices, packed):
    def turn(x, k):
        return lax.ppermute(x, "occj", [(d, d ^ k) for d in range(devices)])

    even = list(range(0, devices, 2))
    held = [vectors] + [turn(vectors, k) for k in even[1:]]
    other = turn(tie(jnp.stack(held), packed), 1)
    return [*held, other], even + [k ^ 1 for k in even]


def virtual_sums(tiles, vir_energy, q):
    e, g = tiles.edge, tiles.rows
    n_above = len(tiles.above)
    first = jnp.array([a for a, _ in tiles.above] + list(range(0, tiles.n, 2)), jnp.int32)[q]
    second = jnp.array([b for _, b in tiles.above] + list(range(1, tiles.n, 2)), jnp.int32)[q]
    a = lax.dynamic_slice_in_dim(vir_energy, first * e, e)
    b = lax.dynamic_slice_in_dim(vir_energy, second * e, e)
    pair = a[:, None] + b[None, :]
    across = jnp.concatenate([pair, pair], axis=1)
    halves = [
        jnp.concatenate([t[:g, None] + t[None, :], t[g:, None] + t[None, :]], axis=1) for t in (a, b)
    ]
    return jnp.where(q < n_above, across, jnp.concatenate(halves, axis=0))


def local(groups, devices, amplitudes, vectors, occupied_fock_block, occ_energy, vir_energy):
    first, second, virtual = amplitudes.shape[:3]
    assert second == 1 and groups * first == devices
    assert groups & (groups - 1) == 0 and devices & (devices - 1) == 0
    tiles = Tiles(devices, virtual)
    edge = tiles.edge
    current = amplitudes.reshape(first, virtual, virtual)
    count = current.size
    fock = occupied_fock_block.astype(WIDE)
    p, q = lax.axis_index("occi"), lax.axis_index("occj")
    place = jnp.stack([p, q]).astype(jnp.int32)
    packed = jax.ShapeDtypeStruct((devices, first, edge, 2 * edge), NARROW)
    upper = jax.ShapeDtypeStruct((devices, first, tiles.rows, 2 * edge), NARROW)
    part = jax.ShapeDtypeStruct((first, first, tiles.rows, 2 * edge), NARROW)
    singles = vectors.shape[0]
    whole = pltpu.VMEM((virtual, singles * virtual), NARROW)
    inner = pltpu.VMEM((singles * virtual, virtual), NARROW)
    square = pltpu.VMEM((virtual, virtual), WIDE)
    chunks = range(2)

    distant = jax.ShapeDtypeStruct((first, edge, 2 * edge), NARROW)
    blocks = pltpu.VMEM(packed.shape, NARROW)
    started = call(functools.partial(pack_kernel, tiles), [distant] * devices, [blocks], count, 6 * count,
                   place, current, specs=[SMEM, VMEM])
    pieces, order = gather_vectors(vectors, devices, started[0])
    held = by_distance(started)
    sums = virtual_sums(tiles, vir_energy, q)

    ladder_flops = first * singles * 4 * virtual**3
    ladder = call(
        functools.partial(first_ladder_kernel, tiles, order), packed, [whole, inner, square],
        ladder_flops, 8 * count, place, current, *pieces, specs=[SMEM] + [VMEM] * (1 + len(pieces)), params=LARGE,
    )
    parts = call(
        functools.partial(sort_kernel, tiles, groups), [part] * (2 * groups), [blocks], count, 4 * count,
        tie(place, ladder), *held, specs=[SMEM] + [VMEM] * devices,
    )
    mirror = [across_first(parts[c * groups:(c + 1) * groups], groups) for c in chunks]
    ladder = exchange(ladder)

    half, other = [], []
    for c in chunks:
        half.append(call(
            functools.partial(half_kernel, tiles, groups, first, c), [part] * groups, [],
            LONG, 6 * count, after(place, *mirror[c]) if c == 0 else place, fock, ladder, *mirror[c],
            specs=[SMEM] * 2 + [VMEM] * (groups + 1),
        ))
        other.append(across_first(half[c], groups))
    back, rest, mixed = [], [], []
    for c in chunks:
        sent, rest_one, *mixed_one = call(
            functools.partial(update_kernel, tiles, groups, first, c),
            [upper, jax.ShapeDtypeStruct((first, devices, *part.shape[2:]), NARROW)] + [part] * groups,
            [pltpu.VMEM((first, devices, *part.shape[2:]), WIDE)],
            LONG, 10 * count, place, fock, occ_energy, sums, *half[c], *other[c],
            specs=[SMEM] * 3 + [VMEM] * (2 * groups + 1),
        )
        back.append(exchange(tie(sent, *back)))
        rest, mixed = rest + [rest_one], mixed + [mixed_one]
    other = [across_first(x, groups) for x in mixed]
    base = call(
        functools.partial(second_ladder_kernel, tiles, order), jax.ShapeDtypeStruct(current.shape, WIDE),
        [whole, inner, square, pltpu.VMEM((virtual, virtual), NARROW)],
        ladder_flops, 12 * count, place, occ_energy, current, *back,
        jnp.broadcast_to(vir_energy[:, None], (virtual, 128)), vir_energy[None, :], *pieces,
        specs=[SMEM] * 2 + [VMEM] * (5 + len(pieces)), params=LARGE,
    )
    last = []
    for c in chunks:
        last = call(
            functools.partial(rest_kernel, tiles, groups, first, c),
            [distant] * devices if c else [upper], [blocks] if c else [],
            2 * count if c else LONG, 8 * count, place, occ_energy, sums, rest[c], *mixed[c], *other[c], *last,
            specs=[SMEM] * 2 + [VMEM] * (2 * groups + 2 + c),
        )
    def by_pair(*shape):
        return pl.BlockSpec((1, *shape), lambda pair: (pair, 0, 0))

    done = pl.pallas_call(
        functools.partial(add_kernel, tiles),
        grid=(first,),
        out_shape=jax.ShapeDtypeStruct(current.shape, WIDE),
        in_specs=[SMEM, by_pair(virtual, virtual)] + [by_pair(edge, 2 * edge)] * devices,
        out_specs=by_pair(virtual, virtual),
        scratch_shapes=[pltpu.VMEM((devices, 1, edge, 2 * edge), NARROW)],
        compiler_params=SMALL,
        input_output_aliases={1: 0},
        cost_estimate=pl.CostEstimate(flops=count, bytes_accessed=10 * count, transcendentals=0),
    )(place, base, *by_distance(last))
    return done.reshape(amplitudes.shape)


def solution(mesh):
    sizes = (mesh.shape["occi"], mesh.shape["occj"])
    return jax.shard_map(
        functools.partial(local, *sizes),
        mesh=mesh,
        in_specs=(P("occi", "occj", None, None), P(None, "occj", None), P(), P(), P()),
        out_specs=P("occi", "occj", None, None),
        check_vma=False,
    )
```

```python
import functools
import math

import jax
import jax.numpy as jnp
from jax import lax
from jax.experimental import pallas as pl
from jax.experimental.pallas import tpu as pltpu
from jax.sharding import PartitionSpec as P

VMEM = pl.BlockSpec(memory_space=pltpu.VMEM)
SMEM = pl.BlockSpec(memory_space=pltpu.SMEM)
PARAMS = pltpu.CompilerParams(vmem_limit_bytes=50 * 2**20)
WIDE = jnp.float32
LONG = 3 * 10**10
NARROW = jnp.bfloat16


class Tiles:
    def __init__(self, devices, virtual):
        n = math.isqrt(2 * devices)
        assert n * n == 2 * devices and n % 2 == 0 and virtual % n == 0
        self.n = n
        self.edge = virtual // n
        self.rows = self.edge // 2
        self.above = [(a, b) for a in range(n) for b in range(a + 1, n)]
        self.diagonal = [(len(self.above) + k // 2, k % 2, k) for k in range(n)]

    def span(self, k):
        return slice(k * self.edge, (k + 1) * self.edge)

    def mirror_within(self, x):
        e, g = self.edge, self.rows
        tile = jnp.concatenate([x[:, :e], x[:, e:]], axis=0).T
        return jnp.concatenate([tile[:g], tile[g:]], axis=1)

    def mirror_across(self, x):
        return jnp.concatenate([x[:, self.edge:], x[:, :self.edge]], axis=1)


def call(body, outs, scratch, flops, moved, *operands, specs):
    return pl.pallas_call(
        body,
        out_shape=outs,
        in_specs=specs,
        out_specs=jax.tree.map(lambda _: VMEM, outs),
        scratch_shapes=scratch,
        compiler_params=PARAMS,
        cost_estimate=pl.CostEstimate(flops=flops, bytes_accessed=moved, transcendentals=0),
    )(*operands)


def pack_pair(tiles, source, out, pair, mirrored=False):
    e, g = tiles.edge, tiles.rows
    straight, turned = (slice(e, None), slice(0, e)) if mirrored else (slice(0, e), slice(e, None))
    for d, (a, b) in enumerate(tiles.above):
        out[d, pair, :, straight] = source[tiles.span(a), tiles.span(b)].astype(NARROW)
        out[d, pair, :, turned] = source[tiles.span(b), tiles.span(a)].astype(WIDE).T.astype(NARROW)
    for d, c, k in tiles.diagonal:
        tile = source[tiles.span(k), tiles.span(k)]
        tile = tile.astype(WIDE).T.astype(NARROW) if mirrored else tile.astype(NARROW)
        out[d, pair, c * g:(c + 1) * g, :e] = tile[:g]
        out[d, pair, c * g:(c + 1) * g, e:] = tile[g:]


def unpack_pair(tiles, chunks, pair, put):
    e = tiles.edge
    for d, (a, b) in enumerate(tiles.above):
        block = jnp.concatenate([chunk[d, pair] for chunk in chunks], axis=0).astype(WIDE)
        put(a, b, block[:, :e])
        put(b, a, block[:, e:].T)
    for d, c, k in tiles.diagonal:
        block = chunks[c][d, pair].astype(WIDE)
        put(k, k, jnp.concatenate([block[:, :e], block[:, e:]], axis=0))


def to_distances(place, whole, outs):
    for k, out in enumerate(outs):
        out[...] = whole[place[1] ^ k]


def from_distances(place, pieces, whole):
    for k, piece in enumerate(pieces):
        whole[place[1] ^ k] = piece[...]


def pack_kernel(tiles, place, source, *refs):
    outs, whole = refs[:-1], refs[-1]
    for pair in range(source.shape[0]):
        pack_pair(tiles, source.at[pair], whole, pair, mirrored=True)
    to_distances(place, whole, outs)


def sort_kernel(tiles, groups, place, *refs):
    pieces, outs, whole = refs[:-2 * groups - 1], refs[-2 * groups - 1:-1], refs[-1]
    first = whole.shape[1]
    from_distances(place, pieces, whole)
    for s in range(groups):
        for u in range(first):
            block = whole[(place[0] ^ s) * first + u]
            for c in range(2):
                outs[c * groups + s][u] = block[:, c * tiles.rows:(c + 1) * tiles.rows]


def assemble(place, order, pieces, whole):
    k = 0
    for piece in pieces:
        count, rows, virtual = piece.shape[-3:]
        for block in range(piece.shape[0] if len(piece.shape) == 4 else 1):
            start = pl.multiple_of((place[1] ^ order[k]) * rows, rows)
            for single in range(count):
                values = piece[block, single] if len(piece.shape) == 4 else piece[single]
                whole[pl.ds(start, rows), single * virtual:(single + 1) * virtual] = values
            k += 1


def ladder_pair(matrix, whole, inner, total):
    virtual = matrix.shape[0]
    for single in range(whole.shape[1] // virtual):
        at = slice(single * virtual, (single + 1) * virtual)
        inner[at, :] = lax.dot_general(
            matrix, whole[:, at], (((1,), (1,)), ((), ())), preferred_element_type=WIDE
        ).astype(NARROW)
    total[...] = jnp.dot(whole[...], inner[...], preferred_element_type=WIDE)


def inverse(x):
    guess = pl.reciprocal(x, approx=True)
    return guess * (2.0 - x * guess)


def first_ladder_kernel(tiles, order, place, source, *refs):
    pieces, (out, whole, inner, total) = refs[:-4], refs[-4:]
    assemble(place, order, pieces, whole)
    for pair in range(source.shape[0]):
        ladder_pair(source[pair].astype(NARROW), whole, inner, total)
        pack_pair(tiles, total, out, pair)


def second_ladder_kernel(tiles, order, place, occ, source, upper, lower, row, column, *refs):
    pieces, (out, whole, inner, total, matrix) = refs[:-5], refs[-5:]
    assemble(place, order, pieces, whole)
    count = source.shape[0]
    for pair in range(count):
        def put(a, b, tile):
            matrix[tiles.span(a), tiles.span(b)] = tile.astype(NARROW)

        unpack_pair(tiles, (upper, lower), pair, put)
        ladder_pair(matrix[...], whole, inner, total)
        base = occ[place[0] * count + pair] + occ[place[1]]
        strip = math.gcd(64, total.shape[0])

        def finish(step, carry):
            at = pl.ds(pl.multiple_of(step * strip, strip), strip)
            own = base - row[at, :1] - column[...]
            out[pair, at, :] = (
                source[pair, at, :] + 2.0 * (matrix[at, :].astype(WIDE) + total[at, :] * inverse(own))
            )
            return carry

        lax.fori_loop(0, total.shape[0] // strip, finish, 0)


def add_kernel(tiles, place, source, *refs):
    pieces, (out, whole) = refs[:-2], refs[-2:]
    from_distances(place, pieces, whole)

    def put(a, b, tile):
        here = (0, tiles.span(a), tiles.span(b))
        out[here] = source[here] + tile

    unpack_pair(tiles, [whole.at[:, :, :tiles.rows], whole.at[:, :, tiles.rows:]], 0, put)


def mix(place, fock, first, load, store, rows):
    total = fock.shape[0]
    strips = rows // 16

    def strip(step, carry):
        u = step // strips
        at = pl.ds(pl.multiple_of(lax.rem(step, strips) * 16, 16), 16)
        taken = [load(k // first, u, k % first, at) for k in range(total)]
        for k in range(total):
            column = (place[0] ^ (k // first)) * first + k % first
            result = None
            for m in range(total):
                line = (place[0] ^ (m // first)) * first + m % first
                term = (-fock[line, column]) * taken[m]
                result = term if result is None else result + term
            store(k // first, u, k % first, column, at, result)
        return carry

    lax.fori_loop(0, first * strips, strip, 0)


def half_kernel(tiles, groups, first, chunk, place, fock, ladder, *refs):
    held, out = refs[:groups], refs[groups:]

    def load(s, u, r, at):
        return held[s][u, r, at, :].astype(WIDE)

    def store(s, u, w, column, at, result):
        rows = pl.ds(pl.multiple_of(chunk * tiles.rows + at.start, 16), at.size)
        out[s][u, w, at, :] = (ladder[column, u, rows, :].astype(WIDE) + result).astype(NARROW)

    mix(place, fock, first, load, store, tiles.rows)


def with_mirror(tiles, place, x, finish):
    across = place[1] < len(tiles.above)

    @pl.when(across)
    def _():
        finish(tiles.mirror_across(x))

    @pl.when(jnp.logical_not(across))
    def _():
        finish(tiles.mirror_within(x))


def update_kernel(tiles, groups, first, chunk, place, fock, occ, sums, *refs):
    own, other = refs[:groups], refs[groups:2 * groups]
    sent, rest = refs[2 * groups:2 * groups + 2]
    out = refs[2 * groups + 2:3 * groups + 2]
    update = refs[3 * groups + 2]
    here = slice(chunk * tiles.rows, (chunk + 1) * tiles.rows)

    def one(step, carry):
        u, w = step // first, lax.rem(step, first)
        for s in range(groups):
            column = (place[0] ^ s) * first + w
            base = occ[place[0] * first + u] + occ[column]

            def finish(mirrored):
                value = (own[s][u, w].astype(WIDE) + mirrored) * inverse(base - sums[here])
                narrow = value.astype(NARROW)
                update[u, s * first + w] = value
                sent[column, u] = narrow
                rest[u, s * first + w] = (2.0 * (value - narrow.astype(WIDE))).astype(NARROW)

            with_mirror(tiles, place, other[s][w, u].astype(WIDE), finish)
        return carry

    lax.fori_loop(0, first * first, one, 0)

    def load(s, u, r, at):
        return update[u, s * first + r, at, :]

    def store(s, u, w, column, at, result):
        out[s][u, w, at, :] = result.astype(NARROW)

    mix(place, fock, first, load, store, tiles.rows)


def rest_kernel(tiles, groups, first, chunk, place, occ, sums, rest, *refs):
    own, other, refs = refs[:groups], refs[groups:2 * groups], refs[2 * groups:]
    out = refs[-1]
    here = slice(chunk * tiles.rows, (chunk + 1) * tiles.rows)
    there = here if chunk else slice(None)
    if chunk:
        out[:, :, :tiles.rows, :] = refs[0][...]

    def one(step, carry):
        u, w = step // first, lax.rem(step, first)
        for s in range(groups):
            column = (place[0] ^ s) * first + w
            base = occ[place[0] * first + u] + occ[column]

            def finish(mirrored):
                value = (own[s][u, w].astype(WIDE) + mirrored) * inverse(base - sums[here])
                out[column, u, there] = (rest[u, s * first + w].astype(WIDE) + value).astype(NARROW)

            with_mirror(tiles, place, other[s][w, u].astype(WIDE), finish)
        return carry

    lax.fori_loop(0, first * first, one, 0)
    if chunk:
        to_distances(place, out, refs[1:-1])


def exchange(blocks):
    return lax.all_to_all(blocks, "occj", split_axis=0, concat_axis=0, tiled=True)


def by_distance(parts):
    devices = len(parts)
    return [parts[0]] + [
        lax.ppermute(parts[k], "occj", [(d, d ^ k) for d in range(devices)])
        for k in range(devices - 1, 0, -1)
    ][::-1]


def across_first(parts, groups):
    return [parts[0]] + [
        lax.ppermute(parts[s], "occi", [(k, k ^ s) for k in range(groups)])
        for s in range(groups - 1, 0, -1)
    ][::-1]


def tie(x, *others):
    return lax.optimization_barrier((x, *others))[0]


def copy_kernel(source, out):
    for k in range(source.shape[0]):
        out[k] = source[k]


def after(x, *others):
    return pl.pallas_call(
        copy_kernel,
        out_shape=jax.ShapeDtypeStruct(x.shape, x.dtype),
        in_specs=[SMEM],
        out_specs=SMEM,
        cost_estimate=pl.CostEstimate(flops=LONG, bytes_accessed=8, transcendentals=0),
    )(tie(x, *others))


def gather_vectors(vectors, devices, packed):
    def turn(x, k):
        return lax.ppermute(x, "occj", [(d, d ^ k) for d in range(devices)])

    even = list(range(0, devices, 2))
    held = [vectors] + [turn(vectors, k) for k in even[1:]]
    other = turn(tie(jnp.stack(held), packed), 1)
    return [*held, other], even + [k ^ 1 for k in even]


def virtual_sums(tiles, vir_energy, q):
    e, g = tiles.edge, tiles.rows
    n_above = len(tiles.above)
    first = jnp.array([a for a, _ in tiles.above] + list(range(0, tiles.n, 2)), jnp.int32)[q]
    second = jnp.array([b for _, b in tiles.above] + list(range(1, tiles.n, 2)), jnp.int32)[q]
    a = lax.dynamic_slice_in_dim(vir_energy, first * e, e)
    b = lax.dynamic_slice_in_dim(vir_energy, second * e, e)
    pair = a[:, None] + b[None, :]
    across = jnp.concatenate([pair, pair], axis=1)
    halves = [
        jnp.concatenate([t[:g, None] + t[None, :], t[g:, None] + t[None, :]], axis=1) for t in (a, b)
    ]
    return jnp.where(q < n_above, across, jnp.concatenate(halves, axis=0))


def local(groups, devices, amplitudes, vectors, occupied_fock_block, occ_energy, vir_energy):
    first, second, virtual = amplitudes.shape[:3]
    assert second == 1 and groups * first == devices
    assert groups & (groups - 1) == 0 and devices & (devices - 1) == 0
    tiles = Tiles(devices, virtual)
    edge = tiles.edge
    current = amplitudes.reshape(first, virtual, virtual)
    count = current.size
    fock = occupied_fock_block.astype(WIDE)
    p, q = lax.axis_index("occi"), lax.axis_index("occj")
    place = jnp.stack([p, q]).astype(jnp.int32)
    packed = jax.ShapeDtypeStruct((devices, first, edge, 2 * edge), NARROW)
    upper = jax.ShapeDtypeStruct((devices, first, tiles.rows, 2 * edge), NARROW)
    part = jax.ShapeDtypeStruct((first, first, tiles.rows, 2 * edge), NARROW)
    singles = vectors.shape[0]
    whole = pltpu.VMEM((virtual, singles * virtual), NARROW)
    inner = pltpu.VMEM((singles * virtual, virtual), NARROW)
    square = pltpu.VMEM((virtual, virtual), WIDE)
    chunks = range(2)

    distant = jax.ShapeDtypeStruct((first, edge, 2 * edge), NARROW)
    blocks = pltpu.VMEM(packed.shape, NARROW)
    started = call(functools.partial(pack_kernel, tiles), [distant] * devices, [blocks], count, 6 * count,
                   place, current, specs=[SMEM, VMEM])
    pieces, order = gather_vectors(vectors, devices, started[0])
    held = by_distance(started)
    sums = virtual_sums(tiles, vir_energy, q)

    ladder_flops = first * singles * 4 * virtual**3
    ladder = call(
        functools.partial(first_ladder_kernel, tiles, order), packed, [whole, inner, square],
        ladder_flops, 8 * count, place, current, *pieces, specs=[SMEM] + [VMEM] * (1 + len(pieces)),
    )
    parts = call(
        functools.partial(sort_kernel, tiles, groups), [part] * (2 * groups), [blocks], count, 4 * count,
        tie(place, ladder), *held, specs=[SMEM] + [VMEM] * devices,
    )
    mirror = [across_first(parts[c * groups:(c + 1) * groups], groups) for c in chunks]
    ladder = exchange(ladder)

    half, other = [], []
    for c in chunks:
        half.append(call(
            functools.partial(half_kernel, tiles, groups, first, c), [part] * groups, [],
            LONG, 6 * count, after(place, *mirror[c]) if c == 0 else place, fock, ladder, *mirror[c],
            specs=[SMEM] * 2 + [VMEM] * (groups + 1),
        ))
        other.append(across_first(half[c], groups))
    back, rest, mixed = [], [], []
    for c in chunks:
        sent, rest_one, *mixed_one = call(
            functools.partial(update_kernel, tiles, groups, first, c),
            [upper, jax.ShapeDtypeStruct((first, devices, *part.shape[2:]), NARROW)] + [part] * groups,
            [pltpu.VMEM((first, devices, *part.shape[2:]), WIDE)],
            LONG, 10 * count, place, fock, occ_energy, sums, *half[c], *other[c],
            specs=[SMEM] * 3 + [VMEM] * (2 * groups + 1),
        )
        back.append(exchange(tie(sent, *back)))
        rest, mixed = rest + [rest_one], mixed + [mixed_one]
    other = [across_first(x, groups) for x in mixed]
    base = call(
        functools.partial(second_ladder_kernel, tiles, order), jax.ShapeDtypeStruct(current.shape, WIDE),
        [whole, inner, square, pltpu.VMEM((virtual, virtual), NARROW)],
        ladder_flops, 12 * count, place, occ_energy, current, *back,
        jnp.broadcast_to(vir_energy[:, None], (virtual, 128)), vir_energy[None, :], *pieces,
        specs=[SMEM] * 2 + [VMEM] * (5 + len(pieces)),
    )
    last = []
    for c in chunks:
        last = call(
            functools.partial(rest_kernel, tiles, groups, first, c),
            [distant] * devices if c else [upper], [blocks] if c else [],
            2 * count if c else LONG, 8 * count, place, occ_energy, sums, rest[c], *mixed[c], *other[c], *last,
            specs=[SMEM] * 2 + [VMEM] * (2 * groups + 2 + c),
        )
    def by_pair(*shape):
        return pl.BlockSpec((1, *shape), lambda pair: (pair, 0, 0))

    done = pl.pallas_call(
        functools.partial(add_kernel, tiles),
        grid=(first,),
        out_shape=jax.ShapeDtypeStruct(current.shape, WIDE),
        in_specs=[SMEM, by_pair(virtual, virtual)] + [by_pair(edge, 2 * edge)] * devices,
        out_specs=by_pair(virtual, virtual),
        scratch_shapes=[pltpu.VMEM((devices, 1, edge, 2 * edge), NARROW)],
        compiler_params=PARAMS,
        input_output_aliases={1: 0},
        cost_estimate=pl.CostEstimate(flops=count, bytes_accessed=10 * count, transcendentals=0),
    )(place, base, *by_distance(last))
    return done.reshape(amplitudes.shape)


def solution(mesh):
    sizes = (mesh.shape["occi"], mesh.shape["occj"])
    return jax.shard_map(
        functools.partial(local, *sizes),
        mesh=mesh,
        in_specs=(P("occi", "occj", None, None), P(None, "occj", None), P(), P(), P()),
        out_specs=P("occi", "occj", None, None),
        check_vma=False,
    )
```

```python
import functools
import math

import jax
import jax.numpy as jnp
from jax import lax
from jax.experimental import pallas as pl
from jax.experimental.pallas import tpu as pltpu
from jax.sharding import PartitionSpec as P

VMEM = pl.BlockSpec(memory_space=pltpu.VMEM)
SMEM = pl.BlockSpec(memory_space=pltpu.SMEM)
PARAMS = pltpu.CompilerParams(vmem_limit_bytes=50 * 2**20)
WIDE = jnp.float32
LONG = 3 * 10**10
NARROW = jnp.bfloat16


class Tiles:
    def __init__(self, devices, virtual):
        n = math.isqrt(2 * devices)
        assert n * n == 2 * devices and n % 2 == 0 and virtual % n == 0
        self.n = n
        self.edge = virtual // n
        self.rows = self.edge // 2
        self.above = [(a, b) for a in range(n) for b in range(a + 1, n)]
        self.diagonal = [(len(self.above) + k // 2, k % 2, k) for k in range(n)]

    def span(self, k):
        return slice(k * self.edge, (k + 1) * self.edge)

    def mirror_within(self, x):
        e, g = self.edge, self.rows
        tile = jnp.concatenate([x[:, :e], x[:, e:]], axis=0).T
        return jnp.concatenate([tile[:g], tile[g:]], axis=1)

    def mirror_across(self, x):
        return jnp.concatenate([x[:, self.edge:], x[:, :self.edge]], axis=1)


def call(body, outs, scratch, flops, moved, *operands, specs):
    return pl.pallas_call(
        body,
        out_shape=outs,
        in_specs=specs,
        out_specs=jax.tree.map(lambda _: VMEM, outs),
        scratch_shapes=scratch,
        compiler_params=PARAMS,
        cost_estimate=pl.CostEstimate(flops=flops, bytes_accessed=moved, transcendentals=0),
    )(*operands)


def pack_pair(tiles, source, out, pair, mirrored=False):
    e, g = tiles.edge, tiles.rows
    straight, turned = (slice(e, None), slice(0, e)) if mirrored else (slice(0, e), slice(e, None))
    for d, (a, b) in enumerate(tiles.above):
        out[d, pair, :, straight] = source[tiles.span(a), tiles.span(b)].astype(NARROW)
        out[d, pair, :, turned] = source[tiles.span(b), tiles.span(a)].astype(WIDE).T.astype(NARROW)
    for d, c, k in tiles.diagonal:
        tile = source[tiles.span(k), tiles.span(k)]
        tile = tile.astype(WIDE).T.astype(NARROW) if mirrored else tile.astype(NARROW)
        out[d, pair, c * g:(c + 1) * g, :e] = tile[:g]
        out[d, pair, c * g:(c + 1) * g, e:] = tile[g:]


def unpack_pair(tiles, blocks, pair, put):
    e, g = tiles.edge, tiles.rows
    for d, (a, b) in enumerate(tiles.above):
        put(a, b, blocks[d, pair, :, :e].astype(WIDE))
        put(b, a, blocks[d, pair, :, e:].astype(WIDE).T)
    for d, c, k in tiles.diagonal:
        upper = blocks[d, pair, c * g:(c + 1) * g, :e]
        lower = blocks[d, pair, c * g:(c + 1) * g, e:]
        put(k, k, jnp.concatenate([upper, lower], axis=0).astype(WIDE))


def to_distances(place, whole, outs):
    for k, out in enumerate(outs):
        out[...] = whole[place[1] ^ k]


def from_distances(place, pieces, whole):
    for k, piece in enumerate(pieces):
        whole[place[1] ^ k] = piece[...]


def pack_kernel(tiles, place, source, *refs):
    outs, whole = refs[:-1], refs[-1]
    for pair in range(source.shape[0]):
        pack_pair(tiles, source.at[pair], whole, pair, mirrored=True)
    to_distances(place, whole, outs)


def sort_kernel(tiles, groups, place, *refs):
    pieces, outs, whole = refs[:-2 * groups - 1], refs[-2 * groups - 1:-1], refs[-1]
    first = whole.shape[1]
    from_distances(place, pieces, whole)
    for s in range(groups):
        for u in range(first):
            block = whole[(place[0] ^ s) * first + u]
            for c in range(2):
                outs[c * groups + s][u] = block[:, c * tiles.rows:(c + 1) * tiles.rows]


def assemble(place, order, pieces, whole):
    k = 0
    for piece in pieces:
        count, rows, virtual = piece.shape[-3:]
        for block in range(piece.shape[0] if len(piece.shape) == 4 else 1):
            start = pl.multiple_of((place[1] ^ order[k]) * rows, rows)
            for single in range(count):
                values = piece[block, single] if len(piece.shape) == 4 else piece[single]
                whole[pl.ds(start, rows), single * virtual:(single + 1) * virtual] = values
            k += 1


def ladder_pair(matrix, whole, inner, total):
    virtual = matrix.shape[0]
    for single in range(whole.shape[1] // virtual):
        at = slice(single * virtual, (single + 1) * virtual)
        inner[at, :] = lax.dot_general(
            matrix, whole[:, at], (((1,), (1,)), ((), ())), preferred_element_type=WIDE
        ).astype(NARROW)
    total[...] = jnp.dot(whole[...], inner[...], preferred_element_type=WIDE)


def inverse(x):
    guess = pl.reciprocal(x, approx=True)
    return guess * (2.0 - x * guess)


def first_ladder_kernel(tiles, order, place, source, *refs):
    pieces, (out, whole, inner, total) = refs[:-4], refs[-4:]
    assemble(place, order, pieces, whole)
    for pair in range(source.shape[0]):
        ladder_pair(source[pair].astype(NARROW), whole, inner, total)
        pack_pair(tiles, total, out, pair)


def second_ladder_kernel(tiles, order, place, occ, source, blocks, row, column, *refs):
    pieces, (out, whole, inner, total, matrix) = refs[:-5], refs[-5:]
    assemble(place, order, pieces, whole)
    count = source.shape[0]
    for pair in range(count):
        def put(a, b, tile):
            matrix[tiles.span(a), tiles.span(b)] = tile.astype(NARROW)

        unpack_pair(tiles, blocks, pair, put)
        ladder_pair(matrix[...], whole, inner, total)
        base = occ[place[0] * count + pair] + occ[place[1]]
        strip = math.gcd(64, total.shape[0])

        def finish(step, carry):
            at = pl.ds(pl.multiple_of(step * strip, strip), strip)
            own = base - row[at, :1] - column[...]
            out[pair, at, :] = (
                source[pair, at, :] + 2.0 * (matrix[at, :].astype(WIDE) + total[at, :] * inverse(own))
            )
            return carry

        lax.fori_loop(0, total.shape[0] // strip, finish, 0)


def add_kernel(tiles, place, source, *refs):
    pieces, (out, whole) = refs[:-2], refs[-2:]
    from_distances(place, pieces, whole)

    def put(a, b, tile):
        here = (0, tiles.span(a), tiles.span(b))
        out[here] = source[here] + tile

    unpack_pair(tiles, whole, 0, put)


def mix(place, fock, first, load, store, rows):
    total = fock.shape[0]
    strips = rows // 16

    def strip(step, carry):
        u = step // strips
        at = pl.ds(pl.multiple_of(lax.rem(step, strips) * 16, 16), 16)
        taken = [load(k // first, u, k % first, at) for k in range(total)]
        for k in range(total):
            column = (place[0] ^ (k // first)) * first + k % first
            result = None
            for m in range(total):
                line = (place[0] ^ (m // first)) * first + m % first
                term = (-fock[line, column]) * taken[m]
                result = term if result is None else result + term
            store(k // first, u, k % first, column, at, result)
        return carry

    lax.fori_loop(0, first * strips, strip, 0)


def half_kernel(tiles, groups, first, chunk, place, fock, ladder, *refs):
    held, out = refs[:groups], refs[groups:]

    def load(s, u, r, at):
        return held[s][u, r, at, :].astype(WIDE)

    def store(s, u, w, column, at, result):
        rows = pl.ds(pl.multiple_of(chunk * tiles.rows + at.start, 16), at.size)
        out[s][u, w, at, :] = (ladder[column, u, rows, :].astype(WIDE) + result).astype(NARROW)

    mix(place, fock, first, load, store, tiles.rows)


def with_mirror(tiles, place, x, finish):
    across = place[1] < len(tiles.above)

    @pl.when(across)
    def _():
        finish(tiles.mirror_across(x))

    @pl.when(jnp.logical_not(across))
    def _():
        finish(tiles.mirror_within(x))


def update_kernel(tiles, groups, first, chunk, place, fock, occ, sums, *refs):
    before, refs = refs[:chunk], refs[chunk:]
    own, other = refs[:groups], refs[groups:2 * groups]
    sent, rest = refs[2 * groups:2 * groups + 2]
    out = refs[2 * groups + 2:3 * groups + 2]
    update = refs[3 * groups + 2]
    here = slice(chunk * tiles.rows, (chunk + 1) * tiles.rows)
    for ref in before:
        sent[:, :, :tiles.rows, :] = ref[...]

    def one(step, carry):
        u, w = step // first, lax.rem(step, first)
        for s in range(groups):
            column = (place[0] ^ s) * first + w
            base = occ[place[0] * first + u] + occ[column]

            def finish(mirrored):
                value = (own[s][u, w].astype(WIDE) + mirrored) * inverse(base - sums[here])
                narrow = value.astype(NARROW)
                update[u, s * first + w] = value
                sent[column, u, here] = narrow
                rest[u, s * first + w] = (2.0 * (value - narrow.astype(WIDE))).astype(NARROW)

            with_mirror(tiles, place, other[s][w, u].astype(WIDE), finish)
        return carry

    lax.fori_loop(0, first * first, one, 0)

    def load(s, u, r, at):
        return update[u, s * first + r, at, :]

    def store(s, u, w, column, at, result):
        out[s][u, w, at, :] = result.astype(NARROW)

    mix(place, fock, first, load, store, tiles.rows)


def rest_kernel(tiles, groups, first, chunk, place, occ, sums, rest, *refs):
    own, other, refs = refs[:groups], refs[groups:2 * groups], refs[2 * groups:]
    out = refs[-1]
    here = slice(chunk * tiles.rows, (chunk + 1) * tiles.rows)
    there = here if chunk else slice(None)
    if chunk:
        out[:, :, :tiles.rows, :] = refs[0][...]

    def one(step, carry):
        u, w = step // first, lax.rem(step, first)
        for s in range(groups):
            column = (place[0] ^ s) * first + w
            base = occ[place[0] * first + u] + occ[column]

            def finish(mirrored):
                value = (own[s][u, w].astype(WIDE) + mirrored) * inverse(base - sums[here])
                out[column, u, there] = (rest[u, s * first + w].astype(WIDE) + value).astype(NARROW)

            with_mirror(tiles, place, other[s][w, u].astype(WIDE), finish)
        return carry

    lax.fori_loop(0, first * first, one, 0)
    if chunk:
        to_distances(place, out, refs[1:-1])


def exchange(blocks):
    return lax.all_to_all(blocks, "occj", split_axis=0, concat_axis=0, tiled=True)


def by_distance(parts):
    devices = len(parts)
    return [parts[0]] + [
        lax.ppermute(parts[k], "occj", [(d, d ^ k) for d in range(devices)]) for k in range(1, devices)
    ]


def across_first(parts, groups):
    return [parts[0]] + [
        lax.ppermute(parts[s], "occi", [(k, k ^ s) for k in range(groups)])
        for s in range(groups - 1, 0, -1)
    ][::-1]


def tie(x, *others):
    return lax.optimization_barrier((x, *others))[0]


def gather_vectors(vectors, devices, packed):
    def turn(x, k):
        return lax.ppermute(x, "occj", [(d, d ^ k) for d in range(devices)])

    even = list(range(0, devices, 2))
    held = [vectors] + [turn(vectors, k) for k in even[1:]]
    other = turn(tie(jnp.stack(held), packed), 1)
    return [*held, other], even + [k ^ 1 for k in even]


def virtual_sums(tiles, vir_energy, q):
    e, g = tiles.edge, tiles.rows
    n_above = len(tiles.above)
    first = jnp.array([a for a, _ in tiles.above] + list(range(0, tiles.n, 2)), jnp.int32)[q]
    second = jnp.array([b for _, b in tiles.above] + list(range(1, tiles.n, 2)), jnp.int32)[q]
    a = lax.dynamic_slice_in_dim(vir_energy, first * e, e)
    b = lax.dynamic_slice_in_dim(vir_energy, second * e, e)
    pair = a[:, None] + b[None, :]
    across = jnp.concatenate([pair, pair], axis=1)
    halves = [
        jnp.concatenate([t[:g, None] + t[None, :], t[g:, None] + t[None, :]], axis=1) for t in (a, b)
    ]
    return jnp.where(q < n_above, across, jnp.concatenate(halves, axis=0))


def local(groups, devices, amplitudes, vectors, occupied_fock_block, occ_energy, vir_energy):
    first, second, virtual = amplitudes.shape[:3]
    assert second == 1 and groups * first == devices
    assert groups & (groups - 1) == 0 and devices & (devices - 1) == 0
    tiles = Tiles(devices, virtual)
    edge = tiles.edge
    current = amplitudes.reshape(first, virtual, virtual)
    count = current.size
    fock = occupied_fock_block.astype(WIDE)
    p, q = lax.axis_index("occi"), lax.axis_index("occj")
    place = jnp.stack([p, q]).astype(jnp.int32)
    packed = jax.ShapeDtypeStruct((devices, first, edge, 2 * edge), NARROW)
    upper = jax.ShapeDtypeStruct((devices, first, tiles.rows, 2 * edge), NARROW)
    part = jax.ShapeDtypeStruct((first, first, tiles.rows, 2 * edge), NARROW)
    singles = vectors.shape[0]
    whole = pltpu.VMEM((virtual, singles * virtual), NARROW)
    inner = pltpu.VMEM((singles * virtual, virtual), NARROW)
    square = pltpu.VMEM((virtual, virtual), WIDE)
    chunks = range(2)

    distant = jax.ShapeDtypeStruct((first, edge, 2 * edge), NARROW)
    blocks = pltpu.VMEM(packed.shape, NARROW)
    started = call(functools.partial(pack_kernel, tiles), [distant] * devices, [blocks], count, 6 * count,
                   place, current, specs=[SMEM, VMEM])
    pieces, order = gather_vectors(vectors, devices, started[0])
    held = by_distance(started)
    sums = virtual_sums(tiles, vir_energy, q)

    ladder_flops = first * singles * 4 * virtual**3
    ladder = call(
        functools.partial(first_ladder_kernel, tiles, order), packed, [whole, inner, square],
        ladder_flops, 8 * count, place, current, *pieces, specs=[SMEM] + [VMEM] * (1 + len(pieces)),
    )
    parts = call(
        functools.partial(sort_kernel, tiles, groups), [part] * (2 * groups), [blocks], count, 4 * count,
        tie(place, ladder), *held, specs=[SMEM] + [VMEM] * devices,
    )
    mirror = [across_first(parts[c * groups:(c + 1) * groups], groups) for c in chunks]
    ladder = exchange(tie(ladder, *held))

    half, other = [], []
    for c in chunks:
        half.append(call(
            functools.partial(half_kernel, tiles, groups, first, c), [part] * groups, [],
            LONG, 6 * count, place, fock, ladder, *mirror[c],
            specs=[SMEM] * 2 + [VMEM] * (groups + 1),
        ))
        other.append(across_first(half[c], groups))
    sent, rest, mixed = [], [], []
    for c in chunks:
        sent_one, rest_one, *mixed_one = call(
            functools.partial(update_kernel, tiles, groups, first, c),
            [(upper, packed)[c], jax.ShapeDtypeStruct((first, devices, *part.shape[2:]), NARROW)] + [part] * groups,
            [pltpu.VMEM((first, devices, *part.shape[2:]), WIDE)],
            LONG, 10 * count, place, fock, occ_energy, sums, *sent, *half[c], *other[c],
            specs=[SMEM] * 3 + [VMEM] * (2 * groups + 1 + c),
        )
        sent, rest, mixed = [sent_one], rest + [rest_one], mixed + [mixed_one]
    other = [across_first(x, groups) for x in mixed]
    back = exchange(sent[0])
    base = call(
        functools.partial(second_ladder_kernel, tiles, order), jax.ShapeDtypeStruct(current.shape, WIDE),
        [whole, inner, square, pltpu.VMEM((virtual, virtual), NARROW)],
        ladder_flops, 12 * count, place, occ_energy, current, back,
        jnp.broadcast_to(vir_energy[:, None], (virtual, 128)), vir_energy[None, :], *pieces,
        specs=[SMEM] * 2 + [VMEM] * (4 + len(pieces)),
    )
    last = []
    for c in chunks:
        last = call(
            functools.partial(rest_kernel, tiles, groups, first, c),
            [distant] * devices if c else [upper], [blocks] if c else [],
            2 * count if c else LONG, 8 * count, place, occ_energy, sums, rest[c], *mixed[c], *other[c], *last,
            specs=[SMEM] * 2 + [VMEM] * (2 * groups + 2 + c),
        )
    def by_pair(*shape):
        return pl.BlockSpec((1, *shape), lambda pair: (pair, 0, 0))

    done = pl.pallas_call(
        functools.partial(add_kernel, tiles),
        grid=(first,),
        out_shape=jax.ShapeDtypeStruct(current.shape, WIDE),
        in_specs=[SMEM, by_pair(virtual, virtual)] + [by_pair(edge, 2 * edge)] * devices,
        out_specs=by_pair(virtual, virtual),
        scratch_shapes=[pltpu.VMEM((devices, 1, edge, 2 * edge), NARROW)],
        compiler_params=PARAMS,
        input_output_aliases={1: 0},
        cost_estimate=pl.CostEstimate(flops=count, bytes_accessed=10 * count, transcendentals=0),
    )(place, base, *by_distance(last))
    return done.reshape(amplitudes.shape)


def solution(mesh):
    sizes = (mesh.shape["occi"], mesh.shape["occj"])
    return jax.shard_map(
        functools.partial(local, *sizes),
        mesh=mesh,
        in_specs=(P("occi", "occj", None, None), P(None, "occj", None), P(), P(), P()),
        out_specs=P("occi", "occj", None, None),
        check_vma=False,
    )
```

```python
import functools
import math

import jax
import jax.numpy as jnp
from jax import lax
from jax.experimental import pallas as pl
from jax.experimental.pallas import tpu as pltpu
from jax.sharding import PartitionSpec as P

VMEM = pl.BlockSpec(memory_space=pltpu.VMEM)
SMEM = pl.BlockSpec(memory_space=pltpu.SMEM)
PARAMS = pltpu.CompilerParams(vmem_limit_bytes=50 * 2**20)
WIDE = jnp.float32
LONG = 3 * 10**10
NARROW = jnp.bfloat16


class Tiles:
    def __init__(self, devices, virtual):
        n = math.isqrt(2 * devices)
        assert n * n == 2 * devices and n % 2 == 0 and virtual % n == 0
        self.n = n
        self.edge = virtual // n
        self.rows = self.edge // 2
        self.above = [(a, b) for a in range(n) for b in range(a + 1, n)]
        self.diagonal = [(len(self.above) + k // 2, k % 2, k) for k in range(n)]

    def span(self, k):
        return slice(k * self.edge, (k + 1) * self.edge)

    def mirror_within(self, x):
        e, g = self.edge, self.rows
        tile = jnp.concatenate([x[:, :e], x[:, e:]], axis=0).T
        return jnp.concatenate([tile[:g], tile[g:]], axis=1)

    def mirror_across(self, x):
        return jnp.concatenate([x[:, self.edge:], x[:, :self.edge]], axis=1)


def call(body, outs, scratch, flops, moved, *operands, specs):
    return pl.pallas_call(
        body,
        out_shape=outs,
        in_specs=specs,
        out_specs=jax.tree.map(lambda _: VMEM, outs),
        scratch_shapes=scratch,
        compiler_params=PARAMS,
        cost_estimate=pl.CostEstimate(flops=flops, bytes_accessed=moved, transcendentals=0),
    )(*operands)


def pack_pair(tiles, source, out, pair, mirrored=False):
    e, g = tiles.edge, tiles.rows
    straight, turned = (slice(e, None), slice(0, e)) if mirrored else (slice(0, e), slice(e, None))
    for d, (a, b) in enumerate(tiles.above):
        out[d, pair, :, straight] = source[tiles.span(a), tiles.span(b)].astype(NARROW)
        out[d, pair, :, turned] = source[tiles.span(b), tiles.span(a)].astype(WIDE).T.astype(NARROW)
    for d, c, k in tiles.diagonal:
        tile = source[tiles.span(k), tiles.span(k)]
        tile = tile.astype(WIDE).T.astype(NARROW) if mirrored else tile.astype(NARROW)
        out[d, pair, c * g:(c + 1) * g, :e] = tile[:g]
        out[d, pair, c * g:(c + 1) * g, e:] = tile[g:]


def unpack_pair(tiles, blocks, pair, put):
    e, g = tiles.edge, tiles.rows
    for d, (a, b) in enumerate(tiles.above):
        put(a, b, blocks[d, pair, :, :e].astype(WIDE))
        put(b, a, blocks[d, pair, :, e:].astype(WIDE).T)
    for d, c, k in tiles.diagonal:
        upper = blocks[d, pair, c * g:(c + 1) * g, :e]
        lower = blocks[d, pair, c * g:(c + 1) * g, e:]
        put(k, k, jnp.concatenate([upper, lower], axis=0).astype(WIDE))


def to_distances(origin, whole, outs):
    for k, out in enumerate(outs):
        out[...] = whole[origin ^ k]


def from_distances(origin, pieces, whole):
    for k, piece in enumerate(pieces):
        whole[origin ^ k] = piece[...]


def pack_kernel(tiles, place, source, *refs):
    outs, whole = refs[:-1], refs[-1]
    for pair in range(source.shape[0]):
        pack_pair(tiles, source.at[pair], whole, pair, mirrored=True)
    to_distances(place[1], whole, outs)


def sort_kernel(tiles, groups, place, *refs):
    pieces, outs, whole = refs[:-2 * groups - 1], refs[-2 * groups - 1:-1], refs[-1]
    first = whole.shape[1]
    from_distances(place[1], pieces, whole)
    for s in range(groups):
        for u in range(first):
            block = whole[(place[0] ^ s) * first + u]
            for c in range(2):
                outs[c * groups + s][u] = block[:, c * tiles.rows:(c + 1) * tiles.rows]


def assemble(place, order, pieces, whole):
    k = 0
    for piece in pieces:
        count, rows, virtual = piece.shape[-3:]
        for block in range(piece.shape[0] if len(piece.shape) == 4 else 1):
            start = pl.multiple_of((place[1] ^ order[k]) * rows, rows)
            for single in range(count):
                values = piece[block, single] if len(piece.shape) == 4 else piece[single]
                whole[pl.ds(start, rows), single * virtual:(single + 1) * virtual] = values
            k += 1


def ladder_pair(matrix, whole, inner, total):
    virtual = matrix.shape[0]
    for single in range(whole.shape[1] // virtual):
        at = slice(single * virtual, (single + 1) * virtual)
        inner[at, :] = lax.dot_general(
            matrix, whole[:, at], (((1,), (1,)), ((), ())), preferred_element_type=WIDE
        ).astype(NARROW)
    total[...] = jnp.dot(whole[...], inner[...], preferred_element_type=WIDE)


def inverse(x):
    guess = pl.reciprocal(x, approx=True)
    return guess * (2.0 - x * guess)


def first_ladder_kernel(tiles, order, place, source, *refs):
    pieces, (out, whole, inner, total) = refs[:-4], refs[-4:]
    assemble(place, order, pieces, whole)
    for pair in range(source.shape[0]):
        ladder_pair(source[pair].astype(NARROW), whole, inner, total)
        pack_pair(tiles, total, out, pair)


def second_ladder_kernel(tiles, order, place, occ, source, blocks, row, column, *refs):
    pieces, (out, whole, inner, total, matrix) = refs[:-5], refs[-5:]
    assemble(place, order, pieces, whole)
    count = source.shape[0]
    for pair in range(count):
        def put(a, b, tile):
            matrix[tiles.span(a), tiles.span(b)] = tile.astype(NARROW)

        unpack_pair(tiles, blocks, pair, put)
        ladder_pair(matrix[...], whole, inner, total)
        base = occ[place[0] * count + pair] + occ[place[1]]
        strip = math.gcd(64, total.shape[0])

        def finish(step, carry):
            at = pl.ds(pl.multiple_of(step * strip, strip), strip)
            own = base - row[at, :1] - column[...]
            out[pair, at, :] = (
                source[pair, at, :] + 2.0 * (matrix[at, :].astype(WIDE) + total[at, :] * inverse(own))
            )
            return carry

        lax.fori_loop(0, total.shape[0] // strip, finish, 0)


def add_kernel(tiles, first, place, source, *refs):
    pieces, (out, whole, turned) = refs[:-3], refs[-3:]
    devices = len(pieces) // 2
    from_distances(place[1], pieces[:devices], whole)
    from_distances(place[0] * first + lax.rem(place[1], first), pieces[devices:], turned)
    e, g = tiles.edge, tiles.rows

    def put(a, b, tile):
        here = (0, tiles.span(a), tiles.span(b))
        out[here] = source[here] + tile

    for d, (a, b) in enumerate(tiles.above):
        block = whole[d, 0].astype(WIDE) + tiles.mirror_across(turned[d, 0].astype(WIDE))
        put(a, b, block[:, :e])
        put(b, a, block[:, e:].T)
    for d, c, k in tiles.diagonal:
        def tile_of(blocks):
            block = blocks[d, 0, c * g:(c + 1) * g].astype(WIDE)
            return jnp.concatenate([block[:, :e], block[:, e:]], axis=0)

        put(k, k, tile_of(whole) + tile_of(turned).T)


def mix(place, fock, first, load, store, rows):
    total = fock.shape[0]
    strips = rows // 16

    def strip(step, carry):
        u = step // strips
        at = pl.ds(pl.multiple_of(lax.rem(step, strips) * 16, 16), 16)
        taken = [load(k // first, u, k % first, at) for k in range(total)]
        for k in range(total):
            column = (place[0] ^ (k // first)) * first + k % first
            result = None
            for m in range(total):
                line = (place[0] ^ (m // first)) * first + m % first
                term = (-fock[line, column]) * taken[m]
                result = term if result is None else result + term
            store(k // first, u, k % first, column, at, result)
        return carry

    lax.fori_loop(0, first * strips, strip, 0)


def half_kernel(tiles, groups, first, chunk, place, fock, ladder, *refs):
    held, out = refs[:groups], refs[groups:]

    def load(s, u, r, at):
        return held[s][u, r, at, :].astype(WIDE)

    def store(s, u, w, column, at, result):
        rows = pl.ds(pl.multiple_of(chunk * tiles.rows + at.start, 16), at.size)
        out[s][u, w, at, :] = (ladder[column, u, rows, :].astype(WIDE) + result).astype(NARROW)

    mix(place, fock, first, load, store, tiles.rows)


def with_mirror(tiles, place, x, finish):
    across = place[1] < len(tiles.above)

    @pl.when(across)
    def _():
        finish(tiles.mirror_across(x))

    @pl.when(jnp.logical_not(across))
    def _():
        finish(tiles.mirror_within(x))


def update_kernel(tiles, groups, first, chunk, place, fock, occ, sums, *refs):
    before, refs = refs[:3 * chunk], refs[3 * chunk:]
    own, other, refs = refs[:groups], refs[groups:2 * groups], refs[2 * groups:]
    update = refs[-1]
    sent, straight, turned = (refs[0], *refs[-3:-1]) if chunk else refs[:3]
    rows = slice(chunk * tiles.rows, (chunk + 1) * tiles.rows)
    there = rows if chunk else slice(None)
    for ref, out in zip(before, (sent, straight, turned)):
        out[:, :, :tiles.rows, :] = ref[...]

    def one(step, carry):
        u, w = step // first, lax.rem(step, first)
        for s in range(groups):
            column = (place[0] ^ s) * first + w
            base = occ[place[0] * first + u] + occ[column]

            def finish(mirrored):
                value = (own[s][u, w].astype(WIDE) + mirrored) * inverse(base - sums[rows])
                update[u, s * first + w] = value
                sent[column, u, there] = value.astype(NARROW)

            with_mirror(tiles, place, other[s][w, u].astype(WIDE), finish)
        return carry

    lax.fori_loop(0, first * first, one, 0)

    def load(s, u, r, at):
        return update[u, s * first + r, at, :]

    def store(s, u, w, column, at, result):
        strip = pl.ds(pl.multiple_of(chunk * tiles.rows + at.start, 16), at.size)
        put = strip if chunk else at
        value = update[u, s * first + w, at, :]
        base = occ[place[0] * first + u] + occ[column]
        share = result * inverse(base - sums[strip, :])
        straight[column, u, put, :] = (
            share + 2.0 * (value - value.astype(NARROW).astype(WIDE))
        ).astype(NARROW)
        turned[(place[0] ^ s) * first + u, w, put, :] = share.astype(NARROW)

    mix(place, fock, first, load, store, tiles.rows)
    if chunk:
        devices = straight.shape[0]
        to_distances(place[1], straight, refs[1:1 + devices])
        to_distances(place[1], turned, refs[1 + devices:1 + 2 * devices])


def exchange(blocks):
    return lax.all_to_all(blocks, "occj", split_axis=0, concat_axis=0, tiled=True)


def by_distance(parts):
    devices = len(parts)
    return [parts[0]] + [
        lax.ppermute(parts[k], "occj", [(d, d ^ k) for d in range(devices)])
        for k in range(devices - 1, 0, -1)
    ][::-1]


def to_mirror(parts, groups):
    devices = len(parts)
    first = devices // groups

    def turn(x, k):
        return lax.ppermute(x, ("occi", "occj"), [
            (p * devices + j, (j ^ k) // first * devices + p * first + (j ^ k) % first)
            for p in range(groups) for j in range(devices)
        ])

    return [turn(x, k) for k, x in enumerate(parts)]


def across_first(parts, groups):
    return [parts[0]] + [
        lax.ppermute(parts[s], "occi", [(k, k ^ s) for k in range(groups)])
        for s in range(groups - 1, 0, -1)
    ][::-1]


def tie(x, *others):
    return lax.optimization_barrier((x, *others))[0]


def copy_kernel(source, out):
    for k in range(source.shape[0]):
        out[k] = source[k]


def after(x, *others):
    return pl.pallas_call(
        copy_kernel,
        out_shape=jax.ShapeDtypeStruct(x.shape, x.dtype),
        in_specs=[SMEM],
        out_specs=SMEM,
        cost_estimate=pl.CostEstimate(flops=LONG, bytes_accessed=8, transcendentals=0),
    )(tie(x, *others))


def gather_vectors(vectors, devices, packed):
    def turn(x, k):
        return lax.ppermute(x, "occj", [(d, d ^ k) for d in range(devices)])

    even = list(range(0, devices, 2))
    held = [vectors] + [turn(vectors, k) for k in even[1:]]
    other = turn(tie(jnp.stack(held), packed), 1)
    return [*held, other], even + [k ^ 1 for k in even]


def virtual_sums(tiles, vir_energy, q):
    e, g = tiles.edge, tiles.rows
    n_above = len(tiles.above)
    first = jnp.array([a for a, _ in tiles.above] + list(range(0, tiles.n, 2)), jnp.int32)[q]
    second = jnp.array([b for _, b in tiles.above] + list(range(1, tiles.n, 2)), jnp.int32)[q]
    a = lax.dynamic_slice_in_dim(vir_energy, first * e, e)
    b = lax.dynamic_slice_in_dim(vir_energy, second * e, e)
    pair = a[:, None] + b[None, :]
    across = jnp.concatenate([pair, pair], axis=1)
    halves = [
        jnp.concatenate([t[:g, None] + t[None, :], t[g:, None] + t[None, :]], axis=1) for t in (a, b)
    ]
    return jnp.where(q < n_above, across, jnp.concatenate(halves, axis=0))


def local(groups, devices, amplitudes, vectors, occupied_fock_block, occ_energy, vir_energy):
    first, second, virtual = amplitudes.shape[:3]
    assert second == 1 and groups * first == devices
    assert groups & (groups - 1) == 0 and devices & (devices - 1) == 0
    tiles = Tiles(devices, virtual)
    edge = tiles.edge
    current = amplitudes.reshape(first, virtual, virtual)
    count = current.size
    fock = occupied_fock_block.astype(WIDE)
    p, q = lax.axis_index("occi"), lax.axis_index("occj")
    place = jnp.stack([p, q]).astype(jnp.int32)
    packed = jax.ShapeDtypeStruct((devices, first, edge, 2 * edge), NARROW)
    upper = jax.ShapeDtypeStruct((devices, first, tiles.rows, 2 * edge), NARROW)
    part = jax.ShapeDtypeStruct((first, first, tiles.rows, 2 * edge), NARROW)
    singles = vectors.shape[0]
    whole = pltpu.VMEM((virtual, singles * virtual), NARROW)
    inner = pltpu.VMEM((singles * virtual, virtual), NARROW)
    square = pltpu.VMEM((virtual, virtual), WIDE)
    chunks = range(2)

    distant = jax.ShapeDtypeStruct((first, edge, 2 * edge), NARROW)
    blocks = pltpu.VMEM(packed.shape, NARROW)
    started = call(functools.partial(pack_kernel, tiles), [distant] * devices, [blocks], count, 6 * count,
                   place, current, specs=[SMEM, VMEM])
    pieces, order = gather_vectors(vectors, devices, started[0])
    held = by_distance(started)
    sums = virtual_sums(tiles, vir_energy, q)

    ladder_flops = first * singles * 4 * virtual**3
    ladder = call(
        functools.partial(first_ladder_kernel, tiles, order), packed, [whole, inner, square],
        ladder_flops, 8 * count, place, current, *pieces, specs=[SMEM] + [VMEM] * (1 + len(pieces)),
    )
    parts = call(
        functools.partial(sort_kernel, tiles, groups), [part] * (2 * groups), [blocks], count, 4 * count,
        tie(place, ladder), *held, specs=[SMEM] + [VMEM] * devices,
    )
    mirror = [across_first(parts[c * groups:(c + 1) * groups], groups) for c in chunks]
    ladder = exchange(ladder)

    half, other = [], []
    for c in chunks:
        half.append(call(
            functools.partial(half_kernel, tiles, groups, first, c), [part] * groups, [],
            LONG, 6 * count, after(place, *mirror[c]) if c == 0 else place, fock, ladder, *mirror[c],
            specs=[SMEM] * 2 + [VMEM] * (groups + 1),
        ))
        other.append(across_first(half[c], groups))
    ready = []
    for c in chunks:
        ready = call(
            functools.partial(update_kernel, tiles, groups, first, c),
            [packed] + [distant] * (2 * devices) if c else [upper] * 3,
            ([blocks] * 2 if c else []) + [pltpu.VMEM((first, devices, *part.shape[2:]), WIDE)],
            LONG, 10 * count, place, fock, occ_energy, sums, *ready, *half[c], *other[c],
            specs=[SMEM] * 3 + [VMEM] * (2 * groups + 1 + 3 * c),
        )
    back = exchange(ready[0])
    last = to_mirror(ready[1 + devices:], groups)
    last = by_distance(ready[1:1 + devices]) + last
    base = call(
        functools.partial(second_ladder_kernel, tiles, order), jax.ShapeDtypeStruct(current.shape, WIDE),
        [whole, inner, square, pltpu.VMEM((virtual, virtual), NARROW)],
        ladder_flops, 12 * count, place, occ_energy, current, back,
        jnp.broadcast_to(vir_energy[:, None], (virtual, 128)), vir_energy[None, :], *pieces,
        specs=[SMEM] * 2 + [VMEM] * (4 + len(pieces)),
    )
    def by_pair(*shape):
        return pl.BlockSpec((1, *shape), lambda pair: (pair, 0, 0))

    done = pl.pallas_call(
        functools.partial(add_kernel, tiles, first),
        grid=(first,),
        out_shape=jax.ShapeDtypeStruct(current.shape, WIDE),
        in_specs=[SMEM, by_pair(virtual, virtual)] + [by_pair(edge, 2 * edge)] * (2 * devices),
        out_specs=by_pair(virtual, virtual),
        scratch_shapes=[pltpu.VMEM((devices, 1, edge, 2 * edge), NARROW)] * 2,
        compiler_params=PARAMS,
        input_output_aliases={1: 0},
        cost_estimate=pl.CostEstimate(flops=count, bytes_accessed=10 * count, transcendentals=0),
    )(place, base, *last)
    return done.reshape(amplitudes.shape)


def solution(mesh):
    sizes = (mesh.shape["occi"], mesh.shape["occj"])
    return jax.shard_map(
        functools.partial(local, *sizes),
        mesh=mesh,
        in_specs=(P("occi", "occj", None, None), P(None, "occj", None), P(), P(), P()),
        out_specs=P("occi", "occj", None, None),
        check_vma=False,
    )
```

```python
import functools
import math

import jax
import jax.numpy as jnp
from jax import lax
from jax.experimental import pallas as pl
from jax.experimental.pallas import tpu as pltpu
from jax.sharding import PartitionSpec as P

VMEM = pl.BlockSpec(memory_space=pltpu.VMEM)
SMEM = pl.BlockSpec(memory_space=pltpu.SMEM)
PARAMS = pltpu.CompilerParams(vmem_limit_bytes=50 * 2**20)
WIDE = jnp.float32
LONG = 3 * 10**10
NARROW = jnp.bfloat16


class Tiles:
    def __init__(self, devices, virtual):
        n = math.isqrt(2 * devices)
        assert n * n == 2 * devices and n % 2 == 0 and virtual % n == 0
        self.n = n
        self.edge = virtual // n
        self.rows = self.edge // 2
        self.above = [(a, b) for a in range(n) for b in range(a + 1, n)]
        self.diagonal = [(len(self.above) + k // 2, k % 2, k) for k in range(n)]

    def span(self, k):
        return slice(k * self.edge, (k + 1) * self.edge)

    def mirror_within(self, x):
        e, g = self.edge, self.rows
        tile = jnp.concatenate([x[:, :e], x[:, e:]], axis=0).T
        return jnp.concatenate([tile[:g], tile[g:]], axis=1)

    def mirror_across(self, x):
        return jnp.concatenate([x[:, self.edge:], x[:, :self.edge]], axis=1)


def call(body, outs, scratch, flops, moved, *operands, specs):
    return pl.pallas_call(
        body,
        out_shape=outs,
        in_specs=specs,
        out_specs=jax.tree.map(lambda _: VMEM, outs),
        scratch_shapes=scratch,
        compiler_params=PARAMS,
        cost_estimate=pl.CostEstimate(flops=flops, bytes_accessed=moved, transcendentals=0),
    )(*operands)


def pack_pair(tiles, source, out, pair, mirrored=False):
    e, g = tiles.edge, tiles.rows
    straight, turned = (slice(e, None), slice(0, e)) if mirrored else (slice(0, e), slice(e, None))
    for d, (a, b) in enumerate(tiles.above):
        out[d, pair, :, straight] = source[tiles.span(a), tiles.span(b)].astype(NARROW)
        out[d, pair, :, turned] = source[tiles.span(b), tiles.span(a)].astype(WIDE).T.astype(NARROW)
    for d, c, k in tiles.diagonal:
        tile = source[tiles.span(k), tiles.span(k)]
        tile = tile.astype(WIDE).T.astype(NARROW) if mirrored else tile.astype(NARROW)
        out[d, pair, c * g:(c + 1) * g, :e] = tile[:g]
        out[d, pair, c * g:(c + 1) * g, e:] = tile[g:]


def unpack_pair(tiles, chunks, pair, put):
    e = tiles.edge
    for d, (a, b) in enumerate(tiles.above):
        block = jnp.concatenate([chunk[d, pair] for chunk in chunks], axis=0).astype(WIDE)
        put(a, b, block[:, :e])
        put(b, a, block[:, e:].T)
    for d, c, k in tiles.diagonal:
        block = chunks[c][d, pair].astype(WIDE)
        put(k, k, jnp.concatenate([block[:, :e], block[:, e:]], axis=0))


def to_distances(origin, whole, outs):
    for k, out in enumerate(outs):
        out[...] = whole[origin ^ k]


def from_distances(origin, pieces, whole):
    for k, piece in enumerate(pieces):
        whole[origin ^ k] = piece[...]


def pack_kernel(tiles, place, source, *refs):
    outs, whole = refs[:-1], refs[-1]
    for pair in range(source.shape[0]):
        pack_pair(tiles, source.at[pair], whole, pair, mirrored=True)
    to_distances(place[1], whole, outs)


def sort_kernel(tiles, groups, place, *refs):
    pieces, outs, whole = refs[:-2 * groups - 1], refs[-2 * groups - 1:-1], refs[-1]
    first = whole.shape[1]
    from_distances(place[1], pieces, whole)
    for s in range(groups):
        for u in range(first):
            block = whole[(place[0] ^ s) * first + u]
            for c in range(2):
                outs[c * groups + s][u] = block[:, c * tiles.rows:(c + 1) * tiles.rows]


def assemble(place, order, pieces, whole):
    k = 0
    for piece in pieces:
        count, rows, virtual = piece.shape[-3:]
        for block in range(piece.shape[0] if len(piece.shape) == 4 else 1):
            start = pl.multiple_of((place[1] ^ order[k]) * rows, rows)
            for single in range(count):
                values = piece[block, single] if len(piece.shape) == 4 else piece[single]
                whole[pl.ds(start, rows), single * virtual:(single + 1) * virtual] = values
            k += 1


def ladder_pair(matrix, whole, inner, total):
    virtual = matrix.shape[0]
    for single in range(whole.shape[1] // virtual):
        at = slice(single * virtual, (single + 1) * virtual)
        inner[at, :] = lax.dot_general(
            matrix, whole[:, at], (((1,), (1,)), ((), ())), preferred_element_type=WIDE
        ).astype(NARROW)
    total[...] = jnp.dot(whole[...], inner[...], preferred_element_type=WIDE)


def inverse(x):
    guess = pl.reciprocal(x, approx=True)
    return guess * (2.0 - x * guess)


def first_ladder_kernel(tiles, order, place, source, *refs):
    pieces, (out, whole, inner, total) = refs[:-4], refs[-4:]
    assemble(place, order, pieces, whole)
    for pair in range(source.shape[0]):
        ladder_pair(source[pair].astype(NARROW), whole, inner, total)
        pack_pair(tiles, total, out, pair)


def second_ladder_kernel(tiles, order, place, occ, source, upper, others, row, column, *refs):
    pieces, (out, whole, inner, total, matrix) = refs[:-5], refs[-5:]
    assemble(place, order, pieces, whole)
    count = source.shape[0]
    for pair in range(count):
        def put(a, b, tile):
            matrix[tiles.span(a), tiles.span(b)] = tile.astype(NARROW)

        unpack_pair(tiles, (upper, others.at[:, 0]), pair, put)
        ladder_pair(matrix[...], whole, inner, total)
        base = occ[place[0] * count + pair] + occ[place[1]]
        strip = math.gcd(64, total.shape[0])

        def finish(step, carry):
            at = pl.ds(pl.multiple_of(step * strip, strip), strip)
            own = base - row[at, :1] - column[...]
            out[pair, at, :] = (
                source[pair, at, :] + 2.0 * (matrix[at, :].astype(WIDE) + total[at, :] * inverse(own))
            )
            return carry

        lax.fori_loop(0, total.shape[0] // strip, finish, 0)


def add_kernel(tiles, first, place, source, others, *refs):
    pieces, (out, turned) = refs[:-2], refs[-2:]
    from_distances(place[0] * first + lax.rem(place[1], first), pieces, turned)
    e, g = tiles.edge, tiles.rows

    def put(a, b, tile):
        here = (0, tiles.span(a), tiles.span(b))
        out[here] = source[here] + tile

    def tile_of(block):
        return jnp.concatenate([block[:, :e], block[:, e:]], axis=0)

    for d, (a, b) in enumerate(tiles.above):
        block = jnp.concatenate([others[d, 1, 0], others[d, 2, 0]], axis=0).astype(WIDE)
        block = block + tiles.mirror_across(turned[d, 0].astype(WIDE))
        put(a, b, block[:, :e])
        put(b, a, block[:, e:].T)
    for d, c, k in tiles.diagonal:
        rows = slice(c * g, (c + 1) * g)
        put(k, k, tile_of(others[d, 1 + c, 0].astype(WIDE)) + tile_of(turned[d, 0, rows].astype(WIDE)).T)


def mix(place, fock, first, load, store, rows):
    total = fock.shape[0]
    strips = rows // 16

    def strip(step, carry):
        u = step // strips
        at = pl.ds(pl.multiple_of(lax.rem(step, strips) * 16, 16), 16)
        taken = [load(k // first, u, k % first, at) for k in range(total)]
        for k in range(total):
            column = (place[0] ^ (k // first)) * first + k % first
            result = None
            for m in range(total):
                line = (place[0] ^ (m // first)) * first + m % first
                term = (-fock[line, column]) * taken[m]
                result = term if result is None else result + term
            store(k // first, u, k % first, column, at, result)
        return carry

    lax.fori_loop(0, first * strips, strip, 0)


def half_kernel(tiles, groups, first, chunk, place, fock, ladder, *refs):
    held, out = refs[:groups], refs[groups:]

    def load(s, u, r, at):
        return held[s][u, r, at, :].astype(WIDE)

    def store(s, u, w, column, at, result):
        rows = pl.ds(pl.multiple_of(chunk * tiles.rows + at.start, 16), at.size)
        out[s][u, w, at, :] = (ladder[column, u, rows, :].astype(WIDE) + result).astype(NARROW)

    mix(place, fock, first, load, store, tiles.rows)


def with_mirror(tiles, place, x, finish):
    across = place[1] < len(tiles.above)

    @pl.when(across)
    def _():
        finish(tiles.mirror_across(x))

    @pl.when(jnp.logical_not(across))
    def _():
        finish(tiles.mirror_within(x))


def update_kernel(tiles, groups, first, chunk, place, fock, occ, sums, *refs):
    before, refs = refs[:2 * chunk], refs[2 * chunk:]
    own, other, refs = refs[:groups], refs[groups:2 * groups], refs[2 * groups:]
    update = refs[-1]
    if chunk:
        sent, straight, turned = refs[0].at[:, 0], refs[0].at[:, 2], refs[-2]
        refs[0][:, 1] = before[0][...]
        turned[:, :, :tiles.rows, :] = before[1][...]
    else:
        sent, straight, turned = refs[:3]
    rows = slice(chunk * tiles.rows, (chunk + 1) * tiles.rows)

    def one(step, carry):
        u, w = step // first, lax.rem(step, first)
        for s in range(groups):
            column = (place[0] ^ s) * first + w
            base = occ[place[0] * first + u] + occ[column]

            def finish(mirrored):
                value = (own[s][u, w].astype(WIDE) + mirrored) * inverse(base - sums[rows])
                update[u, s * first + w] = value
                sent[column, u] = value.astype(NARROW)

            with_mirror(tiles, place, other[s][w, u].astype(WIDE), finish)
        return carry

    lax.fori_loop(0, first * first, one, 0)

    def load(s, u, r, at):
        return update[u, s * first + r, at, :]

    def store(s, u, w, column, at, result):
        strip = pl.ds(pl.multiple_of(chunk * tiles.rows + at.start, 16), at.size)
        value = update[u, s * first + w, at, :]
        base = occ[place[0] * first + u] + occ[column]
        share = result * inverse(base - sums[strip, :])
        straight[column, u, at, :] = (
            share + 2.0 * (value - value.astype(NARROW).astype(WIDE))
        ).astype(NARROW)
        turned[(place[0] ^ s) * first + u, w, strip if chunk else at, :] = share.astype(NARROW)

    mix(place, fock, first, load, store, tiles.rows)
    if chunk:
        to_distances(place[1], turned, refs[1:-2])


def exchange(blocks):
    return lax.all_to_all(blocks, "occj", split_axis=0, concat_axis=0, tiled=True)


def by_distance(parts):
    devices = len(parts)
    return [parts[0]] + [
        lax.ppermute(parts[k], "occj", [(d, d ^ k) for d in range(devices)])
        for k in range(devices - 1, 0, -1)
    ][::-1]


def to_mirror(parts, groups):
    devices = len(parts)
    first = devices // groups

    def turn(x, k):
        return lax.ppermute(x, ("occi", "occj"), [
            (p * devices + j, (j ^ k) // first * devices + p * first + (j ^ k) % first)
            for p in range(groups) for j in range(devices)
        ])

    return [turn(x, k) for k, x in enumerate(parts)]


def across_first(parts, groups):
    return [parts[0]] + [
        lax.ppermute(parts[s], "occi", [(k, k ^ s) for k in range(groups)])
        for s in range(groups - 1, 0, -1)
    ][::-1]


def tie(x, *others):
    return lax.optimization_barrier((x, *others))[0]


def copy_kernel(source, out):
    for k in range(source.shape[0]):
        out[k] = source[k]


def after(x, *others):
    return pl.pallas_call(
        copy_kernel,
        out_shape=jax.ShapeDtypeStruct(x.shape, x.dtype),
        in_specs=[SMEM],
        out_specs=SMEM,
        cost_estimate=pl.CostEstimate(flops=LONG, bytes_accessed=8, transcendentals=0),
    )(tie(x, *others))


def gather_vectors(vectors, devices, packed):
    def turn(x, k):
        return lax.ppermute(x, "occj", [(d, d ^ k) for d in range(devices)])

    even = list(range(0, devices, 2))
    held = [vectors] + [turn(vectors, k) for k in even[1:]]
    other = turn(tie(jnp.stack(held), packed), 1)
    return [*held, other], even + [k ^ 1 for k in even]


def virtual_sums(tiles, vir_energy, q):
    e, g = tiles.edge, tiles.rows
    n_above = len(tiles.above)
    first = jnp.array([a for a, _ in tiles.above] + list(range(0, tiles.n, 2)), jnp.int32)[q]
    second = jnp.array([b for _, b in tiles.above] + list(range(1, tiles.n, 2)), jnp.int32)[q]
    a = lax.dynamic_slice_in_dim(vir_energy, first * e, e)
    b = lax.dynamic_slice_in_dim(vir_energy, second * e, e)
    pair = a[:, None] + b[None, :]
    across = jnp.concatenate([pair, pair], axis=1)
    halves = [
        jnp.concatenate([t[:g, None] + t[None, :], t[g:, None] + t[None, :]], axis=1) for t in (a, b)
    ]
    return jnp.where(q < n_above, across, jnp.concatenate(halves, axis=0))


def local(groups, devices, amplitudes, vectors, occupied_fock_block, occ_energy, vir_energy):
    first, second, virtual = amplitudes.shape[:3]
    assert second == 1 and groups * first == devices
    assert groups & (groups - 1) == 0 and devices & (devices - 1) == 0
    tiles = Tiles(devices, virtual)
    edge = tiles.edge
    current = amplitudes.reshape(first, virtual, virtual)
    count = current.size
    fock = occupied_fock_block.astype(WIDE)
    p, q = lax.axis_index("occi"), lax.axis_index("occj")
    place = jnp.stack([p, q]).astype(jnp.int32)
    packed = jax.ShapeDtypeStruct((devices, first, edge, 2 * edge), NARROW)
    upper = jax.ShapeDtypeStruct((devices, first, tiles.rows, 2 * edge), NARROW)
    part = jax.ShapeDtypeStruct((first, first, tiles.rows, 2 * edge), NARROW)
    shared = jax.ShapeDtypeStruct((devices, 3, first, tiles.rows, 2 * edge), NARROW)
    singles = vectors.shape[0]
    whole = pltpu.VMEM((virtual, singles * virtual), NARROW)
    inner = pltpu.VMEM((singles * virtual, virtual), NARROW)
    square = pltpu.VMEM((virtual, virtual), WIDE)
    chunks = range(2)

    distant = jax.ShapeDtypeStruct((first, edge, 2 * edge), NARROW)
    blocks = pltpu.VMEM(packed.shape, NARROW)
    started = call(functools.partial(pack_kernel, tiles), [distant] * devices, [blocks], count, 6 * count,
                   place, current, specs=[SMEM, VMEM])
    pieces, order = gather_vectors(vectors, devices, started[0])
    held = by_distance(started)
    sums = virtual_sums(tiles, vir_energy, q)

    ladder_flops = first * singles * 4 * virtual**3
    ladder = call(
        functools.partial(first_ladder_kernel, tiles, order), packed, [whole, inner, square],
        ladder_flops, 8 * count, place, current, *pieces, specs=[SMEM] + [VMEM] * (1 + len(pieces)),
    )
    parts = call(
        functools.partial(sort_kernel, tiles, groups), [part] * (2 * groups), [blocks], count, 4 * count,
        tie(place, ladder), *held, specs=[SMEM] + [VMEM] * devices,
    )
    mirror = [across_first(parts[c * groups:(c + 1) * groups], groups) for c in chunks]
    ladder = exchange(ladder)

    half, other = [], []
    for c in chunks:
        half.append(call(
            functools.partial(half_kernel, tiles, groups, first, c), [part] * groups, [],
            LONG, 6 * count, after(place, *mirror[c]) if c == 0 else place, fock, ladder, *mirror[c],
            specs=[SMEM] * 2 + [VMEM] * (groups + 1),
        ))
        other.append(across_first(half[c], groups))
    ready, back = [], []
    for c in chunks:
        ready = call(
            functools.partial(update_kernel, tiles, groups, first, c),
            [shared] + [distant] * devices if c else [upper] * 3,
            ([blocks] if c else []) + [pltpu.VMEM((first, devices, *part.shape[2:]), WIDE)],
            LONG, 10 * count, place, fock, occ_energy, sums, *ready[1:], *half[c], *other[c],
            specs=[SMEM] * 3 + [VMEM] * (2 * groups + 1 + 2 * c),
        )
        back.append(exchange(tie(ready[0], *back)))
    last = to_mirror(ready[1:], groups)
    base = call(
        functools.partial(second_ladder_kernel, tiles, order), jax.ShapeDtypeStruct(current.shape, WIDE),
        [whole, inner, square, pltpu.VMEM((virtual, virtual), NARROW)],
        ladder_flops, 12 * count, place, occ_energy, current, *back,
        jnp.broadcast_to(vir_energy[:, None], (virtual, 128)), vir_energy[None, :], *pieces,
        specs=[SMEM] * 2 + [VMEM] * (5 + len(pieces)),
    )
    def by_pair(*shape):
        return pl.BlockSpec((1, *shape), lambda pair: (pair, 0, 0))

    done = pl.pallas_call(
        functools.partial(add_kernel, tiles, first),
        grid=(first,),
        out_shape=jax.ShapeDtypeStruct(current.shape, WIDE),
        in_specs=[SMEM, by_pair(virtual, virtual)] + [
            pl.BlockSpec((devices, 3, 1, tiles.rows, 2 * edge), lambda pair: (0, 0, pair, 0, 0))
        ] + [by_pair(edge, 2 * edge)] * devices,
        out_specs=by_pair(virtual, virtual),
        scratch_shapes=[pltpu.VMEM((devices, 1, edge, 2 * edge), NARROW)],
        compiler_params=PARAMS,
        input_output_aliases={1: 0},
        cost_estimate=pl.CostEstimate(flops=count, bytes_accessed=10 * count, transcendentals=0),
    )(place, base, back[1], *last)
    return done.reshape(amplitudes.shape)


def solution(mesh):
    sizes = (mesh.shape["occi"], mesh.shape["occj"])
    return jax.shard_map(
        functools.partial(local, *sizes),
        mesh=mesh,
        in_specs=(P("occi", "occj", None, None), P(None, "occj", None), P(), P(), P()),
        out_specs=P("occi", "occj", None, None),
        check_vma=False,
    )
```

```python
import functools
import math

import jax
import jax.numpy as jnp
from jax import lax
from jax.experimental import pallas as pl
from jax.experimental.pallas import tpu as pltpu
from jax.sharding import PartitionSpec as P

VMEM = pl.BlockSpec(memory_space=pltpu.VMEM)
SMEM = pl.BlockSpec(memory_space=pltpu.SMEM)
PARAMS = pltpu.CompilerParams(vmem_limit_bytes=50 * 2**20)
WIDE = jnp.float32
LONG = 3 * 10**10
NARROW = jnp.bfloat16


class Tiles:
    def __init__(self, devices, virtual):
        n = math.isqrt(2 * devices)
        assert n * n == 2 * devices and n % 2 == 0 and virtual % n == 0
        self.n = n
        self.edge = virtual // n
        self.rows = self.edge // 2
        self.above = [(a, b) for a in range(n) for b in range(a + 1, n)]
        self.diagonal = [(len(self.above) + k // 2, k % 2, k) for k in range(n)]

    def span(self, k):
        return slice(k * self.edge, (k + 1) * self.edge)

    def mirror_within(self, x):
        e, g = self.edge, self.rows
        tile = jnp.concatenate([x[:, :e], x[:, e:]], axis=0).T
        return jnp.concatenate([tile[:g], tile[g:]], axis=1)

    def mirror_across(self, x):
        return jnp.concatenate([x[:, self.edge:], x[:, :self.edge]], axis=1)


def call(body, outs, scratch, flops, moved, *operands, specs):
    return pl.pallas_call(
        body,
        out_shape=outs,
        in_specs=specs,
        out_specs=jax.tree.map(lambda _: VMEM, outs),
        scratch_shapes=scratch,
        compiler_params=PARAMS,
        cost_estimate=pl.CostEstimate(flops=flops, bytes_accessed=moved, transcendentals=0),
    )(*operands)


def pack_pair(tiles, source, out, pair, mirrored=False):
    e, g = tiles.edge, tiles.rows
    straight, turned = (slice(e, None), slice(0, e)) if mirrored else (slice(0, e), slice(e, None))
    for d, (a, b) in enumerate(tiles.above):
        out[d, pair, :, straight] = source[tiles.span(a), tiles.span(b)].astype(NARROW)
        out[d, pair, :, turned] = source[tiles.span(b), tiles.span(a)].astype(WIDE).T.astype(NARROW)
    for d, c, k in tiles.diagonal:
        tile = source[tiles.span(k), tiles.span(k)]
        tile = tile.astype(WIDE).T.astype(NARROW) if mirrored else tile.astype(NARROW)
        out[d, pair, c * g:(c + 1) * g, :e] = tile[:g]
        out[d, pair, c * g:(c + 1) * g, e:] = tile[g:]


def unpack_pair(tiles, blocks, pair, put):
    e, g = tiles.edge, tiles.rows
    for d, (a, b) in enumerate(tiles.above):
        put(a, b, blocks[d, pair, :, :e].astype(WIDE))
        put(b, a, blocks[d, pair, :, e:].astype(WIDE).T)
    for d, c, k in tiles.diagonal:
        upper = blocks[d, pair, c * g:(c + 1) * g, :e]
        lower = blocks[d, pair, c * g:(c + 1) * g, e:]
        put(k, k, jnp.concatenate([upper, lower], axis=0).astype(WIDE))


def to_distances(place, whole, outs):
    for k, out in enumerate(outs):
        out[...] = whole[place[1] ^ k]


def from_distances(place, pieces, whole):
    for k, piece in enumerate(pieces):
        whole[place[1] ^ k] = piece[...]


def pack_kernel(tiles, place, source, *refs):
    outs, whole = refs[:-1], refs[-1]
    for pair in range(source.shape[0]):
        pack_pair(tiles, source.at[pair], whole, pair, mirrored=True)
    to_distances(place, whole, outs)


def sort_kernel(tiles, groups, place, *refs):
    pieces, outs, whole = refs[:-2 * groups - 1], refs[-2 * groups - 1:-1], refs[-1]
    first = whole.shape[1]
    from_distances(place, pieces, whole)
    for s in range(groups):
        for u in range(first):
            block = whole[(place[0] ^ s) * first + u]
            for c in range(2):
                outs[c * groups + s][u] = block[:, c * tiles.rows:(c + 1) * tiles.rows]


def assemble(place, order, pieces, whole):
    k = 0
    for piece in pieces:
        count, rows, virtual = piece.shape[-3:]
        for block in range(piece.shape[0] if len(piece.shape) == 4 else 1):
            start = pl.multiple_of((place[1] ^ order[k]) * rows, rows)
            for single in range(count):
                values = piece[block, single] if len(piece.shape) == 4 else piece[single]
                whole[pl.ds(start, rows), single * virtual:(single + 1) * virtual] = values
            k += 1


def ladder_pair(matrix, whole, inner, total):
    virtual = matrix.shape[0]
    for single in range(whole.shape[1] // virtual):
        at = slice(single * virtual, (single + 1) * virtual)
        inner[at, :] = lax.dot_general(
            matrix, whole[:, at], (((1,), (1,)), ((), ())), preferred_element_type=WIDE
        ).astype(NARROW)
    total[...] = jnp.dot(whole[...], inner[...], preferred_element_type=WIDE)


def inverse(x):
    guess = pl.reciprocal(x, approx=True)
    return guess * (2.0 - x * guess)


def first_ladder_kernel(tiles, order, place, source, *refs):
    pieces, (out, whole, inner, total) = refs[:-4], refs[-4:]
    assemble(place, order, pieces, whole)
    for pair in range(source.shape[0]):
        ladder_pair(source[pair].astype(NARROW), whole, inner, total)
        pack_pair(tiles, total, out, pair)


def second_ladder_kernel(tiles, first, place, occ, source, blocks, row, column, whole, out, inner, total, matrix):
    def put(a, b, tile):
        matrix[tiles.span(a), tiles.span(b)] = tile.astype(NARROW)

    unpack_pair(tiles, blocks, 0, put)
    ladder_pair(matrix[...], whole, inner, total)
    base = occ[place[0] * first + pl.program_id(0)] + occ[place[1]]
    strip = math.gcd(64, total.shape[0])

    def finish(step, carry):
        at = pl.ds(pl.multiple_of(step * strip, strip), strip)
        own = base - row[at, :1] - column[...]
        out[0, at, :] = source[0, at, :] + 2.0 * (matrix[at, :].astype(WIDE) + total[at, :] * inverse(own))
        return carry

    lax.fori_loop(0, total.shape[0] // strip, finish, 0)


def add_kernel(tiles, place, source, *refs):
    pieces, (out, whole) = refs[:-2], refs[-2:]
    from_distances(place, pieces, whole)

    def put(a, b, tile):
        here = (0, tiles.span(a), tiles.span(b))
        out[here] = source[here] + tile

    unpack_pair(tiles, whole, 0, put)


def mix(place, fock, first, load, store, rows):
    total = fock.shape[0]
    strips = rows // 16

    def strip(step, carry):
        u = step // strips
        at = pl.ds(pl.multiple_of(lax.rem(step, strips) * 16, 16), 16)
        taken = [load(k // first, u, k % first, at) for k in range(total)]
        for k in range(total):
            column = (place[0] ^ (k // first)) * first + k % first
            result = None
            for m in range(total):
                line = (place[0] ^ (m // first)) * first + m % first
                term = (-fock[line, column]) * taken[m]
                result = term if result is None else result + term
            store(k // first, u, k % first, column, at, result)
        return carry

    lax.fori_loop(0, first * strips, strip, 0)


def half_kernel(tiles, groups, first, chunk, place, fock, ladder, *refs):
    held, out = refs[:groups], refs[groups:]

    def load(s, u, r, at):
        return held[s][u, r, at, :].astype(WIDE)

    def store(s, u, w, column, at, result):
        rows = pl.ds(pl.multiple_of(chunk * tiles.rows + at.start, 16), at.size)
        out[s][u, w, at, :] = (ladder[column, u, rows, :].astype(WIDE) + result).astype(NARROW)

    mix(place, fock, first, load, store, tiles.rows)


def with_mirror(tiles, place, x, finish):
    across = place[1] < len(tiles.above)

    @pl.when(across)
    def _():
        finish(tiles.mirror_across(x))

    @pl.when(jnp.logical_not(across))
    def _():
        finish(tiles.mirror_within(x))


def update_kernel(tiles, groups, first, chunk, place, fock, occ, sums, *refs):
    before, refs = refs[:chunk], refs[chunk:]
    own, other, refs = refs[:groups], refs[groups:2 * groups], refs[2 * groups:]
    (sent, rest), out, (update, local_mixed) = refs[:2], refs[2:groups + 1], refs[groups + 1:]
    here = slice(chunk * tiles.rows, (chunk + 1) * tiles.rows)
    for ref in before:
        sent[:, :, :tiles.rows, :] = ref[...]

    def one(step, carry):
        u, w = step // first, lax.rem(step, first)
        for s in range(groups):
            column = (place[0] ^ s) * first + w
            base = occ[place[0] * first + u] + occ[column]

            def finish(mirrored):
                value = (own[s][u, w].astype(WIDE) + mirrored) * inverse(base - sums[here])
                update[u, s * first + w] = value
                sent[column, u, here] = value.astype(NARROW)

            with_mirror(tiles, place, other[s][w, u].astype(WIDE), finish)
        return carry

    lax.fori_loop(0, first * first, one, 0)

    def load(s, u, r, at):
        return update[u, s * first + r, at, :]

    def lost(value):
        return 2.0 * (value - value.astype(NARROW).astype(WIDE))

    def store(s, u, w, column, at, result):
        if s == 0:
            local_mixed[u, w, at, :] = result
            return
        out[s - 1][u, w, at, :] = result.astype(NARROW)
        strip = pl.ds(pl.multiple_of(chunk * tiles.rows + at.start, 16), at.size)
        base = occ[place[0] * first + u] + occ[column]
        share = result * inverse(base - sums[strip, :])
        rest[u, s * first + w, at, :] = (lost(update[u, s * first + w, at, :]) + share).astype(NARROW)

    mix(place, fock, first, load, store, tiles.rows)

    def within(step, carry):
        u, w = step // first, lax.rem(step, first)
        base = occ[place[0] * first + u] + occ[place[0] * first + w]

        def finish(mirrored):
            share = (local_mixed[u, w] + mirrored) * inverse(base - sums[here])
            rest[u, w] = (lost(update[u, w]) + share).astype(NARROW)

        with_mirror(tiles, place, local_mixed[w, u], finish)
        return carry

    lax.fori_loop(0, first * first, within, 0)


def rest_kernel(tiles, groups, first, chunk, place, occ, sums, rest, *refs):
    other, refs = refs[:groups - 1], refs[groups - 1:]
    out = refs[-1]
    here = slice(chunk * tiles.rows, (chunk + 1) * tiles.rows)
    there = here if chunk else slice(None)
    if chunk:
        out[:, :, :tiles.rows, :] = refs[0][...]

    def one(step, carry):
        u, w = step // first, lax.rem(step, first)
        out[place[0] * first + w, u, there] = rest[u, w]
        for s in range(1, groups):
            column = (place[0] ^ s) * first + w
            base = occ[place[0] * first + u] + occ[column]

            def finish(mirrored):
                value = rest[u, s * first + w].astype(WIDE) + mirrored * inverse(base - sums[here])
                out[column, u, there] = value.astype(NARROW)

            with_mirror(tiles, place, other[s - 1][w, u].astype(WIDE), finish)
        return carry

    lax.fori_loop(0, first * first, one, 0)
    if chunk:
        to_distances(place, out, refs[1:-1])


def exchange(blocks):
    return lax.all_to_all(blocks, "occj", split_axis=0, concat_axis=0, tiled=True)


def by_distance(parts):
    devices = len(parts)
    return [parts[0]] + [
        lax.ppermute(parts[k], "occj", [(d, d ^ k) for d in range(devices)])
        for k in range(devices - 1, 0, -1)
    ][::-1]


def across_first(parts, groups):
    return [parts[0]] + [
        lax.ppermute(parts[s], "occi", [(k, k ^ s) for k in range(groups)])
        for s in range(groups - 1, 0, -1)
    ][::-1]


def tie(x, *others):
    return lax.optimization_barrier((x, *others))[0]


def copy_kernel(source, out):
    for k in range(source.shape[0]):
        out[k] = source[k]


def after(x, *others):
    return pl.pallas_call(
        copy_kernel,
        out_shape=jax.ShapeDtypeStruct(x.shape, x.dtype),
        in_specs=[SMEM],
        out_specs=SMEM,
        cost_estimate=pl.CostEstimate(flops=LONG, bytes_accessed=8, transcendentals=0),
    )(tie(x, *others))


def gather_vectors(vectors, devices, packed):
    def turn(x, k):
        return lax.ppermute(x, "occj", [(d, d ^ k) for d in range(devices)])

    even = list(range(0, devices, 2))
    held = [vectors] + [turn(vectors, k) for k in even[1:]]
    other = turn(tie(jnp.stack(held), packed), 1)
    return [*held, other], even + [k ^ 1 for k in even]


def virtual_sums(tiles, vir_energy, q):
    e, g = tiles.edge, tiles.rows
    n_above = len(tiles.above)
    first = jnp.array([a for a, _ in tiles.above] + list(range(0, tiles.n, 2)), jnp.int32)[q]
    second = jnp.array([b for _, b in tiles.above] + list(range(1, tiles.n, 2)), jnp.int32)[q]
    a = lax.dynamic_slice_in_dim(vir_energy, first * e, e)
    b = lax.dynamic_slice_in_dim(vir_energy, second * e, e)
    pair = a[:, None] + b[None, :]
    across = jnp.concatenate([pair, pair], axis=1)
    halves = [
        jnp.concatenate([t[:g, None] + t[None, :], t[g:, None] + t[None, :]], axis=1) for t in (a, b)
    ]
    return jnp.where(q < n_above, across, jnp.concatenate(halves, axis=0))


def local(groups, devices, amplitudes, vectors, occupied_fock_block, occ_energy, vir_energy):
    first, second, virtual = amplitudes.shape[:3]
    assert second == 1 and groups * first == devices
    assert groups & (groups - 1) == 0 and devices & (devices - 1) == 0
    tiles = Tiles(devices, virtual)
    edge = tiles.edge
    current = amplitudes.reshape(first, virtual, virtual)
    count = current.size
    fock = occupied_fock_block.astype(WIDE)
    p, q = lax.axis_index("occi"), lax.axis_index("occj")
    place = jnp.stack([p, q]).astype(jnp.int32)
    packed = jax.ShapeDtypeStruct((devices, first, edge, 2 * edge), NARROW)
    upper = jax.ShapeDtypeStruct((devices, first, tiles.rows, 2 * edge), NARROW)
    part = jax.ShapeDtypeStruct((first, first, tiles.rows, 2 * edge), NARROW)
    singles = vectors.shape[0]
    inner = pltpu.VMEM((singles * virtual, virtual), NARROW)
    square = pltpu.VMEM((virtual, virtual), WIDE)
    chunks = range(2)

    distant = jax.ShapeDtypeStruct((first, edge, 2 * edge), NARROW)
    blocks = pltpu.VMEM(packed.shape, NARROW)
    started = call(functools.partial(pack_kernel, tiles), [distant] * devices, [blocks], count, 6 * count,
                   place, current, specs=[SMEM, VMEM])
    pieces, order = gather_vectors(vectors, devices, started[0])
    held = by_distance(started)
    sums = virtual_sums(tiles, vir_energy, q)

    ladder_flops = first * singles * 4 * virtual**3
    ladder, whole = call(
        functools.partial(first_ladder_kernel, tiles, order),
        [packed, jax.ShapeDtypeStruct((virtual, singles * virtual), NARROW)], [inner, square],
        ladder_flops, 8 * count, place, current, *pieces, specs=[SMEM] + [VMEM] * (1 + len(pieces)),
    )
    parts = call(
        functools.partial(sort_kernel, tiles, groups), [part] * (2 * groups), [blocks], count, 4 * count,
        tie(place, ladder), *held, specs=[SMEM] + [VMEM] * devices,
    )
    mirror = [across_first(parts[c * groups:(c + 1) * groups], groups) for c in chunks]
    ladder = exchange(ladder)

    half, other = [], []
    for c in chunks:
        half.append(call(
            functools.partial(half_kernel, tiles, groups, first, c), [part] * groups, [],
            LONG, 6 * count, after(place, *mirror[c]) if c == 0 else place, fock, ladder, *mirror[c],
            specs=[SMEM] * 2 + [VMEM] * (groups + 1),
        ))
        other.append(across_first(half[c], groups))
    sent, rest, mixed = [], [], []
    for c in chunks:
        sent_one, rest_one, *mixed_one = call(
            functools.partial(update_kernel, tiles, groups, first, c),
            [(upper, packed)[c], jax.ShapeDtypeStruct((first, devices, *part.shape[2:]), NARROW)] + [part] * (groups - 1),
            [pltpu.VMEM((first, devices, *part.shape[2:]), WIDE), pltpu.VMEM(part.shape, WIDE)],
            LONG, 10 * count, place, fock, occ_energy, sums, *sent, *half[c], *other[c],
            specs=[SMEM] * 3 + [VMEM] * (2 * groups + 1 + c),
        )
        sent, rest, mixed = [sent_one], rest + [rest_one], mixed + [mixed_one]
    other = [across_first([None] + x, groups)[1:] for x in mixed]
    back = exchange(sent[0])
    def by_pair(*shape):
        return pl.BlockSpec((1, *shape), lambda pair: (pair, 0, 0))

    def all_pairs(*shape):
        return pl.BlockSpec(shape, lambda pair: (0, 0))

    base = pl.pallas_call(
        functools.partial(second_ladder_kernel, tiles, first),
        grid=(first,),
        out_shape=jax.ShapeDtypeStruct(current.shape, WIDE),
        in_specs=[
            SMEM, SMEM, by_pair(virtual, virtual),
            pl.BlockSpec((devices, 1, edge, 2 * edge), lambda pair: (0, pair, 0, 0)),
            all_pairs(virtual, 128), all_pairs(1, virtual), all_pairs(*whole.shape),
        ],
        out_specs=by_pair(virtual, virtual),
        scratch_shapes=[inner, square, pltpu.VMEM((virtual, virtual), NARROW)],
        compiler_params=PARAMS,
        cost_estimate=pl.CostEstimate(flops=ladder_flops, bytes_accessed=12 * count, transcendentals=0),
    )(place, occ_energy, current, back, jnp.broadcast_to(vir_energy[:, None], (virtual, 128)),
      vir_energy[None, :], whole)
    last = []
    for c in chunks:
        last = call(
            functools.partial(rest_kernel, tiles, groups, first, c),
            [distant] * devices if c else [upper], [blocks] if c else [],
            LONG, 8 * count, place, occ_energy, sums, rest[c], *other[c], *last,
            specs=[SMEM] * 2 + [VMEM] * (groups + 1 + c),
        )
    done = pl.pallas_call(
        functools.partial(add_kernel, tiles),
        grid=(first,),
        out_shape=jax.ShapeDtypeStruct(current.shape, WIDE),
        in_specs=[SMEM, by_pair(virtual, virtual)] + [by_pair(edge, 2 * edge)] * devices,
        out_specs=by_pair(virtual, virtual),
        scratch_shapes=[pltpu.VMEM((devices, 1, edge, 2 * edge), NARROW)],
        compiler_params=PARAMS,
        input_output_aliases={1: 0},
        cost_estimate=pl.CostEstimate(flops=count, bytes_accessed=10 * count, transcendentals=0),
    )(place, base, *by_distance(last))
    return done.reshape(amplitudes.shape)


def solution(mesh):
    sizes = (mesh.shape["occi"], mesh.shape["occj"])
    return jax.shard_map(
        functools.partial(local, *sizes),
        mesh=mesh,
        in_specs=(P("occi", "occj", None, None), P(None, "occj", None), P(), P(), P()),
        out_specs=P("occi", "occj", None, None),
        check_vma=False,
    )
```

```python
import functools
import math

import jax
import jax.numpy as jnp
from jax import lax
from jax.experimental import pallas as pl
from jax.experimental.pallas import tpu as pltpu
from jax.sharding import PartitionSpec as P

VMEM = pl.BlockSpec(memory_space=pltpu.VMEM)
SMEM = pl.BlockSpec(memory_space=pltpu.SMEM)
PARAMS = pltpu.CompilerParams(vmem_limit_bytes=50 * 2**20)
WIDE = jnp.float32
LONG = 3 * 10**10
NARROW = jnp.bfloat16


class Tiles:
    def __init__(self, devices, virtual):
        n = math.isqrt(2 * devices)
        assert n * n == 2 * devices and n % 2 == 0 and virtual % n == 0
        self.n = n
        self.edge = virtual // n
        self.rows = self.edge // 2
        self.above = [(a, b) for a in range(n) for b in range(a + 1, n)]
        self.diagonal = [(len(self.above) + k // 2, k % 2, k) for k in range(n)]

    def span(self, k):
        return slice(k * self.edge, (k + 1) * self.edge)

    def mirror_within(self, x):
        e, g = self.edge, self.rows
        tile = jnp.concatenate([x[:, :e], x[:, e:]], axis=0).T
        return jnp.concatenate([tile[:g], tile[g:]], axis=1)

    def mirror_across(self, x):
        return jnp.concatenate([x[:, self.edge:], x[:, :self.edge]], axis=1)


def call(body, outs, scratch, flops, moved, *operands, specs):
    return pl.pallas_call(
        body,
        out_shape=outs,
        in_specs=specs,
        out_specs=jax.tree.map(lambda _: VMEM, outs),
        scratch_shapes=scratch,
        compiler_params=PARAMS,
        cost_estimate=pl.CostEstimate(flops=flops, bytes_accessed=moved, transcendentals=0),
    )(*operands)


def pack_pair(tiles, source, out, pair, mirrored=False):
    e, g = tiles.edge, tiles.rows
    straight, turned = (slice(e, None), slice(0, e)) if mirrored else (slice(0, e), slice(e, None))
    for d, (a, b) in enumerate(tiles.above):
        out[d, pair, :, straight] = source[tiles.span(a), tiles.span(b)].astype(NARROW)
        out[d, pair, :, turned] = source[tiles.span(b), tiles.span(a)].astype(WIDE).T.astype(NARROW)
    for d, c, k in tiles.diagonal:
        tile = source[tiles.span(k), tiles.span(k)]
        tile = tile.astype(WIDE).T.astype(NARROW) if mirrored else tile.astype(NARROW)
        out[d, pair, c * g:(c + 1) * g, :e] = tile[:g]
        out[d, pair, c * g:(c + 1) * g, e:] = tile[g:]


def unpack_pair(tiles, blocks, pair, put):
    e, g = tiles.edge, tiles.rows
    for d, (a, b) in enumerate(tiles.above):
        put(a, b, blocks[d, pair, :, :e].astype(WIDE))
        put(b, a, blocks[d, pair, :, e:].astype(WIDE).T)
    for d, c, k in tiles.diagonal:
        upper = blocks[d, pair, c * g:(c + 1) * g, :e]
        lower = blocks[d, pair, c * g:(c + 1) * g, e:]
        put(k, k, jnp.concatenate([upper, lower], axis=0).astype(WIDE))


def to_distances(place, whole, outs):
    for k, out in enumerate(outs):
        out[...] = whole[place[1] ^ k]


def from_distances(place, pieces, whole):
    for k, piece in enumerate(pieces):
        whole[place[1] ^ k] = piece[...]


def pack_kernel(tiles, place, source, *refs):
    outs, whole = refs[:-1], refs[-1]
    for pair in range(source.shape[0]):
        pack_pair(tiles, source.at[pair], whole, pair, mirrored=True)
    to_distances(place, whole, outs)


def sort_kernel(tiles, groups, place, *refs):
    pieces, outs, whole = refs[:-2 * groups - 1], refs[-2 * groups - 1:-1], refs[-1]
    first = whole.shape[1]
    from_distances(place, pieces, whole)
    for s in range(groups):
        for u in range(first):
            block = whole[(place[0] ^ s) * first + u]
            for c in range(2):
                outs[c * groups + s][u] = block[:, c * tiles.rows:(c + 1) * tiles.rows]


def assemble(place, order, pieces, whole):
    k = 0
    for piece in pieces:
        count, rows, virtual = piece.shape[-3:]
        for block in range(piece.shape[0] if len(piece.shape) == 4 else 1):
            start = pl.multiple_of((place[1] ^ order[k]) * rows, rows)
            for single in range(count):
                values = piece[block, single] if len(piece.shape) == 4 else piece[single]
                whole[pl.ds(start, rows), single * virtual:(single + 1) * virtual] = values
            k += 1


def ladder_pair(matrix, whole, inner, total):
    virtual = matrix.shape[0]
    for single in range(whole.shape[1] // virtual):
        at = slice(single * virtual, (single + 1) * virtual)
        inner[at, :] = lax.dot_general(
            matrix, whole[:, at], (((1,), (1,)), ((), ())), preferred_element_type=WIDE
        ).astype(NARROW)
    total[...] = jnp.dot(whole[...], inner[...], preferred_element_type=WIDE)


def inverse(x):
    guess = pl.reciprocal(x, approx=True)
    return guess * (2.0 - x * guess)


def first_ladder_kernel(tiles, order, place, source, *refs):
    pieces, (out, whole, inner, total) = refs[:-4], refs[-4:]
    assemble(place, order, pieces, whole)
    for pair in range(source.shape[0]):
        ladder_pair(source[pair].astype(NARROW), whole, inner, total)
        pack_pair(tiles, total, out, pair)


def second_ladder_kernel(tiles, first, place, occ, source, blocks, row, column, vectors, out,
                         whole, inner, total, matrix, arrived):
    fetch = pltpu.make_async_copy(vectors, whole, arrived)

    @pl.when(pl.program_id(0) == 0)
    def _():
        fetch.start()

    def put(a, b, tile):
        matrix[tiles.span(a), tiles.span(b)] = tile.astype(NARROW)

    unpack_pair(tiles, blocks, 0, put)

    @pl.when(pl.program_id(0) == 0)
    def _():
        fetch.wait()

    ladder_pair(matrix[...], whole, inner, total)
    base = occ[place[0] * first + pl.program_id(0)] + occ[place[1]]
    strip = math.gcd(64, total.shape[0])

    def finish(step, carry):
        at = pl.ds(pl.multiple_of(step * strip, strip), strip)
        own = base - row[at, :1] - column[...]
        out[0, at, :] = source[0, at, :] + 2.0 * (matrix[at, :].astype(WIDE) + total[at, :] * inverse(own))
        return carry

    lax.fori_loop(0, total.shape[0] // strip, finish, 0)


def add_kernel(tiles, place, source, *refs):
    pieces, (out, whole) = refs[:-2], refs[-2:]
    from_distances(place, pieces, whole)

    def put(a, b, tile):
        here = (0, tiles.span(a), tiles.span(b))
        out[here] = source[here] + tile

    unpack_pair(tiles, whole, 0, put)


def mix(place, fock, first, load, store, rows):
    total = fock.shape[0]
    strips = rows // 16

    def strip(step, carry):
        u = step // strips
        at = pl.ds(pl.multiple_of(lax.rem(step, strips) * 16, 16), 16)
        taken = [load(k // first, u, k % first, at) for k in range(total)]
        for k in range(total):
            column = (place[0] ^ (k // first)) * first + k % first
            result = None
            for m in range(total):
                line = (place[0] ^ (m // first)) * first + m % first
                term = (-fock[line, column]) * taken[m]
                result = term if result is None else result + term
            store(k // first, u, k % first, column, at, result)
        return carry

    lax.fori_loop(0, first * strips, strip, 0)


def half_kernel(tiles, groups, first, chunk, place, fock, ladder, *refs):
    held, out = refs[:groups], refs[groups:]

    def load(s, u, r, at):
        return held[s][u, r, at, :].astype(WIDE)

    def store(s, u, w, column, at, result):
        rows = pl.ds(pl.multiple_of(chunk * tiles.rows + at.start, 16), at.size)
        out[s][u, w, at, :] = (ladder[column, u, rows, :].astype(WIDE) + result).astype(NARROW)

    mix(place, fock, first, load, store, tiles.rows)


def with_mirror(tiles, place, x, finish):
    across = place[1] < len(tiles.above)

    @pl.when(across)
    def _():
        finish(tiles.mirror_across(x))

    @pl.when(jnp.logical_not(across))
    def _():
        finish(tiles.mirror_within(x))


def update_kernel(tiles, groups, first, chunk, place, fock, occ, sums, *refs):
    before, refs = refs[:chunk], refs[chunk:]
    own, other, refs = refs[:groups], refs[groups:2 * groups], refs[2 * groups:]
    (sent, rest), out, (update, local_mixed) = refs[:2], refs[2:groups + 1], refs[groups + 1:]
    here = slice(chunk * tiles.rows, (chunk + 1) * tiles.rows)
    for ref in before:
        sent[:, :, :tiles.rows, :] = ref[...]

    def one(step, carry):
        u, w = step // first, lax.rem(step, first)
        for s in range(groups):
            column = (place[0] ^ s) * first + w
            base = occ[place[0] * first + u] + occ[column]

            def finish(mirrored):
                value = (own[s][u, w].astype(WIDE) + mirrored) * inverse(base - sums[here])
                update[u, s * first + w] = value
                sent[column, u, here] = value.astype(NARROW)

            with_mirror(tiles, place, other[s][w, u].astype(WIDE), finish)
        return carry

    lax.fori_loop(0, first * first, one, 0)

    def load(s, u, r, at):
        return update[u, s * first + r, at, :]

    def lost(value):
        return 2.0 * (value - value.astype(NARROW).astype(WIDE))

    def store(s, u, w, column, at, result):
        if s == 0:
            local_mixed[u, w, at, :] = result
            return
        out[s - 1][u, w, at, :] = result.astype(NARROW)
        strip = pl.ds(pl.multiple_of(chunk * tiles.rows + at.start, 16), at.size)
        base = occ[place[0] * first + u] + occ[column]
        share = result * inverse(base - sums[strip, :])
        rest[u, s * first + w, at, :] = (lost(update[u, s * first + w, at, :]) + share).astype(NARROW)

    mix(place, fock, first, load, store, tiles.rows)

    def within(step, carry):
        u, w = step // first, lax.rem(step, first)
        base = occ[place[0] * first + u] + occ[place[0] * first + w]

        def finish(mirrored):
            share = (local_mixed[u, w] + mirrored) * inverse(base - sums[here])
            rest[u, w] = (lost(update[u, w]) + share).astype(NARROW)

        with_mirror(tiles, place, local_mixed[w, u], finish)
        return carry

    lax.fori_loop(0, first * first, within, 0)


def rest_kernel(tiles, groups, first, chunk, place, occ, sums, rest, *refs):
    other, refs = refs[:groups - 1], refs[groups - 1:]
    out = refs[-1]
    here = slice(chunk * tiles.rows, (chunk + 1) * tiles.rows)
    there = here if chunk else slice(None)
    if chunk:
        out[:, :, :tiles.rows, :] = refs[0][...]

    def one(step, carry):
        u, w = step // first, lax.rem(step, first)
        out[place[0] * first + w, u, there] = rest[u, w]
        for s in range(1, groups):
            column = (place[0] ^ s) * first + w
            base = occ[place[0] * first + u] + occ[column]

            def finish(mirrored):
                value = rest[u, s * first + w].astype(WIDE) + mirrored * inverse(base - sums[here])
                out[column, u, there] = value.astype(NARROW)

            with_mirror(tiles, place, other[s - 1][w, u].astype(WIDE), finish)
        return carry

    lax.fori_loop(0, first * first, one, 0)
    if chunk:
        to_distances(place, out, refs[1:-1])


def exchange(blocks):
    return lax.all_to_all(blocks, "occj", split_axis=0, concat_axis=0, tiled=True)


def by_distance(parts):
    devices = len(parts)
    return [parts[0]] + [
        lax.ppermute(parts[k], "occj", [(d, d ^ k) for d in range(devices)])
        for k in range(devices - 1, 0, -1)
    ][::-1]


def across_first(parts, groups):
    return [parts[0]] + [
        lax.ppermute(parts[s], "occi", [(k, k ^ s) for k in range(groups)])
        for s in range(groups - 1, 0, -1)
    ][::-1]


def tie(x, *others):
    return lax.optimization_barrier((x, *others))[0]


def copy_kernel(source, out):
    for k in range(source.shape[0]):
        out[k] = source[k]


def after(x, *others):
    return pl.pallas_call(
        copy_kernel,
        out_shape=jax.ShapeDtypeStruct(x.shape, x.dtype),
        in_specs=[SMEM],
        out_specs=SMEM,
        cost_estimate=pl.CostEstimate(flops=LONG, bytes_accessed=8, transcendentals=0),
    )(tie(x, *others))


def gather_vectors(vectors, devices, packed):
    def turn(x, k):
        return lax.ppermute(x, "occj", [(d, d ^ k) for d in range(devices)])

    even = list(range(0, devices, 2))
    held = [vectors] + [turn(vectors, k) for k in even[1:]]
    other = turn(tie(jnp.stack(held), packed), 1)
    return [*held, other], even + [k ^ 1 for k in even]


def virtual_sums(tiles, vir_energy, q):
    e, g = tiles.edge, tiles.rows
    n_above = len(tiles.above)
    first = jnp.array([a for a, _ in tiles.above] + list(range(0, tiles.n, 2)), jnp.int32)[q]
    second = jnp.array([b for _, b in tiles.above] + list(range(1, tiles.n, 2)), jnp.int32)[q]
    a = lax.dynamic_slice_in_dim(vir_energy, first * e, e)
    b = lax.dynamic_slice_in_dim(vir_energy, second * e, e)
    pair = a[:, None] + b[None, :]
    across = jnp.concatenate([pair, pair], axis=1)
    halves = [
        jnp.concatenate([t[:g, None] + t[None, :], t[g:, None] + t[None, :]], axis=1) for t in (a, b)
    ]
    return jnp.where(q < n_above, across, jnp.concatenate(halves, axis=0))


def local(groups, devices, amplitudes, vectors, occupied_fock_block, occ_energy, vir_energy):
    first, second, virtual = amplitudes.shape[:3]
    assert second == 1 and groups * first == devices
    assert groups & (groups - 1) == 0 and devices & (devices - 1) == 0
    tiles = Tiles(devices, virtual)
    edge = tiles.edge
    current = amplitudes.reshape(first, virtual, virtual)
    count = current.size
    fock = occupied_fock_block.astype(WIDE)
    p, q = lax.axis_index("occi"), lax.axis_index("occj")
    place = jnp.stack([p, q]).astype(jnp.int32)
    packed = jax.ShapeDtypeStruct((devices, first, edge, 2 * edge), NARROW)
    upper = jax.ShapeDtypeStruct((devices, first, tiles.rows, 2 * edge), NARROW)
    part = jax.ShapeDtypeStruct((first, first, tiles.rows, 2 * edge), NARROW)
    singles = vectors.shape[0]
    inner = pltpu.VMEM((singles * virtual, virtual), NARROW)
    square = pltpu.VMEM((virtual, virtual), WIDE)
    chunks = range(2)

    distant = jax.ShapeDtypeStruct((first, edge, 2 * edge), NARROW)
    blocks = pltpu.VMEM(packed.shape, NARROW)
    started = call(functools.partial(pack_kernel, tiles), [distant] * devices, [blocks], count, 6 * count,
                   place, current, specs=[SMEM, VMEM])
    pieces, order = gather_vectors(vectors, devices, started[0])
    held = by_distance(started)
    sums = virtual_sums(tiles, vir_energy, q)

    ladder_flops = first * singles * 4 * virtual**3
    ladder, whole = call(
        functools.partial(first_ladder_kernel, tiles, order),
        [packed, jax.ShapeDtypeStruct((virtual, singles * virtual), NARROW)], [inner, square],
        ladder_flops, 8 * count, place, current, *pieces, specs=[SMEM] + [VMEM] * (1 + len(pieces)),
    )
    parts = call(
        functools.partial(sort_kernel, tiles, groups), [part] * (2 * groups), [blocks], count, 4 * count,
        tie(place, ladder), *held, specs=[SMEM] + [VMEM] * devices,
    )
    mirror = [across_first(parts[c * groups:(c + 1) * groups], groups) for c in chunks]
    ladder = exchange(ladder)

    half, other = [], []
    for c in chunks:
        half.append(call(
            functools.partial(half_kernel, tiles, groups, first, c), [part] * groups, [],
            LONG, 6 * count, after(place, *mirror[c]) if c == 0 else place, fock, ladder, *mirror[c],
            specs=[SMEM] * 2 + [VMEM] * (groups + 1),
        ))
        other.append(across_first(half[c], groups))
    sent, rest, mixed = [], [], []
    for c in chunks:
        sent_one, rest_one, *mixed_one = call(
            functools.partial(update_kernel, tiles, groups, first, c),
            [(upper, packed)[c], jax.ShapeDtypeStruct((first, devices, *part.shape[2:]), NARROW)] + [part] * (groups - 1),
            [pltpu.VMEM((first, devices, *part.shape[2:]), WIDE), pltpu.VMEM(part.shape, WIDE)],
            LONG, 10 * count, place, fock, occ_energy, sums, *sent, *half[c], *other[c],
            specs=[SMEM] * 3 + [VMEM] * (2 * groups + 1 + c),
        )
        sent, rest, mixed = [sent_one], rest + [rest_one], mixed + [mixed_one]
    other = [across_first([None] + x, groups)[1:] for x in mixed]
    back = exchange(tie(sent[0], other[0][min(1, groups - 2)]))
    def by_pair(*shape):
        return pl.BlockSpec((1, *shape), lambda pair: (pair, 0, 0))

    def all_pairs(*shape):
        return pl.BlockSpec(shape, lambda pair: (0, 0))

    base = pl.pallas_call(
        functools.partial(second_ladder_kernel, tiles, first),
        grid=(first,),
        out_shape=jax.ShapeDtypeStruct(current.shape, WIDE),
        in_specs=[
            SMEM, SMEM, by_pair(virtual, virtual),
            pl.BlockSpec((devices, 1, edge, 2 * edge), lambda pair: (0, pair, 0, 0)),
            all_pairs(virtual, 128), all_pairs(1, virtual), pl.BlockSpec(memory_space=pl.ANY),
        ],
        out_specs=by_pair(virtual, virtual),
        scratch_shapes=[
            pltpu.VMEM(whole.shape, NARROW), inner, square, pltpu.VMEM((virtual, virtual), NARROW),
            pltpu.SemaphoreType.DMA,
        ],
        compiler_params=PARAMS,
        cost_estimate=pl.CostEstimate(flops=ladder_flops, bytes_accessed=12 * count, transcendentals=0),
    )(place, occ_energy, current, back, jnp.broadcast_to(vir_energy[:, None], (virtual, 128)),
      vir_energy[None, :], whole)
    last = []
    for c in chunks:
        last = call(
            functools.partial(rest_kernel, tiles, groups, first, c),
            [distant] * devices if c else [upper], [blocks] if c else [],
            LONG, 8 * count, place, occ_energy, sums, rest[c], *other[c], *last,
            specs=[SMEM] * 2 + [VMEM] * (groups + 1 + c),
        )
    done = pl.pallas_call(
        functools.partial(add_kernel, tiles),
        grid=(first,),
        out_shape=jax.ShapeDtypeStruct(current.shape, WIDE),
        in_specs=[SMEM, by_pair(virtual, virtual)] + [by_pair(edge, 2 * edge)] * devices,
        out_specs=by_pair(virtual, virtual),
        scratch_shapes=[pltpu.VMEM((devices, 1, edge, 2 * edge), NARROW)],
        compiler_params=PARAMS,
        input_output_aliases={1: 0},
        cost_estimate=pl.CostEstimate(flops=count, bytes_accessed=10 * count, transcendentals=0),
    )(place, base, *by_distance(last))
    return done.reshape(amplitudes.shape)


def solution(mesh):
    sizes = (mesh.shape["occi"], mesh.shape["occj"])
    return jax.shard_map(
        functools.partial(local, *sizes),
        mesh=mesh,
        in_specs=(P("occi", "occj", None, None), P(None, "occj", None), P(), P(), P()),
        out_specs=P("occi", "occj", None, None),
        check_vma=False,
    )
```

```python
import functools
import math

import jax
import jax.numpy as jnp
from jax import lax
from jax.experimental import pallas as pl
from jax.experimental.pallas import tpu as pltpu
from jax.sharding import PartitionSpec as P

VMEM = pl.BlockSpec(memory_space=pltpu.VMEM)
SMEM = pl.BlockSpec(memory_space=pltpu.SMEM)
PARAMS = pltpu.CompilerParams(vmem_limit_bytes=50 * 2**20)
SMALL = pltpu.CompilerParams(vmem_limit_bytes=20 * 2**20)
WIDE = jnp.float32
LONG = 3 * 10**10
NARROW = jnp.bfloat16


class Tiles:
    def __init__(self, devices, virtual):
        n = math.isqrt(2 * devices)
        assert n * n == 2 * devices and n % 2 == 0 and virtual % n == 0
        self.n = n
        self.edge = virtual // n
        self.rows = self.edge // 2
        self.above = [(a, b) for a in range(n) for b in range(a + 1, n)]
        self.diagonal = [(len(self.above) + k // 2, k % 2, k) for k in range(n)]

    def span(self, k):
        return slice(k * self.edge, (k + 1) * self.edge)

    def mirror_within(self, x):
        e, g = self.edge, self.rows
        tile = jnp.concatenate([x[:, :e], x[:, e:]], axis=0).T
        return jnp.concatenate([tile[:g], tile[g:]], axis=1)

    def mirror_across(self, x):
        return jnp.concatenate([x[:, self.edge:], x[:, :self.edge]], axis=1)


def call(body, outs, scratch, flops, moved, *operands, specs, params=PARAMS):
    return pl.pallas_call(
        body,
        out_shape=outs,
        in_specs=specs,
        out_specs=jax.tree.map(lambda _: VMEM, outs),
        scratch_shapes=scratch,
        compiler_params=params,
        cost_estimate=pl.CostEstimate(flops=flops, bytes_accessed=moved, transcendentals=0),
    )(*operands)


def pack_pair(tiles, source, out, pair, mirrored=False):
    e, g = tiles.edge, tiles.rows
    straight, turned = (slice(e, None), slice(0, e)) if mirrored else (slice(0, e), slice(e, None))
    for d, (a, b) in enumerate(tiles.above):
        out[d, pair, :, straight] = source[tiles.span(a), tiles.span(b)].astype(NARROW)
        out[d, pair, :, turned] = source[tiles.span(b), tiles.span(a)].astype(WIDE).T.astype(NARROW)
    for d, c, k in tiles.diagonal:
        tile = source[tiles.span(k), tiles.span(k)]
        tile = tile.astype(WIDE).T.astype(NARROW) if mirrored else tile.astype(NARROW)
        out[d, pair, c * g:(c + 1) * g, :e] = tile[:g]
        out[d, pair, c * g:(c + 1) * g, e:] = tile[g:]


def unpack_pair(tiles, blocks, pair, put):
    e, g = tiles.edge, tiles.rows
    for d, (a, b) in enumerate(tiles.above):
        put(a, b, blocks[d, pair, :, :e].astype(WIDE))
        put(b, a, blocks[d, pair, :, e:].astype(WIDE).T)
    for d, c, k in tiles.diagonal:
        upper = blocks[d, pair, c * g:(c + 1) * g, :e]
        lower = blocks[d, pair, c * g:(c + 1) * g, e:]
        put(k, k, jnp.concatenate([upper, lower], axis=0).astype(WIDE))


def to_distances(place, whole, outs):
    for k, out in enumerate(outs):
        out[...] = whole[place[1] ^ k]


def from_distances(place, pieces, whole):
    for k, piece in enumerate(pieces):
        whole[place[1] ^ k] = piece[...]


def pack_kernel(tiles, place, source, *refs):
    outs, whole = refs[:-1], refs[-1]
    for pair in range(source.shape[0]):
        pack_pair(tiles, source.at[pair], whole, pair, mirrored=True)
    to_distances(place, whole, outs)


def sort_kernel(tiles, groups, place, *refs):
    pieces, outs, whole = refs[:-2 * groups - 1], refs[-2 * groups - 1:-1], refs[-1]
    first = whole.shape[1]
    from_distances(place, pieces, whole)
    for s in range(groups):
        for u in range(first):
            block = whole[(place[0] ^ s) * first + u]
            for c in range(2):
                outs[c * groups + s][u] = block[:, c * tiles.rows:(c + 1) * tiles.rows]


def assemble(place, order, pieces, whole):
    k = 0
    for piece in pieces:
        count, rows, virtual = piece.shape[-3:]
        for block in range(piece.shape[0] if len(piece.shape) == 4 else 1):
            start = pl.multiple_of((place[1] ^ order[k]) * rows, rows)
            for single in range(count):
                values = piece[block, single] if len(piece.shape) == 4 else piece[single]
                whole[pl.ds(start, rows), single * virtual:(single + 1) * virtual] = values
            k += 1


def ladder_pair(matrix, whole, inner, total):
    virtual = matrix.shape[0]
    for single in range(whole.shape[1] // virtual):
        at = slice(single * virtual, (single + 1) * virtual)
        inner[at, :] = lax.dot_general(
            matrix, whole[:, at], (((1,), (1,)), ((), ())), preferred_element_type=WIDE
        ).astype(NARROW)
    total[...] = jnp.dot(whole[...], inner[...], preferred_element_type=WIDE)


def inverse(x):
    guess = pl.reciprocal(x, approx=True)
    return guess * (2.0 - x * guess)


def first_ladder_kernel(tiles, order, place, source, *refs):
    pieces, (out, whole, inner, total) = refs[:-4], refs[-4:]
    assemble(place, order, pieces, whole)
    for pair in range(source.shape[0]):
        ladder_pair(source[pair].astype(NARROW), whole, inner, total)
        pack_pair(tiles, total, out, pair)


def second_ladder_kernel(tiles, first, place, occ, source, blocks, row, column, whole, out, inner, total, matrix):
    def put(a, b, tile):
        matrix[tiles.span(a), tiles.span(b)] = tile.astype(NARROW)

    unpack_pair(tiles, blocks, 0, put)
    ladder_pair(matrix[...], whole, inner, total)
    base = occ[place[0] * first + pl.program_id(0)] + occ[place[1]]
    strip = math.gcd(64, total.shape[0])

    def finish(step, carry):
        at = pl.ds(pl.multiple_of(step * strip, strip), strip)
        own = base - row[at, :1] - column[...]
        out[0, at, :] = source[0, at, :] + 2.0 * (matrix[at, :].astype(WIDE) + total[at, :] * inverse(own))
        return carry

    lax.fori_loop(0, total.shape[0] // strip, finish, 0)


def add_kernel(tiles, place, source, *refs):
    pieces, (out, whole) = refs[:-2], refs[-2:]
    from_distances(place, pieces, whole)

    def put(a, b, tile):
        here = (0, tiles.span(a), tiles.span(b))
        out[here] = source[here] + tile

    unpack_pair(tiles, whole, 0, put)


def mix(place, fock, first, load, store, rows):
    total = fock.shape[0]
    strips = rows // 16

    def strip(step, carry):
        u = step // strips
        at = pl.ds(pl.multiple_of(lax.rem(step, strips) * 16, 16), 16)
        taken = [load(k // first, u, k % first, at) for k in range(total)]
        for k in range(total):
            column = (place[0] ^ (k // first)) * first + k % first
            result = None
            for m in range(total):
                line = (place[0] ^ (m // first)) * first + m % first
                term = (-fock[line, column]) * taken[m]
                result = term if result is None else result + term
            store(k // first, u, k % first, column, at, result)
        return carry

    lax.fori_loop(0, first * strips, strip, 0)


def half_kernel(tiles, groups, first, chunk, place, fock, ladder, *refs):
    held, out = refs[:groups], refs[groups:]

    def load(s, u, r, at):
        return held[s][u, r, at, :].astype(WIDE)

    def store(s, u, w, column, at, result):
        rows = pl.ds(pl.multiple_of(chunk * tiles.rows + at.start, 16), at.size)
        out[s][u, w, at, :] = (ladder[column, u, rows, :].astype(WIDE) + result).astype(NARROW)

    mix(place, fock, first, load, store, tiles.rows)


def with_mirror(tiles, place, x, finish):
    across = place[1] < len(tiles.above)

    @pl.when(across)
    def _():
        finish(tiles.mirror_across(x))

    @pl.when(jnp.logical_not(across))
    def _():
        finish(tiles.mirror_within(x))


def update_kernel(tiles, groups, first, chunk, place, fock, occ, sums, *refs):
    before, refs = refs[:chunk], refs[chunk:]
    own, other, refs = refs[:groups], refs[groups:2 * groups], refs[2 * groups:]
    (sent, rest), out, (update, local_mixed) = refs[:2], refs[2:groups + 1], refs[groups + 1:]
    here = slice(chunk * tiles.rows, (chunk + 1) * tiles.rows)
    for ref in before:
        sent[:, :, :tiles.rows, :] = ref[...]

    def one(step, carry):
        u, w = step // first, lax.rem(step, first)
        for s in range(groups):
            column = (place[0] ^ s) * first + w
            base = occ[place[0] * first + u] + occ[column]

            def finish(mirrored):
                value = (own[s][u, w].astype(WIDE) + mirrored) * inverse(base - sums[here])
                update[u, s * first + w] = value
                sent[column, u, here] = value.astype(NARROW)

            with_mirror(tiles, place, other[s][w, u].astype(WIDE), finish)
        return carry

    lax.fori_loop(0, first * first, one, 0)

    def load(s, u, r, at):
        return update[u, s * first + r, at, :]

    def lost(value):
        return 2.0 * (value - value.astype(NARROW).astype(WIDE))

    def store(s, u, w, column, at, result):
        if s == 0:
            local_mixed[u, w, at, :] = result
            return
        out[s - 1][u, w, at, :] = result.astype(NARROW)
        strip = pl.ds(pl.multiple_of(chunk * tiles.rows + at.start, 16), at.size)
        base = occ[place[0] * first + u] + occ[column]
        share = result * inverse(base - sums[strip, :])
        rest[u, s * first + w, at, :] = (lost(update[u, s * first + w, at, :]) + share).astype(NARROW)

    mix(place, fock, first, load, store, tiles.rows)

    def within(step, carry):
        u, w = step // first, lax.rem(step, first)
        base = occ[place[0] * first + u] + occ[place[0] * first + w]

        def finish(mirrored):
            share = (local_mixed[u, w] + mirrored) * inverse(base - sums[here])
            rest[u, w] = (lost(update[u, w]) + share).astype(NARROW)

        with_mirror(tiles, place, local_mixed[w, u], finish)
        return carry

    lax.fori_loop(0, first * first, within, 0)


def rest_kernel(tiles, groups, first, chunk, place, occ, sums, rest, *refs):
    other, refs = refs[:groups - 1], refs[groups - 1:]
    out = refs[-1]
    here = slice(chunk * tiles.rows, (chunk + 1) * tiles.rows)
    there = here if chunk else slice(None)
    if chunk:
        out[:, :, :tiles.rows, :] = refs[0][...]

    def one(step, carry):
        u, w = step // first, lax.rem(step, first)
        out[place[0] * first + w, u, there] = rest[u, w]
        for s in range(1, groups):
            column = (place[0] ^ s) * first + w
            base = occ[place[0] * first + u] + occ[column]

            def finish(mirrored):
                value = rest[u, s * first + w].astype(WIDE) + mirrored * inverse(base - sums[here])
                out[column, u, there] = value.astype(NARROW)

            with_mirror(tiles, place, other[s - 1][w, u].astype(WIDE), finish)
        return carry

    lax.fori_loop(0, first * first, one, 0)
    if chunk:
        to_distances(place, out, refs[1:-1])


def exchange(blocks):
    return lax.all_to_all(blocks, "occj", split_axis=0, concat_axis=0, tiled=True)


def by_distance(parts):
    devices = len(parts)
    return [parts[0]] + [
        lax.ppermute(parts[k], "occj", [(d, d ^ k) for d in range(devices)])
        for k in range(devices - 1, 0, -1)
    ][::-1]


def across_first(parts, groups):
    return [parts[0]] + [
        lax.ppermute(parts[s], "occi", [(k, k ^ s) for k in range(groups)])
        for s in range(groups - 1, 0, -1)
    ][::-1]


def tie(x, *others):
    return lax.optimization_barrier((x, *others))[0]


def copy_kernel(source, out):
    for k in range(source.shape[0]):
        out[k] = source[k]


def after(x, *others):
    return pl.pallas_call(
        copy_kernel,
        out_shape=jax.ShapeDtypeStruct(x.shape, x.dtype),
        in_specs=[SMEM],
        out_specs=SMEM,
        cost_estimate=pl.CostEstimate(flops=LONG, bytes_accessed=8, transcendentals=0),
    )(tie(x, *others))


def gather_vectors(vectors, devices, packed):
    def turn(x, k):
        return lax.ppermute(x, "occj", [(d, d ^ k) for d in range(devices)])

    even = list(range(0, devices, 2))
    held = [vectors] + [turn(vectors, k) for k in even[1:]]
    other = turn(tie(jnp.stack(held), packed), 1)
    return [*held, other], even + [k ^ 1 for k in even]


def virtual_sums(tiles, vir_energy, q):
    e, g = tiles.edge, tiles.rows
    n_above = len(tiles.above)
    first = jnp.array([a for a, _ in tiles.above] + list(range(0, tiles.n, 2)), jnp.int32)[q]
    second = jnp.array([b for _, b in tiles.above] + list(range(1, tiles.n, 2)), jnp.int32)[q]
    a = lax.dynamic_slice_in_dim(vir_energy, first * e, e)
    b = lax.dynamic_slice_in_dim(vir_energy, second * e, e)
    pair = a[:, None] + b[None, :]
    across = jnp.concatenate([pair, pair], axis=1)
    halves = [
        jnp.concatenate([t[:g, None] + t[None, :], t[g:, None] + t[None, :]], axis=1) for t in (a, b)
    ]
    return jnp.where(q < n_above, across, jnp.concatenate(halves, axis=0))


def local(groups, devices, amplitudes, vectors, occupied_fock_block, occ_energy, vir_energy):
    first, second, virtual = amplitudes.shape[:3]
    assert second == 1 and groups * first == devices
    assert groups & (groups - 1) == 0 and devices & (devices - 1) == 0
    tiles = Tiles(devices, virtual)
    edge = tiles.edge
    current = amplitudes.reshape(first, virtual, virtual)
    count = current.size
    fock = occupied_fock_block.astype(WIDE)
    p, q = lax.axis_index("occi"), lax.axis_index("occj")
    place = jnp.stack([p, q]).astype(jnp.int32)
    packed = jax.ShapeDtypeStruct((devices, first, edge, 2 * edge), NARROW)
    upper = jax.ShapeDtypeStruct((devices, first, tiles.rows, 2 * edge), NARROW)
    part = jax.ShapeDtypeStruct((first, first, tiles.rows, 2 * edge), NARROW)
    singles = vectors.shape[0]
    inner = pltpu.VMEM((singles * virtual, virtual), NARROW)
    square = pltpu.VMEM((virtual, virtual), WIDE)
    chunks = range(2)

    distant = jax.ShapeDtypeStruct((first, edge, 2 * edge), NARROW)
    blocks = pltpu.VMEM(packed.shape, NARROW)
    started = call(functools.partial(pack_kernel, tiles), [distant] * devices, [blocks], count, 6 * count,
                   place, current, specs=[SMEM, VMEM])
    pieces, order = gather_vectors(vectors, devices, started[0])
    held = by_distance(started)
    sums = virtual_sums(tiles, vir_energy, q)

    ladder_flops = first * singles * 4 * virtual**3
    ladder, whole = call(
        functools.partial(first_ladder_kernel, tiles, order),
        [packed, jax.ShapeDtypeStruct((virtual, singles * virtual), NARROW)], [inner, square],
        ladder_flops, 8 * count, place, current, *pieces, specs=[SMEM] + [VMEM] * (1 + len(pieces)),
    )
    parts = call(
        functools.partial(sort_kernel, tiles, groups), [part] * (2 * groups), [blocks], count, 4 * count,
        tie(place, ladder), *held, specs=[SMEM] + [VMEM] * devices,
    )
    mirror = [across_first(parts[c * groups:(c + 1) * groups], groups) for c in chunks]
    ladder = exchange(ladder)

    half, other = [], []
    for c in chunks:
        half.append(call(
            functools.partial(half_kernel, tiles, groups, first, c), [part] * groups, [],
            LONG, 6 * count, after(place, *mirror[c]) if c == 0 else place, fock, ladder, *mirror[c],
            specs=[SMEM] * 2 + [VMEM] * (groups + 1),
        ))
        other.append(across_first(half[c], groups))
    sent, rest, mixed = [], [], []
    for c in chunks:
        sent_one, rest_one, *mixed_one = call(
            functools.partial(update_kernel, tiles, groups, first, c),
            [(upper, packed)[c], jax.ShapeDtypeStruct((first, devices, *part.shape[2:]), NARROW)] + [part] * (groups - 1),
            [pltpu.VMEM((first, devices, *part.shape[2:]), WIDE), pltpu.VMEM(part.shape, WIDE)],
            LONG, 10 * count, place, fock, occ_energy, sums, *sent, *half[c], *other[c],
            specs=[SMEM] * 3 + [VMEM] * (2 * groups + 1 + c), params=SMALL,
        )
        sent, rest, mixed = [sent_one], rest + [rest_one], mixed + [mixed_one]
    other = [across_first([None] + x, groups)[1:] for x in mixed]
    back = exchange(sent[0])
    def by_pair(*shape):
        return pl.BlockSpec((1, *shape), lambda pair: (pair, 0, 0))

    def all_pairs(*shape):
        return pl.BlockSpec(shape, lambda pair: (0, 0))

    base = pl.pallas_call(
        functools.partial(second_ladder_kernel, tiles, first),
        grid=(first,),
        out_shape=jax.ShapeDtypeStruct(current.shape, WIDE),
        in_specs=[
            SMEM, SMEM, by_pair(virtual, virtual),
            pl.BlockSpec((devices, 1, edge, 2 * edge), lambda pair: (0, pair, 0, 0)),
            all_pairs(virtual, 128), all_pairs(1, virtual), all_pairs(*whole.shape),
        ],
        out_specs=by_pair(virtual, virtual),
        scratch_shapes=[inner, square, pltpu.VMEM((virtual, virtual), NARROW)],
        compiler_params=PARAMS,
        cost_estimate=pl.CostEstimate(flops=ladder_flops, bytes_accessed=12 * count, transcendentals=0),
    )(place, occ_energy, current, back, jnp.broadcast_to(vir_energy[:, None], (virtual, 128)),
      vir_energy[None, :], whole)
    last = []
    for c in chunks:
        last = call(
            functools.partial(rest_kernel, tiles, groups, first, c),
            [distant] * devices if c else [upper], [blocks] if c else [],
            LONG, 8 * count, place, occ_energy, sums, rest[c], *other[c], *last,
            specs=[SMEM] * 2 + [VMEM] * (groups + 1 + c), params=SMALL,
        )
    done = pl.pallas_call(
        functools.partial(add_kernel, tiles),
        grid=(first,),
        out_shape=jax.ShapeDtypeStruct(current.shape, WIDE),
        in_specs=[SMEM, by_pair(virtual, virtual)] + [by_pair(edge, 2 * edge)] * devices,
        out_specs=by_pair(virtual, virtual),
        scratch_shapes=[pltpu.VMEM((devices, 1, edge, 2 * edge), NARROW)],
        compiler_params=PARAMS,
        input_output_aliases={1: 0},
        cost_estimate=pl.CostEstimate(flops=count, bytes_accessed=10 * count, transcendentals=0),
    )(place, base, *by_distance(last))
    return done.reshape(amplitudes.shape)


def solution(mesh):
    sizes = (mesh.shape["occi"], mesh.shape["occj"])
    return jax.shard_map(
        functools.partial(local, *sizes),
        mesh=mesh,
        in_specs=(P("occi", "occj", None, None), P(None, "occj", None), P(), P(), P()),
        out_specs=P("occi", "occj", None, None),
        check_vma=False,
    )
```

```python
import functools
import math

import jax
import jax.numpy as jnp
from jax import lax
from jax.experimental import pallas as pl
from jax.experimental.pallas import tpu as pltpu
from jax.sharding import PartitionSpec as P

VMEM = pl.BlockSpec(memory_space=pltpu.VMEM)
SMEM = pl.BlockSpec(memory_space=pltpu.SMEM)
PARAMS = pltpu.CompilerParams(vmem_limit_bytes=50 * 2**20)
ALONE = pltpu.CompilerParams(vmem_limit_bytes=62 * 2**20)
WIDE = jnp.float32
LONG = 3 * 10**10
NARROW = jnp.bfloat16


class Tiles:
    def __init__(self, devices, virtual):
        n = math.isqrt(2 * devices)
        assert n * n == 2 * devices and n % 2 == 0 and virtual % n == 0
        self.n = n
        self.edge = virtual // n
        self.rows = self.edge // 2
        self.above = [(a, b) for a in range(n) for b in range(a + 1, n)]
        self.diagonal = [(len(self.above) + k // 2, k % 2, k) for k in range(n)]

    def span(self, k):
        return slice(k * self.edge, (k + 1) * self.edge)

    def mirror_within(self, x):
        e, g = self.edge, self.rows
        tile = jnp.concatenate([x[:, :e], x[:, e:]], axis=0).T
        return jnp.concatenate([tile[:g], tile[g:]], axis=1)

    def mirror_across(self, x):
        return jnp.concatenate([x[:, self.edge:], x[:, :self.edge]], axis=1)


def call(body, outs, scratch, flops, moved, *operands, specs):
    return pl.pallas_call(
        body,
        out_shape=outs,
        in_specs=specs,
        out_specs=jax.tree.map(lambda _: VMEM, outs),
        scratch_shapes=scratch,
        compiler_params=PARAMS,
        cost_estimate=pl.CostEstimate(flops=flops, bytes_accessed=moved, transcendentals=0),
    )(*operands)


def pack_pair(tiles, source, out, pair, mirrored=False):
    e, g = tiles.edge, tiles.rows
    straight, turned = (slice(e, None), slice(0, e)) if mirrored else (slice(0, e), slice(e, None))
    for d, (a, b) in enumerate(tiles.above):
        out[d, pair, :, straight] = source[tiles.span(a), tiles.span(b)].astype(NARROW)
        out[d, pair, :, turned] = source[tiles.span(b), tiles.span(a)].astype(WIDE).T.astype(NARROW)
    for d, c, k in tiles.diagonal:
        tile = source[tiles.span(k), tiles.span(k)]
        tile = tile.astype(WIDE).T.astype(NARROW) if mirrored else tile.astype(NARROW)
        out[d, pair, c * g:(c + 1) * g, :e] = tile[:g]
        out[d, pair, c * g:(c + 1) * g, e:] = tile[g:]


def unpack_pair(tiles, blocks, pair, put):
    e, g = tiles.edge, tiles.rows
    for d, (a, b) in enumerate(tiles.above):
        put(a, b, blocks[d, pair, :, :e].astype(WIDE))
        put(b, a, blocks[d, pair, :, e:].astype(WIDE).T)
    for d, c, k in tiles.diagonal:
        upper = blocks[d, pair, c * g:(c + 1) * g, :e]
        lower = blocks[d, pair, c * g:(c + 1) * g, e:]
        put(k, k, jnp.concatenate([upper, lower], axis=0).astype(WIDE))


def to_distances(place, whole, outs):
    for k, out in enumerate(outs):
        out[...] = whole[place[1] ^ k]


def from_distances(place, pieces, whole):
    for k, piece in enumerate(pieces):
        whole[place[1] ^ k] = piece[...]


def pack_kernel(tiles, place, source, *refs):
    outs, whole = refs[:-1], refs[-1]
    for pair in range(source.shape[0]):
        pack_pair(tiles, source.at[pair], whole, pair, mirrored=True)
    to_distances(place, whole, outs)


def sort_kernel(tiles, groups, place, *refs):
    pieces, outs, whole = refs[:-2 * groups - 1], refs[-2 * groups - 1:-1], refs[-1]
    first = whole.shape[1]
    from_distances(place, pieces, whole)
    for s in range(groups):
        for u in range(first):
            block = whole[(place[0] ^ s) * first + u]
            for c in range(2):
                outs[c * groups + s][u] = block[:, c * tiles.rows:(c + 1) * tiles.rows]


def assemble(place, order, pieces, whole):
    k = 0
    for piece in pieces:
        count, rows, virtual = piece.shape[-3:]
        for block in range(piece.shape[0] if len(piece.shape) == 4 else 1):
            start = pl.multiple_of((place[1] ^ order[k]) * rows, rows)
            for single in range(count):
                values = piece[block, single] if len(piece.shape) == 4 else piece[single]
                whole[pl.ds(start, rows), single * virtual:(single + 1) * virtual] = values
            k += 1


def ladder_pair(matrix, whole, inner, total):
    virtual = matrix.shape[0]
    for single in range(whole.shape[1] // virtual):
        at = slice(single * virtual, (single + 1) * virtual)
        inner[at, :] = lax.dot_general(
            matrix, whole[:, at], (((1,), (1,)), ((), ())), preferred_element_type=WIDE
        ).astype(NARROW)
    total[...] = jnp.dot(whole[...], inner[...], preferred_element_type=WIDE)


def inverse(x):
    guess = pl.reciprocal(x, approx=True)
    return guess * (2.0 - x * guess)


def first_ladder_kernel(tiles, order, place, source, *refs):
    pieces, (out, whole, inner, total) = refs[:-4], refs[-4:]
    assemble(place, order, pieces, whole)
    for pair in range(source.shape[0]):
        ladder_pair(source[pair].astype(NARROW), whole, inner, total)
        pack_pair(tiles, total, out, pair)


def second_ladder_kernel(tiles, first, place, occ, source, blocks, row, column, vectors, out,
                         whole, inner, total, matrix, arrived):
    fetch = pltpu.make_async_copy(vectors, whole, arrived)

    @pl.when(pl.program_id(0) == 0)
    def _():
        fetch.start()

    def put(a, b, tile):
        matrix[tiles.span(a), tiles.span(b)] = tile.astype(NARROW)

    unpack_pair(tiles, blocks, 0, put)

    @pl.when(pl.program_id(0) == 0)
    def _():
        fetch.wait()

    ladder_pair(matrix[...], whole, inner, total)
    base = occ[place[0] * first + pl.program_id(0)] + occ[place[1]]
    strip = math.gcd(64, total.shape[0])

    def finish(step, carry):
        at = pl.ds(pl.multiple_of(step * strip, strip), strip)
        own = base - row[at, :1] - column[...]
        out[0, at, :] = source[0, at, :] + 2.0 * (matrix[at, :].astype(WIDE) + total[at, :] * inverse(own))
        return carry

    lax.fori_loop(0, total.shape[0] // strip, finish, 0)


def add_kernel(tiles, place, source, *refs):
    pieces, (out, whole) = refs[:-2], refs[-2:]
    from_distances(place, pieces, whole)

    def put(a, b, tile):
        here = (0, tiles.span(a), tiles.span(b))
        out[here] = source[here] + tile

    unpack_pair(tiles, whole, 0, put)


def mix(place, fock, first, load, store, rows):
    total = fock.shape[0]
    strips = rows // 16

    def strip(step, carry):
        u = step // strips
        at = pl.ds(pl.multiple_of(lax.rem(step, strips) * 16, 16), 16)
        taken = [load(k // first, u, k % first, at) for k in range(total)]
        for k in range(total):
            column = (place[0] ^ (k // first)) * first + k % first
            result = None
            for m in range(total):
                line = (place[0] ^ (m // first)) * first + m % first
                term = (-fock[line, column]) * taken[m]
                result = term if result is None else result + term
            store(k // first, u, k % first, column, at, result)
        return carry

    lax.fori_loop(0, first * strips, strip, 0)


def half_kernel(tiles, groups, first, chunk, place, fock, ladder, *refs):
    held, out = refs[:groups], refs[groups:]

    def load(s, u, r, at):
        return held[s][u, r, at, :].astype(WIDE)

    def store(s, u, w, column, at, result):
        rows = pl.ds(pl.multiple_of(chunk * tiles.rows + at.start, 16), at.size)
        out[s][u, w, at, :] = (ladder[column, u, rows, :].astype(WIDE) + result).astype(NARROW)

    mix(place, fock, first, load, store, tiles.rows)


def with_mirror(tiles, place, x, finish):
    across = place[1] < len(tiles.above)

    @pl.when(across)
    def _():
        finish(tiles.mirror_across(x))

    @pl.when(jnp.logical_not(across))
    def _():
        finish(tiles.mirror_within(x))


def update_kernel(tiles, groups, first, chunk, place, fock, occ, sums, *refs):
    before, refs = refs[:chunk], refs[chunk:]
    own, other, refs = refs[:groups], refs[groups:2 * groups], refs[2 * groups:]
    (sent, rest), out, (update, local_mixed) = refs[:2], refs[2:groups + 1], refs[groups + 1:]
    here = slice(chunk * tiles.rows, (chunk + 1) * tiles.rows)
    for ref in before:
        sent[:, :, :tiles.rows, :] = ref[...]

    def one(step, carry):
        u, w = step // first, lax.rem(step, first)
        for s in range(groups):
            column = (place[0] ^ s) * first + w
            base = occ[place[0] * first + u] + occ[column]

            def finish(mirrored):
                value = (own[s][u, w].astype(WIDE) + mirrored) * inverse(base - sums[here])
                update[u, s * first + w] = value
                sent[column, u, here] = value.astype(NARROW)

            with_mirror(tiles, place, other[s][w, u].astype(WIDE), finish)
        return carry

    lax.fori_loop(0, first * first, one, 0)

    def load(s, u, r, at):
        return update[u, s * first + r, at, :]

    def lost(value):
        return 2.0 * (value - value.astype(NARROW).astype(WIDE))

    def store(s, u, w, column, at, result):
        if s == 0:
            local_mixed[u, w, at, :] = result
            return
        out[s - 1][u, w, at, :] = result.astype(NARROW)
        strip = pl.ds(pl.multiple_of(chunk * tiles.rows + at.start, 16), at.size)
        base = occ[place[0] * first + u] + occ[column]
        share = result * inverse(base - sums[strip, :])
        rest[u, s * first + w, at, :] = (lost(update[u, s * first + w, at, :]) + share).astype(NARROW)

    mix(place, fock, first, load, store, tiles.rows)

    def within(step, carry):
        u, w = step // first, lax.rem(step, first)
        base = occ[place[0] * first + u] + occ[place[0] * first + w]

        def finish(mirrored):
            share = (local_mixed[u, w] + mirrored) * inverse(base - sums[here])
            rest[u, w] = (lost(update[u, w]) + share).astype(NARROW)

        with_mirror(tiles, place, local_mixed[w, u], finish)
        return carry

    lax.fori_loop(0, first * first, within, 0)


def rest_kernel(tiles, groups, first, chunk, place, occ, sums, rest, *refs):
    other, refs = refs[:groups - 1], refs[groups - 1:]
    out = refs[-1]
    here = slice(chunk * tiles.rows, (chunk + 1) * tiles.rows)
    there = here if chunk else slice(None)
    if chunk:
        out[:, :, :tiles.rows, :] = refs[0][...]

    def one(step, carry):
        u, w = step // first, lax.rem(step, first)
        out[place[0] * first + w, u, there] = rest[u, w]
        for s in range(1, groups):
            column = (place[0] ^ s) * first + w
            base = occ[place[0] * first + u] + occ[column]

            def finish(mirrored):
                value = rest[u, s * first + w].astype(WIDE) + mirrored * inverse(base - sums[here])
                out[column, u, there] = value.astype(NARROW)

            with_mirror(tiles, place, other[s - 1][w, u].astype(WIDE), finish)
        return carry

    lax.fori_loop(0, first * first, one, 0)
    if chunk:
        to_distances(place, out, refs[1:-1])


def exchange(blocks):
    return lax.all_to_all(blocks, "occj", split_axis=0, concat_axis=0, tiled=True)


def by_distance(parts):
    devices = len(parts)
    return [parts[0]] + [
        lax.ppermute(parts[k], "occj", [(d, d ^ k) for d in range(devices)])
        for k in range(devices - 1, 0, -1)
    ][::-1]


def across_first(parts, groups):
    return [parts[0]] + [
        lax.ppermute(parts[s], "occi", [(k, k ^ s) for k in range(groups)])
        for s in range(groups - 1, 0, -1)
    ][::-1]


def tie(x, *others):
    return lax.optimization_barrier((x, *others))[0]


def copy_kernel(source, out):
    for k in range(source.shape[0]):
        out[k] = source[k]


def after(x, *others):
    return pl.pallas_call(
        copy_kernel,
        out_shape=jax.ShapeDtypeStruct(x.shape, x.dtype),
        in_specs=[SMEM],
        out_specs=SMEM,
        cost_estimate=pl.CostEstimate(flops=LONG, bytes_accessed=8, transcendentals=0),
    )(tie(x, *others))


def gather_vectors(vectors, devices, packed):
    def turn(x, k):
        return lax.ppermute(x, "occj", [(d, d ^ k) for d in range(devices)])

    even = list(range(0, devices, 2))
    held = [vectors] + [turn(vectors, k) for k in even[1:]]
    other = turn(tie(jnp.stack(held), packed), 1)
    return [*held, other], even + [k ^ 1 for k in even]


def virtual_sums(tiles, vir_energy, q):
    e, g = tiles.edge, tiles.rows
    n_above = len(tiles.above)
    first = jnp.array([a for a, _ in tiles.above] + list(range(0, tiles.n, 2)), jnp.int32)[q]
    second = jnp.array([b for _, b in tiles.above] + list(range(1, tiles.n, 2)), jnp.int32)[q]
    a = lax.dynamic_slice_in_dim(vir_energy, first * e, e)
    b = lax.dynamic_slice_in_dim(vir_energy, second * e, e)
    pair = a[:, None] + b[None, :]
    across = jnp.concatenate([pair, pair], axis=1)
    halves = [
        jnp.concatenate([t[:g, None] + t[None, :], t[g:, None] + t[None, :]], axis=1) for t in (a, b)
    ]
    return jnp.where(q < n_above, across, jnp.concatenate(halves, axis=0))


def local(groups, devices, amplitudes, vectors, occupied_fock_block, occ_energy, vir_energy):
    first, second, virtual = amplitudes.shape[:3]
    assert second == 1 and groups * first == devices
    assert groups & (groups - 1) == 0 and devices & (devices - 1) == 0
    tiles = Tiles(devices, virtual)
    edge = tiles.edge
    current = amplitudes.reshape(first, virtual, virtual)
    count = current.size
    fock = occupied_fock_block.astype(WIDE)
    p, q = lax.axis_index("occi"), lax.axis_index("occj")
    place = jnp.stack([p, q]).astype(jnp.int32)
    packed = jax.ShapeDtypeStruct((devices, first, edge, 2 * edge), NARROW)
    upper = jax.ShapeDtypeStruct((devices, first, tiles.rows, 2 * edge), NARROW)
    part = jax.ShapeDtypeStruct((first, first, tiles.rows, 2 * edge), NARROW)
    singles = vectors.shape[0]
    inner = pltpu.VMEM((singles * virtual, virtual), NARROW)
    square = pltpu.VMEM((virtual, virtual), WIDE)
    chunks = range(2)

    distant = jax.ShapeDtypeStruct((first, edge, 2 * edge), NARROW)
    blocks = pltpu.VMEM(packed.shape, NARROW)
    started = call(functools.partial(pack_kernel, tiles), [distant] * devices, [blocks], count, 6 * count,
                   place, current, specs=[SMEM, VMEM])
    pieces, order = gather_vectors(vectors, devices, started[0])
    held = by_distance(started)
    sums = virtual_sums(tiles, vir_energy, q)

    ladder_flops = first * singles * 4 * virtual**3
    ladder, whole = call(
        functools.partial(first_ladder_kernel, tiles, order),
        [packed, jax.ShapeDtypeStruct((virtual, singles * virtual), NARROW)], [inner, square],
        ladder_flops, 8 * count, place, current, *pieces, specs=[SMEM] + [VMEM] * (1 + len(pieces)),
    )
    parts = call(
        functools.partial(sort_kernel, tiles, groups), [part] * (2 * groups), [blocks], count, 4 * count,
        tie(place, ladder), *held, specs=[SMEM] + [VMEM] * devices,
    )
    mirror = [across_first(parts[c * groups:(c + 1) * groups], groups) for c in chunks]
    ladder = exchange(ladder)

    half, other = [], []
    for c in chunks:
        half.append(call(
            functools.partial(half_kernel, tiles, groups, first, c), [part] * groups, [],
            LONG, 6 * count, after(place, *mirror[c]) if c == 0 else place, fock, ladder, *mirror[c],
            specs=[SMEM] * 2 + [VMEM] * (groups + 1),
        ))
        other.append(across_first(half[c], groups))
    sent, rest, mixed = [], [], []
    for c in chunks:
        sent_one, rest_one, *mixed_one = call(
            functools.partial(update_kernel, tiles, groups, first, c),
            [(upper, packed)[c], jax.ShapeDtypeStruct((first, devices, *part.shape[2:]), NARROW)] + [part] * (groups - 1),
            [pltpu.VMEM((first, devices, *part.shape[2:]), WIDE), pltpu.VMEM(part.shape, WIDE)],
            LONG, 10 * count, place, fock, occ_energy, sums, *sent, *half[c], *other[c],
            specs=[SMEM] * 3 + [VMEM] * (2 * groups + 1 + c),
        )
        sent, rest, mixed = [sent_one], rest + [rest_one], mixed + [mixed_one]
    other = [across_first([None] + x, groups)[1:] for x in mixed]
    back = exchange(sent[0])
    def by_pair(*shape):
        return pl.BlockSpec((1, *shape), lambda pair: (pair, 0, 0))

    def all_pairs(*shape):
        return pl.BlockSpec(shape, lambda pair: (0, 0))

    base = pl.pallas_call(
        functools.partial(second_ladder_kernel, tiles, first),
        grid=(first,),
        out_shape=jax.ShapeDtypeStruct(current.shape, WIDE),
        in_specs=[
            SMEM, SMEM, by_pair(virtual, virtual),
            pl.BlockSpec((devices, 1, edge, 2 * edge), lambda pair: (0, pair, 0, 0)),
            all_pairs(virtual, 128), all_pairs(1, virtual), pl.BlockSpec(memory_space=pl.ANY),
        ],
        out_specs=by_pair(virtual, virtual),
        scratch_shapes=[
            pltpu.VMEM(whole.shape, NARROW), inner, square, pltpu.VMEM((virtual, virtual), NARROW),
            pltpu.SemaphoreType.DMA,
        ],
        compiler_params=ALONE,
        cost_estimate=pl.CostEstimate(flops=ladder_flops, bytes_accessed=12 * count, transcendentals=0),
    )(place, occ_energy, current, back, jnp.broadcast_to(vir_energy[:, None], (virtual, 128)),
      vir_energy[None, :], whole)
    last = []
    for c in chunks:
        last = call(
            functools.partial(rest_kernel, tiles, groups, first, c),
            [distant] * devices if c else [upper], [blocks] if c else [],
            LONG, 8 * count, place, occ_energy, sums, rest[c], *other[c], *last,
            specs=[SMEM] * 2 + [VMEM] * (groups + 1 + c),
        )
    done = pl.pallas_call(
        functools.partial(add_kernel, tiles),
        grid=(first,),
        out_shape=jax.ShapeDtypeStruct(current.shape, WIDE),
        in_specs=[SMEM, by_pair(virtual, virtual)] + [by_pair(edge, 2 * edge)] * devices,
        out_specs=by_pair(virtual, virtual),
        scratch_shapes=[pltpu.VMEM((devices, 1, edge, 2 * edge), NARROW)],
        compiler_params=PARAMS,
        input_output_aliases={1: 0},
        cost_estimate=pl.CostEstimate(flops=count, bytes_accessed=10 * count, transcendentals=0),
    )(place, base, *by_distance(last))
    return done.reshape(amplitudes.shape)


def solution(mesh):
    sizes = (mesh.shape["occi"], mesh.shape["occj"])
    return jax.shard_map(
        functools.partial(local, *sizes),
        mesh=mesh,
        in_specs=(P("occi", "occj", None, None), P(None, "occj", None), P(), P(), P()),
        out_specs=P("occi", "occj", None, None),
        check_vma=False,
    )
```

```python
import functools
import math

import jax
import jax.numpy as jnp
from jax import lax
from jax.experimental import pallas as pl
from jax.experimental.pallas import tpu as pltpu
from jax.sharding import PartitionSpec as P

VMEM = pl.BlockSpec(memory_space=pltpu.VMEM)
SMEM = pl.BlockSpec(memory_space=pltpu.SMEM)
PARAMS = pltpu.CompilerParams(vmem_limit_bytes=50 * 2**20)
WIDE = jnp.float32
LONG = 3 * 10**10
NARROW = jnp.bfloat16


class Tiles:
    def __init__(self, devices, virtual):
        n = math.isqrt(2 * devices)
        assert n * n == 2 * devices and n % 2 == 0 and virtual % n == 0
        self.n = n
        self.edge = virtual // n
        self.rows = self.edge // 2
        self.above = [(a, b) for a in range(n) for b in range(a + 1, n)]
        self.diagonal = [(len(self.above) + k // 2, k % 2, k) for k in range(n)]

    def span(self, k):
        return slice(k * self.edge, (k + 1) * self.edge)

    def mirror_within(self, x):
        e, g = self.edge, self.rows
        tile = jnp.concatenate([x[:, :e], x[:, e:]], axis=0).T
        return jnp.concatenate([tile[:g], tile[g:]], axis=1)

    def mirror_across(self, x):
        return jnp.concatenate([x[:, self.edge:], x[:, :self.edge]], axis=1)


def call(body, outs, scratch, flops, moved, *operands, specs):
    return pl.pallas_call(
        body,
        out_shape=outs,
        in_specs=specs,
        out_specs=jax.tree.map(lambda _: VMEM, outs),
        scratch_shapes=scratch,
        compiler_params=PARAMS,
        cost_estimate=pl.CostEstimate(flops=flops, bytes_accessed=moved, transcendentals=0),
    )(*operands)


def pack_pair(tiles, source, out, pair, mirrored=False):
    e, g = tiles.edge, tiles.rows
    straight, turned = (slice(e, None), slice(0, e)) if mirrored else (slice(0, e), slice(e, None))
    for d, (a, b) in enumerate(tiles.above):
        out[d, pair, :, straight] = source[tiles.span(a), tiles.span(b)].astype(NARROW)
        out[d, pair, :, turned] = source[tiles.span(b), tiles.span(a)].astype(WIDE).T.astype(NARROW)
    for d, c, k in tiles.diagonal:
        tile = source[tiles.span(k), tiles.span(k)]
        tile = tile.astype(WIDE).T.astype(NARROW) if mirrored else tile.astype(NARROW)
        out[d, pair, c * g:(c + 1) * g, :e] = tile[:g]
        out[d, pair, c * g:(c + 1) * g, e:] = tile[g:]


def unpack_pair(tiles, blocks, pair, put):
    e, g = tiles.edge, tiles.rows
    for d, (a, b) in enumerate(tiles.above):
        put(a, b, blocks[d, pair, :, :e].astype(WIDE))
        put(b, a, blocks[d, pair, :, e:].astype(WIDE).T)
    for d, c, k in tiles.diagonal:
        upper = blocks[d, pair, c * g:(c + 1) * g, :e]
        lower = blocks[d, pair, c * g:(c + 1) * g, e:]
        put(k, k, jnp.concatenate([upper, lower], axis=0).astype(WIDE))


def to_distances(place, whole, outs):
    for k, out in enumerate(outs):
        out[...] = whole[place[1] ^ k]


def from_distances(place, pieces, whole):
    for k, piece in enumerate(pieces):
        whole[place[1] ^ k] = piece[...]


def pack_kernel(tiles, place, source, *refs):
    outs, whole = refs[:-1], refs[-1]
    for pair in range(source.shape[0]):
        pack_pair(tiles, source.at[pair], whole, pair, mirrored=True)
    to_distances(place, whole, outs)


def sort_kernel(tiles, groups, place, *refs):
    pieces, outs, whole = refs[:-2 * groups - 1], refs[-2 * groups - 1:-1], refs[-1]
    first = whole.shape[1]
    from_distances(place, pieces, whole)
    for s in range(groups):
        for u in range(first):
            block = whole[(place[0] ^ s) * first + u]
            for c in range(2):
                outs[c * groups + s][u] = block[:, c * tiles.rows:(c + 1) * tiles.rows]


def assemble(place, order, pieces, whole):
    k = 0
    for piece in pieces:
        count, rows, virtual = piece.shape[-3:]
        for block in range(piece.shape[0] if len(piece.shape) == 4 else 1):
            start = pl.multiple_of((place[1] ^ order[k]) * rows, rows)
            for single in range(count):
                values = piece[block, single] if len(piece.shape) == 4 else piece[single]
                whole[pl.ds(start, rows), single * virtual:(single + 1) * virtual] = values
            k += 1


def ladder_pair(matrix, whole, inner, total):
    virtual = matrix.shape[0]
    for single in range(whole.shape[1] // virtual):
        at = slice(single * virtual, (single + 1) * virtual)
        inner[at, :] = lax.dot_general(
            matrix, whole[:, at], (((1,), (1,)), ((), ())), preferred_element_type=WIDE
        ).astype(NARROW)
    total[...] = jnp.dot(whole[...], inner[...], preferred_element_type=WIDE)


def inverse(x):
    guess = pl.reciprocal(x, approx=True)
    return guess * (2.0 - x * guess)


def first_ladder_kernel(tiles, order, place, source, *refs):
    pieces, (out, whole, inner, total) = refs[:-4], refs[-4:]
    assemble(place, order, pieces, whole)
    for pair in range(source.shape[0]):
        ladder_pair(source[pair].astype(NARROW), whole, inner, total)
        pack_pair(tiles, total, out, pair)


def second_ladder_kernel(tiles, first, place, occ, source, blocks, row, column, whole, out, inner, total, matrix):
    def put(a, b, tile):
        matrix[tiles.span(a), tiles.span(b)] = tile.astype(NARROW)

    unpack_pair(tiles, blocks, 0, put)
    ladder_pair(matrix[...], whole, inner, total)
    base = occ[place[0] * first + pl.program_id(0)] + occ[place[1]]
    strip = math.gcd(64, total.shape[0])

    def finish(step, carry):
        at = pl.ds(pl.multiple_of(step * strip, strip), strip)
        own = base - row[at, :1] - column[...]
        out[0, at, :] = source[0, at, :] + 2.0 * (matrix[at, :].astype(WIDE) + total[at, :] * inverse(own))
        return carry

    lax.fori_loop(0, total.shape[0] // strip, finish, 0)


def add_kernel(tiles, place, source, *refs):
    pieces, (out, whole) = refs[:-2], refs[-2:]
    from_distances(place, pieces, whole)

    def put(a, b, tile):
        here = (0, tiles.span(a), tiles.span(b))
        out[here] = source[here] + tile

    unpack_pair(tiles, whole, 0, put)


def mix(place, fock, first, load, store, rows):
    total = fock.shape[0]
    strips = rows // 16

    def strip(step, carry):
        u = step // strips
        at = pl.ds(pl.multiple_of(lax.rem(step, strips) * 16, 16), 16)
        taken = [load(k // first, u, k % first, at) for k in range(total)]
        for k in range(total):
            column = (place[0] ^ (k // first)) * first + k % first
            result = None
            for m in range(total):
                line = (place[0] ^ (m // first)) * first + m % first
                term = (-fock[line, column]) * taken[m]
                result = term if result is None else result + term
            store(k // first, u, k % first, column, at, result)
        return carry

    lax.fori_loop(0, first * strips, strip, 0)


def half_kernel(tiles, groups, first, chunk, place, fock, ladder, *refs):
    held, out = refs[:groups], refs[groups:]

    def load(s, u, r, at):
        return held[s][u, r, at, :].astype(WIDE)

    def store(s, u, w, column, at, result):
        rows = pl.ds(pl.multiple_of(chunk * tiles.rows + at.start, 16), at.size)
        out[s][u, w, at, :] = (ladder[column, u, rows, :].astype(WIDE) + result).astype(NARROW)

    mix(place, fock, first, load, store, tiles.rows)


def with_mirror(tiles, place, x, finish):
    across = place[1] < len(tiles.above)

    @pl.when(across)
    def _():
        finish(tiles.mirror_across(x))

    @pl.when(jnp.logical_not(across))
    def _():
        finish(tiles.mirror_within(x))


def update_kernel(tiles, groups, first, chunk, place, fock, occ, sums, *refs):
    before, refs = refs[:chunk], refs[chunk:]
    own, other, refs = refs[:groups], refs[groups:2 * groups], refs[2 * groups:]
    (sent, rest), out, (update, local_mixed) = refs[:2], refs[2:groups + 1], refs[groups + 1:]
    here = slice(chunk * tiles.rows, (chunk + 1) * tiles.rows)
    for ref in before:
        sent[:, :, :tiles.rows, :] = ref[...]

    def one(step, carry):
        u, w = step // first, lax.rem(step, first)
        for s in range(groups):
            column = (place[0] ^ s) * first + w
            base = occ[place[0] * first + u] + occ[column]

            def finish(mirrored):
                value = (own[s][u, w].astype(WIDE) + mirrored) * inverse(base - sums[here])
                update[u, s * first + w] = value
                sent[column, u, here] = value.astype(NARROW)

            with_mirror(tiles, place, other[s][w, u].astype(WIDE), finish)
        return carry

    lax.fori_loop(0, first * first, one, 0)

    def load(s, u, r, at):
        return update[u, s * first + r, at, :]

    def lost(value):
        return 2.0 * (value - value.astype(NARROW).astype(WIDE))

    def store(s, u, w, column, at, result):
        if s == 0:
            local_mixed[u, w, at, :] = result
            return
        out[s - 1][u, w, at, :] = result.astype(NARROW)
        strip = pl.ds(pl.multiple_of(chunk * tiles.rows + at.start, 16), at.size)
        base = occ[place[0] * first + u] + occ[column]
        share = result * inverse(base - sums[strip, :])
        rest[u, s * first + w, at, :] = (lost(update[u, s * first + w, at, :]) + share).astype(NARROW)

    mix(place, fock, first, load, store, tiles.rows)

    def within(step, carry):
        u, w = step // first, lax.rem(step, first)
        base = occ[place[0] * first + u] + occ[place[0] * first + w]

        def finish(mirrored):
            share = (local_mixed[u, w] + mirrored) * inverse(base - sums[here])
            rest[u, w] = (lost(update[u, w]) + share).astype(NARROW)

        with_mirror(tiles, place, local_mixed[w, u], finish)
        return carry

    lax.fori_loop(0, first * first, within, 0)


def rest_kernel(tiles, groups, first, chunk, place, occ, sums, rest, *refs):
    other, refs = refs[:groups - 1], refs[groups - 1:]
    out = refs[-1]
    here = slice(chunk * tiles.rows, (chunk + 1) * tiles.rows)
    there = here if chunk else slice(None)
    if chunk:
        out[:, :, :tiles.rows, :] = refs[0][...]

    def one(step, carry):
        u, w = step // first, lax.rem(step, first)
        out[place[0] * first + w, u, there] = rest[u, w]
        for s in range(1, groups):
            column = (place[0] ^ s) * first + w
            base = occ[place[0] * first + u] + occ[column]

            def finish(mirrored):
                value = rest[u, s * first + w].astype(WIDE) + mirrored * inverse(base - sums[here])
                out[column, u, there] = value.astype(NARROW)

            with_mirror(tiles, place, other[s - 1][w, u].astype(WIDE), finish)
        return carry

    lax.fori_loop(0, first * first, one, 0)
    if chunk:
        to_distances(place, out, refs[1:-1])


def exchange(blocks):
    return lax.all_to_all(blocks, "occj", split_axis=0, concat_axis=0, tiled=True)


def by_distance(parts):
    devices = len(parts)
    return [parts[0]] + [
        lax.ppermute(parts[k], "occj", [(d, d ^ k) for d in range(devices)])
        for k in range(devices - 1, 0, -1)
    ][::-1]


def across_first(parts, groups):
    return [parts[0]] + [
        lax.ppermute(parts[s], "occi", [(k, k ^ s) for k in range(groups)])
        for s in range(groups - 1, 0, -1)
    ][::-1]


def tie(x, *others):
    return lax.optimization_barrier((x, *others))[0]


def copy_kernel(source, out):
    for k in range(source.shape[0]):
        out[k] = source[k]


def after(x, *others):
    return pl.pallas_call(
        copy_kernel,
        out_shape=jax.ShapeDtypeStruct(x.shape, x.dtype),
        in_specs=[SMEM],
        out_specs=SMEM,
        cost_estimate=pl.CostEstimate(flops=LONG, bytes_accessed=8, transcendentals=0),
    )(tie(x, *others))


def gather_vectors(vectors, devices, packed):
    def turn(x, k):
        return lax.ppermute(x, "occj", [(d, d ^ k) for d in range(devices)])

    even = list(range(0, devices, 2))
    held = [vectors] + [turn(vectors, k) for k in even[1:]]
    other = turn(tie(jnp.stack(held), packed), 1)
    return [*held, other], even + [k ^ 1 for k in even]


def virtual_sums(tiles, vir_energy, q):
    e, g = tiles.edge, tiles.rows
    n_above = len(tiles.above)
    first = jnp.array([a for a, _ in tiles.above] + list(range(0, tiles.n, 2)), jnp.int32)[q]
    second = jnp.array([b for _, b in tiles.above] + list(range(1, tiles.n, 2)), jnp.int32)[q]
    a = lax.dynamic_slice_in_dim(vir_energy, first * e, e)
    b = lax.dynamic_slice_in_dim(vir_energy, second * e, e)
    pair = a[:, None] + b[None, :]
    across = jnp.concatenate([pair, pair], axis=1)
    halves = [
        jnp.concatenate([t[:g, None] + t[None, :], t[g:, None] + t[None, :]], axis=1) for t in (a, b)
    ]
    return jnp.where(q < n_above, across, jnp.concatenate(halves, axis=0))


def local(groups, devices, amplitudes, vectors, occupied_fock_block, occ_energy, vir_energy):
    first, second, virtual = amplitudes.shape[:3]
    assert second == 1 and groups * first == devices
    assert groups & (groups - 1) == 0 and devices & (devices - 1) == 0
    tiles = Tiles(devices, virtual)
    edge = tiles.edge
    current = amplitudes.reshape(first, virtual, virtual)
    count = current.size
    fock = occupied_fock_block.astype(WIDE)
    p, q = lax.axis_index("occi"), lax.axis_index("occj")
    place = jnp.stack([p, q]).astype(jnp.int32)
    packed = jax.ShapeDtypeStruct((devices, first, edge, 2 * edge), NARROW)
    upper = jax.ShapeDtypeStruct((devices, first, tiles.rows, 2 * edge), NARROW)
    part = jax.ShapeDtypeStruct((first, first, tiles.rows, 2 * edge), NARROW)
    singles = vectors.shape[0]
    inner = pltpu.VMEM((singles * virtual, virtual), NARROW)
    square = pltpu.VMEM((virtual, virtual), WIDE)
    chunks = range(2)

    distant = jax.ShapeDtypeStruct((first, edge, 2 * edge), NARROW)
    blocks = pltpu.VMEM(packed.shape, NARROW)
    started = call(functools.partial(pack_kernel, tiles), [distant] * devices, [blocks], count, 6 * count,
                   place, current, specs=[SMEM, VMEM])
    pieces, order = gather_vectors(vectors, devices, started[0])
    held = by_distance(started)

    ladder_flops = first * singles * 4 * virtual**3
    ladder, whole = call(
        functools.partial(first_ladder_kernel, tiles, order),
        [packed, jax.ShapeDtypeStruct((virtual, singles * virtual), NARROW)], [inner, square],
        ladder_flops, 8 * count, place, current, *pieces, specs=[SMEM] + [VMEM] * (1 + len(pieces)),
    )
    parts = call(
        functools.partial(sort_kernel, tiles, groups), [part] * (2 * groups), [blocks], count, 4 * count,
        tie(place, ladder), *held, specs=[SMEM] + [VMEM] * devices,
    )
    mirror = [across_first(parts[c * groups:(c + 1) * groups], groups) for c in chunks]
    sums = virtual_sums(tiles, vir_energy, tie(q, mirror[0][-1]))
    ladder = exchange(ladder)

    half, other = [], []
    for c in chunks:
        half.append(call(
            functools.partial(half_kernel, tiles, groups, first, c), [part] * groups, [],
            LONG, 6 * count, after(place, *mirror[c]) if c == 0 else place, fock, ladder, *mirror[c],
            specs=[SMEM] * 2 + [VMEM] * (groups + 1),
        ))
        other.append(across_first(half[c], groups))
    sent, rest, mixed = [], [], []
    for c in chunks:
        sent_one, rest_one, *mixed_one = call(
            functools.partial(update_kernel, tiles, groups, first, c),
            [(upper, packed)[c], jax.ShapeDtypeStruct((first, devices, *part.shape[2:]), NARROW)] + [part] * (groups - 1),
            [pltpu.VMEM((first, devices, *part.shape[2:]), WIDE), pltpu.VMEM(part.shape, WIDE)],
            LONG, 10 * count, place, fock, occ_energy, sums, *sent, *half[c], *other[c],
            specs=[SMEM] * 3 + [VMEM] * (2 * groups + 1 + c),
        )
        sent, rest, mixed = [sent_one], rest + [rest_one], mixed + [mixed_one]
    other = [across_first([None] + x, groups)[1:] for x in mixed]
    back = exchange(sent[0])
    def by_pair(*shape):
        return pl.BlockSpec((1, *shape), lambda pair: (pair, 0, 0))

    def all_pairs(*shape):
        return pl.BlockSpec(shape, lambda pair: (0, 0))

    base = pl.pallas_call(
        functools.partial(second_ladder_kernel, tiles, first),
        grid=(first,),
        out_shape=jax.ShapeDtypeStruct(current.shape, WIDE),
        in_specs=[
            SMEM, SMEM, by_pair(virtual, virtual),
            pl.BlockSpec((devices, 1, edge, 2 * edge), lambda pair: (0, pair, 0, 0)),
            all_pairs(virtual, 128), all_pairs(1, virtual), all_pairs(*whole.shape),
        ],
        out_specs=by_pair(virtual, virtual),
        scratch_shapes=[inner, square, pltpu.VMEM((virtual, virtual), NARROW)],
        compiler_params=PARAMS,
        cost_estimate=pl.CostEstimate(flops=ladder_flops, bytes_accessed=12 * count, transcendentals=0),
    )(place, occ_energy, current, back, jnp.broadcast_to(vir_energy[:, None], (virtual, 128)),
      vir_energy[None, :], whole)
    last = []
    for c in chunks:
        last = call(
            functools.partial(rest_kernel, tiles, groups, first, c),
            [distant] * devices if c else [upper], [blocks] if c else [],
            LONG, 8 * count, place, occ_energy, sums, rest[c], *other[c], *last,
            specs=[SMEM] * 2 + [VMEM] * (groups + 1 + c),
        )
    done = pl.pallas_call(
        functools.partial(add_kernel, tiles),
        grid=(first,),
        out_shape=jax.ShapeDtypeStruct(current.shape, WIDE),
        in_specs=[SMEM, by_pair(virtual, virtual)] + [by_pair(edge, 2 * edge)] * devices,
        out_specs=by_pair(virtual, virtual),
        scratch_shapes=[pltpu.VMEM((devices, 1, edge, 2 * edge), NARROW)],
        compiler_params=PARAMS,
        input_output_aliases={1: 0},
        cost_estimate=pl.CostEstimate(flops=count, bytes_accessed=10 * count, transcendentals=0),
    )(place, base, *by_distance(last))
    return done.reshape(amplitudes.shape)


def solution(mesh):
    sizes = (mesh.shape["occi"], mesh.shape["occj"])
    return jax.shard_map(
        functools.partial(local, *sizes),
        mesh=mesh,
        in_specs=(P("occi", "occj", None, None), P(None, "occj", None), P(), P(), P()),
        out_specs=P("occi", "occj", None, None),
        check_vma=False,
    )
```

```python
import functools
import math

import jax
import jax.numpy as jnp
from jax import lax
from jax.experimental import pallas as pl
from jax.experimental.pallas import tpu as pltpu
from jax.sharding import PartitionSpec as P

VMEM = pl.BlockSpec(memory_space=pltpu.VMEM)
SMEM = pl.BlockSpec(memory_space=pltpu.SMEM)
PARAMS = pltpu.CompilerParams(vmem_limit_bytes=50 * 2**20)
WIDE = jnp.float32
LONG = 3 * 10**10
NARROW = jnp.bfloat16


class Tiles:
    def __init__(self, devices, virtual):
        n = math.isqrt(2 * devices)
        assert n * n == 2 * devices and n % 2 == 0 and virtual % n == 0
        self.n = n
        self.edge = virtual // n
        self.rows = self.edge // 2
        self.above = [(a, b) for a in range(n) for b in range(a + 1, n)]
        self.diagonal = [(len(self.above) + k // 2, k % 2, k) for k in range(n)]

    def span(self, k):
        return slice(k * self.edge, (k + 1) * self.edge)

    def mirror_within(self, x):
        e, g = self.edge, self.rows
        tile = jnp.concatenate([x[:, :e], x[:, e:]], axis=0).T
        return jnp.concatenate([tile[:g], tile[g:]], axis=1)

    def mirror_across(self, x):
        return jnp.concatenate([x[:, self.edge:], x[:, :self.edge]], axis=1)


def call(body, outs, scratch, flops, moved, *operands, specs):
    return pl.pallas_call(
        body,
        out_shape=outs,
        in_specs=specs,
        out_specs=jax.tree.map(lambda _: VMEM, outs),
        scratch_shapes=scratch,
        compiler_params=PARAMS,
        cost_estimate=pl.CostEstimate(flops=flops, bytes_accessed=moved, transcendentals=0),
    )(*operands)


def pack_pair(tiles, source, out, pair, mirrored=False):
    e, g = tiles.edge, tiles.rows
    straight, turned = (slice(e, None), slice(0, e)) if mirrored else (slice(0, e), slice(e, None))
    for d, (a, b) in enumerate(tiles.above):
        out[d, pair, :, straight] = source[tiles.span(a), tiles.span(b)].astype(NARROW)
        out[d, pair, :, turned] = source[tiles.span(b), tiles.span(a)].astype(WIDE).T.astype(NARROW)
    for d, c, k in tiles.diagonal:
        tile = source[tiles.span(k), tiles.span(k)]
        tile = tile.astype(WIDE).T.astype(NARROW) if mirrored else tile.astype(NARROW)
        out[d, pair, c * g:(c + 1) * g, :e] = tile[:g]
        out[d, pair, c * g:(c + 1) * g, e:] = tile[g:]


def unpack_pair(tiles, blocks, pair, put):
    e, g = tiles.edge, tiles.rows
    for d, (a, b) in enumerate(tiles.above):
        put(a, b, blocks[d, pair, :, :e].astype(WIDE))
        put(b, a, blocks[d, pair, :, e:].astype(WIDE).T)
    for d, c, k in tiles.diagonal:
        upper = blocks[d, pair, c * g:(c + 1) * g, :e]
        lower = blocks[d, pair, c * g:(c + 1) * g, e:]
        put(k, k, jnp.concatenate([upper, lower], axis=0).astype(WIDE))


def to_distances(place, whole, outs):
    for k, out in enumerate(outs):
        out[...] = whole[place[1] ^ k]


def from_distances(place, pieces, whole):
    for k, piece in enumerate(pieces):
        whole[place[1] ^ k] = piece[...]


def pack_kernel(tiles, place, source, *refs):
    outs, whole = refs[:-1], refs[-1]
    for pair in range(source.shape[0]):
        pack_pair(tiles, source.at[pair], whole, pair, mirrored=True)
    to_distances(place, whole, outs)


def sort_kernel(tiles, groups, place, *refs):
    pieces, outs, whole = refs[:-2 * groups - 1], refs[-2 * groups - 1:-1], refs[-1]
    first = whole.shape[1]
    from_distances(place, pieces, whole)
    for s in range(groups):
        for u in range(first):
            block = whole[(place[0] ^ s) * first + u]
            for c in range(2):
                outs[c * groups + s][u] = block[:, c * tiles.rows:(c + 1) * tiles.rows]


def assemble(place, order, pieces, whole):
    k = 0
    for piece in pieces:
        count, rows, virtual = piece.shape[-3:]
        for block in range(piece.shape[0] if len(piece.shape) == 4 else 1):
            start = pl.multiple_of((place[1] ^ order[k]) * rows, rows)
            for single in range(count):
                values = piece[block, single] if len(piece.shape) == 4 else piece[single]
                whole[pl.ds(start, rows), single * virtual:(single + 1) * virtual] = values
            k += 1


def ladder_pair(matrix, whole, inner, total):
    virtual = matrix.shape[0]
    for single in range(whole.shape[1] // virtual):
        at = slice(single * virtual, (single + 1) * virtual)
        inner[at, :] = lax.dot_general(
            matrix, whole[:, at], (((1,), (1,)), ((), ())), preferred_element_type=WIDE
        ).astype(NARROW)
    total[...] = jnp.dot(whole[...], inner[...], preferred_element_type=WIDE)


def inverse(x):
    guess = pl.reciprocal(x, approx=True)
    return guess * (2.0 - x * guess)


def first_ladder_kernel(tiles, order, place, source, *refs):
    pieces, (out, whole, inner, total) = refs[:-4], refs[-4:]
    assemble(place, order, pieces, whole)
    for pair in range(source.shape[0]):
        ladder_pair(source[pair].astype(NARROW), whole, inner, total)
        pack_pair(tiles, total, out, pair)


def second_ladder_kernel(tiles, first, place, occ, source, blocks, row, column, whole, out, inner, total, matrix):
    def put(a, b, tile):
        matrix[tiles.span(a), tiles.span(b)] = tile.astype(NARROW)

    unpack_pair(tiles, blocks, 0, put)
    ladder_pair(matrix[...], whole, inner, total)
    base = occ[place[0] * first + pl.program_id(0)] + occ[place[1]]
    strip = math.gcd(64, total.shape[0])

    def finish(step, carry):
        at = pl.ds(pl.multiple_of(step * strip, strip), strip)
        own = base - row[at, :1] - column[...]
        out[0, at, :] = source[0, at, :] + 2.0 * (matrix[at, :].astype(WIDE) + total[at, :] * inverse(own))
        return carry

    lax.fori_loop(0, total.shape[0] // strip, finish, 0)


def add_kernel(tiles, place, source, *refs):
    pieces, (out, whole) = refs[:-2], refs[-2:]
    from_distances(place, pieces, whole)

    def put(a, b, tile):
        here = (0, tiles.span(a), tiles.span(b))
        out[here] = source[here] + tile

    unpack_pair(tiles, whole, 0, put)


def mix(place, fock, first, load, store, rows):
    total = fock.shape[0]
    strips = rows // 16

    def strip(step, carry):
        u = step // strips
        at = pl.ds(pl.multiple_of(lax.rem(step, strips) * 16, 16), 16)
        taken = [load(k // first, u, k % first, at) for k in range(total)]
        for k in range(total):
            column = (place[0] ^ (k // first)) * first + k % first
            result = None
            for m in range(total):
                line = (place[0] ^ (m // first)) * first + m % first
                term = (-fock[line, column]) * taken[m]
                result = term if result is None else result + term
            store(k // first, u, k % first, column, at, result)
        return carry

    lax.fori_loop(0, first * strips, strip, 0)


def half_kernel(tiles, groups, first, chunk, place, fock, ladder, *refs):
    held, out = refs[:groups], refs[groups:]

    def load(s, u, r, at):
        return held[s][u, r, at, :].astype(WIDE)

    def store(s, u, w, column, at, result):
        rows = pl.ds(pl.multiple_of(chunk * tiles.rows + at.start, 16), at.size)
        out[s][u, w, at, :] = (ladder[column, u, rows, :].astype(WIDE) + result).astype(NARROW)

    mix(place, fock, first, load, store, tiles.rows)


def with_mirror(tiles, place, x, finish):
    across = place[1] < len(tiles.above)

    @pl.when(across)
    def _():
        finish(tiles.mirror_across(x))

    @pl.when(jnp.logical_not(across))
    def _():
        finish(tiles.mirror_within(x))


def update_kernel(tiles, groups, first, chunk, place, fock, occ, sums, *refs):
    before, refs = refs[:chunk], refs[chunk:]
    own, other, refs = refs[:groups], refs[groups:2 * groups], refs[2 * groups:]
    (sent, rest), out, (update, local_mixed) = refs[:2], refs[2:groups + 1], refs[groups + 1:]
    here = slice(chunk * tiles.rows, (chunk + 1) * tiles.rows)
    for ref in before:
        sent[:, :, :tiles.rows, :] = ref[...]

    def one(step, carry):
        u, w = step // first, lax.rem(step, first)
        for s in range(groups):
            column = (place[0] ^ s) * first + w
            base = occ[place[0] * first + u] + occ[column]

            def finish(mirrored):
                value = (own[s][u, w].astype(WIDE) + mirrored) * inverse(base - sums[here])
                update[u, s * first + w] = value
                sent[column, u, here] = value.astype(NARROW)

            with_mirror(tiles, place, other[s][w, u].astype(WIDE), finish)
        return carry

    lax.fori_loop(0, first * first, one, 0)

    def load(s, u, r, at):
        return update[u, s * first + r, at, :]

    def lost(value):
        return 2.0 * (value - value.astype(NARROW).astype(WIDE))

    def store(s, u, w, column, at, result):
        if s == 0:
            local_mixed[u, w, at, :] = result
            return
        out[s - 1][u, w, at, :] = result.astype(NARROW)
        strip = pl.ds(pl.multiple_of(chunk * tiles.rows + at.start, 16), at.size)
        base = occ[place[0] * first + u] + occ[column]
        share = result * inverse(base - sums[strip, :])
        rest[u, s * first + w, at, :] = (lost(update[u, s * first + w, at, :]) + share).astype(NARROW)

    mix(place, fock, first, load, store, tiles.rows)

    def within(step, carry):
        u, w = step // first, lax.rem(step, first)
        base = occ[place[0] * first + u] + occ[place[0] * first + w]

        def finish(mirrored):
            share = (local_mixed[u, w] + mirrored) * inverse(base - sums[here])
            rest[u, w] = (lost(update[u, w]) + share).astype(NARROW)

        with_mirror(tiles, place, local_mixed[w, u], finish)
        return carry

    lax.fori_loop(0, first * first, within, 0)


def rest_kernel(tiles, groups, first, chunk, place, occ, sums, rest, *refs):
    other, refs = refs[:groups - 1], refs[groups - 1:]
    out = refs[-1]
    here = slice(chunk * tiles.rows, (chunk + 1) * tiles.rows)
    there = here if chunk else slice(None)
    if chunk:
        out[:, :, :tiles.rows, :] = refs[0][...]

    def one(step, carry):
        u, w = step // first, lax.rem(step, first)
        out[place[0] * first + w, u, there] = rest[u, w]
        for s in range(1, groups):
            column = (place[0] ^ s) * first + w
            base = occ[place[0] * first + u] + occ[column]

            def finish(mirrored):
                value = rest[u, s * first + w].astype(WIDE) + mirrored * inverse(base - sums[here])
                out[column, u, there] = value.astype(NARROW)

            with_mirror(tiles, place, other[s - 1][w, u].astype(WIDE), finish)
        return carry

    lax.fori_loop(0, first * first, one, 0)
    if chunk:
        to_distances(place, out, refs[1:-1])


def exchange(blocks):
    return lax.all_to_all(blocks, "occj", split_axis=0, concat_axis=0, tiled=True)


def by_distance(parts):
    devices = len(parts)
    return [parts[0]] + [
        lax.ppermute(parts[k], "occj", [(d, d ^ k) for d in range(devices)])
        for k in range(devices - 1, 0, -1)
    ][::-1]


def across_first(parts, groups):
    return [parts[0]] + [
        lax.ppermute(parts[s], "occi", [(k, k ^ s) for k in range(groups)])
        for s in range(groups - 1, 0, -1)
    ][::-1]


def tie(x, *others):
    return lax.optimization_barrier((x, *others))[0]


def copy_kernel(source, out):
    for k in range(source.shape[0]):
        out[k] = source[k]


def after(x, *others):
    return pl.pallas_call(
        copy_kernel,
        out_shape=jax.ShapeDtypeStruct(x.shape, x.dtype),
        in_specs=[SMEM],
        out_specs=SMEM,
        cost_estimate=pl.CostEstimate(flops=LONG, bytes_accessed=8, transcendentals=0),
    )(tie(x, *others))


def gather_vectors(vectors, devices, *earlier):
    def turn(x, k):
        return lax.ppermute(x, "occj", [(d, d ^ k) for d in range(devices)])

    even = list(range(0, devices, 2))
    held = [vectors] + [turn(vectors, k) for k in even[1:]]
    other = turn(tie(jnp.stack(held), *earlier), 1)
    return [*held, other], even + [k ^ 1 for k in even]


def virtual_sums(tiles, vir_energy, q):
    e, g = tiles.edge, tiles.rows
    n_above = len(tiles.above)
    first = jnp.array([a for a, _ in tiles.above] + list(range(0, tiles.n, 2)), jnp.int32)[q]
    second = jnp.array([b for _, b in tiles.above] + list(range(1, tiles.n, 2)), jnp.int32)[q]
    a = lax.dynamic_slice_in_dim(vir_energy, first * e, e)
    b = lax.dynamic_slice_in_dim(vir_energy, second * e, e)
    pair = a[:, None] + b[None, :]
    across = jnp.concatenate([pair, pair], axis=1)
    halves = [
        jnp.concatenate([t[:g, None] + t[None, :], t[g:, None] + t[None, :]], axis=1) for t in (a, b)
    ]
    return jnp.where(q < n_above, across, jnp.concatenate(halves, axis=0))


def local(groups, devices, amplitudes, vectors, occupied_fock_block, occ_energy, vir_energy):
    first, second, virtual = amplitudes.shape[:3]
    assert second == 1 and groups * first == devices
    assert groups & (groups - 1) == 0 and devices & (devices - 1) == 0
    tiles = Tiles(devices, virtual)
    edge = tiles.edge
    current = amplitudes.reshape(first, virtual, virtual)
    count = current.size
    fock = occupied_fock_block.astype(WIDE)
    p, q = lax.axis_index("occi"), lax.axis_index("occj")
    place = jnp.stack([p, q]).astype(jnp.int32)
    packed = jax.ShapeDtypeStruct((devices, first, edge, 2 * edge), NARROW)
    upper = jax.ShapeDtypeStruct((devices, first, tiles.rows, 2 * edge), NARROW)
    part = jax.ShapeDtypeStruct((first, first, tiles.rows, 2 * edge), NARROW)
    singles = vectors.shape[0]
    inner = pltpu.VMEM((singles * virtual, virtual), NARROW)
    square = pltpu.VMEM((virtual, virtual), WIDE)
    chunks = range(2)

    distant = jax.ShapeDtypeStruct((first, edge, 2 * edge), NARROW)
    blocks = pltpu.VMEM(packed.shape, NARROW)
    started = call(functools.partial(pack_kernel, tiles), [distant] * devices, [blocks], count, 6 * count,
                   place, current, specs=[SMEM, VMEM])
    held = by_distance(started)
    pieces, order = gather_vectors(vectors, devices, held[1], held[-1])

    ladder_flops = first * singles * 4 * virtual**3
    ladder, whole = call(
        functools.partial(first_ladder_kernel, tiles, order),
        [packed, jax.ShapeDtypeStruct((virtual, singles * virtual), NARROW)], [inner, square],
        ladder_flops, 8 * count, place, current, *pieces, specs=[SMEM] + [VMEM] * (1 + len(pieces)),
    )
    parts = call(
        functools.partial(sort_kernel, tiles, groups), [part] * (2 * groups), [blocks], count, 4 * count,
        tie(place, ladder), *held, specs=[SMEM] + [VMEM] * devices,
    )
    mirror = [across_first(parts[c * groups:(c + 1) * groups], groups) for c in chunks]
    sums = virtual_sums(tiles, vir_energy, tie(q, mirror[0][-1]))
    ladder = exchange(ladder)

    half, other = [], []
    for c in chunks:
        half.append(call(
            functools.partial(half_kernel, tiles, groups, first, c), [part] * groups, [],
            LONG, 6 * count, after(place, *mirror[c]) if c == 0 else place, fock, ladder, *mirror[c],
            specs=[SMEM] * 2 + [VMEM] * (groups + 1),
        ))
        other.append(across_first(half[c], groups))
    sent, rest, mixed = [], [], []
    for c in chunks:
        sent_one, rest_one, *mixed_one = call(
            functools.partial(update_kernel, tiles, groups, first, c),
            [(upper, packed)[c], jax.ShapeDtypeStruct((first, devices, *part.shape[2:]), NARROW)] + [part] * (groups - 1),
            [pltpu.VMEM((first, devices, *part.shape[2:]), WIDE), pltpu.VMEM(part.shape, WIDE)],
            LONG, 10 * count, place, fock, occ_energy, sums, *sent, *half[c], *other[c],
            specs=[SMEM] * 3 + [VMEM] * (2 * groups + 1 + c),
        )
        sent, rest, mixed = [sent_one], rest + [rest_one], mixed + [mixed_one]
    other = [across_first([None] + x, groups)[1:] for x in mixed]
    back = exchange(sent[0])
    def by_pair(*shape):
        return pl.BlockSpec((1, *shape), lambda pair: (pair, 0, 0))

    def all_pairs(*shape):
        return pl.BlockSpec(shape, lambda pair: (0, 0))

    base = pl.pallas_call(
        functools.partial(second_ladder_kernel, tiles, first),
        grid=(first,),
        out_shape=jax.ShapeDtypeStruct(current.shape, WIDE),
        in_specs=[
            SMEM, SMEM, by_pair(virtual, virtual),
            pl.BlockSpec((devices, 1, edge, 2 * edge), lambda pair: (0, pair, 0, 0)),
            all_pairs(virtual, 128), all_pairs(1, virtual), all_pairs(*whole.shape),
        ],
        out_specs=by_pair(virtual, virtual),
        scratch_shapes=[inner, square, pltpu.VMEM((virtual, virtual), NARROW)],
        compiler_params=PARAMS,
        cost_estimate=pl.CostEstimate(flops=ladder_flops, bytes_accessed=12 * count, transcendentals=0),
    )(place, occ_energy, current, back, jnp.broadcast_to(vir_energy[:, None], (virtual, 128)),
      vir_energy[None, :], whole)
    last = []
    for c in chunks:
        last = call(
            functools.partial(rest_kernel, tiles, groups, first, c),
            [distant] * devices if c else [upper], [blocks] if c else [],
            LONG, 8 * count, place, occ_energy, sums, rest[c], *other[c], *last,
            specs=[SMEM] * 2 + [VMEM] * (groups + 1 + c),
        )
    done = pl.pallas_call(
        functools.partial(add_kernel, tiles),
        grid=(first,),
        out_shape=jax.ShapeDtypeStruct(current.shape, WIDE),
        in_specs=[SMEM, by_pair(virtual, virtual)] + [by_pair(edge, 2 * edge)] * devices,
        out_specs=by_pair(virtual, virtual),
        scratch_shapes=[pltpu.VMEM((devices, 1, edge, 2 * edge), NARROW)],
        compiler_params=PARAMS,
        input_output_aliases={1: 0},
        cost_estimate=pl.CostEstimate(flops=count, bytes_accessed=10 * count, transcendentals=0),
    )(place, base, *by_distance(last))
    return done.reshape(amplitudes.shape)


def solution(mesh):
    sizes = (mesh.shape["occi"], mesh.shape["occj"])
    return jax.shard_map(
        functools.partial(local, *sizes),
        mesh=mesh,
        in_specs=(P("occi", "occj", None, None), P(None, "occj", None), P(), P(), P()),
        out_specs=P("occi", "occj", None, None),
        check_vma=False,
    )
```

```python
import functools
import math

import jax
import jax.numpy as jnp
from jax import lax
from jax.experimental import pallas as pl
from jax.experimental.pallas import tpu as pltpu
from jax.sharding import PartitionSpec as P

VMEM = pl.BlockSpec(memory_space=pltpu.VMEM)
SMEM = pl.BlockSpec(memory_space=pltpu.SMEM)
PARAMS = pltpu.CompilerParams(vmem_limit_bytes=50 * 2**20)
WIDE = jnp.float32
LONG = 3 * 10**10
NARROW = jnp.bfloat16


class Tiles:
    def __init__(self, devices, virtual):
        n = math.isqrt(2 * devices)
        assert n * n == 2 * devices and n % 2 == 0 and virtual % n == 0
        self.n = n
        self.edge = virtual // n
        self.rows = self.edge // 2
        self.above = [(a, b) for a in range(n) for b in range(a + 1, n)]
        self.diagonal = [(len(self.above) + k // 2, k % 2, k) for k in range(n)]

    def span(self, k):
        return slice(k * self.edge, (k + 1) * self.edge)

    def mirror_within(self, x):
        e, g = self.edge, self.rows
        tile = jnp.concatenate([x[:, :e], x[:, e:]], axis=0).T
        return jnp.concatenate([tile[:g], tile[g:]], axis=1)

    def mirror_across(self, x):
        return jnp.concatenate([x[:, self.edge:], x[:, :self.edge]], axis=1)


def call(body, outs, scratch, flops, moved, *operands, specs):
    return pl.pallas_call(
        body,
        out_shape=outs,
        in_specs=specs,
        out_specs=jax.tree.map(lambda _: VMEM, outs),
        scratch_shapes=scratch,
        compiler_params=PARAMS,
        cost_estimate=pl.CostEstimate(flops=flops, bytes_accessed=moved, transcendentals=0),
    )(*operands)


def pack_pair(tiles, source, out, pair, mirrored=False):
    e, g = tiles.edge, tiles.rows
    straight, turned = (slice(e, None), slice(0, e)) if mirrored else (slice(0, e), slice(e, None))
    for d, (a, b) in enumerate(tiles.above):
        out[d, pair, :, straight] = source[tiles.span(a), tiles.span(b)].astype(NARROW)
        out[d, pair, :, turned] = source[tiles.span(b), tiles.span(a)].astype(WIDE).T.astype(NARROW)
    for d, c, k in tiles.diagonal:
        tile = source[tiles.span(k), tiles.span(k)]
        tile = tile.astype(WIDE).T.astype(NARROW) if mirrored else tile.astype(NARROW)
        out[d, pair, c * g:(c + 1) * g, :e] = tile[:g]
        out[d, pair, c * g:(c + 1) * g, e:] = tile[g:]


def unpack_pair(tiles, blocks, pair, put):
    e, g = tiles.edge, tiles.rows
    for d, (a, b) in enumerate(tiles.above):
        put(a, b, blocks[d, pair, :, :e].astype(WIDE))
        put(b, a, blocks[d, pair, :, e:].astype(WIDE).T)
    for d, c, k in tiles.diagonal:
        upper = blocks[d, pair, c * g:(c + 1) * g, :e]
        lower = blocks[d, pair, c * g:(c + 1) * g, e:]
        put(k, k, jnp.concatenate([upper, lower], axis=0).astype(WIDE))


def to_distances(place, whole, outs):
    for k, out in enumerate(outs):
        out[...] = whole[place[1] ^ k]


def from_distances(place, pieces, whole):
    for k, piece in enumerate(pieces):
        whole[place[1] ^ k] = piece[...]


def pack_kernel(tiles, place, source, *refs):
    outs, whole = refs[:-1], refs[-1]
    for pair in range(source.shape[0]):
        pack_pair(tiles, source.at[pair], whole, pair, mirrored=True)
    to_distances(place, whole, outs)


def sort_kernel(tiles, groups, place, *refs):
    pieces, outs, whole = refs[:-2 * groups - 1], refs[-2 * groups - 1:-1], refs[-1]
    first = whole.shape[1]
    from_distances(place, pieces, whole)
    for s in range(groups):
        for u in range(first):
            block = whole[(place[0] ^ s) * first + u]
            for c in range(2):
                outs[c * groups + s][u] = block[:, c * tiles.rows:(c + 1) * tiles.rows]


def assemble(place, order, pieces, whole):
    k = 0
    for piece in pieces:
        count, rows, virtual = piece.shape[-3:]
        for block in range(piece.shape[0] if len(piece.shape) == 4 else 1):
            start = pl.multiple_of((place[1] ^ order[k]) * rows, rows)
            for single in range(count):
                values = piece[block, single] if len(piece.shape) == 4 else piece[single]
                whole[pl.ds(start, rows), single * virtual:(single + 1) * virtual] = values
            k += 1


def ladder_pair(matrix, whole, inner, total):
    virtual = matrix.shape[0]
    for single in range(whole.shape[1] // virtual):
        at = slice(single * virtual, (single + 1) * virtual)
        inner[at, :] = lax.dot_general(
            matrix, whole[:, at], (((1,), (1,)), ((), ())), preferred_element_type=WIDE
        ).astype(NARROW)
    total[...] = jnp.dot(whole[...], inner[...], preferred_element_type=WIDE)


def inverse(x):
    guess = pl.reciprocal(x, approx=True)
    return guess * (2.0 - x * guess)


def first_ladder_kernel(tiles, order, place, source, *refs):
    pieces, (out, whole, inner, total) = refs[:-4], refs[-4:]
    assemble(place, order, pieces, whole)
    for pair in range(source.shape[0]):
        ladder_pair(source[pair].astype(NARROW), whole, inner, total)
        pack_pair(tiles, total, out, pair)


def second_ladder_kernel(tiles, first, place, occ, source, blocks, row, column, whole, out, inner, total, matrix):
    def put(a, b, tile):
        matrix[tiles.span(a), tiles.span(b)] = tile.astype(NARROW)

    unpack_pair(tiles, blocks, 0, put)
    ladder_pair(matrix[...], whole, inner, total)
    base = occ[place[0] * first + pl.program_id(0)] + occ[place[1]]
    strip = math.gcd(64, total.shape[0])

    def finish(step, carry):
        at = pl.ds(pl.multiple_of(step * strip, strip), strip)
        own = base - row[at, :1] - column[...]
        out[0, at, :] = source[0, at, :] + 2.0 * (matrix[at, :].astype(WIDE) + total[at, :] * inverse(own))
        return carry

    lax.fori_loop(0, total.shape[0] // strip, finish, 0)


def add_kernel(tiles, place, source, *refs):
    pieces, (out, whole) = refs[:-2], refs[-2:]
    from_distances(place, pieces, whole)

    def put(a, b, tile):
        here = (0, tiles.span(a), tiles.span(b))
        out[here] = source[here] + tile

    unpack_pair(tiles, whole, 0, put)


def mix(place, fock, first, load, store, rows):
    total = fock.shape[0]
    strips = rows // 16

    def strip(step, carry):
        u = step // strips
        at = pl.ds(pl.multiple_of(lax.rem(step, strips) * 16, 16), 16)
        taken = [load(k // first, u, k % first, at) for k in range(total)]
        for k in range(total):
            column = (place[0] ^ (k // first)) * first + k % first
            result = None
            for m in range(total):
                line = (place[0] ^ (m // first)) * first + m % first
                term = (-fock[line, column]) * taken[m]
                result = term if result is None else result + term
            store(k // first, u, k % first, column, at, result)
        return carry

    lax.fori_loop(0, first * strips, strip, 0)


def half_kernel(tiles, groups, first, chunk, place, fock, ladder, *refs):
    held, out = refs[:groups], refs[groups:]

    def load(s, u, r, at):
        return held[s][u, r, at, :].astype(WIDE)

    def store(s, u, w, column, at, result):
        rows = pl.ds(pl.multiple_of(chunk * tiles.rows + at.start, 16), at.size)
        out[s][u, w, at, :] = (ladder[column, u, rows, :].astype(WIDE) + result).astype(NARROW)

    mix(place, fock, first, load, store, tiles.rows)


def with_mirror(tiles, place, x, finish):
    across = place[1] < len(tiles.above)

    @pl.when(across)
    def _():
        finish(tiles.mirror_across(x))

    @pl.when(jnp.logical_not(across))
    def _():
        finish(tiles.mirror_within(x))


def update_kernel(tiles, groups, first, chunk, place, fock, occ, sums, *refs):
    before, refs = refs[:chunk], refs[chunk:]
    own, other, refs = refs[:groups], refs[groups:2 * groups], refs[2 * groups:]
    (sent, rest), out, (update, local_mixed) = refs[:2], refs[2:groups + 1], refs[groups + 1:]
    here = slice(chunk * tiles.rows, (chunk + 1) * tiles.rows)
    for ref in before:
        sent[:, :, :tiles.rows, :] = ref[...]

    def one(step, carry):
        u, w = step // first, lax.rem(step, first)
        for s in range(groups):
            column = (place[0] ^ s) * first + w
            base = occ[place[0] * first + u] + occ[column]

            def finish(mirrored):
                value = (own[s][u, w].astype(WIDE) + mirrored) * inverse(base - sums[here])
                update[u, s * first + w] = value
                sent[column, u, here] = value.astype(NARROW)

            with_mirror(tiles, place, other[s][w, u].astype(WIDE), finish)
        return carry

    lax.fori_loop(0, first * first, one, 0)

    def load(s, u, r, at):
        return update[u, s * first + r, at, :]

    def lost(value):
        return 2.0 * (value - value.astype(NARROW).astype(WIDE))

    def store(s, u, w, column, at, result):
        if s == 0:
            local_mixed[u, w, at, :] = result
            return
        out[s - 1][u, w, at, :] = result.astype(NARROW)
        strip = pl.ds(pl.multiple_of(chunk * tiles.rows + at.start, 16), at.size)
        base = occ[place[0] * first + u] + occ[column]
        share = result * inverse(base - sums[strip, :])
        rest[u, s * first + w, at, :] = (lost(update[u, s * first + w, at, :]) + share).astype(NARROW)

    mix(place, fock, first, load, store, tiles.rows)

    def within(step, carry):
        u, w = step // first, lax.rem(step, first)
        base = occ[place[0] * first + u] + occ[place[0] * first + w]

        def finish(mirrored):
            share = (local_mixed[u, w] + mirrored) * inverse(base - sums[here])
            rest[u, w] = (lost(update[u, w]) + share).astype(NARROW)

        with_mirror(tiles, place, local_mixed[w, u], finish)
        return carry

    lax.fori_loop(0, first * first, within, 0)


def rest_kernel(tiles, groups, first, chunk, place, occ, sums, rest, *refs):
    other, refs = refs[:groups - 1], refs[groups - 1:]
    out = refs[-1]
    here = slice(chunk * tiles.rows, (chunk + 1) * tiles.rows)
    there = here if chunk else slice(None)
    if chunk:
        out[:, :, :tiles.rows, :] = refs[0][...]

    def one(step, carry):
        u, w = step // first, lax.rem(step, first)
        out[place[0] * first + w, u, there] = rest[u, w]
        for s in range(1, groups):
            column = (place[0] ^ s) * first + w
            base = occ[place[0] * first + u] + occ[column]

            def finish(mirrored):
                value = rest[u, s * first + w].astype(WIDE) + mirrored * inverse(base - sums[here])
                out[column, u, there] = value.astype(NARROW)

            with_mirror(tiles, place, other[s - 1][w, u].astype(WIDE), finish)
        return carry

    lax.fori_loop(0, first * first, one, 0)
    if chunk:
        to_distances(place, out, refs[1:-1])


def exchange(blocks):
    return lax.all_to_all(blocks, "occj", split_axis=0, concat_axis=0, tiled=True)


def by_distance(parts):
    devices = len(parts)
    return [parts[0]] + [
        lax.ppermute(parts[k], "occj", [(d, d ^ k) for d in range(devices)])
        for k in range(devices - 1, 0, -1)
    ][::-1]


def across_first(parts, groups):
    return [parts[0]] + [
        lax.ppermute(parts[s], "occi", [(k, k ^ s) for k in range(groups)])
        for s in range(groups - 1, 0, -1)
    ][::-1]


def tie(x, *others):
    return lax.optimization_barrier((x, *others))[0]


def copy_kernel(source, out):
    for k in range(source.shape[0]):
        out[k] = source[k]


def after(x, *others):
    return pl.pallas_call(
        copy_kernel,
        out_shape=jax.ShapeDtypeStruct(x.shape, x.dtype),
        in_specs=[SMEM],
        out_specs=SMEM,
        cost_estimate=pl.CostEstimate(flops=LONG, bytes_accessed=8, transcendentals=0),
    )(tie(x, *others))


def gather_vectors(vectors, devices, packed):
    def turn(x, k):
        return lax.ppermute(x, "occj", [(d, d ^ k) for d in range(devices)])

    even = list(range(0, devices, 2))
    held = [vectors] + [turn(vectors, k) for k in even[1:]]
    other = turn(tie(jnp.stack(held), packed), 1)
    return [*held, other], even + [k ^ 1 for k in even]


def virtual_sums(tiles, vir_energy, q):
    e, g = tiles.edge, tiles.rows
    n_above = len(tiles.above)
    first = jnp.array([a for a, _ in tiles.above] + list(range(0, tiles.n, 2)), jnp.int32)[q]
    second = jnp.array([b for _, b in tiles.above] + list(range(1, tiles.n, 2)), jnp.int32)[q]
    a = lax.dynamic_slice_in_dim(vir_energy, first * e, e)
    b = lax.dynamic_slice_in_dim(vir_energy, second * e, e)
    pair = a[:, None] + b[None, :]
    across = jnp.concatenate([pair, pair], axis=1)
    halves = [
        jnp.concatenate([t[:g, None] + t[None, :], t[g:, None] + t[None, :]], axis=1) for t in (a, b)
    ]
    return jnp.where(q < n_above, across, jnp.concatenate(halves, axis=0))


def local(groups, devices, amplitudes, vectors, occupied_fock_block, occ_energy, vir_energy):
    first, second, virtual = amplitudes.shape[:3]
    assert second == 1 and groups * first == devices
    assert groups & (groups - 1) == 0 and devices & (devices - 1) == 0
    tiles = Tiles(devices, virtual)
    edge = tiles.edge
    current = amplitudes.reshape(first, virtual, virtual)
    count = current.size
    fock = occupied_fock_block.astype(WIDE)
    p, q = lax.axis_index("occi"), lax.axis_index("occj")
    place = jnp.stack([p, q]).astype(jnp.int32)
    packed = jax.ShapeDtypeStruct((devices, first, edge, 2 * edge), NARROW)
    upper = jax.ShapeDtypeStruct((devices, first, tiles.rows, 2 * edge), NARROW)
    part = jax.ShapeDtypeStruct((first, first, tiles.rows, 2 * edge), NARROW)
    singles = vectors.shape[0]
    inner = pltpu.VMEM((singles * virtual, virtual), NARROW)
    square = pltpu.VMEM((virtual, virtual), WIDE)
    chunks = range(2)

    distant = jax.ShapeDtypeStruct((first, edge, 2 * edge), NARROW)
    blocks = pltpu.VMEM(packed.shape, NARROW)
    started = call(functools.partial(pack_kernel, tiles), [distant] * devices, [blocks], count, 6 * count,
                   place, current, specs=[SMEM, VMEM])
    pieces, order = gather_vectors(vectors, devices, started[0])
    held = by_distance(started)
    sums = virtual_sums(tiles, vir_energy, q)

    ladder_flops = first * singles * 4 * virtual**3
    ladder, whole = call(
        functools.partial(first_ladder_kernel, tiles, order),
        [packed, jax.ShapeDtypeStruct((virtual, singles * virtual), NARROW)], [inner, square],
        ladder_flops, 8 * count, place, current, *pieces, specs=[SMEM] + [VMEM] * (1 + len(pieces)),
    )
    parts = call(
        functools.partial(sort_kernel, tiles, groups), [part] * (2 * groups), [blocks], count, 4 * count,
        tie(place, ladder), *held, specs=[SMEM] + [VMEM] * devices,
    )
    mirror = [across_first(parts[c * groups:(c + 1) * groups], groups) for c in chunks]
    ladder = exchange(ladder)

    half, other = [], []
    for c in chunks:
        half.append(call(
            functools.partial(half_kernel, tiles, groups, first, c), [part] * groups, [],
            LONG, 6 * count, after(place, *mirror[c]) if c == 0 else place, fock, ladder, *mirror[c],
            specs=[SMEM] * 2 + [VMEM] * (groups + 1),
        ))
        other.append(across_first(half[c], groups))
    sent, rest, mixed = [], [], []
    for c in chunks:
        sent_one, rest_one, *mixed_one = call(
            functools.partial(update_kernel, tiles, groups, first, c),
            [(upper, packed)[c], jax.ShapeDtypeStruct((first, devices, *part.shape[2:]), NARROW)] + [part] * (groups - 1),
            [pltpu.VMEM((first, devices, *part.shape[2:]), WIDE), pltpu.VMEM(part.shape, WIDE)],
            LONG, 10 * count, place, fock, occ_energy, sums, *sent, *half[c], *other[c],
            specs=[SMEM] * 3 + [VMEM] * (2 * groups + 1 + c),
        )
        sent, rest, mixed = [sent_one], rest + [rest_one], mixed + [mixed_one]
    other = [across_first([None] + x, groups)[1:] for x in mixed]
    back = exchange(sent[0])
    def by_pair(*shape):
        return pl.BlockSpec((1, *shape), lambda pair: (pair, 0, 0))

    def all_pairs(*shape):
        return pl.BlockSpec(shape, lambda pair: (0, 0))

    base = pl.pallas_call(
        functools.partial(second_ladder_kernel, tiles, first),
        grid=(first,),
        out_shape=jax.ShapeDtypeStruct(current.shape, WIDE),
        in_specs=[
            SMEM, SMEM, by_pair(virtual, virtual),
            pl.BlockSpec((devices, 1, edge, 2 * edge), lambda pair: (0, pair, 0, 0)),
            all_pairs(virtual, 128), all_pairs(1, virtual), all_pairs(*whole.shape),
        ],
        out_specs=by_pair(virtual, virtual),
        scratch_shapes=[inner, square, pltpu.VMEM((virtual, virtual), NARROW)],
        compiler_params=PARAMS,
        cost_estimate=pl.CostEstimate(flops=ladder_flops, bytes_accessed=12 * count, transcendentals=0),
    )(place, occ_energy, current, back, jnp.broadcast_to(vir_energy[:, None], (virtual, 128)),
      vir_energy[None, :], whole)
    last = []
    for c in chunks:
        last = call(
            functools.partial(rest_kernel, tiles, groups, first, c),
            [distant] * devices if c else [upper], [blocks] if c else [],
            LONG, 8 * count, place, occ_energy, sums, rest[c], *other[c], *last,
            specs=[SMEM] * 2 + [VMEM] * (groups + 1 + c),
        )
    done = pl.pallas_call(
        functools.partial(add_kernel, tiles),
        grid=(first,),
        out_shape=jax.ShapeDtypeStruct(current.shape, WIDE),
        in_specs=[SMEM, by_pair(virtual, virtual)] + [by_pair(edge, 2 * edge)] * devices,
        out_specs=by_pair(virtual, virtual),
        scratch_shapes=[pltpu.VMEM((devices, 1, edge, 2 * edge), NARROW)],
        compiler_params=PARAMS,
        cost_estimate=pl.CostEstimate(flops=count, bytes_accessed=10 * count, transcendentals=0),
    )(place, base, *by_distance(last))
    return done.reshape(amplitudes.shape)


def solution(mesh):
    sizes = (mesh.shape["occi"], mesh.shape["occj"])
    return jax.shard_map(
        functools.partial(local, *sizes),
        mesh=mesh,
        in_specs=(P("occi", "occj", None, None), P(None, "occj", None), P(), P(), P()),
        out_specs=P("occi", "occj", None, None),
        check_vma=False,
    )
```

```python
import functools
import math

import jax
import jax.numpy as jnp
from jax import lax
from jax.experimental import pallas as pl
from jax.experimental.pallas import tpu as pltpu
from jax.sharding import PartitionSpec as P

VMEM = pl.BlockSpec(memory_space=pltpu.VMEM)
SMEM = pl.BlockSpec(memory_space=pltpu.SMEM)
PARAMS = pltpu.CompilerParams(vmem_limit_bytes=50 * 2**20)
WIDE = jnp.float32
LONG = 3 * 10**10
NARROW = jnp.bfloat16


class Tiles:
    def __init__(self, devices, virtual):
        n = math.isqrt(2 * devices)
        assert n * n == 2 * devices and n % 2 == 0 and virtual % n == 0
        self.n = n
        self.edge = virtual // n
        self.rows = self.edge // 2
        self.above = [(a, b) for a in range(n) for b in range(a + 1, n)]
        self.diagonal = [(len(self.above) + k // 2, k % 2, k) for k in range(n)]

    def span(self, k):
        return slice(k * self.edge, (k + 1) * self.edge)

    def mirror_within(self, x):
        e, g = self.edge, self.rows
        tile = jnp.concatenate([x[:, :e], x[:, e:]], axis=0).T
        return jnp.concatenate([tile[:g], tile[g:]], axis=1)

    def mirror_across(self, x):
        return jnp.concatenate([x[:, self.edge:], x[:, :self.edge]], axis=1)


def call(body, outs, scratch, flops, moved, *operands, specs):
    return pl.pallas_call(
        body,
        out_shape=outs,
        in_specs=specs,
        out_specs=jax.tree.map(lambda _: VMEM, outs),
        scratch_shapes=scratch,
        compiler_params=PARAMS,
        cost_estimate=pl.CostEstimate(flops=flops, bytes_accessed=moved, transcendentals=0),
    )(*operands)


def pack_pair(tiles, source, out, pair, mirrored=False):
    e, g = tiles.edge, tiles.rows
    straight, turned = (slice(e, None), slice(0, e)) if mirrored else (slice(0, e), slice(e, None))
    for d, (a, b) in enumerate(tiles.above):
        out[d, pair, :, straight] = source[tiles.span(a), tiles.span(b)].astype(NARROW)
        out[d, pair, :, turned] = source[tiles.span(b), tiles.span(a)].astype(WIDE).T.astype(NARROW)
    for d, c, k in tiles.diagonal:
        tile = source[tiles.span(k), tiles.span(k)]
        tile = tile.astype(WIDE).T.astype(NARROW) if mirrored else tile.astype(NARROW)
        out[d, pair, c * g:(c + 1) * g, :e] = tile[:g]
        out[d, pair, c * g:(c + 1) * g, e:] = tile[g:]


def unpack_pair(tiles, blocks, pair, put):
    e, g = tiles.edge, tiles.rows
    for d, (a, b) in enumerate(tiles.above):
        put(a, b, blocks[d, pair, :, :e].astype(WIDE))
        put(b, a, blocks[d, pair, :, e:].astype(WIDE).T)
    for d, c, k in tiles.diagonal:
        upper = blocks[d, pair, c * g:(c + 1) * g, :e]
        lower = blocks[d, pair, c * g:(c + 1) * g, e:]
        put(k, k, jnp.concatenate([upper, lower], axis=0).astype(WIDE))


def to_distances(place, whole, outs):
    for k, out in enumerate(outs):
        out[...] = whole[place[1] ^ k]


def from_distances(place, pieces, whole):
    for k, piece in enumerate(pieces):
        whole[place[1] ^ k] = piece[...]


def pack_kernel(tiles, place, source, *refs):
    outs, whole = refs[:-1], refs[-1]
    for pair in range(source.shape[0]):
        pack_pair(tiles, source.at[pair], whole, pair, mirrored=True)
    to_distances(place, whole, outs)


def sort_kernel(tiles, groups, place, *refs):
    pieces, outs, whole = refs[:-2 * groups - 1], refs[-2 * groups - 1:-1], refs[-1]
    first = whole.shape[1]
    from_distances(place, pieces, whole)
    for s in range(groups):
        for u in range(first):
            block = whole[(place[0] ^ s) * first + u]
            for c in range(2):
                outs[c * groups + s][u] = block[:, c * tiles.rows:(c + 1) * tiles.rows]


def assemble(place, order, pieces, whole):
    k = 0
    for piece in pieces:
        count, rows, virtual = piece.shape[-3:]
        for block in range(piece.shape[0] if len(piece.shape) == 4 else 1):
            start = pl.multiple_of((place[1] ^ order[k]) * rows, rows)
            for single in range(count):
                values = piece[block, single] if len(piece.shape) == 4 else piece[single]
                whole[pl.ds(start, rows), single * virtual:(single + 1) * virtual] = values
            k += 1


def ladder_pair(matrix, whole, inner, total):
    virtual = matrix.shape[0]
    for single in range(whole.shape[1] // virtual):
        at = slice(single * virtual, (single + 1) * virtual)
        inner[at, :] = lax.dot_general(
            matrix, whole[:, at], (((1,), (1,)), ((), ())), preferred_element_type=WIDE
        ).astype(NARROW)
    total[...] = jnp.dot(whole[...], inner[...], preferred_element_type=WIDE)


def inverse(x):
    guess = pl.reciprocal(x, approx=True)
    return guess * (2.0 - x * guess)


def first_ladder_kernel(tiles, order, place, source, *refs):
    pieces, (out, whole, inner, total) = refs[:-4], refs[-4:]
    assemble(place, order, pieces, whole)
    for pair in range(source.shape[0]):
        ladder_pair(source[pair].astype(NARROW), whole, inner, total)
        pack_pair(tiles, total, out, pair)


def second_ladder_kernel(tiles, first, place, occ, source, blocks, row, column, whole, out, inner, total, matrix):
    def put(a, b, tile):
        matrix[tiles.span(a), tiles.span(b)] = tile.astype(NARROW)

    unpack_pair(tiles, blocks, 0, put)
    ladder_pair(matrix[...], whole, inner, total)
    base = occ[place[0] * first + pl.program_id(0)] + occ[place[1]]
    strip = math.gcd(64, total.shape[0])

    def finish(step, carry):
        at = pl.ds(pl.multiple_of(step * strip, strip), strip)
        own = base - row[at, :1] - column[...]
        out[0, at, :] = source[0, at, :] + 2.0 * (matrix[at, :].astype(WIDE) + total[at, :] * inverse(own))
        return carry

    lax.fori_loop(0, total.shape[0] // strip, finish, 0)


def add_kernel(tiles, place, source, *refs):
    pieces, (out, whole) = refs[:-2], refs[-2:]
    from_distances(place, pieces, whole)

    def put(a, b, tile):
        here = (0, tiles.span(a), tiles.span(b))
        out[here] = source[here] + tile

    unpack_pair(tiles, whole, 0, put)


def mix(place, fock, first, load, store, rows):
    total = fock.shape[0]
    strips = rows // 16

    def strip(step, carry):
        u = step // strips
        at = pl.ds(pl.multiple_of(lax.rem(step, strips) * 16, 16), 16)
        taken = [load(k // first, u, k % first, at) for k in range(total)]
        for k in range(total):
            column = (place[0] ^ (k // first)) * first + k % first
            result = None
            for m in range(total):
                line = (place[0] ^ (m // first)) * first + m % first
                term = (-fock[line, column]) * taken[m]
                result = term if result is None else result + term
            store(k // first, u, k % first, column, at, result)
        return carry

    lax.fori_loop(0, first * strips, strip, 0)


def half_kernel(tiles, groups, first, chunk, place, fock, ladder, *refs):
    held, out = refs[:groups], refs[groups:]

    def load(s, u, r, at):
        return held[s][u, r, at, :].astype(WIDE)

    def store(s, u, w, column, at, result):
        rows = pl.ds(pl.multiple_of(chunk * tiles.rows + at.start, 16), at.size)
        out[s][u, w, at, :] = (ladder[column, u, rows, :].astype(WIDE) + result).astype(NARROW)

    mix(place, fock, first, load, store, tiles.rows)


def with_mirror(tiles, place, x, finish):
    across = place[1] < len(tiles.above)

    @pl.when(across)
    def _():
        finish(tiles.mirror_across(x))

    @pl.when(jnp.logical_not(across))
    def _():
        finish(tiles.mirror_within(x))


def update_kernel(tiles, groups, first, chunk, place, fock, occ, sums, *refs):
    before, refs = refs[:chunk], refs[chunk:]
    own, other, refs = refs[:groups], refs[groups:2 * groups], refs[2 * groups:]
    (sent, rest), out, (update, local_mixed) = refs[:2], refs[2:groups + 1], refs[groups + 1:]
    here = slice(chunk * tiles.rows, (chunk + 1) * tiles.rows)
    for ref in before:
        sent[:, :, :tiles.rows, :] = ref[...]

    def one(step, carry):
        u, w = step // first, lax.rem(step, first)
        for s in range(groups):
            column = (place[0] ^ s) * first + w
            base = occ[place[0] * first + u] + occ[column]

            def finish(mirrored):
                value = (own[s][u, w].astype(WIDE) + mirrored) * inverse(base - sums[here])
                update[u, s * first + w] = value
                sent[column, u, here] = value.astype(NARROW)

            with_mirror(tiles, place, other[s][w, u].astype(WIDE), finish)
        return carry

    lax.fori_loop(0, first * first, one, 0)

    def load(s, u, r, at):
        return update[u, s * first + r, at, :]

    def lost(value):
        return 2.0 * (value - value.astype(NARROW).astype(WIDE))

    def store(s, u, w, column, at, result):
        if s == 0:
            local_mixed[u, w, at, :] = result
            return
        out[s - 1][u, w, at, :] = result.astype(NARROW)
        strip = pl.ds(pl.multiple_of(chunk * tiles.rows + at.start, 16), at.size)
        base = occ[place[0] * first + u] + occ[column]
        share = result * inverse(base - sums[strip, :])
        rest[u, s * first + w, at, :] = (lost(update[u, s * first + w, at, :]) + share).astype(NARROW)

    mix(place, fock, first, load, store, tiles.rows)

    def within(step, carry):
        u, w = step // first, lax.rem(step, first)
        base = occ[place[0] * first + u] + occ[place[0] * first + w]

        def finish(mirrored):
            share = (local_mixed[u, w] + mirrored) * inverse(base - sums[here])
            rest[u, w] = (lost(update[u, w]) + share).astype(NARROW)

        with_mirror(tiles, place, local_mixed[w, u], finish)
        return carry

    lax.fori_loop(0, first * first, within, 0)


def rest_kernel(tiles, groups, first, chunk, place, occ, sums, rest, *refs):
    other, refs = refs[:groups - 1], refs[groups - 1:]
    out = refs[-1]
    here = slice(chunk * tiles.rows, (chunk + 1) * tiles.rows)
    there = here if chunk else slice(None)
    if chunk:
        out[:, :, :tiles.rows, :] = refs[0][...]

    def one(step, carry):
        u, w = step // first, lax.rem(step, first)
        out[place[0] * first + w, u, there] = rest[u, w]
        for s in range(1, groups):
            column = (place[0] ^ s) * first + w
            base = occ[place[0] * first + u] + occ[column]

            def finish(mirrored):
                value = rest[u, s * first + w].astype(WIDE) + mirrored * inverse(base - sums[here])
                out[column, u, there] = value.astype(NARROW)

            with_mirror(tiles, place, other[s - 1][w, u].astype(WIDE), finish)
        return carry

    lax.fori_loop(0, first * first, one, 0)
    if chunk:
        to_distances(place, out, refs[1:-1])


def exchange(blocks):
    return lax.all_to_all(blocks, "occj", split_axis=0, concat_axis=0, tiled=True)


def by_distance(parts):
    devices = len(parts)
    return [parts[0]] + [
        lax.ppermute(parts[k], "occj", [(d, d ^ k) for d in range(devices)])
        for k in range(devices - 1, 0, -1)
    ][::-1]


def across_first(parts, groups):
    return [parts[0]] + [
        lax.ppermute(parts[s], "occi", [(k, k ^ s) for k in range(groups)])
        for s in range(groups - 1, 0, -1)
    ][::-1]


def tie(x, *others):
    return lax.optimization_barrier((x, *others))[0]


def copy_kernel(source, out):
    for k in range(source.shape[0]):
        out[k] = source[k]


def after(x, *others):
    return pl.pallas_call(
        copy_kernel,
        out_shape=jax.ShapeDtypeStruct(x.shape, x.dtype),
        in_specs=[SMEM],
        out_specs=SMEM,
        cost_estimate=pl.CostEstimate(flops=LONG, bytes_accessed=8, transcendentals=0),
    )(tie(x, *others))


def gather_vectors(vectors, devices, packed):
    def turn(x, k):
        return lax.ppermute(x, "occj", [(d, d ^ k) for d in range(devices)])

    even = list(range(0, devices, 2))
    held = [vectors] + [turn(vectors, k) for k in even[1:]]
    other = turn(tie(jnp.stack(held), packed), 1)
    return [*held, other], even + [k ^ 1 for k in even]


def virtual_sums(tiles, vir_energy, q):
    e, g = tiles.edge, tiles.rows
    n_above = len(tiles.above)
    first = jnp.array([a for a, _ in tiles.above] + list(range(0, tiles.n, 2)), jnp.int32)[q]
    second = jnp.array([b for _, b in tiles.above] + list(range(1, tiles.n, 2)), jnp.int32)[q]
    a = lax.dynamic_slice_in_dim(vir_energy, first * e, e)
    b = lax.dynamic_slice_in_dim(vir_energy, second * e, e)
    pair = a[:, None] + b[None, :]
    across = jnp.concatenate([pair, pair], axis=1)
    halves = [
        jnp.concatenate([t[:g, None] + t[None, :], t[g:, None] + t[None, :]], axis=1) for t in (a, b)
    ]
    return jnp.where(q < n_above, across, jnp.concatenate(halves, axis=0))


def local(groups, devices, amplitudes, vectors, occupied_fock_block, occ_energy, vir_energy):
    first, second, virtual = amplitudes.shape[:3]
    assert second == 1 and groups * first == devices
    assert groups & (groups - 1) == 0 and devices & (devices - 1) == 0
    tiles = Tiles(devices, virtual)
    edge = tiles.edge
    current = amplitudes.reshape(first, virtual, virtual)
    count = current.size
    fock = occupied_fock_block.astype(WIDE)
    p, q = lax.axis_index("occi"), lax.axis_index("occj")
    place = jnp.stack([p, q]).astype(jnp.int32)
    packed = jax.ShapeDtypeStruct((devices, first, edge, 2 * edge), NARROW)
    upper = jax.ShapeDtypeStruct((devices, first, tiles.rows, 2 * edge), NARROW)
    part = jax.ShapeDtypeStruct((first, first, tiles.rows, 2 * edge), NARROW)
    singles = vectors.shape[0]
    inner = pltpu.VMEM((singles * virtual, virtual), NARROW)
    square = pltpu.VMEM((virtual, virtual), WIDE)
    chunks = range(2)

    distant = jax.ShapeDtypeStruct((first, edge, 2 * edge), NARROW)
    blocks = pltpu.VMEM(packed.shape, NARROW)
    started = call(functools.partial(pack_kernel, tiles), [distant] * devices, [blocks], count, 6 * count,
                   place, current, specs=[SMEM, VMEM])
    pieces, order = gather_vectors(vectors, devices, started[0])
    held = by_distance(started)
    sums = virtual_sums(tiles, vir_energy, q)

    ladder_flops = first * singles * 4 * virtual**3
    ladder, whole = call(
        functools.partial(first_ladder_kernel, tiles, order),
        [packed, jax.ShapeDtypeStruct((virtual, singles * virtual), NARROW)], [inner, square],
        ladder_flops, 8 * count, place, current, *pieces, specs=[SMEM] + [VMEM] * (1 + len(pieces)),
    )
    parts = call(
        functools.partial(sort_kernel, tiles, groups), [part] * (2 * groups), [blocks], count, 4 * count,
        tie(place, ladder), *held, specs=[SMEM] + [VMEM] * devices,
    )
    mirror = [across_first(parts[c * groups:(c + 1) * groups], groups) for c in chunks]
    ladder = exchange(ladder)

    half, other = [], []
    for c in chunks:
        half.append(call(
            functools.partial(half_kernel, tiles, groups, first, c), [part] * groups, [],
            LONG, 6 * count, after(place, *mirror[c]) if c == 0 else place, fock, ladder, *mirror[c],
            specs=[SMEM] * 2 + [VMEM] * (groups + 1),
        ))
        other.append(across_first(half[c], groups))
    sent, rest, mixed = [], [], []
    for c in chunks:
        sent_one, rest_one, *mixed_one = call(
            functools.partial(update_kernel, tiles, groups, first, c),
            [(upper, packed)[c], jax.ShapeDtypeStruct((first, devices, *part.shape[2:]), NARROW)] + [part] * (groups - 1),
            [pltpu.VMEM((first, devices, *part.shape[2:]), WIDE), pltpu.VMEM(part.shape, WIDE)],
            LONG, 10 * count, place, fock, occ_energy, sums, *sent, *half[c], *other[c],
            specs=[SMEM] * 3 + [VMEM] * (2 * groups + 1 + c),
        )
        sent, rest, mixed = [sent_one], rest + [rest_one], mixed + [mixed_one]
    other = [across_first([None] + x, groups)[1:] for x in mixed]
    back = exchange(sent[0])
    def by_pair(*shape):
        return pl.BlockSpec((1, *shape), lambda pair: (pair, 0, 0))

    def all_pairs(*shape):
        return pl.BlockSpec(shape, lambda pair: (0, 0))

    base = pl.pallas_call(
        functools.partial(second_ladder_kernel, tiles, first),
        grid=(first,),
        out_shape=jax.ShapeDtypeStruct(current.shape, WIDE),
        in_specs=[
            SMEM, SMEM, by_pair(virtual, virtual),
            pl.BlockSpec((devices, 1, edge, 2 * edge), lambda pair: (0, pair, 0, 0)),
            all_pairs(virtual, 128), all_pairs(1, virtual), all_pairs(*whole.shape),
        ],
        out_specs=by_pair(virtual, virtual),
        scratch_shapes=[inner, square, pltpu.VMEM((virtual, virtual), NARROW)],
        compiler_params=PARAMS,
        cost_estimate=pl.CostEstimate(flops=ladder_flops, bytes_accessed=12 * count, transcendentals=0),
    )(place, occ_energy, current, back, jnp.broadcast_to(vir_energy[:, None], (virtual, 128)),
      vir_energy[None, :], whole)
    last = []
    for c in chunks:
        last = call(
            functools.partial(rest_kernel, tiles, groups, first, c),
            [distant] * devices if c else [upper], [blocks] if c else [],
            LONG, 8 * count, place, occ_energy, sums, rest[c], *other[c], *(last if c else [whole]),
            specs=[SMEM] * 2 + [VMEM] * (groups + 2),
        )
    done = pl.pallas_call(
        functools.partial(add_kernel, tiles),
        grid=(first,),
        out_shape=jax.ShapeDtypeStruct(current.shape, WIDE),
        in_specs=[SMEM, by_pair(virtual, virtual)] + [by_pair(edge, 2 * edge)] * devices,
        out_specs=by_pair(virtual, virtual),
        scratch_shapes=[pltpu.VMEM((devices, 1, edge, 2 * edge), NARROW)],
        compiler_params=PARAMS,
        input_output_aliases={1: 0},
        cost_estimate=pl.CostEstimate(flops=count, bytes_accessed=10 * count, transcendentals=0),
    )(place, base, *by_distance(last))
    return done.reshape(amplitudes.shape)


def solution(mesh):
    sizes = (mesh.shape["occi"], mesh.shape["occj"])
    return jax.shard_map(
        functools.partial(local, *sizes),
        mesh=mesh,
        in_specs=(P("occi", "occj", None, None), P(None, "occj", None), P(), P(), P()),
        out_specs=P("occi", "occj", None, None),
        check_vma=False,
    )
```

```python
import functools
import math

import jax
import jax.numpy as jnp
from jax import lax
from jax.experimental import pallas as pl
from jax.experimental.pallas import tpu as pltpu
from jax.sharding import PartitionSpec as P

VMEM = pl.BlockSpec(memory_space=pltpu.VMEM)
SMEM = pl.BlockSpec(memory_space=pltpu.SMEM)
PARAMS = pltpu.CompilerParams(vmem_limit_bytes=50 * 2**20)
WIDE = jnp.float32
LONG = 3 * 10**10
NARROW = jnp.bfloat16


class Tiles:
    def __init__(self, devices, virtual):
        n = math.isqrt(2 * devices)
        assert n * n == 2 * devices and n % 2 == 0 and virtual % n == 0
        self.n = n
        self.edge = virtual // n
        self.rows = self.edge // 2
        self.above = [(a, b) for a in range(n) for b in range(a + 1, n)]
        self.diagonal = [(len(self.above) + k // 2, k % 2, k) for k in range(n)]

    def span(self, k):
        return slice(k * self.edge, (k + 1) * self.edge)

    def mirror_within(self, x):
        e, g = self.edge, self.rows
        tile = jnp.concatenate([x[:, :e], x[:, e:]], axis=0).T
        return jnp.concatenate([tile[:g], tile[g:]], axis=1)

    def mirror_across(self, x):
        return jnp.concatenate([x[:, self.edge:], x[:, :self.edge]], axis=1)


def call(body, outs, scratch, flops, moved, *operands, specs):
    return pl.pallas_call(
        body,
        out_shape=outs,
        in_specs=specs,
        out_specs=jax.tree.map(lambda _: VMEM, outs),
        scratch_shapes=scratch,
        compiler_params=PARAMS,
        cost_estimate=pl.CostEstimate(flops=flops, bytes_accessed=moved, transcendentals=0),
    )(*operands)


def pack_pair(tiles, source, out, pair, mirrored=False):
    e, g = tiles.edge, tiles.rows
    straight, turned = (slice(e, None), slice(0, e)) if mirrored else (slice(0, e), slice(e, None))
    for d, (a, b) in enumerate(tiles.above):
        out[d, pair, :, straight] = source[tiles.span(a), tiles.span(b)].astype(NARROW)
        out[d, pair, :, turned] = source[tiles.span(b), tiles.span(a)].astype(WIDE).T.astype(NARROW)
    for d, c, k in tiles.diagonal:
        tile = source[tiles.span(k), tiles.span(k)]
        tile = tile.astype(WIDE).T.astype(NARROW) if mirrored else tile.astype(NARROW)
        out[d, pair, c * g:(c + 1) * g, :e] = tile[:g]
        out[d, pair, c * g:(c + 1) * g, e:] = tile[g:]


def unpack_pair(tiles, blocks, pair, put):
    e, g = tiles.edge, tiles.rows
    for d, (a, b) in enumerate(tiles.above):
        put(a, b, blocks[d, pair, :, :e].astype(WIDE))
        put(b, a, blocks[d, pair, :, e:].astype(WIDE).T)
    for d, c, k in tiles.diagonal:
        upper = blocks[d, pair, c * g:(c + 1) * g, :e]
        lower = blocks[d, pair, c * g:(c + 1) * g, e:]
        put(k, k, jnp.concatenate([upper, lower], axis=0).astype(WIDE))


def to_distances(place, whole, outs):
    for k, out in enumerate(outs):
        out[...] = whole[place[1] ^ k]


def from_distances(place, pieces, whole):
    for k, piece in enumerate(pieces):
        whole[place[1] ^ k] = piece[...]


def pack_kernel(tiles, place, source, *refs):
    outs, whole = refs[:-1], refs[-1]
    for pair in range(source.shape[0]):
        pack_pair(tiles, source.at[pair], whole, pair, mirrored=True)
    to_distances(place, whole, outs)


def sort_kernel(tiles, groups, place, *refs):
    pieces, outs, whole = refs[:-2 * groups - 1], refs[-2 * groups - 1:-1], refs[-1]
    first = whole.shape[1]
    from_distances(place, pieces, whole)
    for s in range(groups):
        for u in range(first):
            block = whole[(place[0] ^ s) * first + u]
            for c in range(2):
                outs[c * groups + s][u] = block[:, c * tiles.rows:(c + 1) * tiles.rows]


def assemble(place, order, pieces, whole):
    k = 0
    for piece in pieces:
        count, rows, virtual = piece.shape[-3:]
        for block in range(piece.shape[0] if len(piece.shape) == 4 else 1):
            start = pl.multiple_of((place[1] ^ order[k]) * rows, rows)
            for single in range(count):
                values = piece[block, single] if len(piece.shape) == 4 else piece[single]
                whole[pl.ds(start, rows), single * virtual:(single + 1) * virtual] = values
            k += 1


def half_transform(matrix, whole, inner):
    virtual = matrix.shape[0]
    for single in range(whole.shape[1] // virtual):
        at = slice(single * virtual, (single + 1) * virtual)
        inner[at, :] = lax.dot_general(
            matrix, whole[:, at], (((1,), (1,)), ((), ())), preferred_element_type=WIDE
        ).astype(NARROW)


def ladder_pair(matrix, whole, inner, total):
    half_transform(matrix, whole, inner)
    total[...] = jnp.dot(whole[...], inner[...], preferred_element_type=WIDE)


def inverse(x):
    guess = pl.reciprocal(x, approx=True)
    return guess * (2.0 - x * guess)


def first_ladder_kernel(tiles, order, place, source, *refs):
    pieces, (out, whole, inner, total) = refs[:-4], refs[-4:]
    assemble(place, order, pieces, whole)
    for pair in range(source.shape[0]):
        ladder_pair(source[pair].astype(NARROW), whole, inner, total)
        pack_pair(tiles, total, out, pair)


def second_ladder_kernel(tiles, first, place, occ, source, blocks, row, column, whole, out, inner, matrix):
    def put(a, b, tile):
        matrix[tiles.span(a), tiles.span(b)] = tile.astype(NARROW)

    unpack_pair(tiles, blocks, 0, put)
    half_transform(matrix[...], whole, inner)
    base = occ[place[0] * first + pl.program_id(0)] + occ[place[1]]
    half = matrix.shape[0] // 2
    for start in (0, half):
        at = slice(start, start + half)
        total = jnp.dot(whole[at, :], inner[...], preferred_element_type=WIDE)
        own = base - row[at, :1] - column[...]
        out[0, at, :] = source[0, at, :] + 2.0 * (matrix[at, :].astype(WIDE) + total * inverse(own))


def add_kernel(tiles, place, source, *refs):
    pieces, (out, whole) = refs[:-2], refs[-2:]
    from_distances(place, pieces, whole)

    def put(a, b, tile):
        here = (0, tiles.span(a), tiles.span(b))
        out[here] = source[here] + tile

    unpack_pair(tiles, whole, 0, put)


def mix(place, fock, first, load, store, rows):
    total = fock.shape[0]
    strips = rows // 16

    def strip(step, carry):
        u = step // strips
        at = pl.ds(pl.multiple_of(lax.rem(step, strips) * 16, 16), 16)
        taken = [load(k // first, u, k % first, at) for k in range(total)]
        for k in range(total):
            column = (place[0] ^ (k // first)) * first + k % first
            result = None
            for m in range(total):
                line = (place[0] ^ (m // first)) * first + m % first
                term = (-fock[line, column]) * taken[m]
                result = term if result is None else result + term
            store(k // first, u, k % first, column, at, result)
        return carry

    lax.fori_loop(0, first * strips, strip, 0)


def half_kernel(tiles, groups, first, chunk, place, fock, ladder, *refs):
    held, out = refs[:groups], refs[groups:]

    def load(s, u, r, at):
        return held[s][u, r, at, :].astype(WIDE)

    def store(s, u, w, column, at, result):
        rows = pl.ds(pl.multiple_of(chunk * tiles.rows + at.start, 16), at.size)
        out[s][u, w, at, :] = (ladder[column, u, rows, :].astype(WIDE) + result).astype(NARROW)

    mix(place, fock, first, load, store, tiles.rows)


def with_mirror(tiles, place, x, finish):
    across = place[1] < len(tiles.above)

    @pl.when(across)
    def _():
        finish(tiles.mirror_across(x).astype(WIDE))

    @pl.when(jnp.logical_not(across))
    def _():
        finish(tiles.mirror_within(x).astype(WIDE))


def update_kernel(tiles, groups, first, chunk, place, fock, occ, sums, *refs):
    before, refs = refs[:chunk], refs[chunk:]
    own, other, refs = refs[:groups], refs[groups:2 * groups], refs[2 * groups:]
    (sent, rest), out, (update, local_mixed) = refs[:2], refs[2:groups + 1], refs[groups + 1:]
    here = slice(chunk * tiles.rows, (chunk + 1) * tiles.rows)
    for ref in before:
        sent[:, :, :tiles.rows, :] = ref[...]

    def one(step, carry):
        u, w = step // first, lax.rem(step, first)
        for s in range(groups):
            column = (place[0] ^ s) * first + w
            base = occ[place[0] * first + u] + occ[column]

            def finish(mirrored):
                value = (own[s][u, w].astype(WIDE) + mirrored) * inverse(base - sums[here])
                update[u, s * first + w] = value
                sent[column, u, here] = value.astype(NARROW)

            with_mirror(tiles, place, other[s][w, u], finish)
        return carry

    lax.fori_loop(0, first * first, one, 0)

    def load(s, u, r, at):
        return update[u, s * first + r, at, :]

    def lost(value):
        return 2.0 * (value - value.astype(NARROW).astype(WIDE))

    def store(s, u, w, column, at, result):
        if s == 0:
            local_mixed[u, w, at, :] = result
            return
        out[s - 1][u, w, at, :] = result.astype(NARROW)
        strip = pl.ds(pl.multiple_of(chunk * tiles.rows + at.start, 16), at.size)
        base = occ[place[0] * first + u] + occ[column]
        share = result * inverse(base - sums[strip, :])
        rest[u, s * first + w, at, :] = (lost(update[u, s * first + w, at, :]) + share).astype(NARROW)

    mix(place, fock, first, load, store, tiles.rows)

    def within(step, carry):
        u, w = step // first, lax.rem(step, first)
        base = occ[place[0] * first + u] + occ[place[0] * first + w]

        def finish(mirrored):
            share = (local_mixed[u, w] + mirrored) * inverse(base - sums[here])
            rest[u, w] = (lost(update[u, w]) + share).astype(NARROW)

        with_mirror(tiles, place, local_mixed[w, u], finish)
        return carry

    lax.fori_loop(0, first * first, within, 0)


def rest_kernel(tiles, groups, first, chunk, place, occ, sums, rest, *refs):
    other, refs = refs[:groups - 1], refs[groups - 1:]
    out = refs[-1]
    here = slice(chunk * tiles.rows, (chunk + 1) * tiles.rows)
    there = here if chunk else slice(None)
    if chunk:
        out[:, :, :tiles.rows, :] = refs[0][...]

    def one(step, carry):
        u, w = step // first, lax.rem(step, first)
        out[place[0] * first + w, u, there] = rest[u, w]
        for s in range(1, groups):
            column = (place[0] ^ s) * first + w
            base = occ[place[0] * first + u] + occ[column]

            def finish(mirrored):
                value = rest[u, s * first + w].astype(WIDE) + mirrored * inverse(base - sums[here])
                out[column, u, there] = value.astype(NARROW)

            with_mirror(tiles, place, other[s - 1][w, u], finish)
        return carry

    lax.fori_loop(0, first * first, one, 0)
    if chunk:
        to_distances(place, out, refs[1:-1])


def exchange(blocks):
    return lax.all_to_all(blocks, "occj", split_axis=0, concat_axis=0, tiled=True)


def by_distance(parts):
    devices = len(parts)
    return [parts[0]] + [
        lax.ppermute(parts[k], "occj", [(d, d ^ k) for d in range(devices)])
        for k in range(devices - 1, 0, -1)
    ][::-1]


def across_first(parts, groups):
    return [parts[0]] + [
        lax.ppermute(parts[s], "occi", [(k, k ^ s) for k in range(groups)])
        for s in range(groups - 1, 0, -1)
    ][::-1]


def tie(x, *others):
    return lax.optimization_barrier((x, *others))[0]


def copy_kernel(source, out):
    for k in range(source.shape[0]):
        out[k] = source[k]


def after(x, *others):
    return pl.pallas_call(
        copy_kernel,
        out_shape=jax.ShapeDtypeStruct(x.shape, x.dtype),
        in_specs=[SMEM],
        out_specs=SMEM,
        cost_estimate=pl.CostEstimate(flops=LONG, bytes_accessed=8, transcendentals=0),
    )(tie(x, *others))


def gather_vectors(vectors, devices, packed):
    def turn(x, k):
        return lax.ppermute(x, "occj", [(d, d ^ k) for d in range(devices)])

    even = list(range(0, devices, 2))
    held = [vectors] + [turn(vectors, k) for k in even[1:]]
    other = turn(tie(jnp.stack(held), packed), 1)
    return [*held, other], even + [k ^ 1 for k in even]


def virtual_sums(tiles, vir_energy, q):
    e, g = tiles.edge, tiles.rows
    n_above = len(tiles.above)
    first = jnp.array([a for a, _ in tiles.above] + list(range(0, tiles.n, 2)), jnp.int32)[q]
    second = jnp.array([b for _, b in tiles.above] + list(range(1, tiles.n, 2)), jnp.int32)[q]
    a = lax.dynamic_slice_in_dim(vir_energy, first * e, e)
    b = lax.dynamic_slice_in_dim(vir_energy, second * e, e)
    pair = a[:, None] + b[None, :]
    across = jnp.concatenate([pair, pair], axis=1)
    halves = [
        jnp.concatenate([t[:g, None] + t[None, :], t[g:, None] + t[None, :]], axis=1) for t in (a, b)
    ]
    return jnp.where(q < n_above, across, jnp.concatenate(halves, axis=0))


def local(groups, devices, amplitudes, vectors, occupied_fock_block, occ_energy, vir_energy):
    first, second, virtual = amplitudes.shape[:3]
    assert second == 1 and groups * first == devices
    assert groups & (groups - 1) == 0 and devices & (devices - 1) == 0
    tiles = Tiles(devices, virtual)
    edge = tiles.edge
    current = amplitudes.reshape(first, virtual, virtual)
    count = current.size
    fock = occupied_fock_block.astype(WIDE)
    p, q = lax.axis_index("occi"), lax.axis_index("occj")
    place = jnp.stack([p, q]).astype(jnp.int32)
    packed = jax.ShapeDtypeStruct((devices, first, edge, 2 * edge), NARROW)
    upper = jax.ShapeDtypeStruct((devices, first, tiles.rows, 2 * edge), NARROW)
    part = jax.ShapeDtypeStruct((first, first, tiles.rows, 2 * edge), NARROW)
    singles = vectors.shape[0]
    inner = pltpu.VMEM((singles * virtual, virtual), NARROW)
    square = pltpu.VMEM((virtual, virtual), WIDE)
    chunks = range(2)

    distant = jax.ShapeDtypeStruct((first, edge, 2 * edge), NARROW)
    blocks = pltpu.VMEM(packed.shape, NARROW)
    started = call(functools.partial(pack_kernel, tiles), [distant] * devices, [blocks], count, 6 * count,
                   place, current, specs=[SMEM, VMEM])
    pieces, order = gather_vectors(vectors, devices, started[0])
    held = by_distance(started)
    sums = virtual_sums(tiles, vir_energy, q)

    ladder_flops = first * singles * 4 * virtual**3
    ladder, whole = call(
        functools.partial(first_ladder_kernel, tiles, order),
        [packed, jax.ShapeDtypeStruct((virtual, singles * virtual), NARROW)], [inner, square],
        ladder_flops, 8 * count, place, current, *pieces, specs=[SMEM] + [VMEM] * (1 + len(pieces)),
    )
    parts = call(
        functools.partial(sort_kernel, tiles, groups), [part] * (2 * groups), [blocks], count, 4 * count,
        tie(place, ladder), *held, specs=[SMEM] + [VMEM] * devices,
    )
    mirror = [across_first(parts[c * groups:(c + 1) * groups], groups) for c in chunks]
    ladder = exchange(ladder)

    half, other = [], []
    for c in chunks:
        half.append(call(
            functools.partial(half_kernel, tiles, groups, first, c), [part] * groups, [],
            LONG, 6 * count, after(place, *mirror[c]) if c == 0 else place, fock, ladder, *mirror[c],
            specs=[SMEM] * 2 + [VMEM] * (groups + 1),
        ))
        other.append(across_first(half[c], groups))
    sent, rest, mixed = [], [], []
    for c in chunks:
        sent_one, rest_one, *mixed_one = call(
            functools.partial(update_kernel, tiles, groups, first, c),
            [(upper, packed)[c], jax.ShapeDtypeStruct((first, devices, *part.shape[2:]), NARROW)] + [part] * (groups - 1),
            [pltpu.VMEM((first, devices, *part.shape[2:]), WIDE), pltpu.VMEM(part.shape, WIDE)],
            LONG, 10 * count, place, fock, occ_energy, sums, *sent, *half[c], *other[c],
            specs=[SMEM] * 3 + [VMEM] * (2 * groups + 1 + c),
        )
        sent, rest, mixed = [sent_one], rest + [rest_one], mixed + [mixed_one]
    other = [across_first([None] + x, groups)[1:] for x in mixed]
    back = exchange(sent[0])
    def by_pair(*shape):
        return pl.BlockSpec((1, *shape), lambda pair: (pair, 0, 0))

    def all_pairs(*shape):
        return pl.BlockSpec(shape, lambda pair: (0, 0))

    base = pl.pallas_call(
        functools.partial(second_ladder_kernel, tiles, first),
        grid=(first,),
        out_shape=jax.ShapeDtypeStruct(current.shape, WIDE),
        in_specs=[
            SMEM, SMEM, by_pair(virtual, virtual),
            pl.BlockSpec((devices, 1, edge, 2 * edge), lambda pair: (0, pair, 0, 0)),
            all_pairs(virtual, 128), all_pairs(1, virtual), all_pairs(*whole.shape),
        ],
        out_specs=by_pair(virtual, virtual),
        scratch_shapes=[inner, pltpu.VMEM((virtual, virtual), NARROW)],
        compiler_params=PARAMS,
        cost_estimate=pl.CostEstimate(flops=ladder_flops, bytes_accessed=12 * count, transcendentals=0),
    )(place, occ_energy, current, back, jnp.broadcast_to(vir_energy[:, None], (virtual, 128)),
      vir_energy[None, :], whole)
    last = []
    for c in chunks:
        last = call(
            functools.partial(rest_kernel, tiles, groups, first, c),
            [distant] * devices if c else [upper], [blocks] if c else [],
            LONG, 8 * count, place, occ_energy, sums, rest[c], *other[c], *last,
            specs=[SMEM] * 2 + [VMEM] * (groups + 1 + c),
        )
    done = pl.pallas_call(
        functools.partial(add_kernel, tiles),
        grid=(first,),
        out_shape=jax.ShapeDtypeStruct(current.shape, WIDE),
        in_specs=[SMEM, by_pair(virtual, virtual)] + [by_pair(edge, 2 * edge)] * devices,
        out_specs=by_pair(virtual, virtual),
        scratch_shapes=[pltpu.VMEM((devices, 1, edge, 2 * edge), NARROW)],
        compiler_params=PARAMS,
        input_output_aliases={1: 0},
        cost_estimate=pl.CostEstimate(flops=count, bytes_accessed=10 * count, transcendentals=0),
    )(place, base, *by_distance(last))
    return done.reshape(amplitudes.shape)


def solution(mesh):
    sizes = (mesh.shape["occi"], mesh.shape["occj"])
    return jax.shard_map(
        functools.partial(local, *sizes),
        mesh=mesh,
        in_specs=(P("occi", "occj", None, None), P(None, "occj", None), P(), P(), P()),
        out_specs=P("occi", "occj", None, None),
        check_vma=False,
    )
```

```python
import functools
import math

import jax
import jax.numpy as jnp
from jax import lax
from jax.experimental import pallas as pl
from jax.experimental.pallas import tpu as pltpu
from jax.sharding import PartitionSpec as P

VMEM = pl.BlockSpec(memory_space=pltpu.VMEM)
SMEM = pl.BlockSpec(memory_space=pltpu.SMEM)
PARAMS = pltpu.CompilerParams(vmem_limit_bytes=50 * 2**20)
WIDE = jnp.float32
LONG = 3 * 10**10
NARROW = jnp.bfloat16


class Tiles:
    def __init__(self, devices, virtual):
        n = math.isqrt(2 * devices)
        assert n * n == 2 * devices and n % 2 == 0 and virtual % n == 0
        self.n = n
        self.edge = virtual // n
        self.rows = self.edge // 2
        self.above = [(a, b) for a in range(n) for b in range(a + 1, n)]
        self.diagonal = [(len(self.above) + k // 2, k % 2, k) for k in range(n)]

    def span(self, k):
        return slice(k * self.edge, (k + 1) * self.edge)

    def mirror_within(self, x):
        e, g = self.edge, self.rows
        tile = jnp.concatenate([x[:, :e], x[:, e:]], axis=0).T
        return jnp.concatenate([tile[:g], tile[g:]], axis=1)

    def mirror_across(self, x):
        return jnp.concatenate([x[:, self.edge:], x[:, :self.edge]], axis=1)


def call(body, outs, scratch, flops, moved, *operands, specs):
    return pl.pallas_call(
        body,
        out_shape=outs,
        in_specs=specs,
        out_specs=jax.tree.map(lambda _: VMEM, outs),
        scratch_shapes=scratch,
        compiler_params=PARAMS,
        cost_estimate=pl.CostEstimate(flops=flops, bytes_accessed=moved, transcendentals=0),
    )(*operands)


def pack_pair(tiles, source, out, pair, mirrored=False):
    e, g = tiles.edge, tiles.rows
    straight, turned = (slice(e, None), slice(0, e)) if mirrored else (slice(0, e), slice(e, None))
    for d, (a, b) in enumerate(tiles.above):
        out[d, pair, :, straight] = source[tiles.span(a), tiles.span(b)].astype(NARROW)
        out[d, pair, :, turned] = source[tiles.span(b), tiles.span(a)].astype(NARROW).T
    for d, c, k in tiles.diagonal:
        tile = source[tiles.span(k), tiles.span(k)]
        tile = tile.astype(NARROW).T if mirrored else tile.astype(NARROW)
        out[d, pair, c * g:(c + 1) * g, :e] = tile[:g]
        out[d, pair, c * g:(c + 1) * g, e:] = tile[g:]


def unpack_pair(tiles, blocks, pair, put):
    e, g = tiles.edge, tiles.rows
    for d, (a, b) in enumerate(tiles.above):
        put(a, b, blocks[d, pair, :, :e].astype(WIDE))
        put(b, a, blocks[d, pair, :, e:].T.astype(WIDE))
    for d, c, k in tiles.diagonal:
        upper = blocks[d, pair, c * g:(c + 1) * g, :e]
        lower = blocks[d, pair, c * g:(c + 1) * g, e:]
        put(k, k, jnp.concatenate([upper, lower], axis=0).astype(WIDE))


def to_distances(place, whole, outs):
    for k, out in enumerate(outs):
        out[...] = whole[place[1] ^ k]


def from_distances(place, pieces, whole):
    for k, piece in enumerate(pieces):
        whole[place[1] ^ k] = piece[...]


def pack_kernel(tiles, place, source, *refs):
    outs, whole = refs[:-1], refs[-1]
    for pair in range(source.shape[0]):
        pack_pair(tiles, source.at[pair], whole, pair, mirrored=True)
    to_distances(place, whole, outs)


def sort_kernel(tiles, groups, place, *refs):
    pieces, outs, whole = refs[:-2 * groups - 1], refs[-2 * groups - 1:-1], refs[-1]
    first = whole.shape[1]
    from_distances(place, pieces, whole)
    for s in range(groups):
        for u in range(first):
            block = whole[(place[0] ^ s) * first + u]
            for c in range(2):
                outs[c * groups + s][u] = block[:, c * tiles.rows:(c + 1) * tiles.rows]


def assemble(place, order, pieces, whole):
    k = 0
    for piece in pieces:
        count, rows, virtual = piece.shape[-3:]
        for block in range(piece.shape[0] if len(piece.shape) == 4 else 1):
            start = pl.multiple_of((place[1] ^ order[k]) * rows, rows)
            for single in range(count):
                values = piece[block, single] if len(piece.shape) == 4 else piece[single]
                whole[pl.ds(start, rows), single * virtual:(single + 1) * virtual] = values
            k += 1


def half_transform(matrix, whole, inner):
    virtual = matrix.shape[0]
    for single in range(whole.shape[1] // virtual):
        at = slice(single * virtual, (single + 1) * virtual)
        inner[at, :] = lax.dot_general(
            matrix, whole[:, at], (((1,), (1,)), ((), ())), preferred_element_type=WIDE
        ).astype(NARROW)


def ladder_pair(matrix, whole, inner, total):
    half_transform(matrix, whole, inner)
    total[...] = jnp.dot(whole[...], inner[...], preferred_element_type=WIDE)


def inverse(x):
    guess = pl.reciprocal(x, approx=True)
    return guess * (2.0 - x * guess)


def first_ladder_kernel(tiles, order, place, source, *refs):
    pieces, (out, whole, inner, total) = refs[:-4], refs[-4:]
    assemble(place, order, pieces, whole)
    for pair in range(source.shape[0]):
        ladder_pair(source[pair].astype(NARROW), whole, inner, total)
        pack_pair(tiles, total, out, pair)


def second_ladder_kernel(tiles, first, place, occ, source, blocks, row, column, whole, out, inner, matrix):
    def put(a, b, tile):
        matrix[tiles.span(a), tiles.span(b)] = tile.astype(NARROW)

    unpack_pair(tiles, blocks, 0, put)
    half_transform(matrix[...], whole, inner)
    base = occ[place[0] * first + pl.program_id(0)] + occ[place[1]]
    half = matrix.shape[0] // 2
    for start in (0, half):
        at = slice(start, start + half)
        total = jnp.dot(whole[at, :], inner[...], preferred_element_type=WIDE)
        own = base - row[at, :1] - column[...]
        out[0, at, :] = source[0, at, :] + 2.0 * (matrix[at, :].astype(WIDE) + total * inverse(own))


def add_kernel(tiles, place, source, *refs):
    pieces, (out, whole) = refs[:-2], refs[-2:]
    from_distances(place, pieces, whole)

    def put(a, b, tile):
        here = (0, tiles.span(a), tiles.span(b))
        out[here] = source[here] + tile

    unpack_pair(tiles, whole, 0, put)


def mix(place, fock, first, load, store, rows):
    total = fock.shape[0]
    strips = rows // 16

    def strip(step, carry):
        u = step // strips
        at = pl.ds(pl.multiple_of(lax.rem(step, strips) * 16, 16), 16)
        taken = [load(k // first, u, k % first, at) for k in range(total)]
        for k in range(total):
            column = (place[0] ^ (k // first)) * first + k % first
            result = None
            for m in range(total):
                line = (place[0] ^ (m // first)) * first + m % first
                term = (-fock[line, column]) * taken[m]
                result = term if result is None else result + term
            store(k // first, u, k % first, column, at, result)
        return carry

    lax.fori_loop(0, first * strips, strip, 0)


def half_kernel(tiles, groups, first, chunk, place, fock, ladder, *refs):
    held, out = refs[:groups], refs[groups:]

    def load(s, u, r, at):
        return held[s][u, r, at, :].astype(WIDE)

    def store(s, u, w, column, at, result):
        rows = pl.ds(pl.multiple_of(chunk * tiles.rows + at.start, 16), at.size)
        out[s][u, w, at, :] = (ladder[column, u, rows, :].astype(WIDE) + result).astype(NARROW)

    mix(place, fock, first, load, store, tiles.rows)


def with_mirror(tiles, place, x, finish):
    across = place[1] < len(tiles.above)

    @pl.when(across)
    def _():
        finish(tiles.mirror_across(x).astype(WIDE))

    @pl.when(jnp.logical_not(across))
    def _():
        finish(tiles.mirror_within(x).astype(WIDE))


def update_kernel(tiles, groups, first, chunk, place, fock, occ, sums, *refs):
    before, refs = refs[:chunk], refs[chunk:]
    own, other, refs = refs[:groups], refs[groups:2 * groups], refs[2 * groups:]
    (sent, rest), out, (update, local_mixed) = refs[:2], refs[2:groups + 1], refs[groups + 1:]
    here = slice(chunk * tiles.rows, (chunk + 1) * tiles.rows)
    for ref in before:
        sent[:, :, :tiles.rows, :] = ref[...]

    def one(step, carry):
        u, w = step // first, lax.rem(step, first)
        for s in range(groups):
            column = (place[0] ^ s) * first + w
            base = occ[place[0] * first + u] + occ[column]

            def finish(mirrored):
                value = (own[s][u, w].astype(WIDE) + mirrored) * inverse(base - sums[here])
                update[u, s * first + w] = value
                sent[column, u, here] = value.astype(NARROW)

            with_mirror(tiles, place, other[s][w, u], finish)
        return carry

    lax.fori_loop(0, first * first, one, 0)

    def load(s, u, r, at):
        return update[u, s * first + r, at, :]

    def lost(value):
        return 2.0 * (value - value.astype(NARROW).astype(WIDE))

    def store(s, u, w, column, at, result):
        if s == 0:
            local_mixed[u, w, at, :] = result
            return
        out[s - 1][u, w, at, :] = result.astype(NARROW)
        strip = pl.ds(pl.multiple_of(chunk * tiles.rows + at.start, 16), at.size)
        base = occ[place[0] * first + u] + occ[column]
        share = result * inverse(base - sums[strip, :])
        rest[u, s * first + w, at, :] = (lost(update[u, s * first + w, at, :]) + share).astype(NARROW)

    mix(place, fock, first, load, store, tiles.rows)

    def within(step, carry):
        u, w = step // first, lax.rem(step, first)
        base = occ[place[0] * first + u] + occ[place[0] * first + w]

        def finish(mirrored):
            share = (local_mixed[u, w] + mirrored) * inverse(base - sums[here])
            rest[u, w] = (lost(update[u, w]) + share).astype(NARROW)

        with_mirror(tiles, place, local_mixed[w, u], finish)
        return carry

    lax.fori_loop(0, first * first, within, 0)


def rest_kernel(tiles, groups, first, chunk, place, occ, sums, rest, *refs):
    other, refs = refs[:groups - 1], refs[groups - 1:]
    out = refs[-1]
    here = slice(chunk * tiles.rows, (chunk + 1) * tiles.rows)
    there = here if chunk else slice(None)
    if chunk:
        out[:, :, :tiles.rows, :] = refs[0][...]

    def one(step, carry):
        u, w = step // first, lax.rem(step, first)
        out[place[0] * first + w, u, there] = rest[u, w]
        for s in range(1, groups):
            column = (place[0] ^ s) * first + w
            base = occ[place[0] * first + u] + occ[column]

            def finish(mirrored):
                value = rest[u, s * first + w].astype(WIDE) + mirrored * inverse(base - sums[here])
                out[column, u, there] = value.astype(NARROW)

            with_mirror(tiles, place, other[s - 1][w, u], finish)
        return carry

    lax.fori_loop(0, first * first, one, 0)
    if chunk:
        to_distances(place, out, refs[1:-1])


def exchange(blocks):
    return lax.all_to_all(blocks, "occj", split_axis=0, concat_axis=0, tiled=True)


def by_distance(parts):
    devices = len(parts)
    return [parts[0]] + [
        lax.ppermute(parts[k], "occj", [(d, d ^ k) for d in range(devices)])
        for k in range(devices - 1, 0, -1)
    ][::-1]


def across_first(parts, groups):
    return [parts[0]] + [
        lax.ppermute(parts[s], "occi", [(k, k ^ s) for k in range(groups)])
        for s in range(groups - 1, 0, -1)
    ][::-1]


def tie(x, *others):
    return lax.optimization_barrier((x, *others))[0]


def copy_kernel(source, out):
    for k in range(source.shape[0]):
        out[k] = source[k]


def after(x, *others):
    return pl.pallas_call(
        copy_kernel,
        out_shape=jax.ShapeDtypeStruct(x.shape, x.dtype),
        in_specs=[SMEM],
        out_specs=SMEM,
        cost_estimate=pl.CostEstimate(flops=LONG, bytes_accessed=8, transcendentals=0),
    )(tie(x, *others))


def gather_vectors(vectors, devices, packed):
    def turn(x, k):
        return lax.ppermute(x, "occj", [(d, d ^ k) for d in range(devices)])

    even = list(range(0, devices, 2))
    held = [vectors] + [turn(vectors, k) for k in even[1:]]
    other = turn(tie(jnp.stack(held), packed), 1)
    return [*held, other], even + [k ^ 1 for k in even]


def virtual_sums(tiles, vir_energy, q):
    e, g = tiles.edge, tiles.rows
    n_above = len(tiles.above)
    first = jnp.array([a for a, _ in tiles.above] + list(range(0, tiles.n, 2)), jnp.int32)[q]
    second = jnp.array([b for _, b in tiles.above] + list(range(1, tiles.n, 2)), jnp.int32)[q]
    a = lax.dynamic_slice_in_dim(vir_energy, first * e, e)
    b = lax.dynamic_slice_in_dim(vir_energy, second * e, e)
    pair = a[:, None] + b[None, :]
    across = jnp.concatenate([pair, pair], axis=1)
    halves = [
        jnp.concatenate([t[:g, None] + t[None, :], t[g:, None] + t[None, :]], axis=1) for t in (a, b)
    ]
    return jnp.where(q < n_above, across, jnp.concatenate(halves, axis=0))


def local(groups, devices, amplitudes, vectors, occupied_fock_block, occ_energy, vir_energy):
    first, second, virtual = amplitudes.shape[:3]
    assert second == 1 and groups * first == devices
    assert groups & (groups - 1) == 0 and devices & (devices - 1) == 0
    tiles = Tiles(devices, virtual)
    edge = tiles.edge
    current = amplitudes.reshape(first, virtual, virtual)
    count = current.size
    fock = occupied_fock_block.astype(WIDE)
    p, q = lax.axis_index("occi"), lax.axis_index("occj")
    place = jnp.stack([p, q]).astype(jnp.int32)
    packed = jax.ShapeDtypeStruct((devices, first, edge, 2 * edge), NARROW)
    upper = jax.ShapeDtypeStruct((devices, first, tiles.rows, 2 * edge), NARROW)
    part = jax.ShapeDtypeStruct((first, first, tiles.rows, 2 * edge), NARROW)
    singles = vectors.shape[0]
    inner = pltpu.VMEM((singles * virtual, virtual), NARROW)
    square = pltpu.VMEM((virtual, virtual), WIDE)
    chunks = range(2)

    distant = jax.ShapeDtypeStruct((first, edge, 2 * edge), NARROW)
    blocks = pltpu.VMEM(packed.shape, NARROW)
    started = call(functools.partial(pack_kernel, tiles), [distant] * devices, [blocks], count, 6 * count,
                   place, current, specs=[SMEM, VMEM])
    pieces, order = gather_vectors(vectors, devices, started[0])
    held = by_distance(started)
    sums = virtual_sums(tiles, vir_energy, q)

    ladder_flops = first * singles * 4 * virtual**3
    ladder, whole = call(
        functools.partial(first_ladder_kernel, tiles, order),
        [packed, jax.ShapeDtypeStruct((virtual, singles * virtual), NARROW)], [inner, square],
        ladder_flops, 8 * count, place, current, *pieces, specs=[SMEM] + [VMEM] * (1 + len(pieces)),
    )
    parts = call(
        functools.partial(sort_kernel, tiles, groups), [part] * (2 * groups), [blocks], count, 4 * count,
        tie(place, ladder), *held, specs=[SMEM] + [VMEM] * devices,
    )
    mirror = [across_first(parts[c * groups:(c + 1) * groups], groups) for c in chunks]
    ladder = exchange(ladder)

    half, other = [], []
    for c in chunks:
        half.append(call(
            functools.partial(half_kernel, tiles, groups, first, c), [part] * groups, [],
            LONG, 6 * count, after(place, *mirror[c]) if c == 0 else place, fock, ladder, *mirror[c],
            specs=[SMEM] * 2 + [VMEM] * (groups + 1),
        ))
        other.append(across_first(half[c], groups))
    sent, rest, mixed = [], [], []
    for c in chunks:
        sent_one, rest_one, *mixed_one = call(
            functools.partial(update_kernel, tiles, groups, first, c),
            [(upper, packed)[c], jax.ShapeDtypeStruct((first, devices, *part.shape[2:]), NARROW)] + [part] * (groups - 1),
            [pltpu.VMEM((first, devices, *part.shape[2:]), WIDE), pltpu.VMEM(part.shape, WIDE)],
            LONG, 10 * count, place, fock, occ_energy, sums, *sent, *half[c], *other[c],
            specs=[SMEM] * 3 + [VMEM] * (2 * groups + 1 + c),
        )
        sent, rest, mixed = [sent_one], rest + [rest_one], mixed + [mixed_one]
    other = [across_first([None] + x, groups)[1:] for x in mixed]
    back = exchange(sent[0])
    def by_pair(*shape):
        return pl.BlockSpec((1, *shape), lambda pair: (pair, 0, 0))

    def all_pairs(*shape):
        return pl.BlockSpec(shape, lambda pair: (0, 0))

    base = pl.pallas_call(
        functools.partial(second_ladder_kernel, tiles, first),
        grid=(first,),
        out_shape=jax.ShapeDtypeStruct(current.shape, WIDE),
        in_specs=[
            SMEM, SMEM, by_pair(virtual, virtual),
            pl.BlockSpec((devices, 1, edge, 2 * edge), lambda pair: (0, pair, 0, 0)),
            all_pairs(virtual, 128), all_pairs(1, virtual), all_pairs(*whole.shape),
        ],
        out_specs=by_pair(virtual, virtual),
        scratch_shapes=[inner, pltpu.VMEM((virtual, virtual), NARROW)],
        compiler_params=PARAMS,
        cost_estimate=pl.CostEstimate(flops=ladder_flops, bytes_accessed=12 * count, transcendentals=0),
    )(place, occ_energy, current, back, jnp.broadcast_to(vir_energy[:, None], (virtual, 128)),
      vir_energy[None, :], whole)
    last = []
    for c in chunks:
        last = call(
            functools.partial(rest_kernel, tiles, groups, first, c),
            [distant] * devices if c else [upper], [blocks] if c else [],
            LONG, 8 * count, place, occ_energy, sums, rest[c], *other[c], *last,
            specs=[SMEM] * 2 + [VMEM] * (groups + 1 + c),
        )
    done = pl.pallas_call(
        functools.partial(add_kernel, tiles),
        grid=(first,),
        out_shape=jax.ShapeDtypeStruct(current.shape, WIDE),
        in_specs=[SMEM, by_pair(virtual, virtual)] + [by_pair(edge, 2 * edge)] * devices,
        out_specs=by_pair(virtual, virtual),
        scratch_shapes=[pltpu.VMEM((devices, 1, edge, 2 * edge), NARROW)],
        compiler_params=PARAMS,
        input_output_aliases={1: 0},
        cost_estimate=pl.CostEstimate(flops=count, bytes_accessed=10 * count, transcendentals=0),
    )(place, base, *by_distance(last))
    return done.reshape(amplitudes.shape)


def solution(mesh):
    sizes = (mesh.shape["occi"], mesh.shape["occj"])
    return jax.shard_map(
        functools.partial(local, *sizes),
        mesh=mesh,
        in_specs=(P("occi", "occj", None, None), P(None, "occj", None), P(), P(), P()),
        out_specs=P("occi", "occj", None, None),
        check_vma=False,
    )
```

```python
import functools
import math

import jax
import jax.numpy as jnp
from jax import lax
from jax.experimental import pallas as pl
from jax.experimental.pallas import tpu as pltpu
from jax.sharding import PartitionSpec as P

VMEM = pl.BlockSpec(memory_space=pltpu.VMEM)
SMEM = pl.BlockSpec(memory_space=pltpu.SMEM)
PARAMS = pltpu.CompilerParams(vmem_limit_bytes=50 * 2**20)
WIDE = jnp.float32
LONG = 3 * 10**10
NARROW = jnp.bfloat16


class Tiles:
    def __init__(self, devices, virtual):
        n = math.isqrt(2 * devices)
        assert n * n == 2 * devices and n % 2 == 0 and virtual % n == 0
        self.n = n
        self.edge = virtual // n
        self.rows = self.edge // 2
        self.above = [(a, b) for a in range(n) for b in range(a + 1, n)]
        self.diagonal = [(len(self.above) + k // 2, k % 2, k) for k in range(n)]

    def span(self, k):
        return slice(k * self.edge, (k + 1) * self.edge)

    def mirror_within(self, x):
        e, g = self.edge, self.rows
        tile = jnp.concatenate([x[:, :e], x[:, e:]], axis=0).T
        return jnp.concatenate([tile[:g], tile[g:]], axis=1)

    def mirror_across(self, x):
        return jnp.concatenate([x[:, self.edge:], x[:, :self.edge]], axis=1)


def call(body, outs, scratch, flops, moved, *operands, specs):
    return pl.pallas_call(
        body,
        out_shape=outs,
        in_specs=specs,
        out_specs=jax.tree.map(lambda _: VMEM, outs),
        scratch_shapes=scratch,
        compiler_params=PARAMS,
        cost_estimate=pl.CostEstimate(flops=flops, bytes_accessed=moved, transcendentals=0),
    )(*operands)


def pack_pair(tiles, source, out, pair, mirrored=False):
    e, g = tiles.edge, tiles.rows
    straight, turned = (slice(e, None), slice(0, e)) if mirrored else (slice(0, e), slice(e, None))
    for d, (a, b) in enumerate(tiles.above):
        out[d, pair, :, straight] = source[tiles.span(a), tiles.span(b)].astype(NARROW)
        out[d, pair, :, turned] = source[tiles.span(b), tiles.span(a)].astype(NARROW).T
    for d, c, k in tiles.diagonal:
        tile = source[tiles.span(k), tiles.span(k)]
        tile = tile.astype(NARROW).T if mirrored else tile.astype(NARROW)
        out[d, pair, c * g:(c + 1) * g, :e] = tile[:g]
        out[d, pair, c * g:(c + 1) * g, e:] = tile[g:]


def unpack_pair(tiles, blocks, pair, put):
    e, g = tiles.edge, tiles.rows
    for d, (a, b) in enumerate(tiles.above):
        put(a, b, blocks[d, pair, :, :e].astype(WIDE))
        put(b, a, blocks[d, pair, :, e:].T.astype(WIDE))
    for d, c, k in tiles.diagonal:
        upper = blocks[d, pair, c * g:(c + 1) * g, :e]
        lower = blocks[d, pair, c * g:(c + 1) * g, e:]
        put(k, k, jnp.concatenate([upper, lower], axis=0).astype(WIDE))


def to_distances(place, whole, outs):
    for k, out in enumerate(outs):
        out[...] = whole[place[1] ^ k]


def from_distances(place, pieces, whole):
    for k, piece in enumerate(pieces):
        whole[place[1] ^ k] = piece[...]


def pack_kernel(tiles, place, source, *refs):
    outs, whole = refs[:-1], refs[-1]
    for pair in range(source.shape[0]):
        pack_pair(tiles, source.at[pair], whole, pair, mirrored=True)
    to_distances(place, whole, outs)


def sort_kernel(tiles, groups, place, *refs):
    pieces, outs, whole = refs[:-2 * groups - 1], refs[-2 * groups - 1:-1], refs[-1]
    first = whole.shape[1]
    from_distances(place, pieces, whole)
    for s in range(groups):
        for u in range(first):
            block = whole[(place[0] ^ s) * first + u]
            for c in range(2):
                outs[c * groups + s][u] = block[:, c * tiles.rows:(c + 1) * tiles.rows]


def assemble(place, order, pieces, whole):
    k = 0
    for piece in pieces:
        count, rows, virtual = piece.shape[-3:]
        for block in range(piece.shape[0] if len(piece.shape) == 4 else 1):
            start = pl.multiple_of((place[1] ^ order[k]) * rows, rows)
            for single in range(count):
                values = piece[block, single] if len(piece.shape) == 4 else piece[single]
                whole[pl.ds(start, rows), single * virtual:(single + 1) * virtual] = values
            k += 1


def half_transform(matrix, whole, inner):
    virtual = matrix.shape[0]
    for single in range(whole.shape[1] // virtual):
        at = slice(single * virtual, (single + 1) * virtual)
        inner[at, :] = lax.dot_general(
            matrix, whole[:, at], (((1,), (1,)), ((), ())), preferred_element_type=WIDE
        ).astype(NARROW)


def ladder_pair(matrix, whole, inner, total):
    half_transform(matrix, whole, inner)
    total[...] = jnp.dot(whole[...], inner[...], preferred_element_type=WIDE)


def inverse(x):
    guess = pl.reciprocal(x, approx=True)
    return guess * (2.0 - x * guess)


def first_ladder_kernel(tiles, order, place, source, *refs):
    pieces, (out, whole, inner, total) = refs[:-4], refs[-4:]
    assemble(place, order, pieces, whole)
    for pair in range(source.shape[0]):
        ladder_pair(source[pair].astype(NARROW), whole, inner, total)
        pack_pair(tiles, total, out, pair)


def second_ladder_kernel(tiles, first, place, occ, source, blocks, row, column, whole, out, inner, matrix):
    def put(a, b, tile):
        matrix[tiles.span(a), tiles.span(b)] = tile.astype(NARROW)

    unpack_pair(tiles, blocks, 0, put)
    half_transform(matrix[...], whole, inner)
    base = occ[place[0] * first + pl.program_id(0)] + occ[place[1]]
    half = matrix.shape[0] // 2
    for start in (0, half):
        at = slice(start, start + half)
        total = jnp.dot(whole[at, :], inner[...], preferred_element_type=WIDE)
        own = base - row[at, :1] - column[...]
        out[0, at, :] = source[0, at, :] + 2.0 * (matrix[at, :].astype(WIDE) + total * inverse(own))


def add_kernel(tiles, place, source, *refs):
    pieces, (out, whole) = refs[:-2], refs[-2:]
    from_distances(place, pieces, whole)

    def put(a, b, tile):
        here = (0, tiles.span(a), tiles.span(b))
        out[here] = source[here] + tile

    unpack_pair(tiles, whole, 0, put)


def mix(place, fock, first, load, store, rows):
    total = fock.shape[0]
    strips = rows // 16

    def strip(step, carry):
        u = step // strips
        at = pl.ds(pl.multiple_of(lax.rem(step, strips) * 16, 16), 16)
        taken = [load(k // first, u, k % first, at) for k in range(total)]
        for k in range(total):
            column = (place[0] ^ (k // first)) * first + k % first
            result = None
            for m in range(total):
                line = (place[0] ^ (m // first)) * first + m % first
                term = (-fock[line, column]) * taken[m]
                result = term if result is None else result + term
            store(k // first, u, k % first, column, at, result)
        return carry

    lax.fori_loop(0, first * strips, strip, 0, unroll=2)


def half_kernel(tiles, groups, first, chunk, place, fock, ladder, *refs):
    held, out = refs[:groups], refs[groups:]

    def load(s, u, r, at):
        return held[s][u, r, at, :].astype(WIDE)

    def store(s, u, w, column, at, result):
        rows = pl.ds(pl.multiple_of(chunk * tiles.rows + at.start, 16), at.size)
        out[s][u, w, at, :] = (ladder[column, u, rows, :].astype(WIDE) + result).astype(NARROW)

    mix(place, fock, first, load, store, tiles.rows)


def with_mirror(tiles, place, x, finish):
    across = place[1] < len(tiles.above)

    @pl.when(across)
    def _():
        finish(tiles.mirror_across(x).astype(WIDE))

    @pl.when(jnp.logical_not(across))
    def _():
        finish(tiles.mirror_within(x).astype(WIDE))


def update_kernel(tiles, groups, first, chunk, place, fock, occ, sums, *refs):
    before, refs = refs[:chunk], refs[chunk:]
    own, other, refs = refs[:groups], refs[groups:2 * groups], refs[2 * groups:]
    (sent, rest), out, (update, local_mixed) = refs[:2], refs[2:groups + 1], refs[groups + 1:]
    here = slice(chunk * tiles.rows, (chunk + 1) * tiles.rows)
    for ref in before:
        sent[:, :, :tiles.rows, :] = ref[...]

    def one(step, carry):
        u, w = step // first, lax.rem(step, first)
        for s in range(groups):
            column = (place[0] ^ s) * first + w
            base = occ[place[0] * first + u] + occ[column]

            def finish(mirrored):
                value = (own[s][u, w].astype(WIDE) + mirrored) * inverse(base - sums[here])
                update[u, s * first + w] = value
                sent[column, u, here] = value.astype(NARROW)

            with_mirror(tiles, place, other[s][w, u], finish)
        return carry

    lax.fori_loop(0, first * first, one, 0)

    def load(s, u, r, at):
        return update[u, s * first + r, at, :]

    def lost(value):
        return 2.0 * (value - value.astype(NARROW).astype(WIDE))

    def store(s, u, w, column, at, result):
        if s == 0:
            local_mixed[u, w, at, :] = result
            return
        out[s - 1][u, w, at, :] = result.astype(NARROW)
        strip = pl.ds(pl.multiple_of(chunk * tiles.rows + at.start, 16), at.size)
        base = occ[place[0] * first + u] + occ[column]
        share = result * inverse(base - sums[strip, :])
        rest[u, s * first + w, at, :] = (lost(update[u, s * first + w, at, :]) + share).astype(NARROW)

    mix(place, fock, first, load, store, tiles.rows)

    def within(step, carry):
        u, w = step // first, lax.rem(step, first)
        base = occ[place[0] * first + u] + occ[place[0] * first + w]

        def finish(mirrored):
            share = (local_mixed[u, w] + mirrored) * inverse(base - sums[here])
            rest[u, w] = (lost(update[u, w]) + share).astype(NARROW)

        with_mirror(tiles, place, local_mixed[w, u], finish)
        return carry

    lax.fori_loop(0, first * first, within, 0)


def rest_kernel(tiles, groups, first, chunk, place, occ, sums, rest, *refs):
    other, refs = refs[:groups - 1], refs[groups - 1:]
    out = refs[-1]
    here = slice(chunk * tiles.rows, (chunk + 1) * tiles.rows)
    there = here if chunk else slice(None)
    if chunk:
        out[:, :, :tiles.rows, :] = refs[0][...]

    def one(step, carry):
        u, w = step // first, lax.rem(step, first)
        out[place[0] * first + w, u, there] = rest[u, w]
        for s in range(1, groups):
            column = (place[0] ^ s) * first + w
            base = occ[place[0] * first + u] + occ[column]

            def finish(mirrored):
                value = rest[u, s * first + w].astype(WIDE) + mirrored * inverse(base - sums[here])
                out[column, u, there] = value.astype(NARROW)

            with_mirror(tiles, place, other[s - 1][w, u], finish)
        return carry

    lax.fori_loop(0, first * first, one, 0)
    if chunk:
        to_distances(place, out, refs[1:-1])


def exchange(blocks):
    return lax.all_to_all(blocks, "occj", split_axis=0, concat_axis=0, tiled=True)


def by_distance(parts):
    devices = len(parts)
    return [parts[0]] + [
        lax.ppermute(parts[k], "occj", [(d, d ^ k) for d in range(devices)])
        for k in range(devices - 1, 0, -1)
    ][::-1]


def across_first(parts, groups):
    return [parts[0]] + [
        lax.ppermute(parts[s], "occi", [(k, k ^ s) for k in range(groups)])
        for s in range(groups - 1, 0, -1)
    ][::-1]


def tie(x, *others):
    return lax.optimization_barrier((x, *others))[0]


def copy_kernel(source, out):
    for k in range(source.shape[0]):
        out[k] = source[k]


def after(x, *others):
    return pl.pallas_call(
        copy_kernel,
        out_shape=jax.ShapeDtypeStruct(x.shape, x.dtype),
        in_specs=[SMEM],
        out_specs=SMEM,
        cost_estimate=pl.CostEstimate(flops=LONG, bytes_accessed=8, transcendentals=0),
    )(tie(x, *others))


def gather_vectors(vectors, devices, packed):
    def turn(x, k):
        return lax.ppermute(x, "occj", [(d, d ^ k) for d in range(devices)])

    even = list(range(0, devices, 2))
    held = [vectors] + [turn(vectors, k) for k in even[1:]]
    other = turn(tie(jnp.stack(held), packed), 1)
    return [*held, other], even + [k ^ 1 for k in even]


def virtual_sums(tiles, vir_energy, q):
    e, g = tiles.edge, tiles.rows
    n_above = len(tiles.above)
    first = jnp.array([a for a, _ in tiles.above] + list(range(0, tiles.n, 2)), jnp.int32)[q]
    second = jnp.array([b for _, b in tiles.above] + list(range(1, tiles.n, 2)), jnp.int32)[q]
    a = lax.dynamic_slice_in_dim(vir_energy, first * e, e)
    b = lax.dynamic_slice_in_dim(vir_energy, second * e, e)
    pair = a[:, None] + b[None, :]
    across = jnp.concatenate([pair, pair], axis=1)
    halves = [
        jnp.concatenate([t[:g, None] + t[None, :], t[g:, None] + t[None, :]], axis=1) for t in (a, b)
    ]
    return jnp.where(q < n_above, across, jnp.concatenate(halves, axis=0))


def local(groups, devices, amplitudes, vectors, occupied_fock_block, occ_energy, vir_energy):
    first, second, virtual = amplitudes.shape[:3]
    assert second == 1 and groups * first == devices
    assert groups & (groups - 1) == 0 and devices & (devices - 1) == 0
    tiles = Tiles(devices, virtual)
    edge = tiles.edge
    current = amplitudes.reshape(first, virtual, virtual)
    count = current.size
    fock = occupied_fock_block.astype(WIDE)
    p, q = lax.axis_index("occi"), lax.axis_index("occj")
    place = jnp.stack([p, q]).astype(jnp.int32)
    packed = jax.ShapeDtypeStruct((devices, first, edge, 2 * edge), NARROW)
    upper = jax.ShapeDtypeStruct((devices, first, tiles.rows, 2 * edge), NARROW)
    part = jax.ShapeDtypeStruct((first, first, tiles.rows, 2 * edge), NARROW)
    singles = vectors.shape[0]
    inner = pltpu.VMEM((singles * virtual, virtual), NARROW)
    square = pltpu.VMEM((virtual, virtual), WIDE)
    chunks = range(2)

    distant = jax.ShapeDtypeStruct((first, edge, 2 * edge), NARROW)
    blocks = pltpu.VMEM(packed.shape, NARROW)
    started = call(functools.partial(pack_kernel, tiles), [distant] * devices, [blocks], count, 6 * count,
                   place, current, specs=[SMEM, VMEM])
    pieces, order = gather_vectors(vectors, devices, started[0])
    held = by_distance(started)
    sums = virtual_sums(tiles, vir_energy, q)

    ladder_flops = first * singles * 4 * virtual**3
    ladder, whole = call(
        functools.partial(first_ladder_kernel, tiles, order),
        [packed, jax.ShapeDtypeStruct((virtual, singles * virtual), NARROW)], [inner, square],
        ladder_flops, 8 * count, place, current, *pieces, specs=[SMEM] + [VMEM] * (1 + len(pieces)),
    )
    parts = call(
        functools.partial(sort_kernel, tiles, groups), [part] * (2 * groups), [blocks], count, 4 * count,
        tie(place, ladder), *held, specs=[SMEM] + [VMEM] * devices,
    )
    mirror = [across_first(parts[c * groups:(c + 1) * groups], groups) for c in chunks]
    ladder = exchange(ladder)

    half, other = [], []
    for c in chunks:
        half.append(call(
            functools.partial(half_kernel, tiles, groups, first, c), [part] * groups, [],
            LONG, 6 * count, after(place, *mirror[c]) if c == 0 else place, fock, ladder, *mirror[c],
            specs=[SMEM] * 2 + [VMEM] * (groups + 1),
        ))
        other.append(across_first(half[c], groups))
    sent, rest, mixed = [], [], []
    for c in chunks:
        sent_one, rest_one, *mixed_one = call(
            functools.partial(update_kernel, tiles, groups, first, c),
            [(upper, packed)[c], jax.ShapeDtypeStruct((first, devices, *part.shape[2:]), NARROW)] + [part] * (groups - 1),
            [pltpu.VMEM((first, devices, *part.shape[2:]), WIDE), pltpu.VMEM(part.shape, WIDE)],
            LONG, 10 * count, place, fock, occ_energy, sums, *sent, *half[c], *other[c],
            specs=[SMEM] * 3 + [VMEM] * (2 * groups + 1 + c),
        )
        sent, rest, mixed = [sent_one], rest + [rest_one], mixed + [mixed_one]
    other = [across_first([None] + x, groups)[1:] for x in mixed]
    back = exchange(sent[0])
    def by_pair(*shape):
        return pl.BlockSpec((1, *shape), lambda pair: (pair, 0, 0))

    def all_pairs(*shape):
        return pl.BlockSpec(shape, lambda pair: (0, 0))

    base = pl.pallas_call(
        functools.partial(second_ladder_kernel, tiles, first),
        grid=(first,),
        out_shape=jax.ShapeDtypeStruct(current.shape, WIDE),
        in_specs=[
            SMEM, SMEM, by_pair(virtual, virtual),
            pl.BlockSpec((devices, 1, edge, 2 * edge), lambda pair: (0, pair, 0, 0)),
            all_pairs(virtual, 128), all_pairs(1, virtual), all_pairs(*whole.shape),
        ],
        out_specs=by_pair(virtual, virtual),
        scratch_shapes=[inner, pltpu.VMEM((virtual, virtual), NARROW)],
        compiler_params=PARAMS,
        cost_estimate=pl.CostEstimate(flops=ladder_flops, bytes_accessed=12 * count, transcendentals=0),
    )(place, occ_energy, current, back, jnp.broadcast_to(vir_energy[:, None], (virtual, 128)),
      vir_energy[None, :], whole)
    last = []
    for c in chunks:
        last = call(
            functools.partial(rest_kernel, tiles, groups, first, c),
            [distant] * devices if c else [upper], [blocks] if c else [],
            LONG, 8 * count, place, occ_energy, sums, rest[c], *other[c], *last,
            specs=[SMEM] * 2 + [VMEM] * (groups + 1 + c),
        )
    done = pl.pallas_call(
        functools.partial(add_kernel, tiles),
        grid=(first,),
        out_shape=jax.ShapeDtypeStruct(current.shape, WIDE),
        in_specs=[SMEM, by_pair(virtual, virtual)] + [by_pair(edge, 2 * edge)] * devices,
        out_specs=by_pair(virtual, virtual),
        scratch_shapes=[pltpu.VMEM((devices, 1, edge, 2 * edge), NARROW)],
        compiler_params=PARAMS,
        input_output_aliases={1: 0},
        cost_estimate=pl.CostEstimate(flops=count, bytes_accessed=10 * count, transcendentals=0),
    )(place, base, *by_distance(last))
    return done.reshape(amplitudes.shape)


def solution(mesh):
    sizes = (mesh.shape["occi"], mesh.shape["occj"])
    return jax.shard_map(
        functools.partial(local, *sizes),
        mesh=mesh,
        in_specs=(P("occi", "occj", None, None), P(None, "occj", None), P(), P(), P()),
        out_specs=P("occi", "occj", None, None),
        check_vma=False,
    )
```
